32 devices in a mesh: expert: 4 (over z), dp: 8 (over y, x, core).
Axes of the slice: x: 2, y: 2, z: 4, core: 2. Of those that a mesh axis runs over, the one named last changes fastest.
Arguments:
- tokens: bfloat16 [1024, 2048], P('dp'), may hold values from -6 to 6
- cotangent: bfloat16 [1024, 2048], P('dp'), may hold values from -6 to 6
- expert_ids: int32 [1024, 4], P('dp'), may hold values from 0 to 7, all different within a row; in each aligned block of 64 rows (0 to 63, 64 to 127, ...) at most 64 rows name the same one
- gate_probs: bfloat16 [1024, 4], P('dp'), may hold values from 0.049804688 to 0.29882812
- weights: bfloat16 [3, 1536, 4096], P(None, 'dp', 'expert'), may hold values from -0.125 to 0.125
- first_moment: bfloat16 [3, 1536, 4096], P(None, 'dp', 'expert'), may hold values from -4 to 4
- second_moment: bfloat16 [3, 1536, 4096], P(None, 'dp', 'expert'), may hold values from 0.099609375 to 1
Outputs:
- new_first: bfloat16 [3, 1536, 4096], P(None, 'dp', 'expert')
- new_second: bfloat16 [3, 1536, 4096], P(None, 'dp', 'expert')
- update: bfloat16 [3, 1536, 4096], P(None, 'dp', 'expert')
The draws below stay inside these ranges and needn't reach their ends.
Inputs may be any that keep to these rules, and one draw needn't show every extreme that they name: `expert_ids`: each token names 4 different experts. Split the tokens in order into aligned blocks of 64 tokens: within a block no expert is named by more than 64 tokens, and in every draw some expert is named by exactly 64 tokens of some block.
All inputs are finite; a program needn't handle non-finite values.
Results may differ from the reference program's by a relative error of at most 0.0068.
Values may be sent and summed in bfloat16 or wider, within the bound.
No kernel may reach another device: no remote copies, remote signals or barrier semaphores. Data moves between devices by JAX's collectives and lax.ppermute only.
A program may use at most 64 MiB of HBM per device.

```python
import math
import jax
import jax.numpy as jnp
import numpy as np
from jax import lax

D = 2048
FF = 384
TOK_DEV = 128
SLICES = 2
HS = 192
GROUPS = 1
PLACES = 8
EXPERTS = 8
TOP = 4
CAP = 64
TOKENS = 1024
N_EXPERT = 4


def steps_of(own_key, dims, split, low, high):
    loudness = 1.0
    for position, parts in split:
        steps = jax.random.uniform(jax.random.fold_in(jax.random.fold_in(own_key, 6), position), (parts,), jnp.float32, low / len(split), high / len(split))
        loudness = loudness * jnp.repeat(jnp.exp(steps), dims[position] // parts).reshape((-1,) + (1,) * (len(dims) - 1 - position))
    return loudness


def routed_block(rng, own, number, rows, number_of, top, most, lean):
    order = jax.random.permutation(rng, number_of)
    crowded, ordinary = load_shares(number_of, rows * top, most, lean, True), load_shares(number_of, rows * top, most, lean, False)
    places = jnp.arange(number_of)

    def named(sizes, turn):
        used = int((sizes > 0).sum())
        fixed = max(1, used // 4)
        passed = fixed + (places - fixed + turn * (used - fixed)) % max(1, number_of - fixed)
        return jnp.zeros((number_of,), jnp.int32).at[order[jnp.where(places < fixed, places, passed)]].set(jnp.asarray(sizes, jnp.int32))

    sizes = jnp.where(number % 4 == 0, named(crowded, number // 4), named(ordinary, number - number // 4 - 1))
    mixed = jax.random.permutation(jax.random.fold_in(own, 3), number_of)
    source_of, sink = mixed[0:number_of // 2 * 2:2], mixed[1:number_of // 2 * 2:2]
    margin = jnp.minimum(sizes[source_of] - 1, most - sizes[sink]) // 2
    margin = jnp.where((source_of == order[0]) | (sink == order[0]) | (sizes[sink] == 0), 0, jnp.maximum(margin, 0))
    passed = jax.random.randint(jax.random.fold_in(own, 4), (number_of // 2,), 0, 1 << 20) % (margin + 1)
    sizes = sizes.at[source_of].add(-passed).at[sink].add(passed)
    labels = jnp.searchsorted(jnp.cumsum(sizes), jnp.arange(rows * top), side="right").astype(jnp.int32)
    grid = labels.reshape(top, rows).T
    grid = grid[jax.random.permutation(jax.random.fold_in(own, 1), rows)]
    turn = jax.random.randint(jax.random.fold_in(own, 2), (rows, 1), 0, top)
    return jnp.take_along_axis(grid, (jnp.arange(top)[None, :] + turn) % top, axis=1)


def load_shares(amount, total, limit, slope, full):
    loads = [(1 << 20) // math.isqrt(rank ** slope) + 1 for rank in range(1, amount + 1)]
    largest = limit if full else min(limit, max(-(-total // amount), total * loads[0] // sum(loads)))
    least = 1 if total - largest >= amount - 1 else 0
    holding, surplus = [largest] + [least] * (amount - 1), total - largest - least * (amount - 1)
    while surplus > 0:
        free = [i for i in range(1, amount) if holding[i] < largest] or [i for i in range(1, amount) if holding[i] < limit]
        mass, budget = sum([loads[i] for i in free]), surplus
        for i in free:
            extra = min(limit - holding[i], max(1, budget * loads[i] // mass), surplus)
            holding[i] = holding[i] + extra
            surplus = surplus - extra
    return np.array(holding)


def noise(key, dims, deviation, most, split=(), held_as=jnp.bfloat16):
    factor_of = steps_of(key, dims, split, -0.22, 0.18) if split else 1.0
    result = jax.random.normal(key, dims, jnp.float32) * deviation * factor_of
    return jnp.minimum(jnp.maximum(result, -most), most).astype(held_as)


def setup_inputs(seed: int = 0) -> dict:
    streams_of = jax.random.split(jax.random.key(seed), 8)
    tokens = noise(streams_of[0], (TOKENS, D), 1.0, 6.0, ((0, 8),))
    cotangent = noise(streams_of[1], (TOKENS, D), 1.0, 6.0, ((0, 8),))
    expert_ids_keys = jax.random.split(jax.random.fold_in(streams_of[2], 1), TOKENS // (TOK_DEV // 2))
    expert_ids_turns = jax.random.permutation(jax.random.fold_in(streams_of[2], 3), TOKENS // (TOK_DEV // 2))
    expert_ids = jax.vmap(lambda own, number: routed_block(jax.random.fold_in(streams_of[2], 2), own, number, TOK_DEV // 2, EXPERTS, TOP, CAP, 2))(expert_ids_keys, expert_ids_turns).reshape((TOKENS, TOP))
    gate_probs = jnp.clip(0.049804688 + 0.24902344 * jax.random.uniform(streams_of[3], (TOKENS, TOP), jnp.float32) ** steps_of(streams_of[3], (TOKENS, TOP), ((0, 8),), -0.2, 0.2), 0.049804688, 0.29882812).astype(jnp.bfloat16)
    weights = noise(streams_of[4], (3, PLACES * HS, N_EXPERT * (D // 2)), D ** -0.5, 0.125, ((1, 8), (2, 4)))
    first_moment = noise(streams_of[5], (3, PLACES * HS, N_EXPERT * (D // 2)), 1.0, 4.0, ((1, 8), (2, 4)))
    second_moment = jnp.clip(jnp.exp(math.log(1.0) - 2.306499 * jax.random.uniform(streams_of[6], (3, PLACES * HS, N_EXPERT * (D // 2)), jnp.float32) ** steps_of(streams_of[6], (3, PLACES * HS, N_EXPERT * (D // 2)), ((1, 8), (2, 4)), -0.2, 0.2)), 0.099609375, 1.0).astype(jnp.bfloat16)
    return dict(tokens=tokens, cotangent=cotangent, expert_ids=expert_ids, gate_probs=gate_probs, weights=weights, first_moment=first_moment, second_moment=second_moment)


beta_one = 0.9
beta_two = 0.95
step_count = 10
epsilon = 1e-08

def unpack(array):
    shaped = array.reshape(3, PLACES, HS, GROUPS, SLICES, 2, D // 2)
    shaped = jnp.transpose(shaped, (3, 1, 0, 4, 2, 5, 6))
    return shaped.reshape(EXPERTS, 3, FF, D)

def pack(array):
    shaped = array.reshape(GROUPS, PLACES, 3, SLICES, HS, 2, D // 2)
    shaped = jnp.transpose(shaped, (2, 1, 4, 0, 3, 5, 6))
    return shaped.reshape(3, PLACES * HS, GROUPS * SLICES * 2 * (D // 2))

def contract_last(left, right):
    return lax.dot_general(left, right, (((1,), (1,)), ((), ())), preferred_element_type=jnp.float32)

def contract_first(left, right):
    return lax.dot_general(left, right, (((0,), (0,)), ((), ())), preferred_element_type=jnp.float32)

def reference(tokens, cotangent, expert_ids, gate_probs, weights, first_moment, second_moment):
    half = TOK_DEV // 2
    blocks = TOKENS // half
    slots = blocks * CAP
    token_index = jnp.arange(TOKENS, dtype=jnp.int32)
    block_of = token_index // half
    padded_tokens = jnp.concatenate([tokens, jnp.zeros((1, D), tokens.dtype)], 0)
    padded_cot = jnp.concatenate([cotangent, jnp.zeros((1, D), cotangent.dtype)], 0)
    gates_float = gate_probs.astype(jnp.float32)

    def one_expert(packed):
        expert, mats, first, second = packed
        hit = expert_ids == expert
        member = lax.optimization_barrier(jnp.sum(hit.astype(jnp.int32), axis=1))
        gate = lax.optimization_barrier(jnp.sum(jnp.where(hit, gates_float, jnp.float32(0.0)), axis=1))
        member_blocks = member.reshape(blocks, half)
        rank = (jnp.cumsum(member_blocks, axis=1) - member_blocks).reshape(-1)
        slot = jnp.where(member == 1, block_of * CAP + rank, slots).astype(jnp.int32)
        table = jnp.full((slots,), TOKENS, jnp.int32).at[slot].set(token_index, mode='drop')
        rows = padded_tokens[table]
        cots = padded_cot[table]
        weight_rows = jnp.concatenate([gate, jnp.zeros((1,), jnp.float32)], 0)[table]
        gate_w = mats[0]
        up_w = mats[1]
        down_w = mats[2]
        hg = contract_last(rows, gate_w)
        hu = contract_last(rows, up_w)
        sig = jax.nn.sigmoid(hg)
        act = (hg * sig * hu).astype(jnp.bfloat16)
        dz = (weight_rows[:, None] * cots.astype(jnp.float32)).astype(jnp.bfloat16)
        dact = contract_last(dz, down_w)
        dhg = (dact * hu * sig * (1.0 + hg * (1.0 - sig))).astype(jnp.bfloat16)
        dhu = (dact * hg * sig).astype(jnp.bfloat16)
        grad = jnp.stack([contract_first(dhg, rows), contract_first(dhu, rows), contract_first(act, dz)])
        moment_one = beta_one * first.astype(jnp.float32) + (1.0 - beta_one) * grad
        moment_two = beta_two * second.astype(jnp.float32) + (1.0 - beta_two) * grad * grad
        step = moment_one / (1.0 - beta_one ** step_count) / (jnp.sqrt(moment_two / (1.0 - beta_two ** step_count)) + epsilon)
        return (moment_one.astype(jnp.bfloat16), moment_two.astype(jnp.bfloat16), step.astype(jnp.bfloat16))
    experts = jnp.arange(EXPERTS, dtype=jnp.int32)
    outs = lax.map(one_expert, (experts, unpack(weights), unpack(first_moment), unpack(second_moment)))
    return (pack(outs[0]), pack(outs[1]), pack(outs[2]))
```

```python
import functools

import jax
import jax.numpy as jnp
from jax import lax
from jax.experimental import pallas as pl
from jax.experimental.pallas import tpu as pltpu
from jax.sharding import PartitionSpec as P

beta_one = 0.9
beta_two = 0.95
step_count = 10
epsilon = 1e-08


def from_partner(value, axis, distance):
    mask = 2**distance
    pairs = [(source, source ^ mask) for source in range(lax.axis_size(axis))]
    return lax.ppermute(value, axis, pairs)


def contract_last(left, right):
    return lax.dot_general(
        left, right, (((1,), (1,)), ((), ())), preferred_element_type=jnp.float32
    )


def contract_first(left, right):
    return lax.dot_general(
        left, right, (((0,), (0,)), ((), ())), preferred_element_type=jnp.float32
    )


def split_halves(grad, replica, width_half):
    keep = lax.dynamic_slice_in_dim(grad, replica * width_half, width_half, grad.ndim - 1)
    give = lax.dynamic_slice_in_dim(grad, (1 - replica) * width_half, width_half, grad.ndim - 1)
    return (keep, give)


def route_block(block_ids, block_gates, group, n_data, capacity):
    count = block_ids.shape[0]
    top = block_ids.shape[1]
    target = block_ids - group * n_data
    inside = block_ids // n_data == group
    onehot = (
        (target[:, :, None] == jnp.arange(n_data, dtype=jnp.int32)[None, None, :])
        & inside[:, :, None]
    ).astype(jnp.int32)
    per_token = jnp.sum(onehot, axis=1)
    earlier = jnp.cumsum(per_token, axis=0) - per_token
    rank = jnp.sum(onehot * earlier[:, None, :], axis=2)
    total_slots = n_data * capacity
    slot = jnp.where(inside, target * capacity + rank, total_slots).reshape(-1)
    token_of = jnp.broadcast_to(jnp.arange(count, dtype=jnp.int32)[:, None], (count, top)).reshape(
        -1
    )
    table = jnp.full((total_slots,), count, jnp.int32).at[slot].set(token_of, mode="drop")
    gate_slot = (
        jnp.zeros((total_slots,), jnp.bfloat16).at[slot].set(block_gates.reshape(-1), mode="drop")
    )
    return (table, gate_slot)


def routed_plan(tokens, cotangent, expert_ids, gate_probs, weights, first_moment, second_moment):
    n_expert = lax.axis_size("expert")
    n_data = lax.axis_size("dp")
    slices = min(4, n_expert // 2)
    place = lax.axis_index("expert")
    replica = place % 2
    group = place // (2 * slices)
    groups = n_expert // (2 * slices)
    experts_total = groups * n_data
    half = tokens.shape[0] // 2
    width_half = weights.shape[2]
    top = expert_ids.shape[1]
    capacity = max(2, 2 * half * top // experts_total)
    start = replica * half
    own_ids = lax.dynamic_slice_in_dim(expert_ids, start, half, 0)
    own_gates = lax.dynamic_slice_in_dim(gate_probs, start, half, 0)
    table, gate_slot = route_block(own_ids, own_gates, group, n_data, capacity)
    source_tokens = lax.dynamic_slice_in_dim(tokens, start, half, 0)
    source_cot = lax.dynamic_slice_in_dim(cotangent, start, half, 0)
    columns = source_tokens.shape[1]
    padded_tokens = jnp.concatenate([source_tokens, jnp.zeros((1, columns), jnp.bfloat16)], 0)
    padded_cot = jnp.concatenate([source_cot, jnp.zeros((1, columns), jnp.bfloat16)], 0)
    send_rows = padded_tokens[table].reshape(n_data, -1, columns)
    send_cot = padded_cot[table].reshape(n_data, -1, columns)
    send_gates = gate_slot.reshape(n_data, -1)
    rows_in, gates_in = (
        lax.all_to_all(send_rows, "dp", split_axis=0, concat_axis=0, tiled=True),
        lax.all_to_all(send_gates, "dp", split_axis=0, concat_axis=0, tiled=True),
    )
    rows = rows_in.reshape(-1, columns)
    gate_rows = gates_in.reshape(-1).astype(jnp.float32)
    partner = from_partner(weights, "expert", 0)
    lower = jnp.where(replica == 0, weights, partner)
    upper = jnp.where(replica == 0, partner, weights)
    full = jnp.concatenate([lower, upper], 2)
    hg = contract_last(rows, full[0])
    hu = contract_last(rows, full[1])
    sig = jax.nn.sigmoid(hg)
    act = (hg * sig * hu).astype(jnp.bfloat16)
    cot_in = lax.all_to_all(send_cot, "dp", split_axis=0, concat_axis=0, tiled=True)
    cots = cot_in.reshape(-1, columns)
    dz = (gate_rows[:, None] * cots.astype(jnp.float32)).astype(jnp.bfloat16)
    dact = contract_last(dz, full[2])
    grad_down = contract_first(act, dz)
    dhg = (dact * hu * sig * (1.0 + hg * (1.0 - sig))).astype(jnp.bfloat16)
    dhu = (dact * hg * sig).astype(jnp.bfloat16)
    grad_gate = contract_first(dhg, rows)
    grad_up = contract_first(dhu, rows)
    stacked = jnp.stack([grad_gate, grad_up, grad_down])
    keep, give = split_halves(stacked, replica, width_half)
    total = keep + from_partner(give, "expert", 0)
    moment_one = beta_one * first_moment.astype(jnp.float32) + (1.0 - beta_one) * total
    moment_two = beta_two * second_moment.astype(jnp.float32) + (1.0 - beta_two) * total * total
    step = (
        moment_one
        / (1.0 - beta_one**step_count)
        / (jnp.sqrt(moment_two / (1.0 - beta_two**step_count)) + epsilon)
    )
    return (
        moment_one.astype(jnp.bfloat16),
        moment_two.astype(jnp.bfloat16),
        step.astype(jnp.bfloat16),
    )


VMEM_LIMIT = 48 * 1024 * 1024


def params():
    return pltpu.CompilerParams(vmem_limit_bytes=VMEM_LIMIT)


def cost(flops, moved):
    return pl.CostEstimate(flops=flops, bytes_accessed=moved, transcendentals=0)


def whole():
    return pl.BlockSpec(memory_space=pltpu.VMEM)


def pack_kernel(replica_ref, ids_ref, gates_ref, tokens_ref, cot_ref, x_ref, y_ref):
    count = tokens_ref.shape[0]
    x_ref[...] = tokens_ref[...]
    y_ref[0:count, :] = cot_ref[...]
    ids = ids_ref[...]
    gates = gates_ref[...].astype(jnp.float32)
    slots = y_ref.shape[0] - count
    row = lax.broadcasted_iota(jnp.int32, (slots, count), 0)
    gate = jnp.zeros((slots, count), jnp.float32)
    for k in range(ids.shape[0]):
        gate = gate + jnp.where(row == ids[k : k + 1, :], gates[k : k + 1, :], 0.0)
    y_ref[count:, :] = jnp.zeros((slots, y_ref.shape[1]), jnp.bfloat16)
    y_ref[count:, 0:count] = gate.astype(jnp.bfloat16)


def pack_own(replica, ids, gates, tokens, cotangent, width, slots):
    count, top = ids.shape
    column = lambda i, replica_ref: (0, replica_ref[0])
    start = lambda i, replica_ref: (0, 0)
    return pl.pallas_call(
        pack_kernel,
        grid_spec=pltpu.PrefetchScalarGridSpec(
            num_scalar_prefetch=1,
            grid=(1,),
            in_specs=[
                pl.BlockSpec((top, count), start),
                pl.BlockSpec((top, count), start),
                pl.BlockSpec((count, width), column),
                pl.BlockSpec((count, width), column),
            ],
            out_specs=[
                pl.BlockSpec((count, width), start),
                pl.BlockSpec((count + slots, width), start),
            ],
        ),
        out_shape=[
            jax.ShapeDtypeStruct((count, width), jnp.bfloat16),
            jax.ShapeDtypeStruct((count + slots, width), jnp.bfloat16),
        ],
        compiler_params=params(),
        cost_estimate=cost(1000, 8 * count * width),
    )(replica.reshape(1), ids.T, gates.T, tokens, cotangent)


def joined(refs, count):
    parts = [ref[0:count, :] for ref in refs]
    return parts[0] if len(parts) == 1 else jnp.concatenate(parts, 0)


def partial_kernel(n, first, last, count, w_ref, *refs):
    blocks, (own_ref, send_ref) = refs[:n], refs[n:]
    mats, hidden, width = w_ref.shape
    left = w_ref[first:last].reshape((last - first) * hidden, width)
    value = contract_last(left, joined(blocks, count))
    own_ref[...] = value
    send_ref[...] = value.astype(jnp.bfloat16)


def partials(weights, blocks, first, last, count):
    hidden, width = weights.shape[1:]
    shape = ((last - first) * hidden, count * len(blocks))
    return pl.pallas_call(
        functools.partial(partial_kernel, len(blocks), first, last, count),
        in_specs=[whole()] * (1 + len(blocks)),
        out_specs=[whole()] * 2,
        out_shape=[
            jax.ShapeDtypeStruct(shape, jnp.float32),
            jax.ShapeDtypeStruct(shape, jnp.bfloat16),
        ],
        compiler_params=params(),
        cost_estimate=cost(
            2 * shape[0] * shape[1] * width, 2 * (shape[0] + shape[1]) * width + 6 * shape[0] * shape[1]
        ),
    )(weights, *blocks)


def gate_row(expert_ref, y_refs, count):
    rows = []
    for ref in y_refs:
        held = ref[count:, 0:count].astype(jnp.float32)
        index = lax.broadcasted_iota(jnp.int32, held.shape, 0)
        rows.append(jnp.sum(jnp.where(index == expert_ref[0], held, 0.0), 0, keepdims=True))
    return rows[0] if len(rows) == 1 else jnp.concatenate(rows, 1)


def hidden_grads(gate, own_gu, got_gu, own_d, got_d):
    hidden = own_d.shape[0]
    gu = own_gu[...] + got_gu[...].astype(jnp.float32)
    hg, hu = gu[0:hidden], gu[hidden:]
    dact = gate * (own_d[...] + got_d[...].astype(jnp.float32))
    sig = jax.nn.sigmoid(hg)
    silu = hg * sig
    act = (gate * (silu * hu)).astype(jnp.bfloat16)
    dhg = (dact * hu * sig * (1.0 + hg * (1.0 - sig))).astype(jnp.bfloat16)
    dhu = (dact * silu).astype(jnp.bfloat16)
    return dhg, dhu, act


def plain(left, right):
    return lax.dot_general(
        left, right, (((1,), (0,)), ((), ())), preferred_element_type=jnp.float32
    )


def grad_kernel(n, count, has_acc, expert_ref, own_gu, got_gu, own_d, got_d, *refs):
    xs, ys = refs[:n], refs[n : 2 * n]
    out_ref = refs[-1]
    gate = gate_row(expert_ref, ys, count)
    dhg, dhu, act = hidden_grads(gate, own_gu, got_gu, own_d, got_d)
    x = joined(xs, count)
    y = joined(ys, count)
    for m, (left, right) in enumerate(((dhg, x), (dhu, x), (act, y))):
        value = plain(left, right)
        out_ref[m] = value + refs[2 * n][m] if has_acc else value


def smem():
    return pl.BlockSpec(memory_space=pltpu.SMEM)


def add_grads(expert, part, xs, ys, acc, count, width):
    n = len(xs)
    hidden = part[2].shape[0]
    shape = (3, hidden, width)
    operands = [expert, *part, *xs, *ys] + ([] if acc is None else [acc])
    return pl.pallas_call(
        functools.partial(grad_kernel, n, count, acc is not None),
        in_specs=[smem()] + [whole()] * (len(operands) - 1),
        out_specs=whole(),
        out_shape=jax.ShapeDtypeStruct(shape, jnp.float32),
        input_output_aliases={} if acc is None else {len(operands) - 1: 0},
        compiler_params=params(),
        cost_estimate=cost(6 * hidden * width * n * count, 8 * 3 * hidden * width),
    )(*operands)


def last_kernel(n, count, expert_ref, own_gu, got_gu, own_d, got_d, *refs):
    xs, ys = refs[:n], refs[n : 2 * n]
    acc_ref, first_ref, second_ref = refs[2 * n : 2 * n + 3]
    one_ref, two_ref, step_ref, left_ref = refs[2 * n + 3 :]
    m = pl.program_id(1)

    @pl.when((m == 0) & (pl.program_id(0) == 0))
    def _():
        gate = gate_row(expert_ref, ys, count)
        dhg, dhu, act = hidden_grads(gate, own_gu, got_gu, own_d, got_d)
        left_ref[0] = dhg
        left_ref[1] = dhu
        left_ref[2] = act

    def finish(right):
        grad = acc_ref[0] + plain(left_ref[m], right)
        moment_one = beta_one * first_ref[0].astype(jnp.float32) + (1.0 - beta_one) * grad
        moment_two = beta_two * second_ref[0].astype(jnp.float32) + (1.0 - beta_two) * grad * grad
        one_ref[0] = moment_one.astype(jnp.bfloat16)
        two_ref[0] = moment_two.astype(jnp.bfloat16)
        scaled = moment_two * (1.0 / (1.0 - beta_two**step_count))
        below = scaled * lax.rsqrt(scaled) + epsilon
        step = moment_one * (1.0 / (1.0 - beta_one**step_count)) / below
        step_ref[0] = step.astype(jnp.bfloat16)

    @pl.when(m < 2)
    def _():
        finish(joined(xs, count))

    @pl.when(m == 2)
    def _():
        finish(joined(ys, count))


def last_grads(expert, part, xs, ys, acc, first_moment, second_moment, count, columns):
    n = len(xs)
    mats, hidden, width = first_moment.shape
    tile = pl.BlockSpec((1, hidden, columns), lambda j, m: (m, 0, j))
    out = jax.ShapeDtypeStruct(first_moment.shape, jnp.bfloat16)
    flat = lambda value: pl.BlockSpec(value.shape, lambda j, m: (0, 0))
    strip = lambda value: pl.BlockSpec((value.shape[0], columns), lambda j, m: (0, j))
    gates_in = [flat(value) for value in part]
    return pl.pallas_call(
        functools.partial(last_kernel, n, count),
        grid=(width // columns, mats),
        in_specs=[smem()]
        + gates_in
        + [strip(value) for value in xs]
        + [strip(value) for value in ys]
        + [tile] * 3,
        out_specs=[tile] * 3,
        out_shape=[out] * 3,
        scratch_shapes=[pltpu.VMEM((mats, hidden, n * count), jnp.bfloat16)],
        compiler_params=params(),
        cost_estimate=cost(6 * hidden * width * n * count, 24 * hidden * width * mats),
    )(expert, *part, *xs, *ys, acc, first_moment, second_moment)


def from_masked(value, axis, mask):
    pairs = [(source, source ^ mask) for source in range(lax.axis_size(axis))]
    return lax.ppermute(value, axis, pairs)


def dense_plan(tokens, cotangent, expert_ids, gate_probs, weights, first_moment, second_moment):
    n_expert = lax.axis_size("expert")
    n_data = lax.axis_size("dp")
    slices = min(4, n_expert // 2)
    place = lax.axis_index("expert")
    replica = place % 2
    group = place // (2 * slices)
    groups = n_expert // (2 * slices)
    experts_total = groups * n_data
    expert = (group * n_data + lax.axis_index("dp")).astype(jnp.int32).reshape(1)
    count = tokens.shape[0]
    width = weights.shape[2]
    slots = -(-experts_total // 16) * 16
    x_own, y_own = pack_own(
        replica.astype(jnp.int32), expert_ids, gate_probs, tokens, cotangent, width, slots
    )
    xs = {0: x_own}
    ys = {0: y_own}
    far = [mask for mask in range(2, n_data, 2)]
    for mask in far:
        xs[mask] = from_masked(x_own, "dp", mask)
        ys[mask] = from_masked(y_own, "dp", mask)
    for mask in [0] + far:
        xs[mask + 1] = from_masked(xs[mask], "dp", 1)
        ys[mask + 1] = from_masked(ys[mask], "dp", 1)
    near = [mask for mask in far if mask & (mask - 1) == 0]
    rest = [mask for mask in far if mask & (mask - 1)]
    chunks = [[0, 1], [m + c for m in near for c in (0, 1)], [m + c for m in rest for c in (0, 1)]]
    chunks = [chunk for chunk in chunks if chunk]
    acc = None
    for number, chunk in enumerate(chunks):
        x_chunk = [xs[m] for m in chunk]
        y_chunk = [ys[m] for m in chunk]
        own_gu, send_gu = partials(weights, x_chunk, 0, 2, count)
        own_d, send_d = partials(weights, y_chunk, 2, 3, count)
        got_gu = from_masked(send_gu, "expert", 1)
        got_d = from_masked(send_d, "expert", 1)
        part = (own_gu, got_gu, own_d, got_d)
        if number < len(chunks) - 1:
            acc = add_grads(expert, part, x_chunk, y_chunk, acc, count, width)
    return tuple(
        last_grads(expert, part, x_chunk, y_chunk, acc, first_moment, second_moment, count, width // 2)
    )


def per_device(tokens, cotangent, expert_ids, gate_probs, weights, first_moment, second_moment):
    n_expert = lax.axis_size("expert")
    n_data = lax.axis_size("dp")
    slices = min(4, n_expert // 2)
    experts_total = n_expert // (2 * slices) * n_data
    half = tokens.shape[0] // 2
    dense = 2 * half * expert_ids.shape[1] // experts_total >= half
    plan = dense_plan if dense and n_data in (4, 8) else routed_plan
    return plan(
        tokens, cotangent, expert_ids, gate_probs, weights, first_moment, second_moment
    )


def solution(mesh):
    in_specs = (
        P("dp", None),
        P("dp", None),
        P("dp", None),
        P("dp", None),
        P(None, "dp", "expert"),
        P(None, "dp", "expert"),
        P(None, "dp", "expert"),
    )
    out_specs = (P(None, "dp", "expert"), P(None, "dp", "expert"), P(None, "dp", "expert"))
    return jax.shard_map(
        per_device, mesh=mesh, in_specs=in_specs, out_specs=out_specs, check_vma=False
    )
```

```python
import functools

import jax
import jax.numpy as jnp
from jax import lax
from jax.experimental import pallas as pl
from jax.experimental.pallas import tpu as pltpu
from jax.sharding import PartitionSpec as P

beta_one = 0.9
beta_two = 0.95
step_count = 10
epsilon = 1e-08


def from_partner(value, axis, distance):
    mask = 2**distance
    pairs = [(source, source ^ mask) for source in range(lax.axis_size(axis))]
    return lax.ppermute(value, axis, pairs)


def contract_last(left, right):
    return lax.dot_general(
        left, right, (((1,), (1,)), ((), ())), preferred_element_type=jnp.float32
    )


def contract_first(left, right):
    return lax.dot_general(
        left, right, (((0,), (0,)), ((), ())), preferred_element_type=jnp.float32
    )


def split_halves(grad, replica, width_half):
    keep = lax.dynamic_slice_in_dim(grad, replica * width_half, width_half, grad.ndim - 1)
    give = lax.dynamic_slice_in_dim(grad, (1 - replica) * width_half, width_half, grad.ndim - 1)
    return (keep, give)


def route_block(block_ids, block_gates, group, n_data, capacity):
    count = block_ids.shape[0]
    top = block_ids.shape[1]
    target = block_ids - group * n_data
    inside = block_ids // n_data == group
    onehot = (
        (target[:, :, None] == jnp.arange(n_data, dtype=jnp.int32)[None, None, :])
        & inside[:, :, None]
    ).astype(jnp.int32)
    per_token = jnp.sum(onehot, axis=1)
    earlier = jnp.cumsum(per_token, axis=0) - per_token
    rank = jnp.sum(onehot * earlier[:, None, :], axis=2)
    total_slots = n_data * capacity
    slot = jnp.where(inside, target * capacity + rank, total_slots).reshape(-1)
    token_of = jnp.broadcast_to(jnp.arange(count, dtype=jnp.int32)[:, None], (count, top)).reshape(
        -1
    )
    table = jnp.full((total_slots,), count, jnp.int32).at[slot].set(token_of, mode="drop")
    gate_slot = (
        jnp.zeros((total_slots,), jnp.bfloat16).at[slot].set(block_gates.reshape(-1), mode="drop")
    )
    return (table, gate_slot)


def routed_plan(tokens, cotangent, expert_ids, gate_probs, weights, first_moment, second_moment):
    n_expert = lax.axis_size("expert")
    n_data = lax.axis_size("dp")
    slices = min(4, n_expert // 2)
    place = lax.axis_index("expert")
    replica = place % 2
    group = place // (2 * slices)
    groups = n_expert // (2 * slices)
    experts_total = groups * n_data
    half = tokens.shape[0] // 2
    width_half = weights.shape[2]
    top = expert_ids.shape[1]
    capacity = max(2, 2 * half * top // experts_total)
    start = replica * half
    own_ids = lax.dynamic_slice_in_dim(expert_ids, start, half, 0)
    own_gates = lax.dynamic_slice_in_dim(gate_probs, start, half, 0)
    table, gate_slot = route_block(own_ids, own_gates, group, n_data, capacity)
    source_tokens = lax.dynamic_slice_in_dim(tokens, start, half, 0)
    source_cot = lax.dynamic_slice_in_dim(cotangent, start, half, 0)
    columns = source_tokens.shape[1]
    padded_tokens = jnp.concatenate([source_tokens, jnp.zeros((1, columns), jnp.bfloat16)], 0)
    padded_cot = jnp.concatenate([source_cot, jnp.zeros((1, columns), jnp.bfloat16)], 0)
    send_rows = padded_tokens[table].reshape(n_data, -1, columns)
    send_cot = padded_cot[table].reshape(n_data, -1, columns)
    send_gates = gate_slot.reshape(n_data, -1)
    rows_in, gates_in = (
        lax.all_to_all(send_rows, "dp", split_axis=0, concat_axis=0, tiled=True),
        lax.all_to_all(send_gates, "dp", split_axis=0, concat_axis=0, tiled=True),
    )
    rows = rows_in.reshape(-1, columns)
    gate_rows = gates_in.reshape(-1).astype(jnp.float32)
    partner = from_partner(weights, "expert", 0)
    lower = jnp.where(replica == 0, weights, partner)
    upper = jnp.where(replica == 0, partner, weights)
    full = jnp.concatenate([lower, upper], 2)
    hg = contract_last(rows, full[0])
    hu = contract_last(rows, full[1])
    sig = jax.nn.sigmoid(hg)
    act = (hg * sig * hu).astype(jnp.bfloat16)
    cot_in = lax.all_to_all(send_cot, "dp", split_axis=0, concat_axis=0, tiled=True)
    cots = cot_in.reshape(-1, columns)
    dz = (gate_rows[:, None] * cots.astype(jnp.float32)).astype(jnp.bfloat16)
    dact = contract_last(dz, full[2])
    grad_down = contract_first(act, dz)
    dhg = (dact * hu * sig * (1.0 + hg * (1.0 - sig))).astype(jnp.bfloat16)
    dhu = (dact * hg * sig).astype(jnp.bfloat16)
    grad_gate = contract_first(dhg, rows)
    grad_up = contract_first(dhu, rows)
    stacked = jnp.stack([grad_gate, grad_up, grad_down])
    keep, give = split_halves(stacked, replica, width_half)
    total = keep + from_partner(give, "expert", 0)
    moment_one = beta_one * first_moment.astype(jnp.float32) + (1.0 - beta_one) * total
    moment_two = beta_two * second_moment.astype(jnp.float32) + (1.0 - beta_two) * total * total
    step = (
        moment_one
        / (1.0 - beta_one**step_count)
        / (jnp.sqrt(moment_two / (1.0 - beta_two**step_count)) + epsilon)
    )
    return (
        moment_one.astype(jnp.bfloat16),
        moment_two.astype(jnp.bfloat16),
        step.astype(jnp.bfloat16),
    )


VMEM_LIMIT = 16 * 1024 * 1024


def params():
    return pltpu.CompilerParams(vmem_limit_bytes=VMEM_LIMIT)


def cost(flops, moved):
    return pl.CostEstimate(flops=flops, bytes_accessed=moved, transcendentals=0)


def whole():
    return pl.BlockSpec(memory_space=pltpu.VMEM)


def in_hbm():
    return pl.BlockSpec(memory_space=pltpu.HBM)


def smem():
    return pl.BlockSpec(memory_space=pltpu.SMEM)


def pack_kernel(
    replica_ref, ids_hbm, gates_hbm, tokens_ref, cot_ref, out_ref, ids_ref, gates_ref, sems
):
    count = tokens_ref.shape[0]
    width = out_ref.shape[1]
    columns = pl.ds(pl.multiple_of(replica_ref[0] * width, width), width)
    copies = [
        pltpu.make_async_copy(ids_hbm, ids_ref, sems.at[0]),
        pltpu.make_async_copy(gates_hbm, gates_ref, sems.at[1]),
        pltpu.make_async_copy(tokens_ref.at[:, columns], out_ref.at[0:count, :], sems.at[2]),
        pltpu.make_async_copy(cot_ref.at[:, columns], out_ref.at[count : 2 * count, :], sems.at[3]),
    ]
    for copy in copies:
        copy.start()
    copies[0].wait()
    copies[1].wait()
    ids = ids_ref[...]
    gates = gates_ref[...].astype(jnp.float32)
    slots = out_ref.shape[0] - 2 * count
    row = lax.broadcasted_iota(jnp.int32, (slots, count), 0)
    gate = jnp.zeros((slots, count), jnp.float32)
    for k in range(ids.shape[0]):
        gate = gate + jnp.where(row == ids[k : k + 1, :], gates[k : k + 1, :], 0.0)
    out_ref[2 * count :, 0:count] = gate.astype(jnp.bfloat16)
    out_ref[2 * count :, count:] = jnp.zeros((slots, width - count), jnp.bfloat16)
    copies[2].wait()
    copies[3].wait()


def pack_own(replica, ids, gates, tokens, cotangent, width, slots):
    count, top = ids.shape
    return pl.pallas_call(
        pack_kernel,
        in_specs=[smem()] + [in_hbm()] * 4,
        out_specs=whole(),
        out_shape=jax.ShapeDtypeStruct((2 * count + slots, width), jnp.bfloat16),
        scratch_shapes=[
            pltpu.VMEM((top, count), ids.dtype),
            pltpu.VMEM((top, count), gates.dtype),
            pltpu.SemaphoreType.DMA((4,)),
        ],
        compiler_params=params(),
        cost_estimate=cost(1000, 8 * count * width),
    )(replica.reshape(1), ids.T, gates.T, tokens, cotangent)


def joined(refs, first, count):
    parts = [ref[first : first + count, :] for ref in refs]
    return parts[0] if len(parts) == 1 else jnp.concatenate(parts, 0)


def partial_kernel(n, count, w_ref, after_ref, *refs):
    blocks, (own_ref, send_ref, token_ref) = refs[:n], refs[n:]
    mats, hidden, width = w_ref.shape
    gu = contract_last(w_ref[0:2].reshape(2 * hidden, width), joined(blocks, 0, count))
    own_ref[0 : 2 * hidden] = gu
    send_ref[0 : 2 * hidden] = gu.astype(jnp.bfloat16)
    down = contract_last(w_ref[2], joined(blocks, count, count))
    own_ref[2 * hidden :] = down
    send_ref[2 * hidden :] = down.astype(jnp.bfloat16)
    token_ref[...] = jnp.zeros_like(token_ref)


def partials(weights, after, blocks, count):
    mats, hidden, width = weights.shape
    shape = (mats * hidden, count * len(blocks))
    return pl.pallas_call(
        functools.partial(partial_kernel, len(blocks), count),
        in_specs=[whole()] * (2 + len(blocks)),
        out_specs=[whole()] * 3,
        out_shape=[
            jax.ShapeDtypeStruct(shape, jnp.float32),
            jax.ShapeDtypeStruct(shape, jnp.bfloat16),
            jax.ShapeDtypeStruct((8, 128), jnp.float32),
        ],
        compiler_params=params(),
        cost_estimate=cost(2 * shape[0] * shape[1] * width, 6 * shape[0] * shape[1]),
    )(weights, after, *blocks)


def gate_row(expert_ref, blocks, count):
    rows = []
    for ref in blocks:
        held = ref[2 * count :, 0:count].astype(jnp.float32)
        index = lax.broadcasted_iota(jnp.int32, held.shape, 0)
        rows.append(jnp.sum(jnp.where(index == expert_ref[0], held, 0.0), 0, keepdims=True))
    return rows[0] if len(rows) == 1 else jnp.concatenate(rows, 1)


def hidden_grads(gate, own, got):
    total = own[...] + got[...].astype(jnp.float32)
    hidden = total.shape[0] // 3
    hg, hu = total[0:hidden], total[hidden : 2 * hidden]
    dact = gate * total[2 * hidden :]
    sig = jax.nn.sigmoid(hg)
    silu = hg * sig
    act = (gate * (silu * hu)).astype(jnp.bfloat16)
    dhg = (dact * hu * sig * (1.0 + hg * (1.0 - sig))).astype(jnp.bfloat16)
    dhu = (dact * silu).astype(jnp.bfloat16)
    return dhg, dhu, act


def plain(left, right):
    return lax.dot_general(
        left, right, (((1,), (0,)), ((), ())), preferred_element_type=jnp.float32
    )


def grad_kernel(n, count, has_acc, expert_ref, after_ref, own, got, *refs):
    blocks = refs[:n]
    out_ref, token_ref = refs[-2:]
    dhg, dhu, act = hidden_grads(gate_row(expert_ref, blocks, count), own, got)
    x = joined(blocks, 0, count)
    y = joined(blocks, count, count)
    for m, (left, right) in enumerate(((dhg, x), (dhu, x), (act, y))):
        value = plain(left, right)
        out_ref[m] = value + refs[n][m] if has_acc else value
    token_ref[...] = jnp.zeros_like(token_ref)


def add_grads(expert, after, own, got, blocks, acc, count):
    n = len(blocks)
    width = blocks[0].shape[1]
    shape = (3, own.shape[0] // 3, width)
    operands = [expert, after, own, got, *blocks] + ([] if acc is None else [acc])
    return pl.pallas_call(
        functools.partial(grad_kernel, n, count, acc is not None),
        in_specs=[smem()] + [whole()] * (len(operands) - 1),
        out_specs=[whole()] * 2,
        out_shape=[
            jax.ShapeDtypeStruct(shape, jnp.float32),
            jax.ShapeDtypeStruct((8, 128), jnp.float32),
        ],
        input_output_aliases={} if acc is None else {len(operands) - 1: 0},
        compiler_params=params(),
        cost_estimate=cost(2 * own.shape[0] * width * n * count, 8 * own.shape[0] * width),
    )(*operands)


def last_kernel(n, count, expert_ref, own, got, *refs):
    blocks = refs[:n]
    acc_ref, first_ref, second_ref, one_ref, two_ref, step_ref, left_ref = refs[n:]
    m = pl.program_id(1)

    @pl.when((m == 0) & (pl.program_id(0) == 0))
    def _():
        dhg, dhu, act = hidden_grads(gate_row(expert_ref, blocks, count), own, got)
        left_ref[0] = dhg
        left_ref[1] = dhu
        left_ref[2] = act

    def finish(right):
        grad = acc_ref[0] + plain(left_ref[m], right)
        moment_one = beta_one * first_ref[0].astype(jnp.float32) + (1.0 - beta_one) * grad
        moment_two = beta_two * second_ref[0].astype(jnp.float32) + (1.0 - beta_two) * grad * grad
        one_ref[0] = moment_one.astype(jnp.bfloat16)
        two_ref[0] = moment_two.astype(jnp.bfloat16)
        scaled = moment_two * (1.0 / (1.0 - beta_two**step_count))
        below = scaled * lax.rsqrt(scaled) + epsilon
        step = moment_one * (1.0 / (1.0 - beta_one**step_count)) / below
        step_ref[0] = step.astype(jnp.bfloat16)

    @pl.when(m < 2)
    def _():
        finish(joined(blocks, 0, count))

    @pl.when(m == 2)
    def _():
        finish(joined(blocks, count, count))


def last_grads(expert, own, got, blocks, acc, first_moment, second_moment, count, columns):
    n = len(blocks)
    mats, hidden, width = first_moment.shape
    tile = pl.BlockSpec((1, hidden, columns), lambda j, m: (m, 0, j))
    out = jax.ShapeDtypeStruct(first_moment.shape, jnp.bfloat16)
    strip = lambda value: pl.BlockSpec((value.shape[0], columns), lambda j, m: (0, j))
    return pl.pallas_call(
        functools.partial(last_kernel, n, count),
        grid=(width // columns, mats),
        in_specs=[smem(), whole(), whole()] + [strip(value) for value in blocks] + [tile] * 3,
        out_specs=[tile] * 3,
        out_shape=[out] * 3,
        scratch_shapes=[pltpu.VMEM((mats, hidden, n * count), jnp.bfloat16)],
        compiler_params=params(),
        cost_estimate=cost(6 * hidden * width * n * count, 24 * hidden * width * mats),
    )(expert, own, got, *blocks, acc, first_moment, second_moment)


def from_masked(value, axis, mask):
    pairs = [(source, source ^ mask) for source in range(lax.axis_size(axis))]
    return lax.ppermute(value, axis, pairs)


def dense_plan(tokens, cotangent, expert_ids, gate_probs, weights, first_moment, second_moment):
    n_data = lax.axis_size("dp")
    place = lax.axis_index("expert")
    core = lax.axis_index("dp") % 2
    slices = min(4, lax.axis_size("expert") // 2)
    expert = (place // (2 * slices) * n_data + lax.axis_index("dp")).astype(jnp.int32).reshape(1)
    experts_total = lax.axis_size("expert") // (2 * slices) * n_data
    count = tokens.shape[0]
    width = weights.shape[2]
    slots = -(-experts_total // 16) * 16
    own = pack_own(
        (place % 2).astype(jnp.int32), expert_ids, gate_probs, tokens, cotangent, width, slots
    )
    over_x = from_masked(own, "dp", 2)
    over_y = from_masked(own, "dp", 4)
    onward = [(p, p ^ 4 if p % 2 == 0 else p ^ 2) for p in range(n_data)]
    far = lax.ppermute(jnp.where(core == 0, over_x, over_y), "dp", onward)
    chunks = [
        [block for mine in group for block in (mine, from_masked(mine, "dp", 1))]
        for group in ([own], [over_x, over_y], [far])
    ]
    token = jnp.zeros((8, 128), jnp.float32)
    parts = []
    acc = None
    for number, blocks in enumerate(chunks):
        mine, send, token = partials(weights, token, blocks, count)
        parts.append((mine, from_masked(send, "expert", 1)))
        if number > 0:
            acc, token = add_grads(
                expert, token, *parts[number - 1], chunks[number - 1], acc, count
            )
    return tuple(
        last_grads(
            expert, *parts[-1], chunks[-1], acc, first_moment, second_moment, count, width // 2
        )
    )


def per_device(tokens, cotangent, expert_ids, gate_probs, weights, first_moment, second_moment):
    n_expert = lax.axis_size("expert")
    n_data = lax.axis_size("dp")
    slices = min(4, n_expert // 2)
    experts_total = n_expert // (2 * slices) * n_data
    half = tokens.shape[0] // 2
    dense = 2 * half * expert_ids.shape[1] // experts_total >= half
    plan = dense_plan if dense and n_data == 8 else routed_plan
    return plan(
        tokens, cotangent, expert_ids, gate_probs, weights, first_moment, second_moment
    )


def solution(mesh):
    in_specs = (
        P("dp", None),
        P("dp", None),
        P("dp", None),
        P("dp", None),
        P(None, "dp", "expert"),
        P(None, "dp", "expert"),
        P(None, "dp", "expert"),
    )
    out_specs = (P(None, "dp", "expert"), P(None, "dp", "expert"), P(None, "dp", "expert"))
    return jax.shard_map(
        per_device, mesh=mesh, in_specs=in_specs, out_specs=out_specs, check_vma=False
    )
```

```python
import functools

import jax
import jax.numpy as jnp
from jax import lax
from jax.experimental import pallas as pl
from jax.experimental.pallas import tpu as pltpu
from jax.sharding import PartitionSpec as P

beta_one = 0.9
beta_two = 0.95
step_count = 10
epsilon = 1e-08


def from_partner(value, axis, distance):
    mask = 2**distance
    pairs = [(source, source ^ mask) for source in range(lax.axis_size(axis))]
    return lax.ppermute(value, axis, pairs)


def contract_last(left, right):
    return lax.dot_general(
        left, right, (((1,), (1,)), ((), ())), preferred_element_type=jnp.float32
    )


def contract_first(left, right):
    return lax.dot_general(
        left, right, (((0,), (0,)), ((), ())), preferred_element_type=jnp.float32
    )


def split_halves(grad, replica, width_half):
    keep = lax.dynamic_slice_in_dim(grad, replica * width_half, width_half, grad.ndim - 1)
    give = lax.dynamic_slice_in_dim(grad, (1 - replica) * width_half, width_half, grad.ndim - 1)
    return (keep, give)


def route_block(block_ids, block_gates, group, n_data, capacity):
    count = block_ids.shape[0]
    top = block_ids.shape[1]
    target = block_ids - group * n_data
    inside = block_ids // n_data == group
    onehot = (
        (target[:, :, None] == jnp.arange(n_data, dtype=jnp.int32)[None, None, :])
        & inside[:, :, None]
    ).astype(jnp.int32)
    per_token = jnp.sum(onehot, axis=1)
    earlier = jnp.cumsum(per_token, axis=0) - per_token
    rank = jnp.sum(onehot * earlier[:, None, :], axis=2)
    total_slots = n_data * capacity
    slot = jnp.where(inside, target * capacity + rank, total_slots).reshape(-1)
    token_of = jnp.broadcast_to(jnp.arange(count, dtype=jnp.int32)[:, None], (count, top)).reshape(
        -1
    )
    table = jnp.full((total_slots,), count, jnp.int32).at[slot].set(token_of, mode="drop")
    gate_slot = (
        jnp.zeros((total_slots,), jnp.bfloat16).at[slot].set(block_gates.reshape(-1), mode="drop")
    )
    return (table, gate_slot)


def routed_plan(tokens, cotangent, expert_ids, gate_probs, weights, first_moment, second_moment):
    n_expert = lax.axis_size("expert")
    n_data = lax.axis_size("dp")
    slices = min(4, n_expert // 2)
    place = lax.axis_index("expert")
    replica = place % 2
    group = place // (2 * slices)
    groups = n_expert // (2 * slices)
    experts_total = groups * n_data
    half = tokens.shape[0] // 2
    width_half = weights.shape[2]
    top = expert_ids.shape[1]
    capacity = max(2, 2 * half * top // experts_total)
    start = replica * half
    own_ids = lax.dynamic_slice_in_dim(expert_ids, start, half, 0)
    own_gates = lax.dynamic_slice_in_dim(gate_probs, start, half, 0)
    table, gate_slot = route_block(own_ids, own_gates, group, n_data, capacity)
    source_tokens = lax.dynamic_slice_in_dim(tokens, start, half, 0)
    source_cot = lax.dynamic_slice_in_dim(cotangent, start, half, 0)
    columns = source_tokens.shape[1]
    padded_tokens = jnp.concatenate([source_tokens, jnp.zeros((1, columns), jnp.bfloat16)], 0)
    padded_cot = jnp.concatenate([source_cot, jnp.zeros((1, columns), jnp.bfloat16)], 0)
    send_rows = padded_tokens[table].reshape(n_data, -1, columns)
    send_cot = padded_cot[table].reshape(n_data, -1, columns)
    send_gates = gate_slot.reshape(n_data, -1)
    rows_in, gates_in = (
        lax.all_to_all(send_rows, "dp", split_axis=0, concat_axis=0, tiled=True),
        lax.all_to_all(send_gates, "dp", split_axis=0, concat_axis=0, tiled=True),
    )
    rows = rows_in.reshape(-1, columns)
    gate_rows = gates_in.reshape(-1).astype(jnp.float32)
    partner = from_partner(weights, "expert", 0)
    lower = jnp.where(replica == 0, weights, partner)
    upper = jnp.where(replica == 0, partner, weights)
    full = jnp.concatenate([lower, upper], 2)
    hg = contract_last(rows, full[0])
    hu = contract_last(rows, full[1])
    sig = jax.nn.sigmoid(hg)
    act = (hg * sig * hu).astype(jnp.bfloat16)
    cot_in = lax.all_to_all(send_cot, "dp", split_axis=0, concat_axis=0, tiled=True)
    cots = cot_in.reshape(-1, columns)
    dz = (gate_rows[:, None] * cots.astype(jnp.float32)).astype(jnp.bfloat16)
    dact = contract_last(dz, full[2])
    grad_down = contract_first(act, dz)
    dhg = (dact * hu * sig * (1.0 + hg * (1.0 - sig))).astype(jnp.bfloat16)
    dhu = (dact * hg * sig).astype(jnp.bfloat16)
    grad_gate = contract_first(dhg, rows)
    grad_up = contract_first(dhu, rows)
    stacked = jnp.stack([grad_gate, grad_up, grad_down])
    keep, give = split_halves(stacked, replica, width_half)
    total = keep + from_partner(give, "expert", 0)
    moment_one = beta_one * first_moment.astype(jnp.float32) + (1.0 - beta_one) * total
    moment_two = beta_two * second_moment.astype(jnp.float32) + (1.0 - beta_two) * total * total
    step = (
        moment_one
        / (1.0 - beta_one**step_count)
        / (jnp.sqrt(moment_two / (1.0 - beta_two**step_count)) + epsilon)
    )
    return (
        moment_one.astype(jnp.bfloat16),
        moment_two.astype(jnp.bfloat16),
        step.astype(jnp.bfloat16),
    )


VMEM_LIMIT = 16 * 1024 * 1024


def params():
    return pltpu.CompilerParams(vmem_limit_bytes=VMEM_LIMIT)


def cost(flops, moved):
    return pl.CostEstimate(flops=flops // 1, bytes_accessed=moved // 1, transcendentals=0)


def whole():
    return pl.BlockSpec(memory_space=pltpu.VMEM)


def in_hbm():
    return pl.BlockSpec(memory_space=pltpu.HBM)


def unread():
    return pl.BlockSpec(memory_space=pl.ANY)


def smem():
    return pl.BlockSpec(memory_space=pltpu.SMEM)


def keep_hbm(value):
    return pltpu.with_memory_space_constraint(value, pltpu.HBM)


def pack_kernel(
    replica_ref, ids_hbm, gates_hbm, tokens_ref, cot_ref, out_ref, ids_ref, gates_ref, sems
):
    count = tokens_ref.shape[0]
    width = out_ref.shape[1]
    columns = pl.ds(pl.multiple_of(replica_ref[0] * width, width), width)
    copies = [
        pltpu.make_async_copy(ids_hbm, ids_ref, sems.at[0]),
        pltpu.make_async_copy(gates_hbm, gates_ref, sems.at[1]),
        pltpu.make_async_copy(tokens_ref.at[:, columns], out_ref.at[0:count, :], sems.at[2]),
        pltpu.make_async_copy(cot_ref.at[:, columns], out_ref.at[count : 2 * count, :], sems.at[3]),
    ]
    for copy in copies:
        copy.start()
    copies[0].wait()
    copies[1].wait()
    ids = ids_ref[...]
    gates = gates_ref[...].astype(jnp.float32)
    slots = out_ref.shape[0] - 2 * count
    row = lax.broadcasted_iota(jnp.int32, (slots, count), 0)
    gate = jnp.zeros((slots, count), jnp.float32)
    for k in range(ids.shape[0]):
        gate = gate + jnp.where(row == ids[k : k + 1, :], gates[k : k + 1, :], 0.0)
    out_ref[2 * count :, 0:count] = gate.astype(jnp.bfloat16)
    out_ref[2 * count :, count:] = jnp.zeros((slots, width - count), jnp.bfloat16)
    copies[2].wait()
    copies[3].wait()


def pack_own(replica, ids, gates, tokens, cotangent, width, slots):
    count, top = ids.shape
    return pl.pallas_call(
        pack_kernel,
        in_specs=[smem()] + [in_hbm()] * 4,
        out_specs=whole(),
        out_shape=jax.ShapeDtypeStruct((2 * count + slots, width), jnp.bfloat16),
        scratch_shapes=[
            pltpu.VMEM((top, count), ids.dtype),
            pltpu.VMEM((top, count), gates.dtype),
            pltpu.SemaphoreType.DMA((4,)),
        ],
        compiler_params=params(),
        cost_estimate=cost(1000, 8 * count * width),
    )(replica.reshape(1), *[keep_hbm(value) for value in (ids.T, gates.T, tokens, cotangent)])


def views(refs, kinds, count):
    xs, ys = [], []
    for ref, kind in zip(refs, kinds):
        for part in [ref.at[0], ref.at[1]] if kind == "both" else [ref]:
            if kind == "x":
                xs.append(part)
            elif kind == "y":
                ys.append(part)
            else:
                xs.append(part.at[0:count, :])
                ys.append(part.at[count:, :])
    return xs, ys


def joined(refs, count):
    parts = [ref[0:count, :] for ref in refs]
    return parts[0] if len(parts) == 1 else jnp.concatenate(parts, 0)


def kinds_of(chunk):
    return tuple(kind for kind, value in chunk)


def values_of(chunk):
    return [value for kind, value in chunk]


def tokens_in(kinds, count):
    return count * sum({"xy": 1, "both": 2, "x": 1, "y": 0}[kind] for kind in kinds)


def partial_kernel(kinds, count, w_ref, after_ref, *refs):
    n = len(kinds)
    xs, ys = views(refs[:n], kinds, count)
    send_ref, token_ref = refs[n:]
    mats, hidden, width = w_ref.shape
    gu = contract_last(w_ref[0:2].reshape(2 * hidden, width), joined(xs, count))
    send_ref[0 : 2 * hidden, :] = gu.astype(jnp.bfloat16)
    down = contract_last(w_ref[2], joined(ys, count))
    send_ref[2 * hidden :, :] = down.astype(jnp.bfloat16)
    token_ref[...] = jnp.zeros_like(token_ref)


def partials(weights, after, chunk, count):
    mats, hidden, width = weights.shape
    kinds = kinds_of(chunk)
    shape = (mats * hidden, tokens_in(kinds, count))
    return pl.pallas_call(
        functools.partial(partial_kernel, kinds, count),
        in_specs=[whole(), unread()] + [whole()] * len(kinds),
        out_specs=[whole()] * 2,
        out_shape=[
            jax.ShapeDtypeStruct(shape, jnp.bfloat16),
            jax.ShapeDtypeStruct((8, 128), jnp.float32),
        ],
        compiler_params=params(),
        cost_estimate=cost(2 * shape[0] * shape[1] * width, 6 * shape[0] * shape[1]),
    )(weights, after, *values_of(chunk))


def gate_row(expert_ref, ys, count):
    rows = []
    for ref in ys:
        held = ref[count:, 0:count].astype(jnp.float32)
        index = lax.broadcasted_iota(jnp.int32, held.shape, 0)
        rows.append(jnp.sum(jnp.where(index == expert_ref[0], held, 0.0), 0, keepdims=True))
    return rows[0] if len(rows) == 1 else jnp.concatenate(rows, 1)


def hidden_grads(gate, own, got):
    total = own[...].astype(jnp.float32) + got[...].astype(jnp.float32)
    hidden = total.shape[0] // 3
    hg, hu = total[0:hidden], total[hidden : 2 * hidden]
    dact = gate * total[2 * hidden :]
    sig = jax.nn.sigmoid(hg)
    silu = hg * sig
    act = (gate * (silu * hu)).astype(jnp.bfloat16)
    dhg = (dact * hu * sig * (1.0 + hg * (1.0 - sig))).astype(jnp.bfloat16)
    dhu = (dact * silu).astype(jnp.bfloat16)
    return dhg, dhu, act


def plain(left, right):
    return lax.dot_general(
        left, right, (((1,), (0,)), ((), ())), preferred_element_type=jnp.float32
    )


def onward_kernel(kinds, count, core_ref, expert_ref, own, got, x_ref, y_ref, *refs):
    n = len(kinds)
    both_ref, out_ref, left_ref = refs[n:]
    both_ref[0] = x_ref[...]
    both_ref[1] = y_ref[...]

    @pl.when(core_ref[0] == 0)
    def _():
        out_ref[...] = x_ref[...]

    @pl.when(core_ref[0] != 0)
    def _():
        out_ref[...] = y_ref[...]

    xs, ys = views(refs[:n], kinds, count)
    for m, value in enumerate(hidden_grads(gate_row(expert_ref, ys, count), own, got)):
        left_ref[m] = value


def pick_onward(core, expert, own, got, over_x, over_y, chunk, count):
    kinds = kinds_of(chunk)
    return pl.pallas_call(
        functools.partial(onward_kernel, kinds, count),
        in_specs=[smem(), smem()] + [whole()] * (4 + len(kinds)),
        out_specs=[whole()] * 3,
        out_shape=[
            jax.ShapeDtypeStruct((2, *over_x.shape), over_x.dtype),
            jax.ShapeDtypeStruct(over_x.shape, over_x.dtype),
            jax.ShapeDtypeStruct((3, own.shape[0] // 3, own.shape[1]), jnp.bfloat16),
        ],
        compiler_params=params(),
        cost_estimate=cost(1000, 4 * over_x.size),
    )(core.reshape(1), expert, own, got, over_x, over_y, *values_of(chunk))


def pass_kernel(count, after_ref, in_ref, x_ref, y_ref):
    x_ref[...] = in_ref[0:count, :]
    y_ref[...] = in_ref[count:, :]


def passed_on(after, value, count):
    rows, width = value.shape
    return pl.pallas_call(
        functools.partial(pass_kernel, count),
        in_specs=[unread(), whole()],
        out_specs=[whole()] * 2,
        out_shape=[
            jax.ShapeDtypeStruct((count, width), value.dtype),
            jax.ShapeDtypeStruct((rows - count, width), value.dtype),
        ],
        compiler_params=params(),
        cost_estimate=cost(1000, 2 * value.size),
    )(after, value)


def first_kernel(kinds, count, after_ref, left_ref, *refs):
    n = len(kinds)
    xs, ys = views(refs[:n], kinds, count)
    out_ref, token_ref = refs[n:]
    x = joined(xs, count)
    out_ref[0] = plain(left_ref[0], x)
    out_ref[1] = plain(left_ref[1], x)
    out_ref[2] = plain(left_ref[2], joined(ys, count))
    token_ref[...] = jnp.zeros_like(token_ref)


def first_grads(after, left, chunk, count):
    kinds = kinds_of(chunk)
    mats, hidden, tokens = left.shape
    width = chunk[0][1].shape[-1]
    return pl.pallas_call(
        functools.partial(first_kernel, kinds, count),
        in_specs=[unread()] + [whole()] * (1 + len(kinds)),
        out_specs=[whole()] * 2,
        out_shape=[
            jax.ShapeDtypeStruct((mats, hidden, width), jnp.float32),
            jax.ShapeDtypeStruct((8, 128), jnp.float32),
        ],
        compiler_params=params(),
        cost_estimate=cost(6 * hidden * width * tokens, 12 * hidden * width),
    )(after, left, *values_of(chunk))


def grad_kernel(kinds, count, expert_ref, after_ref, own, got, *refs):
    n = len(kinds)
    xs, ys = views(refs[:n], kinds, count)
    acc_ref, out_ref, token_ref = refs[n:]
    dhg, dhu, act = hidden_grads(gate_row(expert_ref, ys, count), own, got)
    x = joined(xs, count)
    out_ref[0] = acc_ref[0] + plain(dhg, x)
    out_ref[1] = acc_ref[1] + plain(dhu, x)
    out_ref[2] = acc_ref[2] + plain(act, joined(ys, count))
    token_ref[...] = jnp.zeros_like(token_ref)


def add_grads(expert, after, own, got, chunk, acc, count):
    kinds = kinds_of(chunk)
    mats, hidden, width = acc.shape
    return pl.pallas_call(
        functools.partial(grad_kernel, kinds, count),
        in_specs=[smem(), unread()] + [whole()] * (3 + len(kinds)),
        out_specs=[whole()] * 2,
        out_shape=[
            jax.ShapeDtypeStruct(acc.shape, jnp.float32),
            jax.ShapeDtypeStruct((8, 128), jnp.float32),
        ],
        input_output_aliases={4 + len(kinds): 0},
        compiler_params=params(),
        cost_estimate=cost(2 * mats * hidden * width * own.shape[1], 8 * mats * hidden * width),
    )(expert, after, own, got, *values_of(chunk), acc)


def last_kernel(kinds, count, expert_ref, own, got, *refs):
    n = len(kinds)
    xs, ys = views(refs[:n], kinds, count)
    acc_ref, first_ref, second_ref, one_ref, two_ref, step_ref, left_ref = refs[n:]
    m = pl.program_id(1)

    @pl.when((m == 0) & (pl.program_id(0) == 0))
    def _():
        for k, value in enumerate(hidden_grads(gate_row(expert_ref, ys, count), own, got)):
            left_ref[k] = value

    def finish(right):
        grad = acc_ref[0] + plain(left_ref[m], right)
        moment_one = beta_one * first_ref[0].astype(jnp.float32) + (1.0 - beta_one) * grad
        moment_two = beta_two * second_ref[0].astype(jnp.float32) + (1.0 - beta_two) * (grad * grad)
        one_ref[0] = moment_one.astype(jnp.bfloat16)
        two_ref[0] = moment_two.astype(jnp.bfloat16)
        scaled = moment_two * (1.0 / (1.0 - beta_two**step_count))
        below = scaled * lax.rsqrt(scaled) + epsilon
        guess = pl.reciprocal(below, approx=True)
        inverse = guess * (2.0 - below * guess)
        step = moment_one * (1.0 / (1.0 - beta_one**step_count)) * inverse
        step_ref[0] = step.astype(jnp.bfloat16)

    @pl.when(m < 2)
    def _():
        finish(joined(xs, count))

    @pl.when(m == 2)
    def _():
        finish(joined(ys, count))


def last_grads(expert, own, got, chunk, acc, first_moment, second_moment, count, columns):
    kinds = kinds_of(chunk)
    blocks = values_of(chunk)
    mats, hidden, width = first_moment.shape
    tile = pl.BlockSpec((1, hidden, columns), lambda j, m: (m, 0, j))
    out = jax.ShapeDtypeStruct(first_moment.shape, jnp.bfloat16)
    strip = lambda value: pl.BlockSpec((value.shape[0], columns), lambda j, m: (0, j))
    return pl.pallas_call(
        functools.partial(last_kernel, kinds, count),
        grid=(width // columns, mats),
        in_specs=[smem(), whole(), whole()] + [strip(value) for value in blocks] + [tile] * 3,
        out_specs=[tile] * 3,
        out_shape=[out] * 3,
        scratch_shapes=[pltpu.VMEM((mats, hidden, own.shape[1]), jnp.bfloat16)],
        compiler_params=params(),
        cost_estimate=cost(
            2 * mats * hidden * width * own.shape[1], 8 * hidden * width * mats
        ),
    )(expert, own, got, *blocks, acc, first_moment, second_moment)


def from_masked(value, axis, mask):
    pairs = [(source, source ^ mask) for source in range(lax.axis_size(axis))]
    return lax.ppermute(value, axis, pairs)


def dense_plan(tokens, cotangent, expert_ids, gate_probs, weights, first_moment, second_moment):
    n_data = lax.axis_size("dp")
    place = lax.axis_index("expert")
    core = lax.axis_index("dp") % 2
    slices = min(4, lax.axis_size("expert") // 2)
    expert = (place // (2 * slices) * n_data + lax.axis_index("dp")).astype(jnp.int32).reshape(1)
    experts_total = lax.axis_size("expert") // (2 * slices) * n_data
    count = tokens.shape[0]
    width = weights.shape[2]
    slots = -(-experts_total // 16) * 16
    own = pack_own(
        (place % 2).astype(jnp.int32), expert_ids, gate_probs, tokens, cotangent, width, slots
    )
    over_x = from_masked(own, "dp", 2)
    over_y = from_masked(own, "dp", 4)
    first = [("xy", own), ("xy", from_masked(own, "dp", 1))]
    send, token = partials(weights, own, first, count)
    both, picked, left = pick_onward(
        core.astype(jnp.int32), expert, send, from_masked(send, "expert", 1), over_x, over_y, first, count
    )
    onward = [(p, p ^ 4 if p % 2 == 0 else p ^ 2) for p in range(n_data)]
    far = lax.ppermute(picked, "dp", onward)
    near = [("both", both), ("both", from_masked(both, "dp", 1))]
    acc, token = first_grads(picked, left, first, count)
    near_send, token = partials(weights, token, near, count)
    near_got = from_masked(near_send, "expert", 1)
    far_x, far_y = passed_on(token, far, count)
    final = [
        ("x", far_x),
        ("y", far_y),
        ("x", from_masked(far_x, "dp", 1)),
        ("y", from_masked(far_y, "dp", 1)),
    ]
    send, token = partials(weights, token, final, count)
    got = from_masked(send, "expert", 1)
    acc, token = add_grads(expert, token, near_send, near_got, near, acc, count)
    return tuple(
        last_grads(expert, send, got, final, acc, first_moment, second_moment, count, width // 2)
    )


def per_device(tokens, cotangent, expert_ids, gate_probs, weights, first_moment, second_moment):
    n_expert = lax.axis_size("expert")
    n_data = lax.axis_size("dp")
    slices = min(4, n_expert // 2)
    experts_total = n_expert // (2 * slices) * n_data
    half = tokens.shape[0] // 2
    dense = 2 * half * expert_ids.shape[1] // experts_total >= half
    plan = dense_plan if dense and n_data == 8 else routed_plan
    return plan(
        tokens, cotangent, expert_ids, gate_probs, weights, first_moment, second_moment
    )


def solution(mesh):
    in_specs = (
        P("dp", None),
        P("dp", None),
        P("dp", None),
        P("dp", None),
        P(None, "dp", "expert"),
        P(None, "dp", "expert"),
        P(None, "dp", "expert"),
    )
    out_specs = (P(None, "dp", "expert"), P(None, "dp", "expert"), P(None, "dp", "expert"))
    return jax.shard_map(
        per_device, mesh=mesh, in_specs=in_specs, out_specs=out_specs, check_vma=False
    )
```

```python
import functools

import jax
import jax.numpy as jnp
from jax import lax
from jax.experimental import pallas as pl
from jax.experimental.pallas import tpu as pltpu
from jax.sharding import PartitionSpec as P

beta_one = 0.9
beta_two = 0.95
step_count = 10
epsilon = 1e-08


def from_partner(value, axis, distance):
    mask = 2**distance
    pairs = [(source, source ^ mask) for source in range(lax.axis_size(axis))]
    return lax.ppermute(value, axis, pairs)


def contract_last(left, right):
    return lax.dot_general(
        left, right, (((1,), (1,)), ((), ())), preferred_element_type=jnp.float32
    )


def contract_first(left, right):
    return lax.dot_general(
        left, right, (((0,), (0,)), ((), ())), preferred_element_type=jnp.float32
    )


def split_halves(grad, replica, width_half):
    keep = lax.dynamic_slice_in_dim(grad, replica * width_half, width_half, grad.ndim - 1)
    give = lax.dynamic_slice_in_dim(grad, (1 - replica) * width_half, width_half, grad.ndim - 1)
    return (keep, give)


def route_block(block_ids, block_gates, group, n_data, capacity):
    count = block_ids.shape[0]
    top = block_ids.shape[1]
    target = block_ids - group * n_data
    inside = block_ids // n_data == group
    onehot = (
        (target[:, :, None] == jnp.arange(n_data, dtype=jnp.int32)[None, None, :])
        & inside[:, :, None]
    ).astype(jnp.int32)
    per_token = jnp.sum(onehot, axis=1)
    earlier = jnp.cumsum(per_token, axis=0) - per_token
    rank = jnp.sum(onehot * earlier[:, None, :], axis=2)
    total_slots = n_data * capacity
    slot = jnp.where(inside, target * capacity + rank, total_slots).reshape(-1)
    token_of = jnp.broadcast_to(jnp.arange(count, dtype=jnp.int32)[:, None], (count, top)).reshape(
        -1
    )
    table = jnp.full((total_slots,), count, jnp.int32).at[slot].set(token_of, mode="drop")
    gate_slot = (
        jnp.zeros((total_slots,), jnp.bfloat16).at[slot].set(block_gates.reshape(-1), mode="drop")
    )
    return (table, gate_slot)


def routed_plan(tokens, cotangent, expert_ids, gate_probs, weights, first_moment, second_moment):
    n_expert = lax.axis_size("expert")
    n_data = lax.axis_size("dp")
    slices = min(4, n_expert // 2)
    place = lax.axis_index("expert")
    replica = place % 2
    group = place // (2 * slices)
    groups = n_expert // (2 * slices)
    experts_total = groups * n_data
    half = tokens.shape[0] // 2
    width_half = weights.shape[2]
    top = expert_ids.shape[1]
    capacity = max(2, 2 * half * top // experts_total)
    start = replica * half
    own_ids = lax.dynamic_slice_in_dim(expert_ids, start, half, 0)
    own_gates = lax.dynamic_slice_in_dim(gate_probs, start, half, 0)
    table, gate_slot = route_block(own_ids, own_gates, group, n_data, capacity)
    source_tokens = lax.dynamic_slice_in_dim(tokens, start, half, 0)
    source_cot = lax.dynamic_slice_in_dim(cotangent, start, half, 0)
    columns = source_tokens.shape[1]
    padded_tokens = jnp.concatenate([source_tokens, jnp.zeros((1, columns), jnp.bfloat16)], 0)
    padded_cot = jnp.concatenate([source_cot, jnp.zeros((1, columns), jnp.bfloat16)], 0)
    send_rows = padded_tokens[table].reshape(n_data, -1, columns)
    send_cot = padded_cot[table].reshape(n_data, -1, columns)
    send_gates = gate_slot.reshape(n_data, -1)
    rows_in, gates_in = (
        lax.all_to_all(send_rows, "dp", split_axis=0, concat_axis=0, tiled=True),
        lax.all_to_all(send_gates, "dp", split_axis=0, concat_axis=0, tiled=True),
    )
    rows = rows_in.reshape(-1, columns)
    gate_rows = gates_in.reshape(-1).astype(jnp.float32)
    partner = from_partner(weights, "expert", 0)
    lower = jnp.where(replica == 0, weights, partner)
    upper = jnp.where(replica == 0, partner, weights)
    full = jnp.concatenate([lower, upper], 2)
    hg = contract_last(rows, full[0])
    hu = contract_last(rows, full[1])
    sig = jax.nn.sigmoid(hg)
    act = (hg * sig * hu).astype(jnp.bfloat16)
    cot_in = lax.all_to_all(send_cot, "dp", split_axis=0, concat_axis=0, tiled=True)
    cots = cot_in.reshape(-1, columns)
    dz = (gate_rows[:, None] * cots.astype(jnp.float32)).astype(jnp.bfloat16)
    dact = contract_last(dz, full[2])
    grad_down = contract_first(act, dz)
    dhg = (dact * hu * sig * (1.0 + hg * (1.0 - sig))).astype(jnp.bfloat16)
    dhu = (dact * hg * sig).astype(jnp.bfloat16)
    grad_gate = contract_first(dhg, rows)
    grad_up = contract_first(dhu, rows)
    stacked = jnp.stack([grad_gate, grad_up, grad_down])
    keep, give = split_halves(stacked, replica, width_half)
    total = keep + from_partner(give, "expert", 0)
    moment_one = beta_one * first_moment.astype(jnp.float32) + (1.0 - beta_one) * total
    moment_two = beta_two * second_moment.astype(jnp.float32) + (1.0 - beta_two) * total * total
    step = (
        moment_one
        / (1.0 - beta_one**step_count)
        / (jnp.sqrt(moment_two / (1.0 - beta_two**step_count)) + epsilon)
    )
    return (
        moment_one.astype(jnp.bfloat16),
        moment_two.astype(jnp.bfloat16),
        step.astype(jnp.bfloat16),
    )


VMEM_LIMIT = 16 * 1024 * 1024


def params():
    return pltpu.CompilerParams(vmem_limit_bytes=VMEM_LIMIT)


def cost(flops, moved):
    return pl.CostEstimate(flops=flops, bytes_accessed=moved, transcendentals=0)


def whole():
    return pl.BlockSpec(memory_space=pltpu.VMEM)


def in_hbm():
    return pl.BlockSpec(memory_space=pltpu.HBM)


def unread():
    return pl.BlockSpec(memory_space=pl.ANY)


def smem():
    return pl.BlockSpec(memory_space=pltpu.SMEM)


def keep_hbm(value):
    return pltpu.with_memory_space_constraint(value, pltpu.HBM)


def pack_kernel(
    replica_ref,
    ids_hbm,
    gates_hbm,
    tokens_ref,
    cot_ref,
    w_hbm,
    x_ref,
    y_ref,
    own_ref,
    w_ref,
    ids_ref,
    gates_ref,
    sems,
):
    count = tokens_ref.shape[0]
    width = x_ref.shape[1]
    columns = pl.ds(pl.multiple_of(replica_ref[0] * width, width), width)
    copies = [
        pltpu.make_async_copy(ids_hbm, ids_ref, sems.at[0]),
        pltpu.make_async_copy(gates_hbm, gates_ref, sems.at[1]),
        pltpu.make_async_copy(tokens_ref.at[:, columns], x_ref, sems.at[2]),
        pltpu.make_async_copy(cot_ref.at[:, columns], y_ref.at[0:count, :], sems.at[3]),
        pltpu.make_async_copy(w_hbm, w_ref, sems.at[4]),
    ]
    for copy in copies:
        copy.start()
    copies[0].wait()
    copies[1].wait()
    ids = ids_ref[...]
    gates = gates_ref[...].astype(jnp.float32)
    slots = y_ref.shape[0] - count
    row = lax.broadcasted_iota(jnp.int32, (slots, count), 0)
    gate = jnp.zeros((slots, count), jnp.float32)
    for k in range(ids.shape[0]):
        gate = gate + jnp.where(row == ids[k : k + 1, :], gates[k : k + 1, :], 0.0)
    y_ref[count:, 0:count] = gate.astype(jnp.bfloat16)
    y_ref[count:, count:] = jnp.zeros((slots, width - count), jnp.bfloat16)
    own_ref[2 * count :, :] = y_ref[count:, :]
    copies[2].wait()
    own_ref[0:count, :] = x_ref[...]
    copies[3].wait()
    own_ref[count : 2 * count, :] = y_ref[0:count, :]
    copies[4].wait()


def pack_own(replica, ids, gates, tokens, cotangent, weights, slots):
    count, top = ids.shape
    width = weights.shape[2]
    return pl.pallas_call(
        pack_kernel,
        in_specs=[smem()] + [in_hbm()] * 5,
        out_specs=[whole()] * 4,
        out_shape=[
            jax.ShapeDtypeStruct((rows, width), jnp.bfloat16)
            for rows in (count, count + slots, 2 * count + slots)
        ]
        + [jax.ShapeDtypeStruct(weights.shape, weights.dtype)],
        scratch_shapes=[
            pltpu.VMEM((top, count), ids.dtype),
            pltpu.VMEM((top, count), gates.dtype),
            pltpu.SemaphoreType.DMA((5,)),
        ],
        compiler_params=params(),
        cost_estimate=cost(1000, 8 * count * width),
    )(replica.reshape(1), *[keep_hbm(value) for value in (ids.T, gates.T, tokens, cotangent, weights)])


def views(refs, kinds, count):
    xs, ys, gates = [], [], []
    for ref, kind in zip(refs, kinds):
        for part in [ref.at[0], ref.at[1]] if ref.ndim == 3 else [ref]:
            rows = part.shape[0]
            if kind == "xy":
                xs.append(part[0:count, :])
            if kind == "x":
                xs.append(part[...])
            if kind in ("xy", "y of xy"):
                ys.append(part[count : 2 * count, :])
                gates.append(part[2 * count :, 0:count])
            if kind == "y":
                ys.append(part[...])
            if kind == "y, gates":
                ys.append(part[0 : count // 2, :])
                gates.append(part[count // 2 :, 0:count])
    return xs, ys, gates


def joined(parts):
    return parts[0] if len(parts) == 1 else jnp.concatenate(parts, 0)


def kinds_of(chunk):
    return tuple(kind for kind, value in chunk)


def values_of(chunk):
    return [value for kind, value in chunk]


def partial_kernel(kinds, count, w_ref, after_ref, *refs):
    n = len(kinds)
    xs, ys, gates = views(refs[:n], kinds, count)
    outs, token_ref = list(refs[n:-1]), refs[-1]
    mats, hidden, width = w_ref.shape
    if xs:
        gu = contract_last(w_ref[0:2].reshape(2 * hidden, width), joined(xs))
    if ys:
        down = contract_last(w_ref[2], joined(ys))
    parts = ([gu] if xs else []) + ([down] if ys else [])
    out_ref = outs[0]
    row = 0
    for part in parts:
        for first in range(0, part.shape[1], count):
            piece = part[:, first : first + count]
            out_ref[row : row + piece.shape[0], :] = piece.astype(jnp.bfloat16)
            row = row + piece.shape[0]
    token_ref[...] = jnp.zeros_like(token_ref)


def partials(weights, after, chunk, rows, count):
    hidden, width = weights.shape[1:]
    kinds = kinds_of(chunk)
    return pl.pallas_call(
        functools.partial(partial_kernel, kinds, count),
        in_specs=[whole(), unread()] + [whole()] * len(kinds),
        out_specs=[whole()] * 2,
        out_shape=[
            jax.ShapeDtypeStruct((rows * hidden, count), jnp.bfloat16),
            jax.ShapeDtypeStruct((8, 128), jnp.float32),
        ],
        compiler_params=params(),
        cost_estimate=cost(2 * rows * hidden * count * width, 6 * rows * hidden * count),
    )(weights, after, *values_of(chunk))


def gate_row(expert_ref, gates):
    rows = []
    for held in gates:
        held = held.astype(jnp.float32)
        index = lax.broadcasted_iota(jnp.int32, held.shape, 0)
        rows.append(jnp.sum(jnp.where(index == expert_ref[0], held, 0.0), 0, keepdims=True))
    return rows[0] if len(rows) == 1 else jnp.concatenate(rows, 1)


def hidden_grads(gate, pairs):
    parts = []
    for own, *got in pairs:
        part = own[...].astype(jnp.float32)
        parts.append(part + got[0][...].astype(jnp.float32) if got else part)
    total = parts[0] if len(parts) == 1 else jnp.concatenate(parts, 0)
    blocks = gate.shape[1] // total.shape[1]
    hidden = total.shape[0] // (3 * blocks)
    row = lambda first: total[first * hidden : (first + 1) * hidden]
    side = lambda firsts: jnp.concatenate([row(first) for first in firsts], 1)
    hg = side(range(0, 2 * blocks, 2))
    hu = side(range(1, 2 * blocks, 2))
    down = side(range(2 * blocks, 3 * blocks))
    dact = gate * down
    sig = jax.nn.sigmoid(hg)
    silu = hg * sig
    act = (gate * (silu * hu)).astype(jnp.bfloat16)
    dhg = (dact * hu * sig * (1.0 + hg * (1.0 - sig))).astype(jnp.bfloat16)
    dhu = (dact * silu).astype(jnp.bfloat16)
    return dhg, dhu, act


def plain(left, right):
    return lax.dot_general(
        left, right, (((1,), (0,)), ((), ())), preferred_element_type=jnp.float32
    )


def onward_kernel(kinds, count, core_ref, expert_ref, after_ref, *refs):
    own, got, near_own, near_got, x0_ref, x1_ref, y0_ref, y1_ref = refs[:8]
    blocks = refs[8 : 8 + len(kinds)]
    both_ref, out_ref, left_ref, sum_ref = refs[8 + len(kinds) :]
    both_ref[0, 0:count, :] = x0_ref[...]
    both_ref[1, 0:count, :] = x1_ref[...]
    both_ref[0, count:, :] = y0_ref[...]
    both_ref[1, count:, :] = y1_ref[...]

    def pick(near, more):
        out_ref[0:count, :] = near[...]
        out_ref[count:, :] = more[...]

    @pl.when(core_ref[0] == 0)
    def _():
        pick(x0_ref, y0_ref)

    @pl.when(core_ref[0] != 0)
    def _():
        pick(x1_ref, y1_ref)

    sum_ref[...] = near_own[...].astype(jnp.float32) + near_got[...].astype(jnp.float32)
    xs, ys, gates = views(blocks, kinds, count)
    for m, value in enumerate(hidden_grads(gate_row(expert_ref, gates), [(own, got)])):
        left_ref[m] = value


def pick_onward(core, expert, after, pair, near_pair, near_x, near_y, chunk, count):
    kinds = kinds_of(chunk)
    rows, width = near_x[0].shape[0] + near_y[0].shape[0], near_x[0].shape[1]
    operands = [*pair, *near_pair, *near_x, *near_y, *values_of(chunk)]
    return pl.pallas_call(
        functools.partial(onward_kernel, kinds, count),
        in_specs=[smem(), smem(), unread()] + [whole()] * len(operands),
        out_specs=[whole()] * 4,
        out_shape=[
            jax.ShapeDtypeStruct((2, rows, width), jnp.bfloat16),
            jax.ShapeDtypeStruct((rows, width), jnp.bfloat16),
            jax.ShapeDtypeStruct((3, pair[0].shape[0] // 6, 2 * count), jnp.bfloat16),
            jax.ShapeDtypeStruct(near_pair[0].shape, jnp.float32),
        ],
        compiler_params=params(),
        cost_estimate=cost(1000, 8 * near_x[0].size),
    )(core.reshape(1), expert, after, *operands)


def pass_kernel(after_ref, in_ref, *outs):
    row = 0
    for out_ref in outs:
        out_ref[...] = in_ref[row : row + out_ref.shape[0], :]
        row = row + out_ref.shape[0]


def passed_on(after, value, cuts):
    width = value.shape[1]
    return pl.pallas_call(
        pass_kernel,
        in_specs=[unread(), whole()],
        out_specs=[whole()] * len(cuts),
        out_shape=[jax.ShapeDtypeStruct((rows, width), value.dtype) for rows in cuts],
        compiler_params=params(),
        cost_estimate=cost(1000, 2 * value.size),
    )(after, value)


def first_kernel(kinds, count, after_ref, left_ref, *refs):
    n = len(kinds)
    xs, ys, gates = views(refs[:n], kinds, count)
    out_ref, token_ref = refs[n:]
    x = joined(xs)
    out_ref[0] = plain(left_ref[0], x)
    out_ref[1] = plain(left_ref[1], x)
    out_ref[2] = plain(left_ref[2], joined(ys))
    token_ref[...] = jnp.zeros_like(token_ref)


def first_grads(after, left, chunk, count):
    kinds = kinds_of(chunk)
    mats, hidden, tokens = left.shape
    width = chunk[0][1].shape[-1]
    return pl.pallas_call(
        functools.partial(first_kernel, kinds, count),
        in_specs=[unread()] + [whole()] * (1 + len(kinds)),
        out_specs=[whole()] * 2,
        out_shape=[
            jax.ShapeDtypeStruct((mats, hidden, width), jnp.float32),
            jax.ShapeDtypeStruct((8, 128), jnp.float32),
        ],
        compiler_params=params(),
        cost_estimate=cost(6 * hidden * width * tokens, 12 * hidden * width),
    )(after, left, *values_of(chunk))


def grad_kernel(kinds, count, expert_ref, sum_ref, own, got, *refs):
    n = len(kinds)
    xs, ys, gates = views(refs[:n], kinds, count)
    acc_ref, out_ref = refs[n:]
    lefts = hidden_grads(gate_row(expert_ref, gates), [(sum_ref,), (own, got)])
    x = joined(xs)
    for m, right in enumerate((x, x, joined(ys))):
        out_ref[m] = acc_ref[m] + plain(lefts[m], right)


def add_grads(expert, near_sum, pair, chunk, acc, count):
    kinds = kinds_of(chunk)
    mats, hidden, width = acc.shape
    operands = [near_sum, *pair, *values_of(chunk), acc]
    return pl.pallas_call(
        functools.partial(grad_kernel, kinds, count),
        in_specs=[smem()] + [whole()] * len(operands),
        out_specs=whole(),
        out_shape=jax.ShapeDtypeStruct(acc.shape, jnp.float32),
        input_output_aliases={len(operands): 0},
        compiler_params=params(),
        cost_estimate=cost(
            2 * mats * hidden * width * 4 * count, 8 * mats * hidden * width
        ),
    )(expert, *operands)


def last_kernel(kinds, count, expert_ref, own, got, *refs):
    n = len(kinds)
    xs, ys, gates = views(refs[:n], kinds, count)
    acc_ref, first_ref, second_ref, one_ref, two_ref, step_ref, left_ref = refs[n:]
    m = pl.program_id(1)

    @pl.when((m == 0) & (pl.program_id(0) == 0))
    def _():
        for k, value in enumerate(hidden_grads(gate_row(expert_ref, gates), [(own, got)])):
            left_ref[k] = value

    def finish(right):
        grad = acc_ref[0] + plain(left_ref[m], right)
        moment_one = beta_one * first_ref[0].astype(jnp.float32) + (1.0 - beta_one) * grad
        moment_two = beta_two * second_ref[0].astype(jnp.float32) + (1.0 - beta_two) * (grad * grad)
        one_ref[0] = moment_one.astype(jnp.bfloat16)
        two_ref[0] = moment_two.astype(jnp.bfloat16)
        scaled = moment_two * (1.0 / (1.0 - beta_two**step_count))
        below = scaled * lax.rsqrt(scaled) + epsilon
        guess = pl.reciprocal(below, approx=True)
        inverse = guess * (2.0 - below * guess)
        step = moment_one * (1.0 / (1.0 - beta_one**step_count)) * inverse
        step_ref[0] = step.astype(jnp.bfloat16)

    @pl.when(m < 2)
    def _():
        finish(joined(xs))

    @pl.when(m == 2)
    def _():
        finish(joined(ys))


def last_grads(expert, own, got, chunk, acc, first_moment, second_moment, count, columns):
    kinds = kinds_of(chunk)
    blocks = values_of(chunk)
    mats, hidden, width = first_moment.shape
    tile = pl.BlockSpec((1, hidden, columns), lambda j, m: (m, 0, j))
    out = jax.ShapeDtypeStruct(first_moment.shape, jnp.bfloat16)
    strip = lambda value: pl.BlockSpec((value.shape[0], columns), lambda j, m: (0, j))
    return pl.pallas_call(
        functools.partial(last_kernel, kinds, count),
        grid=(width // columns, mats),
        in_specs=[smem(), whole(), whole()] + [strip(value) for value in blocks] + [tile] * 3,
        out_specs=[tile] * 3,
        out_shape=[out] * 3,
        scratch_shapes=[pltpu.VMEM((mats, hidden, 2 * count), jnp.bfloat16)],
        compiler_params=params(),
        cost_estimate=cost(
            4 * mats * hidden * width * count, 8 * hidden * width * mats
        ),
    )(expert, own, got, *blocks, acc, first_moment, second_moment)


def from_masked(value, axis, mask):
    pairs = [(source, source ^ mask) for source in range(lax.axis_size(axis))]
    return lax.ppermute(value, axis, pairs)


def dense_plan(tokens, cotangent, expert_ids, gate_probs, weights, first_moment, second_moment):
    n_data = lax.axis_size("dp")
    place = lax.axis_index("expert")
    core = lax.axis_index("dp") % 2
    slices = min(4, lax.axis_size("expert") // 2)
    expert = (place // (2 * slices) * n_data + lax.axis_index("dp")).astype(jnp.int32).reshape(1)
    experts_total = lax.axis_size("expert") // (2 * slices) * n_data
    count = tokens.shape[0]
    width = weights.shape[2]
    slots = -(-experts_total // 16) * 16
    x_own, y_own, own, weights = pack_own(
        (place % 2).astype(jnp.int32), expert_ids, gate_probs, tokens, cotangent, weights, slots
    )
    other = lambda value: from_masked(value, "dp", 1)
    partner = lambda value: from_masked(value, "expert", 1)
    first = [("xy", own), ("xy", other(own))]
    send, token = partials(weights, own, first, 6, count)
    first_pair = (send, partner(send))
    near_x = [from_masked(x_own, "dp", mask) for mask in (2, 4)]
    near_y = [from_masked(y_own, "dp", mask) for mask in (2, 4)]
    send, token = partials(weights, token, [("x", near_x[0])], 2, count)
    near_pair = (send, partner(send))
    both, picked, left, near_sum = pick_onward(
        core.astype(jnp.int32), expert, token, first_pair, near_pair, near_x, near_y, first, count
    )
    onward = [(p, p ^ 4 if p % 2 == 0 else p ^ 2) for p in range(n_data)]
    far = lax.ppermute(picked, "dp", onward)
    acc, token = first_grads(picked, left, first, count)
    swapped = other(both)
    more = [("x", near_x[1]), ("y of xy", both), ("xy", swapped)]
    send, token = partials(weights, token, more, 10, count)
    more_pair = (send, partner(send))
    pieces = passed_on(token, far, (count // 2, count // 2, count // 2, count // 2 + slots))
    pieces = [*pieces, *[other(value) for value in pieces]]
    final = list(zip(("x", "x", "y", "y, gates") * 2, pieces))
    send, token = partials(weights, token, final, 6, count)
    got = partner(send)
    near = [("xy", both), ("xy", swapped)]
    acc = add_grads(expert, near_sum, more_pair, near, acc, count)
    return tuple(
        last_grads(expert, send, got, final, acc, first_moment, second_moment, count, width // 2)
    )


def per_device(tokens, cotangent, expert_ids, gate_probs, weights, first_moment, second_moment):
    n_expert = lax.axis_size("expert")
    n_data = lax.axis_size("dp")
    slices = min(4, n_expert // 2)
    experts_total = n_expert // (2 * slices) * n_data
    half = tokens.shape[0] // 2
    dense = 2 * half * expert_ids.shape[1] // experts_total >= half
    plan = dense_plan if dense and n_data == 8 else routed_plan
    return plan(
        tokens, cotangent, expert_ids, gate_probs, weights, first_moment, second_moment
    )


def solution(mesh):
    in_specs = (
        P("dp", None),
        P("dp", None),
        P("dp", None),
        P("dp", None),
        P(None, "dp", "expert"),
        P(None, "dp", "expert"),
        P(None, "dp", "expert"),
    )
    out_specs = (P(None, "dp", "expert"), P(None, "dp", "expert"), P(None, "dp", "expert"))
    return jax.shard_map(
        per_device, mesh=mesh, in_specs=in_specs, out_specs=out_specs, check_vma=False
    )
```

```python
import functools

import jax
import jax.numpy as jnp
from jax import lax
from jax.experimental import pallas as pl
from jax.experimental.pallas import tpu as pltpu
from jax.sharding import PartitionSpec as P

beta_one = 0.9
beta_two = 0.95
step_count = 10
epsilon = 1e-08


def from_partner(value, axis, distance):
    mask = 2**distance
    pairs = [(source, source ^ mask) for source in range(lax.axis_size(axis))]
    return lax.ppermute(value, axis, pairs)


def contract_last(left, right):
    return lax.dot_general(
        left, right, (((1,), (1,)), ((), ())), preferred_element_type=jnp.float32
    )


def contract_first(left, right):
    return lax.dot_general(
        left, right, (((0,), (0,)), ((), ())), preferred_element_type=jnp.float32
    )


def split_halves(grad, replica, width_half):
    keep = lax.dynamic_slice_in_dim(grad, replica * width_half, width_half, grad.ndim - 1)
    give = lax.dynamic_slice_in_dim(grad, (1 - replica) * width_half, width_half, grad.ndim - 1)
    return (keep, give)


def route_block(block_ids, block_gates, group, n_data, capacity):
    count = block_ids.shape[0]
    top = block_ids.shape[1]
    target = block_ids - group * n_data
    inside = block_ids // n_data == group
    onehot = (
        (target[:, :, None] == jnp.arange(n_data, dtype=jnp.int32)[None, None, :])
        & inside[:, :, None]
    ).astype(jnp.int32)
    per_token = jnp.sum(onehot, axis=1)
    earlier = jnp.cumsum(per_token, axis=0) - per_token
    rank = jnp.sum(onehot * earlier[:, None, :], axis=2)
    total_slots = n_data * capacity
    slot = jnp.where(inside, target * capacity + rank, total_slots).reshape(-1)
    token_of = jnp.broadcast_to(jnp.arange(count, dtype=jnp.int32)[:, None], (count, top)).reshape(
        -1
    )
    table = jnp.full((total_slots,), count, jnp.int32).at[slot].set(token_of, mode="drop")
    gate_slot = (
        jnp.zeros((total_slots,), jnp.bfloat16).at[slot].set(block_gates.reshape(-1), mode="drop")
    )
    return (table, gate_slot)


def routed_plan(tokens, cotangent, expert_ids, gate_probs, weights, first_moment, second_moment):
    n_expert = lax.axis_size("expert")
    n_data = lax.axis_size("dp")
    slices = min(4, n_expert // 2)
    place = lax.axis_index("expert")
    replica = place % 2
    group = place // (2 * slices)
    groups = n_expert // (2 * slices)
    experts_total = groups * n_data
    half = tokens.shape[0] // 2
    width_half = weights.shape[2]
    top = expert_ids.shape[1]
    capacity = max(2, 2 * half * top // experts_total)
    start = replica * half
    own_ids = lax.dynamic_slice_in_dim(expert_ids, start, half, 0)
    own_gates = lax.dynamic_slice_in_dim(gate_probs, start, half, 0)
    table, gate_slot = route_block(own_ids, own_gates, group, n_data, capacity)
    source_tokens = lax.dynamic_slice_in_dim(tokens, start, half, 0)
    source_cot = lax.dynamic_slice_in_dim(cotangent, start, half, 0)
    columns = source_tokens.shape[1]
    padded_tokens = jnp.concatenate([source_tokens, jnp.zeros((1, columns), jnp.bfloat16)], 0)
    padded_cot = jnp.concatenate([source_cot, jnp.zeros((1, columns), jnp.bfloat16)], 0)
    send_rows = padded_tokens[table].reshape(n_data, -1, columns)
    send_cot = padded_cot[table].reshape(n_data, -1, columns)
    send_gates = gate_slot.reshape(n_data, -1)
    rows_in, gates_in = (
        lax.all_to_all(send_rows, "dp", split_axis=0, concat_axis=0, tiled=True),
        lax.all_to_all(send_gates, "dp", split_axis=0, concat_axis=0, tiled=True),
    )
    rows = rows_in.reshape(-1, columns)
    gate_rows = gates_in.reshape(-1).astype(jnp.float32)
    partner = from_partner(weights, "expert", 0)
    lower = jnp.where(replica == 0, weights, partner)
    upper = jnp.where(replica == 0, partner, weights)
    full = jnp.concatenate([lower, upper], 2)
    hg = contract_last(rows, full[0])
    hu = contract_last(rows, full[1])
    sig = jax.nn.sigmoid(hg)
    act = (hg * sig * hu).astype(jnp.bfloat16)
    cot_in = lax.all_to_all(send_cot, "dp", split_axis=0, concat_axis=0, tiled=True)
    cots = cot_in.reshape(-1, columns)
    dz = (gate_rows[:, None] * cots.astype(jnp.float32)).astype(jnp.bfloat16)
    dact = contract_last(dz, full[2])
    grad_down = contract_first(act, dz)
    dhg = (dact * hu * sig * (1.0 + hg * (1.0 - sig))).astype(jnp.bfloat16)
    dhu = (dact * hg * sig).astype(jnp.bfloat16)
    grad_gate = contract_first(dhg, rows)
    grad_up = contract_first(dhu, rows)
    stacked = jnp.stack([grad_gate, grad_up, grad_down])
    keep, give = split_halves(stacked, replica, width_half)
    total = keep + from_partner(give, "expert", 0)
    moment_one = beta_one * first_moment.astype(jnp.float32) + (1.0 - beta_one) * total
    moment_two = beta_two * second_moment.astype(jnp.float32) + (1.0 - beta_two) * total * total
    step = (
        moment_one
        / (1.0 - beta_one**step_count)
        / (jnp.sqrt(moment_two / (1.0 - beta_two**step_count)) + epsilon)
    )
    return (
        moment_one.astype(jnp.bfloat16),
        moment_two.astype(jnp.bfloat16),
        step.astype(jnp.bfloat16),
    )


VMEM_LIMIT = 16 * 1024 * 1024


def params():
    return pltpu.CompilerParams(vmem_limit_bytes=VMEM_LIMIT)


def cost(flops, moved):
    return pl.CostEstimate(flops=flops, bytes_accessed=moved, transcendentals=0)


def whole():
    return pl.BlockSpec(memory_space=pltpu.VMEM)


def in_hbm():
    return pl.BlockSpec(memory_space=pltpu.HBM)


def unread():
    return pl.BlockSpec(memory_space=pl.ANY)


def smem():
    return pl.BlockSpec(memory_space=pltpu.SMEM)


def keep_hbm(value):
    return pltpu.with_memory_space_constraint(value, pltpu.HBM)


def pack_kernel(
    replica_ref,
    ids_hbm,
    gates_hbm,
    tokens_ref,
    cot_ref,
    x_ref,
    y_ref,
    own_ref,
    ids_ref,
    gates_ref,
    sems,
):
    count = tokens_ref.shape[0]
    width = x_ref.shape[1]
    columns = pl.ds(pl.multiple_of(replica_ref[0] * width, width), width)
    copies = [
        pltpu.make_async_copy(ids_hbm, ids_ref, sems.at[0]),
        pltpu.make_async_copy(gates_hbm, gates_ref, sems.at[1]),
        pltpu.make_async_copy(tokens_ref.at[:, columns], x_ref, sems.at[2]),
        pltpu.make_async_copy(cot_ref.at[:, columns], y_ref.at[0:count, :], sems.at[3]),
    ]
    for copy in copies:
        copy.start()
    copies[0].wait()
    copies[1].wait()
    ids = ids_ref[...]
    gates = gates_ref[...].astype(jnp.float32)
    slots = y_ref.shape[0] - count
    row = lax.broadcasted_iota(jnp.int32, (slots, count), 0)
    gate = jnp.zeros((slots, count), jnp.float32)
    for k in range(ids.shape[0]):
        gate = gate + jnp.where(row == ids[k : k + 1, :], gates[k : k + 1, :], 0.0)
    y_ref[count:, 0:count] = gate.astype(jnp.bfloat16)
    y_ref[count:, count:] = jnp.zeros((slots, width - count), jnp.bfloat16)
    own_ref[2 * count :, :] = y_ref[count:, :]
    copies[2].wait()
    own_ref[0:count, :] = x_ref[...]
    copies[3].wait()
    own_ref[count : 2 * count, :] = y_ref[0:count, :]


def pack_own(replica, ids, gates, tokens, cotangent, width, slots):
    count, top = ids.shape
    return pl.pallas_call(
        pack_kernel,
        in_specs=[smem()] + [in_hbm()] * 4,
        out_specs=[whole()] * 3,
        out_shape=[
            jax.ShapeDtypeStruct((rows, width), jnp.bfloat16)
            for rows in (count, count + slots, 2 * count + slots)
        ],
        scratch_shapes=[
            pltpu.VMEM((top, count), ids.dtype),
            pltpu.VMEM((top, count), gates.dtype),
            pltpu.SemaphoreType.DMA((4,)),
        ],
        compiler_params=params(),
        cost_estimate=cost(1000, 8 * count * width),
    )(replica.reshape(1), *[keep_hbm(value) for value in (ids.T, gates.T, tokens, cotangent)])


def views(refs, kinds, count):
    xs, ys, gates = [], [], []
    for ref, kind in zip(refs, kinds):
        for part in [ref.at[0], ref.at[1]] if ref.ndim == 3 else [ref]:
            rows = part.shape[0]
            if kind == "xy":
                xs.append(part[0:count, :])
            if kind == "x":
                xs.append(part[...])
            if kind in ("xy", "y of xy"):
                ys.append(part[count : 2 * count, :])
                gates.append(part[2 * count :, 0:count])
            if kind == "y":
                ys.append(part[...])
            if kind == "y, gates":
                ys.append(part[0 : count // 2, :])
                gates.append(part[count // 2 :, 0:count])
    return xs, ys, gates


def joined(parts):
    return parts[0] if len(parts) == 1 else jnp.concatenate(parts, 0)


def kinds_of(chunk):
    return tuple(kind for kind, value in chunk)


def values_of(chunk):
    return [value for kind, value in chunk]


def store_partials(parts, count, out_ref):
    row = 0
    for part in parts:
        for first in range(0, part.shape[1], count):
            piece = part[:, first : first + count]
            out_ref[row : row + piece.shape[0], :] = piece.astype(jnp.bfloat16)
            row = row + piece.shape[0]


def partial_kernel(kinds, count, w_ref, after_ref, *refs):
    n = len(kinds)
    xs, ys, gates = views(refs[:n], kinds, count)
    outs = refs[n:-1]
    mats, hidden, width = w_ref.shape
    parts = []
    if xs:
        parts.append(contract_last(w_ref[0:2].reshape(2 * hidden, width), joined(xs)))
    if ys:
        parts.append(contract_last(w_ref[2], joined(ys)))
    if len(outs) == 1:
        store_partials(parts, count, outs[0])
    else:
        for part, out_ref in zip(parts, outs):
            store_partials([part], count, out_ref)
    refs[-1][...] = jnp.zeros_like(refs[-1])


def partials(weights, after, chunk, rows, count):
    hidden, width = weights.shape[1:]
    kinds = kinds_of(chunk)
    total = sum(rows) * hidden * count
    return pl.pallas_call(
        functools.partial(partial_kernel, kinds, count),
        in_specs=[whole(), unread()] + [whole()] * len(kinds),
        out_specs=[whole()] * (len(rows) + 1),
        out_shape=[jax.ShapeDtypeStruct((k * hidden, count), jnp.bfloat16) for k in rows]
        + [jax.ShapeDtypeStruct((8, 128), jnp.float32)],
        compiler_params=params(),
        cost_estimate=cost(2 * total * width, 6 * total),
    )(weights, after, *values_of(chunk))


def start_kernel(kinds, count, w_hbm, *refs):
    n = len(kinds)
    out_ref, token_ref, w_ref, sems = refs[n:]
    mats, hidden, width = w_ref.shape
    copies = [pltpu.make_async_copy(w_hbm.at[m], w_ref.at[m], sems.at[m]) for m in range(mats)]
    for copy in copies:
        copy.start()
    xs, ys, gates = views(refs[:n], kinds, count)
    token_ref[...] = jnp.zeros_like(token_ref)
    parts = []
    for k, right in enumerate((joined(xs), joined(xs), joined(ys))):
        copies[k].wait()
        parts.append(contract_last(w_ref[k], right))
    gate, up, down = parts
    for k in range(gate.shape[1] // count):
        side = slice(k * count, (k + 1) * count)
        for m, part in ((2 * k, gate), (2 * k + 1, up), (gate.shape[1] // count * 2 + k, down)):
            out_ref[m * hidden : (m + 1) * hidden, :] = part[:, side].astype(jnp.bfloat16)


def start_partials(weights, chunk, rows, count):
    mats, hidden, width = weights.shape
    kinds = kinds_of(chunk)
    total = rows * hidden * count
    return pl.pallas_call(
        functools.partial(start_kernel, kinds, count),
        in_specs=[in_hbm()] + [whole()] * len(kinds),
        out_specs=[whole()] * 3,
        out_shape=[
            jax.ShapeDtypeStruct((rows * hidden, count), jnp.bfloat16),
            jax.ShapeDtypeStruct((8, 128), jnp.float32),
            jax.ShapeDtypeStruct(weights.shape, weights.dtype),
        ],
        scratch_shapes=[pltpu.SemaphoreType.DMA((mats,))],
        compiler_params=params(),
        cost_estimate=cost(2 * total * width, 6 * total),
    )(keep_hbm(weights), *values_of(chunk))


def gate_row(expert_ref, gates):
    rows = []
    for held in gates:
        held = held.astype(jnp.float32)
        index = lax.broadcasted_iota(jnp.int32, held.shape, 0)
        rows.append(jnp.sum(jnp.where(index == expert_ref[0], held, 0.0), 0, keepdims=True))
    return rows[0] if len(rows) == 1 else jnp.concatenate(rows, 1)


def summed(pairs):
    parts = []
    for own, *got in pairs:
        part = own[...].astype(jnp.float32)
        parts.append(part + got[0][...].astype(jnp.float32) if got else part)
    return parts[0] if len(parts) == 1 else jnp.concatenate(parts, 0)


def beside(total, hidden, firsts):
    parts = [total[first * hidden : (first + 1) * hidden] for first in firsts]
    return jnp.concatenate(parts, 1)


def activation(hg, hu, gate):
    sig = jax.nn.sigmoid(hg)
    silu = hg * sig
    return sig, silu, (gate * (silu * hu)).astype(jnp.bfloat16)


def hidden_slopes(hg, hu, sig, silu, dact):
    dhg = (dact * hu * sig * (1.0 + hg * (1.0 - sig))).astype(jnp.bfloat16)
    dhu = (dact * silu).astype(jnp.bfloat16)
    return dhg, dhu


def hidden_grads(gate, pairs):
    total = summed(pairs)
    blocks = gate.shape[1] // total.shape[1]
    hidden = total.shape[0] // (3 * blocks)
    hg = beside(total, hidden, range(0, 2 * blocks, 2))
    hu = beside(total, hidden, range(1, 2 * blocks, 2))
    dact = gate * beside(total, hidden, range(2 * blocks, 3 * blocks))
    sig, silu, act = activation(hg, hu, gate)
    return (*hidden_slopes(hg, hu, sig, silu, dact), act)


def plain(left, right):
    return lax.dot_general(
        left, right, (((1,), (0,)), ((), ())), preferred_element_type=jnp.float32
    )


def onward_kernel(kinds, core_ref, expert_ref, after_ref, *refs):
    own, got, near_own, near_got, x0_ref, x1_ref, y0_ref, y1_ref = refs[:8]
    both_ref, out_ref, first_ref, sum_ref, gate_ref = refs[8 + len(kinds) :]
    count = x0_ref.shape[0]
    gates = views(refs[8 : 8 + len(kinds)], kinds, count)[2]
    gate_ref[...] = jnp.broadcast_to(gate_row(expert_ref, gates), gate_ref.shape)
    both_ref[0, 0:count, :] = x0_ref[...]
    both_ref[1, 0:count, :] = x1_ref[...]
    both_ref[0, count:, :] = y0_ref[...]
    both_ref[1, count:, :] = y1_ref[...]

    def pick(near, more):
        out_ref[0:count, :] = near[...]
        out_ref[count:, :] = more[...]

    @pl.when(core_ref[0] == 0)
    def _():
        pick(x0_ref, y0_ref)

    @pl.when(core_ref[0] != 0)
    def _():
        pick(x1_ref, y1_ref)

    first_ref[...] = own[...].astype(jnp.float32) + got[...].astype(jnp.float32)
    sum_ref[...] = near_own[...].astype(jnp.float32) + near_got[...].astype(jnp.float32)


def pick_onward(core, expert, after, pair, near_pair, near_x, near_y, chunk):
    rows, width = near_x[0].shape[0] + near_y[0].shape[0], near_x[0].shape[1]
    operands = [*pair, *near_pair, *near_x, *near_y, *values_of(chunk)]
    return pl.pallas_call(
        functools.partial(onward_kernel, kinds_of(chunk)),
        in_specs=[smem(), smem(), unread()] + [whole()] * len(operands),
        out_specs=[whole()] * 5,
        out_shape=[
            jax.ShapeDtypeStruct((2, rows, width), jnp.bfloat16),
            jax.ShapeDtypeStruct((rows, width), jnp.bfloat16),
            jax.ShapeDtypeStruct(pair[0].shape, jnp.float32),
            jax.ShapeDtypeStruct(near_pair[0].shape, jnp.float32),
            jax.ShapeDtypeStruct((8, 2 * near_x[0].shape[0]), jnp.float32),
        ],
        compiler_params=params(),
        cost_estimate=cost(1000, 8 * near_x[0].size),
    )(core.reshape(1), expert, after, *operands)


def pass_kernel(after_ref, in_ref, *outs):
    row = 0
    for out_ref in outs:
        out_ref[...] = in_ref[row : row + out_ref.shape[0], :]
        row = row + out_ref.shape[0]


def passed_on(after, value, cuts):
    width = value.shape[1]
    return pl.pallas_call(
        pass_kernel,
        in_specs=[unread(), whole()],
        out_specs=[whole()] * len(cuts),
        out_shape=[jax.ShapeDtypeStruct((rows, width), value.dtype) for rows in cuts],
        compiler_params=params(),
        cost_estimate=cost(1000, 2 * value.size),
    )(after, value)


def first_kernel(kinds, count, gate_ref, after_ref, sum_ref, *refs):
    n = len(kinds)
    xs, ys, gates = views(refs[:n], kinds, count)
    out_ref, token_ref = refs[n:]
    lefts = hidden_grads(gate_ref[0:1, :], [(sum_ref,)])
    x = joined(xs)
    for m, right in enumerate((x, x, joined(ys))):
        out_ref[m] = plain(lefts[m], right)
    token_ref[...] = jnp.zeros_like(token_ref)


def first_grads(gate, after, total, chunk, hidden, count):
    kinds = kinds_of(chunk)
    width = chunk[0][1].shape[-1]
    return pl.pallas_call(
        functools.partial(first_kernel, kinds, count),
        in_specs=[whole(), unread()] + [whole()] * (1 + len(kinds)),
        out_specs=[whole()] * 2,
        out_shape=[
            jax.ShapeDtypeStruct((3, hidden, width), jnp.float32),
            jax.ShapeDtypeStruct((8, 128), jnp.float32),
        ],
        compiler_params=params(),
        cost_estimate=cost(2 * total.size * width, 12 * hidden * width),
    )(gate, after, total, *values_of(chunk))


def grad_kernel(kinds, count, expert_ref, sum_ref, own, got, *refs):
    n = len(kinds)
    xs, ys, gates = views(refs[:n], kinds, count)
    acc_ref, out_ref = refs[n:]
    lefts = hidden_grads(gate_row(expert_ref, gates), [(sum_ref,), (own, got)])
    x = joined(xs)
    for m, right in enumerate((x, x, joined(ys))):
        out_ref[m] = acc_ref[m] + plain(lefts[m], right)


def add_grads(expert, near_sum, pair, chunk, acc, count):
    kinds = kinds_of(chunk)
    mats, hidden, width = acc.shape
    operands = [near_sum, *pair, *values_of(chunk), acc]
    return pl.pallas_call(
        functools.partial(grad_kernel, kinds, count),
        in_specs=[smem()] + [whole()] * len(operands),
        out_specs=whole(),
        out_shape=jax.ShapeDtypeStruct(acc.shape, jnp.float32),
        input_output_aliases={len(operands): 0},
        compiler_params=params(),
        cost_estimate=cost(
            2 * mats * hidden * width * 4 * count, 8 * mats * hidden * width
        ),
    )(expert, *operands)


def adam(grad, first_ref, second_ref, one_ref, two_ref, step_ref):
    moment_one = beta_one * first_ref[0].astype(jnp.float32) + (1.0 - beta_one) * grad
    moment_two = beta_two * second_ref[0].astype(jnp.float32) + (1.0 - beta_two) * (grad * grad)
    one_ref[0] = moment_one.astype(jnp.bfloat16)
    two_ref[0] = moment_two.astype(jnp.bfloat16)
    scaled = moment_two * (1.0 / (1.0 - beta_two**step_count))
    below = scaled * lax.rsqrt(scaled) + epsilon
    guess = pl.reciprocal(below, approx=True)
    inverse = guess * (2.0 - below * guess)
    step = moment_one * (1.0 / (1.0 - beta_one**step_count)) * inverse
    step_ref[0] = step.astype(jnp.bfloat16)


def gate_up(own, got):
    total = summed([(own, got)])
    hidden = total.shape[0] // 4
    return beside(total, hidden, (0, 2)), beside(total, hidden, (1, 3))


def down_kernel(kinds, count, expert_ref, own, got, *refs):
    n = len(kinds)
    acc_ref, first_ref, second_ref, one_ref, two_ref, step_ref, act_ref = refs[n:]
    xs, ys, gates = views(refs[:n], kinds, count)

    @pl.when(pl.program_id(0) == 0)
    def _():
        act_ref[...] = activation(*gate_up(own, got), gate_row(expert_ref, gates))[2]

    grad = acc_ref[0] + plain(act_ref[...], joined(ys))
    adam(grad, first_ref, second_ref, one_ref, two_ref, step_ref)


def down_update(expert, pair, chunk, acc, first_moment, second_moment, count, columns):
    kinds = kinds_of(chunk)
    mats, hidden, width = first_moment.shape
    tile = pl.BlockSpec((1, hidden, columns), lambda j: (2, 0, j))
    strip = lambda value: pl.BlockSpec((value.shape[0], columns), lambda j: (0, j))
    return pl.pallas_call(
        functools.partial(down_kernel, kinds, count),
        grid=(width // columns,),
        in_specs=[smem(), whole(), whole()]
        + [strip(value) for value in values_of(chunk)]
        + [tile] * 3,
        out_specs=[tile] * 3,
        out_shape=[jax.ShapeDtypeStruct(first_moment.shape, jnp.bfloat16)] * 3,
        scratch_shapes=[pltpu.VMEM((hidden, 2 * count), jnp.bfloat16)],
        compiler_params=params(),
        cost_estimate=cost(4 * hidden * width * count, 14 * hidden * width),
    )(expert, *pair, *values_of(chunk), acc, first_moment, second_moment)


def slopes_kernel(kinds, count, expert_ref, own, got, own_d, got_d, *refs):
    n = len(kinds)
    acc_ref, first_ref, second_ref = refs[n : n + 3]
    one_ref, two_ref, step_ref, left_ref = refs[n + 6 :]
    xs, ys, gates = views(refs[:n], kinds, count)
    m = pl.program_id(1)

    @pl.when((pl.program_id(0) == 0) & (m == 0))
    def _():
        gate = gate_row(expert_ref, gates)
        hg, hu = gate_up(own, got)
        down = summed([(own_d, got_d)])
        dact = gate * beside(down, down.shape[0] // 2, (0, 1))
        sig, silu, act = activation(hg, hu, gate)
        left_ref[0], left_ref[1] = hidden_slopes(hg, hu, sig, silu, dact)

    grad = acc_ref[0] + plain(left_ref[m], joined(xs))
    adam(grad, first_ref, second_ref, one_ref, two_ref, step_ref)


def slopes_update(expert, pair, down_pair, chunk, acc, moments, done, count, columns):
    kinds = kinds_of(chunk)
    mats, hidden, width = acc.shape
    tile = pl.BlockSpec((1, hidden, columns), lambda j, m: (m, 0, j))
    strip = lambda value: pl.BlockSpec((value.shape[0], columns), lambda j, m: (0, j))
    operands = [expert, *pair, *down_pair, *values_of(chunk), acc, *moments, *done]
    return pl.pallas_call(
        functools.partial(slopes_kernel, kinds, count),
        grid=(width // columns, 2),
        in_specs=[smem()]
        + [whole()] * 4
        + [strip(value) for value in values_of(chunk)]
        + [tile] * 3
        + [unread()] * 3,
        out_specs=[tile] * 3,
        out_shape=[jax.ShapeDtypeStruct(acc.shape, jnp.bfloat16)] * 3,
        input_output_aliases={len(operands) - 3 + k: k for k in range(3)},
        scratch_shapes=[pltpu.VMEM((2, hidden, 2 * count), jnp.bfloat16)],
        compiler_params=params(),
        cost_estimate=cost(8 * hidden * width * count, 28 * hidden * width),
    )(*operands)


def from_masked(value, axis, mask):
    pairs = [(source, source ^ mask) for source in range(lax.axis_size(axis))]
    return lax.ppermute(value, axis, pairs)


def dense_plan(tokens, cotangent, expert_ids, gate_probs, weights, first_moment, second_moment):
    n_data = lax.axis_size("dp")
    place = lax.axis_index("expert")
    core = lax.axis_index("dp") % 2
    slices = min(4, lax.axis_size("expert") // 2)
    expert = (place // (2 * slices) * n_data + lax.axis_index("dp")).astype(jnp.int32).reshape(1)
    experts_total = lax.axis_size("expert") // (2 * slices) * n_data
    count = tokens.shape[0]
    width = weights.shape[2]
    slots = -(-experts_total // 16) * 16
    x_own, y_own, own = pack_own(
        (place % 2).astype(jnp.int32), expert_ids, gate_probs, tokens, cotangent, width, slots
    )
    other = lambda value: from_masked(value, "dp", 1)
    partner = lambda value: from_masked(value, "expert", 1)
    first = [("xy", own), ("xy", other(own))]
    send, token, weights = start_partials(weights, first, 6, count)
    first_pair = (send, partner(send))
    near_x = [from_masked(x_own, "dp", mask) for mask in (2, 4)]
    near_y = [from_masked(y_own, "dp", mask) for mask in (2, 4)]
    send, token = partials(weights, token, [("x", near_x[0])], (2,), count)
    near_pair = (send, partner(send))
    both, picked, first_sum, near_sum, gate = pick_onward(
        core.astype(jnp.int32), expert, token, first_pair, near_pair, near_x, near_y, first
    )
    onward = [(p, p ^ 4 if p % 2 == 0 else p ^ 2) for p in range(n_data)]
    far = lax.ppermute(picked, "dp", onward)
    acc, token = first_grads(gate, picked, first_sum, first, weights.shape[1], count)
    swapped = other(both)
    more = [("x", near_x[1]), ("y of xy", both), ("xy", swapped)]
    send, token = partials(weights, token, more, (10,), count)
    more_pair = (send, partner(send))
    pieces = passed_on(token, far, (count // 2, count // 2, count // 2, count // 2 + slots))
    pieces = [*pieces, *[other(value) for value in pieces]]
    final = list(zip(("x", "x", "y", "y, gates") * 2, pieces))
    send, send_d, token = partials(weights, token, final, (4, 2), count)
    pair, down_pair = (send, partner(send)), (send_d, partner(send_d))
    near = [("xy", both), ("xy", swapped)]
    acc = add_grads(expert, near_sum, more_pair, near, acc, count)
    moments = (first_moment, second_moment)
    final_y = [block for block in final if block[0] != "x"]
    final_x = [block for block in final if block[0] != "y"]
    done = down_update(expert, pair, final_y, acc, *moments, count, width // 2)
    return tuple(
        slopes_update(expert, pair, down_pair, final_x, acc, moments, done, count, width // 2)
    )


def per_device(tokens, cotangent, expert_ids, gate_probs, weights, first_moment, second_moment):
    n_expert = lax.axis_size("expert")
    n_data = lax.axis_size("dp")
    slices = min(4, n_expert // 2)
    experts_total = n_expert // (2 * slices) * n_data
    half = tokens.shape[0] // 2
    dense = 2 * half * expert_ids.shape[1] // experts_total >= half
    plan = dense_plan if dense and n_data == 8 else routed_plan
    return plan(
        tokens, cotangent, expert_ids, gate_probs, weights, first_moment, second_moment
    )


def solution(mesh):
    in_specs = (
        P("dp", None),
        P("dp", None),
        P("dp", None),
        P("dp", None),
        P(None, "dp", "expert"),
        P(None, "dp", "expert"),
        P(None, "dp", "expert"),
    )
    out_specs = (P(None, "dp", "expert"), P(None, "dp", "expert"), P(None, "dp", "expert"))
    return jax.shard_map(
        per_device, mesh=mesh, in_specs=in_specs, out_specs=out_specs, check_vma=False
    )
```

```python
import functools

import jax
import jax.numpy as jnp
from jax import lax
from jax.experimental import pallas as pl
from jax.experimental.pallas import tpu as pltpu
from jax.sharding import PartitionSpec as P

beta_one = 0.9
beta_two = 0.95
step_count = 10
epsilon = 1e-08


def from_partner(value, axis, distance):
    mask = 2**distance
    pairs = [(source, source ^ mask) for source in range(lax.axis_size(axis))]
    return lax.ppermute(value, axis, pairs)


def contract_last(left, right):
    return lax.dot_general(
        left, right, (((1,), (1,)), ((), ())), preferred_element_type=jnp.float32
    )


def contract_first(left, right):
    return lax.dot_general(
        left, right, (((0,), (0,)), ((), ())), preferred_element_type=jnp.float32
    )


def split_halves(grad, replica, width_half):
    keep = lax.dynamic_slice_in_dim(grad, replica * width_half, width_half, grad.ndim - 1)
    give = lax.dynamic_slice_in_dim(grad, (1 - replica) * width_half, width_half, grad.ndim - 1)
    return (keep, give)


def route_block(block_ids, block_gates, group, n_data, capacity):
    count = block_ids.shape[0]
    top = block_ids.shape[1]
    target = block_ids - group * n_data
    inside = block_ids // n_data == group
    onehot = (
        (target[:, :, None] == jnp.arange(n_data, dtype=jnp.int32)[None, None, :])
        & inside[:, :, None]
    ).astype(jnp.int32)
    per_token = jnp.sum(onehot, axis=1)
    earlier = jnp.cumsum(per_token, axis=0) - per_token
    rank = jnp.sum(onehot * earlier[:, None, :], axis=2)
    total_slots = n_data * capacity
    slot = jnp.where(inside, target * capacity + rank, total_slots).reshape(-1)
    token_of = jnp.broadcast_to(jnp.arange(count, dtype=jnp.int32)[:, None], (count, top)).reshape(
        -1
    )
    table = jnp.full((total_slots,), count, jnp.int32).at[slot].set(token_of, mode="drop")
    gate_slot = (
        jnp.zeros((total_slots,), jnp.bfloat16).at[slot].set(block_gates.reshape(-1), mode="drop")
    )
    return (table, gate_slot)


def routed_plan(tokens, cotangent, expert_ids, gate_probs, weights, first_moment, second_moment):
    n_expert = lax.axis_size("expert")
    n_data = lax.axis_size("dp")
    slices = min(4, n_expert // 2)
    place = lax.axis_index("expert")
    replica = place % 2
    group = place // (2 * slices)
    groups = n_expert // (2 * slices)
    experts_total = groups * n_data
    half = tokens.shape[0] // 2
    width_half = weights.shape[2]
    top = expert_ids.shape[1]
    capacity = max(2, 2 * half * top // experts_total)
    start = replica * half
    own_ids = lax.dynamic_slice_in_dim(expert_ids, start, half, 0)
    own_gates = lax.dynamic_slice_in_dim(gate_probs, start, half, 0)
    table, gate_slot = route_block(own_ids, own_gates, group, n_data, capacity)
    source_tokens = lax.dynamic_slice_in_dim(tokens, start, half, 0)
    source_cot = lax.dynamic_slice_in_dim(cotangent, start, half, 0)
    columns = source_tokens.shape[1]
    padded_tokens = jnp.concatenate([source_tokens, jnp.zeros((1, columns), jnp.bfloat16)], 0)
    padded_cot = jnp.concatenate([source_cot, jnp.zeros((1, columns), jnp.bfloat16)], 0)
    send_rows = padded_tokens[table].reshape(n_data, -1, columns)
    send_cot = padded_cot[table].reshape(n_data, -1, columns)
    send_gates = gate_slot.reshape(n_data, -1)
    rows_in, gates_in = (
        lax.all_to_all(send_rows, "dp", split_axis=0, concat_axis=0, tiled=True),
        lax.all_to_all(send_gates, "dp", split_axis=0, concat_axis=0, tiled=True),
    )
    rows = rows_in.reshape(-1, columns)
    gate_rows = gates_in.reshape(-1).astype(jnp.float32)
    partner = from_partner(weights, "expert", 0)
    lower = jnp.where(replica == 0, weights, partner)
    upper = jnp.where(replica == 0, partner, weights)
    full = jnp.concatenate([lower, upper], 2)
    hg = contract_last(rows, full[0])
    hu = contract_last(rows, full[1])
    sig = jax.nn.sigmoid(hg)
    act = (hg * sig * hu).astype(jnp.bfloat16)
    cot_in = lax.all_to_all(send_cot, "dp", split_axis=0, concat_axis=0, tiled=True)
    cots = cot_in.reshape(-1, columns)
    dz = (gate_rows[:, None] * cots.astype(jnp.float32)).astype(jnp.bfloat16)
    dact = contract_last(dz, full[2])
    grad_down = contract_first(act, dz)
    dhg = (dact * hu * sig * (1.0 + hg * (1.0 - sig))).astype(jnp.bfloat16)
    dhu = (dact * hg * sig).astype(jnp.bfloat16)
    grad_gate = contract_first(dhg, rows)
    grad_up = contract_first(dhu, rows)
    stacked = jnp.stack([grad_gate, grad_up, grad_down])
    keep, give = split_halves(stacked, replica, width_half)
    total = keep + from_partner(give, "expert", 0)
    moment_one = beta_one * first_moment.astype(jnp.float32) + (1.0 - beta_one) * total
    moment_two = beta_two * second_moment.astype(jnp.float32) + (1.0 - beta_two) * total * total
    step = (
        moment_one
        / (1.0 - beta_one**step_count)
        / (jnp.sqrt(moment_two / (1.0 - beta_two**step_count)) + epsilon)
    )
    return (
        moment_one.astype(jnp.bfloat16),
        moment_two.astype(jnp.bfloat16),
        step.astype(jnp.bfloat16),
    )


VMEM_LIMIT = 16 * 1024 * 1024


def params():
    return pltpu.CompilerParams(vmem_limit_bytes=VMEM_LIMIT)


def cost(flops, moved):
    return pl.CostEstimate(flops=flops, bytes_accessed=moved, transcendentals=0)


def whole():
    return pl.BlockSpec(memory_space=pltpu.VMEM)


def in_hbm():
    return pl.BlockSpec(memory_space=pltpu.HBM)


def unread():
    return pl.BlockSpec(memory_space=pl.ANY)


def expert_here():
    slices = min(4, lax.axis_size("expert") // 2)
    group = lax.axis_index("expert") // (2 * slices)
    return group * lax.axis_size("dp") + lax.axis_index("dp")


def keep_hbm(value):
    return pltpu.with_memory_space_constraint(value, pltpu.HBM)


def pack_kernel(
    ids_hbm,
    gates_hbm,
    tokens_ref,
    cot_ref,
    w_hbm,
    x_ref,
    y_ref,
    own_ref,
    w_ref,
    ids_ref,
    gates_ref,
    sems,
):
    count = tokens_ref.shape[0]
    width = x_ref.shape[1]
    columns = pl.ds(pl.multiple_of(lax.axis_index("expert") % 2 * width, width), width)
    copies = [
        pltpu.make_async_copy(ids_hbm, ids_ref, sems.at[0]),
        pltpu.make_async_copy(gates_hbm, gates_ref, sems.at[1]),
        pltpu.make_async_copy(tokens_ref.at[:, columns], x_ref, sems.at[2]),
        pltpu.make_async_copy(cot_ref.at[:, columns], y_ref.at[0:count, :], sems.at[3]),
        pltpu.make_async_copy(tokens_ref.at[:, columns], own_ref.at[0:count, :], sems.at[4]),
        pltpu.make_async_copy(cot_ref.at[:, columns], own_ref.at[count : 2 * count, :], sems.at[5]),
        pltpu.make_async_copy(w_hbm, w_ref, sems.at[6]),
    ]
    for copy in copies:
        copy.start()
    copies[0].wait()
    copies[1].wait()
    ids = ids_ref[...]
    gates = gates_ref[...].astype(jnp.float32)
    slots = y_ref.shape[0] - count
    row = lax.broadcasted_iota(jnp.int32, (slots, count), 0)
    gate = jnp.zeros((slots, count), jnp.float32)
    for k in range(ids.shape[0]):
        gate = gate + jnp.where(row == ids[k : k + 1, :], gates[k : k + 1, :], 0.0)
    y_ref[count:, 0:count] = gate.astype(jnp.bfloat16)
    y_ref[count:, count:] = jnp.zeros((slots, width - count), jnp.bfloat16)
    own_ref[2 * count :, :] = y_ref[count:, :]
    for copy in copies[2:]:
        copy.wait()


def pack_own(ids, gates, tokens, cotangent, weights, slots):
    count, top = ids.shape
    width = weights.shape[2]
    return pl.pallas_call(
        pack_kernel,
        in_specs=[in_hbm()] * 5,
        out_specs=[whole()] * 4,
        out_shape=[
            jax.ShapeDtypeStruct((rows, width), jnp.bfloat16)
            for rows in (count, count + slots, 2 * count + slots)
        ]
        + [jax.ShapeDtypeStruct(weights.shape, weights.dtype)],
        scratch_shapes=[
            pltpu.VMEM((top, count), ids.dtype),
            pltpu.VMEM((top, count), gates.dtype),
            pltpu.SemaphoreType.DMA((7,)),
        ],
        compiler_params=params(),
        cost_estimate=cost(1000, 8 * count * width),
    )(*[keep_hbm(value) for value in (ids.T, gates.T, tokens, cotangent, weights)])


def views(refs, kinds, count):
    xs, ys, gates = [], [], []
    for ref, kind in zip(refs, kinds):
        if kind in ("first x", "second x"):
            xs.append(ref[0 if kind == "first x" else 1])
            continue
        if kind == "x, y, y":
            rows = (ref.shape[0] - count) // 2
            xs.append(ref[0:count, :])
            for row in (count, count + rows):
                ys.append(ref[row : row + count, :])
                gates.append(ref[row + count : row + rows, 0:count])
            continue
        for part in [ref.at[0], ref.at[1]] if ref.ndim == 3 else [ref]:
            if kind == "x":
                xs.append(part[...])
            if kind == "xy":
                xs.append(part[0:count, :])
                ys.append(part[count : 2 * count, :])
                gates.append(part[2 * count :, 0:count])
            if kind == "y":
                ys.append(part[...])
            if kind == "y, gates":
                ys.append(part[0:count, :])
                gates.append(part[count:, 0:count])
            if kind == "half y, gates":
                ys.append(part[0 : count // 2, :])
                gates.append(part[count // 2 :, 0:count])
    return xs, ys, gates


def joined(parts):
    return parts[0] if len(parts) == 1 else jnp.concatenate(parts, 0)


def kinds_of(chunk):
    return tuple(kind for kind, value in chunk)


def values_of(chunk):
    return [value for kind, value in chunk]


def store_partials(parts, count, out_ref):
    row = 0
    for part in parts:
        for first in range(0, part.shape[1], count):
            piece = part[:, first : first + count]
            out_ref[row : row + piece.shape[0], :] = piece.astype(jnp.bfloat16)
            row = row + piece.shape[0]


def partial_kernel(kinds, count, w_ref, after_ref, *refs):
    n = len(kinds)
    xs, ys, gates = views(refs[:n], kinds, count)
    outs = refs[n:-1]
    mats, hidden, width = w_ref.shape
    parts = []
    if xs:
        parts.append(contract_last(w_ref[0:2].reshape(2 * hidden, width), joined(xs)))
    if ys:
        parts.append(contract_last(w_ref[2], joined(ys)))
    if len(outs) == 1:
        store_partials(parts, count, outs[0])
    else:
        for part, out_ref in zip(parts, outs):
            store_partials([part], count, out_ref)
    refs[-1][...] = jnp.zeros_like(refs[-1])


def partials(weights, after, chunk, rows, count):
    hidden, width = weights.shape[1:]
    kinds = kinds_of(chunk)
    total = sum(rows) * hidden * count
    return pl.pallas_call(
        functools.partial(partial_kernel, kinds, count),
        in_specs=[whole(), unread()] + [whole()] * len(kinds),
        out_specs=[whole()] * (len(rows) + 1),
        out_shape=[jax.ShapeDtypeStruct((k * hidden, count), jnp.bfloat16) for k in rows]
        + [jax.ShapeDtypeStruct((8, 128), jnp.float32)],
        compiler_params=params(),
        cost_estimate=cost(2 * total * width, 6 * total),
    )(weights, after, *values_of(chunk))


def start_kernel(kinds, count, w_hbm, *refs):
    n = len(kinds)
    out_ref, token_ref, w_ref, sems = refs[n:]
    mats, hidden, width = w_ref.shape
    copies = [pltpu.make_async_copy(w_hbm.at[m], w_ref.at[m], sems.at[m]) for m in range(mats)]
    for copy in copies:
        copy.start()
    xs, ys, gates = views(refs[:n], kinds, count)
    token_ref[...] = jnp.zeros_like(token_ref)
    parts = []
    for k, right in enumerate((joined(xs), joined(xs), joined(ys))):
        copies[k].wait()
        parts.append(contract_last(w_ref[k], right))
    gate, up, down = parts
    for k in range(gate.shape[1] // count):
        side = slice(k * count, (k + 1) * count)
        for m, part in ((2 * k, gate), (2 * k + 1, up), (gate.shape[1] // count * 2 + k, down)):
            out_ref[m * hidden : (m + 1) * hidden, :] = part[:, side].astype(jnp.bfloat16)


def start_partials(weights, chunk, rows, count):
    mats, hidden, width = weights.shape
    kinds = kinds_of(chunk)
    total = rows * hidden * count
    return pl.pallas_call(
        functools.partial(start_kernel, kinds, count),
        in_specs=[in_hbm()] + [whole()] * len(kinds),
        out_specs=[whole()] * 3,
        out_shape=[
            jax.ShapeDtypeStruct((rows * hidden, count), jnp.bfloat16),
            jax.ShapeDtypeStruct((8, 128), jnp.float32),
            jax.ShapeDtypeStruct(weights.shape, weights.dtype),
        ],
        scratch_shapes=[pltpu.SemaphoreType.DMA((mats,))],
        compiler_params=params(),
        cost_estimate=cost(2 * total * width, 6 * total),
    )(keep_hbm(weights), *values_of(chunk))


def gate_row(gates):
    rows = []
    expert = expert_here()
    for held in gates:
        held = held.astype(jnp.float32)
        index = lax.broadcasted_iota(jnp.int32, held.shape, 0)
        rows.append(jnp.sum(jnp.where(index == expert, held, 0.0), 0, keepdims=True))
    return rows[0] if len(rows) == 1 else jnp.concatenate(rows, 1)


def summed(pairs):
    parts = []
    for own, *got in pairs:
        part = own[...].astype(jnp.float32)
        parts.append(part + got[0][...].astype(jnp.float32) if got else part)
    return parts[0] if len(parts) == 1 else jnp.concatenate(parts, 0)


def beside(total, hidden, firsts):
    parts = [total[first * hidden : (first + 1) * hidden] for first in firsts]
    return jnp.concatenate(parts, 1)


def activation(hg, hu, gate):
    sig = jax.nn.sigmoid(hg)
    silu = hg * sig
    return sig, silu, (gate * (silu * hu)).astype(jnp.bfloat16)


def hidden_slopes(hg, hu, sig, silu, dact):
    dhg = (dact * hu * sig * (1.0 + hg * (1.0 - sig))).astype(jnp.bfloat16)
    dhu = (dact * silu).astype(jnp.bfloat16)
    return dhg, dhu


def hidden_grads(gate, pairs):
    total = summed(pairs)
    blocks = gate.shape[1] // total.shape[1]
    hidden = total.shape[0] // (3 * blocks)
    hg = beside(total, hidden, range(0, 2 * blocks, 2))
    hu = beside(total, hidden, range(1, 2 * blocks, 2))
    dact = gate * beside(total, hidden, range(2 * blocks, 3 * blocks))
    sig, silu, act = activation(hg, hu, gate)
    return (*hidden_slopes(hg, hu, sig, silu, dact), act)


def plain(left, right):
    return lax.dot_general(
        left, right, (((1,), (0,)), ((), ())), preferred_element_type=jnp.float32
    )


def onward_kernel(kinds, after_ref, own, got, near_own, near_got, *refs):
    x0_ref, x1_ref, s0_ref, y0_ref, y1_ref = refs[:5]
    pair_ref, rest_ref, out_ref, first_ref, sum_ref, gate_ref = refs[5 + len(kinds) :]
    count, rows = x0_ref.shape[0], y0_ref.shape[0]
    gates = views(refs[5 : 5 + len(kinds)], kinds, count)[2]
    gate_ref[...] = jnp.broadcast_to(gate_row(gates), gate_ref.shape)
    pair_ref[0] = x0_ref[...]
    pair_ref[1] = s0_ref[...]
    rest_ref[0:count, :] = x1_ref[...]
    rest_ref[count : count + rows, :] = y0_ref[...]
    rest_ref[count + rows :, :] = y1_ref[...]
    core = lax.axis_index("dp") % 2

    @pl.when(core == 0)
    def _():
        out_ref[0:count, :] = x0_ref[...]
        out_ref[count:, :] = y0_ref[...]

    @pl.when(core != 0)
    def _():
        out_ref[0:count, :] = x1_ref[...]
        out_ref[count:, :] = y1_ref[...]

    first_ref[...] = own[...].astype(jnp.float32) + got[...].astype(jnp.float32)
    sum_ref[...] = near_own[...].astype(jnp.float32) + near_got[...].astype(jnp.float32)


def pick_onward(after, pair, near_pair, near_x, other_x, near_y, chunk):
    count, width = other_x.shape
    rows = near_y[0].shape[0]
    operands = [*pair, *near_pair, *near_x, other_x, *near_y, *values_of(chunk)]
    return pl.pallas_call(
        functools.partial(onward_kernel, kinds_of(chunk)),
        in_specs=[unread()] + [whole()] * len(operands),
        out_specs=[whole()] * 6,
        out_shape=[
            jax.ShapeDtypeStruct((2, count, width), jnp.bfloat16),
            jax.ShapeDtypeStruct((count + 2 * rows, width), jnp.bfloat16),
            jax.ShapeDtypeStruct((count + rows, width), jnp.bfloat16),
            jax.ShapeDtypeStruct(pair[0].shape, jnp.float32),
            jax.ShapeDtypeStruct(near_pair[0].shape, jnp.float32),
            jax.ShapeDtypeStruct((8, 2 * count), jnp.float32),
        ],
        compiler_params=params(),
        cost_estimate=cost(1000, 8 * other_x.size),
    )(after, *operands)


def pass_kernel(after_ref, in_ref, *outs):
    row = 0
    for out_ref in outs:
        out_ref[...] = in_ref[row : row + out_ref.shape[0], :]
        row = row + out_ref.shape[0]


def passed_on(after, value, cuts):
    width = value.shape[1]
    return pl.pallas_call(
        pass_kernel,
        in_specs=[unread(), whole()],
        out_specs=[whole()] * len(cuts),
        out_shape=[jax.ShapeDtypeStruct((rows, width), value.dtype) for rows in cuts],
        compiler_params=params(),
        cost_estimate=cost(1000, 2 * value.size),
    )(after, value)


def first_kernel(kinds, count, gate_ref, after_ref, sum_ref, *refs):
    n = len(kinds)
    xs, ys, gates = views(refs[:n], kinds, count)
    out_ref, token_ref = refs[n:]
    lefts = hidden_grads(gate_ref[0:1, :], [(sum_ref,)])
    x = joined(xs)
    for m, right in enumerate((x, x, joined(ys))):
        out_ref[m] = plain(lefts[m], right)
    token_ref[...] = jnp.zeros_like(token_ref)


def first_grads(gate, after, total, chunk, hidden, count):
    kinds = kinds_of(chunk)
    width = chunk[0][1].shape[-1]
    return pl.pallas_call(
        functools.partial(first_kernel, kinds, count),
        in_specs=[whole(), unread()] + [whole()] * (1 + len(kinds)),
        out_specs=[whole()] * 2,
        out_shape=[
            jax.ShapeDtypeStruct((3, hidden, width), jnp.float32),
            jax.ShapeDtypeStruct((8, 128), jnp.float32),
        ],
        compiler_params=params(),
        cost_estimate=cost(2 * total.size * width, 12 * hidden * width),
    )(gate, after, total, *values_of(chunk))


def grad_kernel(kinds, count, sum_ref, own, got, *refs):
    n = len(kinds)
    xs, ys, gates = views(refs[:n], kinds, count)
    acc_ref, out_ref = refs[n:]
    lefts = hidden_grads(gate_row(gates), [(sum_ref,), (own, got)])
    x = joined(xs)
    for m, right in enumerate((x, x, joined(ys))):
        out_ref[m] = acc_ref[m] + plain(lefts[m], right)


def add_grads(near_sum, pair, chunk, acc, count):
    kinds = kinds_of(chunk)
    mats, hidden, width = acc.shape
    operands = [near_sum, *pair, *values_of(chunk), acc]
    return pl.pallas_call(
        functools.partial(grad_kernel, kinds, count),
        in_specs=[whole()] * len(operands),
        out_specs=whole(),
        out_shape=jax.ShapeDtypeStruct(acc.shape, jnp.float32),
        input_output_aliases={len(operands) - 1: 0},
        compiler_params=params(),
        cost_estimate=cost(
            2 * mats * hidden * width * 4 * count, 8 * mats * hidden * width
        ),
    )(*operands)


def adam(grad, first, second):
    moment_one = beta_one * first.astype(jnp.float32) + (1.0 - beta_one) * grad
    moment_two = beta_two * second.astype(jnp.float32) + (1.0 - beta_two) * (grad * grad)
    root = (1.0 / (1.0 - beta_two**step_count)) ** 0.5
    below = moment_two * lax.rsqrt(moment_two) + epsilon / root
    scaled = moment_one * (1.0 / (1.0 - beta_one**step_count) / root)
    step = scaled * pl.reciprocal(below, approx=True)
    return [value.astype(jnp.bfloat16) for value in (moment_one, moment_two, step)]


def gate_up(own, got):
    total = summed([(own, got)])
    hidden = total.shape[0] // 4
    return beside(total, hidden, (0, 2)), beside(total, hidden, (1, 3))


def down_kernel(kinds, count, own, got, *refs):
    n = len(kinds)
    acc_ref, first_ref, second_ref, *outs = refs[n:]
    xs, ys, gates = views(refs[:n], kinds, count)
    act = activation(*gate_up(own, got), gate_row(gates))[2]
    grad = acc_ref[2] + plain(act, joined(ys))
    for out_ref, value in zip(outs, adam(grad, first_ref[2], second_ref[2])):
        out_ref[...] = value


def down_update(pair, chunk, acc, moments, count):
    kinds = kinds_of(chunk)
    mats, hidden, width = acc.shape
    operands = [*pair, *values_of(chunk), acc, *moments]
    return pl.pallas_call(
        functools.partial(down_kernel, kinds, count),
        in_specs=[whole()] * len(operands),
        out_specs=[whole()] * 3,
        out_shape=[jax.ShapeDtypeStruct((hidden, width), jnp.bfloat16)] * 3,
        compiler_params=params(),
        cost_estimate=cost(4 * hidden * width * count, 14 * hidden * width),
    )(*operands)


def slopes_kernel(kinds, count, own, got, own_d, got_d, *refs):
    n = len(kinds)
    acc_ref, first_ref, second_ref = refs[n : n + 3]
    done, outs = refs[n + 3 : n + 6], refs[n + 6 : n + 9]
    held, sems = refs[n + 9 : n + 12], refs[n + 12]
    copies = [
        pltpu.make_async_copy(done[k], outs[k].at[2], sems.at[2, k]) for k in range(3)
    ]
    for copy in copies:
        copy.start()
    xs, ys, gates = views(refs[:n], kinds, count)
    hg, hu = gate_up(own, got)
    down = summed([(own_d, got_d)])
    dact = gate_row(gates) * beside(down, down.shape[0] // 2, (0, 1))
    sig, silu, act = activation(hg, hu, 1.0)
    right = joined(xs)
    for m, left in enumerate(hidden_slopes(hg, hu, sig, silu, dact)):
        grad = acc_ref[m] + plain(left, right)
        for k, value in enumerate(adam(grad, first_ref[m], second_ref[m])):
            held[k][m] = value
            copies.append(pltpu.make_async_copy(held[k].at[m], outs[k].at[m], sems.at[m, k]))
            copies[-1].start()
    for copy in copies:
        copy.wait()


def slopes_update(pair, down_pair, chunk, acc, moments, done, count):
    kinds = kinds_of(chunk)
    mats, hidden, width = acc.shape
    operands = [*pair, *down_pair, *values_of(chunk), acc, *moments, *done]
    return pl.pallas_call(
        functools.partial(slopes_kernel, kinds, count),
        in_specs=[whole()] * len(operands),
        out_specs=[in_hbm()] * 3,
        out_shape=[jax.ShapeDtypeStruct(acc.shape, jnp.bfloat16)] * 3,
        scratch_shapes=[pltpu.VMEM((2, hidden, width), jnp.bfloat16)] * 3
        + [pltpu.SemaphoreType.DMA((3, 3))],
        compiler_params=params(),
        cost_estimate=cost(8 * hidden * width * count, 28 * hidden * width),
    )(*operands)


def from_masked(value, axis, mask):
    pairs = [(source, source ^ mask) for source in range(lax.axis_size(axis))]
    return lax.ppermute(value, axis, pairs)


def dense_plan(tokens, cotangent, expert_ids, gate_probs, weights, first_moment, second_moment):
    n_data = lax.axis_size("dp")
    slices = min(4, lax.axis_size("expert") // 2)
    experts_total = lax.axis_size("expert") // (2 * slices) * n_data
    count = tokens.shape[0]
    hidden, width = weights.shape[1:]
    slots = -(-experts_total // 16) * 16
    other = lambda value: from_masked(value, "dp", 1)
    partner = lambda value: from_masked(value, "expert", 1)
    x_own, y_own, own, weights = pack_own(
        expert_ids, gate_probs, tokens, cotangent, weights, slots
    )
    first = [("xy", own), ("xy", other(own))]
    send, token = partials(weights, own, first, (6,), count)
    first_pair = (send, partner(send))
    near_x = [from_masked(x_own, "dp", mask) for mask in (2, 4)]
    near_y = [from_masked(y_own, "dp", mask) for mask in (2, 4)]
    send, token = partials(weights, token, [("x", near_x[0]), ("", near_x[1])], (2,), count)
    near_pair = (send, partner(send))
    x_pair, rest, picked, first_sum, near_sum, gate = pick_onward(
        token, first_pair, near_pair, near_x, other(near_x[0]), near_y, first
    )
    onward = [(p, p ^ 4 if p % 2 == 0 else p ^ 2) for p in range(n_data)]
    far = lax.ppermute(picked, "dp", onward)
    acc, token = first_grads(gate, picked, first_sum, first, hidden, count)
    ends = [("x, y, y", rest), ("second x", x_pair), ("x, y, y", other(rest))]
    send, token = partials(weights, token, ends, (10,), count)
    more_pair = (send, partner(send))
    pieces = passed_on(token, far, (count // 2, count // 2, count // 2, count // 2 + slots))
    pieces = [*pieces, *[other(value) for value in pieces]]
    final = list(zip(("x", "x", "y", "half y, gates") * 2, pieces))
    send, send_d, token = partials(weights, token, final, (4, 2), count)
    pair, down_pair = (send, partner(send)), (send_d, partner(send_d))
    near = [("first x", x_pair), *ends]
    acc = add_grads(near_sum, more_pair, near, acc, count)
    moments = (first_moment, second_moment)
    final_y = [block for block in final if block[0] != "x"]
    final_x = [block for block in final if block[0] != "y"]
    done = down_update(pair, final_y, acc, moments, count)
    return tuple(slopes_update(pair, down_pair, final_x, acc, moments, done, count))


def per_device(tokens, cotangent, expert_ids, gate_probs, weights, first_moment, second_moment):
    n_expert = lax.axis_size("expert")
    n_data = lax.axis_size("dp")
    slices = min(4, n_expert // 2)
    experts_total = n_expert // (2 * slices) * n_data
    half = tokens.shape[0] // 2
    dense = 2 * half * expert_ids.shape[1] // experts_total >= half
    plan = dense_plan if dense and n_data == 8 else routed_plan
    return plan(
        tokens, cotangent, expert_ids, gate_probs, weights, first_moment, second_moment
    )


def solution(mesh):
    in_specs = (
        P("dp", None),
        P("dp", None),
        P("dp", None),
        P("dp", None),
        P(None, "dp", "expert"),
        P(None, "dp", "expert"),
        P(None, "dp", "expert"),
    )
    out_specs = (P(None, "dp", "expert"), P(None, "dp", "expert"), P(None, "dp", "expert"))
    return jax.shard_map(
        per_device, mesh=mesh, in_specs=in_specs, out_specs=out_specs, check_vma=False
    )
```

```python
import functools

import jax
import jax.numpy as jnp
from jax import lax
from jax.experimental import pallas as pl
from jax.experimental.pallas import tpu as pltpu
from jax.sharding import PartitionSpec as P

beta_one = 0.9
beta_two = 0.95
step_count = 10
epsilon = 1e-08


def from_partner(value, axis, distance):
    mask = 2**distance
    pairs = [(source, source ^ mask) for source in range(lax.axis_size(axis))]
    return lax.ppermute(value, axis, pairs)


def contract_last(left, right):
    return lax.dot_general(
        left, right, (((1,), (1,)), ((), ())), preferred_element_type=jnp.float32
    )


def contract_first(left, right):
    return lax.dot_general(
        left, right, (((0,), (0,)), ((), ())), preferred_element_type=jnp.float32
    )


def split_halves(grad, replica, width_half):
    keep = lax.dynamic_slice_in_dim(grad, replica * width_half, width_half, grad.ndim - 1)
    give = lax.dynamic_slice_in_dim(grad, (1 - replica) * width_half, width_half, grad.ndim - 1)
    return (keep, give)


def route_block(block_ids, block_gates, group, n_data, capacity):
    count = block_ids.shape[0]
    top = block_ids.shape[1]
    target = block_ids - group * n_data
    inside = block_ids // n_data == group
    onehot = (
        (target[:, :, None] == jnp.arange(n_data, dtype=jnp.int32)[None, None, :])
        & inside[:, :, None]
    ).astype(jnp.int32)
    per_token = jnp.sum(onehot, axis=1)
    earlier = jnp.cumsum(per_token, axis=0) - per_token
    rank = jnp.sum(onehot * earlier[:, None, :], axis=2)
    total_slots = n_data * capacity
    slot = jnp.where(inside, target * capacity + rank, total_slots).reshape(-1)
    token_of = jnp.broadcast_to(jnp.arange(count, dtype=jnp.int32)[:, None], (count, top)).reshape(
        -1
    )
    table = jnp.full((total_slots,), count, jnp.int32).at[slot].set(token_of, mode="drop")
    gate_slot = (
        jnp.zeros((total_slots,), jnp.bfloat16).at[slot].set(block_gates.reshape(-1), mode="drop")
    )
    return (table, gate_slot)


def routed_plan(tokens, cotangent, expert_ids, gate_probs, weights, first_moment, second_moment):
    n_expert = lax.axis_size("expert")
    n_data = lax.axis_size("dp")
    slices = min(4, n_expert // 2)
    place = lax.axis_index("expert")
    replica = place % 2
    group = place // (2 * slices)
    groups = n_expert // (2 * slices)
    experts_total = groups * n_data
    half = tokens.shape[0] // 2
    width_half = weights.shape[2]
    top = expert_ids.shape[1]
    capacity = max(2, 2 * half * top // experts_total)
    start = replica * half
    own_ids = lax.dynamic_slice_in_dim(expert_ids, start, half, 0)
    own_gates = lax.dynamic_slice_in_dim(gate_probs, start, half, 0)
    table, gate_slot = route_block(own_ids, own_gates, group, n_data, capacity)
    source_tokens = lax.dynamic_slice_in_dim(tokens, start, half, 0)
    source_cot = lax.dynamic_slice_in_dim(cotangent, start, half, 0)
    columns = source_tokens.shape[1]
    padded_tokens = jnp.concatenate([source_tokens, jnp.zeros((1, columns), jnp.bfloat16)], 0)
    padded_cot = jnp.concatenate([source_cot, jnp.zeros((1, columns), jnp.bfloat16)], 0)
    send_rows = padded_tokens[table].reshape(n_data, -1, columns)
    send_cot = padded_cot[table].reshape(n_data, -1, columns)
    send_gates = gate_slot.reshape(n_data, -1)
    rows_in, gates_in = (
        lax.all_to_all(send_rows, "dp", split_axis=0, concat_axis=0, tiled=True),
        lax.all_to_all(send_gates, "dp", split_axis=0, concat_axis=0, tiled=True),
    )
    rows = rows_in.reshape(-1, columns)
    gate_rows = gates_in.reshape(-1).astype(jnp.float32)
    partner = from_partner(weights, "expert", 0)
    lower = jnp.where(replica == 0, weights, partner)
    upper = jnp.where(replica == 0, partner, weights)
    full = jnp.concatenate([lower, upper], 2)
    hg = contract_last(rows, full[0])
    hu = contract_last(rows, full[1])
    sig = jax.nn.sigmoid(hg)
    act = (hg * sig * hu).astype(jnp.bfloat16)
    cot_in = lax.all_to_all(send_cot, "dp", split_axis=0, concat_axis=0, tiled=True)
    cots = cot_in.reshape(-1, columns)
    dz = (gate_rows[:, None] * cots.astype(jnp.float32)).astype(jnp.bfloat16)
    dact = contract_last(dz, full[2])
    grad_down = contract_first(act, dz)
    dhg = (dact * hu * sig * (1.0 + hg * (1.0 - sig))).astype(jnp.bfloat16)
    dhu = (dact * hg * sig).astype(jnp.bfloat16)
    grad_gate = contract_first(dhg, rows)
    grad_up = contract_first(dhu, rows)
    stacked = jnp.stack([grad_gate, grad_up, grad_down])
    keep, give = split_halves(stacked, replica, width_half)
    total = keep + from_partner(give, "expert", 0)
    moment_one = beta_one * first_moment.astype(jnp.float32) + (1.0 - beta_one) * total
    moment_two = beta_two * second_moment.astype(jnp.float32) + (1.0 - beta_two) * total * total
    step = (
        moment_one
        / (1.0 - beta_one**step_count)
        / (jnp.sqrt(moment_two / (1.0 - beta_two**step_count)) + epsilon)
    )
    return (
        moment_one.astype(jnp.bfloat16),
        moment_two.astype(jnp.bfloat16),
        step.astype(jnp.bfloat16),
    )


VMEM_LIMIT = 16 * 1024 * 1024


def params():
    return pltpu.CompilerParams(vmem_limit_bytes=VMEM_LIMIT)


def cost(flops, moved):
    return pl.CostEstimate(flops=flops, bytes_accessed=moved, transcendentals=0)


def whole():
    return pl.BlockSpec(memory_space=pltpu.VMEM)


def in_hbm():
    return pl.BlockSpec(memory_space=pltpu.HBM)


def unread():
    return pl.BlockSpec(memory_space=pl.ANY)


def expert_here():
    slices = min(4, lax.axis_size("expert") // 2)
    group = lax.axis_index("expert") // (2 * slices)
    return group * lax.axis_size("dp") + lax.axis_index("dp")


def keep_hbm(value):
    return pltpu.with_memory_space_constraint(value, pltpu.HBM)


def pack_kernel(
    ids_hbm,
    gates_hbm,
    tokens_ref,
    cot_ref,
    w_hbm,
    x_ref,
    y_ref,
    own_ref,
    w_ref,
    ids_ref,
    gates_ref,
    sems,
):
    count = tokens_ref.shape[0]
    width = x_ref.shape[1]
    columns = pl.ds(pl.multiple_of(lax.axis_index("expert") % 2 * width, width), width)
    copies = [
        pltpu.make_async_copy(ids_hbm, ids_ref, sems.at[0]),
        pltpu.make_async_copy(gates_hbm, gates_ref, sems.at[1]),
        pltpu.make_async_copy(tokens_ref.at[:, columns], x_ref, sems.at[2]),
        pltpu.make_async_copy(cot_ref.at[:, columns], y_ref.at[0:count, :], sems.at[3]),
        pltpu.make_async_copy(tokens_ref.at[:, columns], own_ref.at[0:count, :], sems.at[4]),
        pltpu.make_async_copy(cot_ref.at[:, columns], own_ref.at[count : 2 * count, :], sems.at[5]),
        pltpu.make_async_copy(w_hbm, w_ref, sems.at[6]),
    ]
    for copy in copies:
        copy.start()
    copies[0].wait()
    copies[1].wait()
    ids = ids_ref[...]
    gates = gates_ref[...].astype(jnp.float32)
    slots = y_ref.shape[0] - count
    row = lax.broadcasted_iota(jnp.int32, (slots, count), 0)
    gate = jnp.zeros((slots, count), jnp.float32)
    for k in range(ids.shape[0]):
        gate = gate + jnp.where(row == ids[k : k + 1, :], gates[k : k + 1, :], 0.0)
    y_ref[count:, 0:count] = gate.astype(jnp.bfloat16)
    y_ref[count:, count:] = jnp.zeros((slots, width - count), jnp.bfloat16)
    own_ref[2 * count :, :] = y_ref[count:, :]
    for copy in copies[2:]:
        copy.wait()


def pack_own(ids, gates, tokens, cotangent, weights, slots):
    count, top = ids.shape
    width = weights.shape[2]
    return pl.pallas_call(
        pack_kernel,
        in_specs=[in_hbm()] * 5,
        out_specs=[whole()] * 4,
        out_shape=[
            jax.ShapeDtypeStruct((rows, width), jnp.bfloat16)
            for rows in (count, count + slots, 2 * count + slots)
        ]
        + [jax.ShapeDtypeStruct(weights.shape, weights.dtype)],
        scratch_shapes=[
            pltpu.VMEM((top, count), ids.dtype),
            pltpu.VMEM((top, count), gates.dtype),
            pltpu.SemaphoreType.DMA((7,)),
        ],
        compiler_params=params(),
        cost_estimate=cost(1000, 8 * count * width),
    )(*[keep_hbm(value) for value in (ids.T, gates.T, tokens, cotangent, weights)])


def views(refs, kinds, count):
    xs, ys, gates = [], [], []
    for ref, kind in zip(refs, kinds):
        if kind in ("first x", "second x"):
            xs.append(ref[0 if kind == "first x" else 1])
            continue
        if kind == "x, y, y":
            rows = (ref.shape[0] - count) // 2
            xs.append(ref[0:count, :])
            for row in (count, count + rows):
                ys.append(ref[row : row + count, :])
                gates.append(ref[row + count : row + rows, 0:count])
            continue
        for part in [ref.at[0], ref.at[1]] if ref.ndim == 3 else [ref]:
            if kind == "x":
                xs.append(part[...])
            if kind == "xy":
                xs.append(part[0:count, :])
                ys.append(part[count : 2 * count, :])
                gates.append(part[2 * count :, 0:count])
            if kind == "y":
                ys.append(part[...])
            if kind == "y, gates":
                ys.append(part[0:count, :])
                gates.append(part[count:, 0:count])
            if kind == "half y, gates":
                ys.append(part[0 : count // 2, :])
                gates.append(part[count // 2 :, 0:count])
    return xs, ys, gates


def joined(parts):
    return parts[0] if len(parts) == 1 else jnp.concatenate(parts, 0)


def kinds_of(chunk):
    return tuple(kind for kind, value in chunk)


def values_of(chunk):
    return [value for kind, value in chunk]


def store_partials(parts, count, out_ref):
    row = 0
    for part in parts:
        for first in range(0, part.shape[1], count):
            piece = part[:, first : first + count]
            out_ref[row : row + piece.shape[0], :] = piece.astype(jnp.bfloat16)
            row = row + piece.shape[0]


def partial_kernel(kinds, count, tokened, w_ref, after_ref, *refs):
    n = len(kinds)
    xs, ys, gates = views(refs[:n], kinds, count)
    outs = refs[n : n + len(refs[n:]) - tokened]
    mats, hidden, width = w_ref.shape
    parts = []
    if xs:
        parts.append(contract_last(w_ref[0:2].reshape(2 * hidden, width), joined(xs)))
    if ys:
        parts.append(contract_last(w_ref[2], joined(ys)))
    if len(outs) == 1:
        store_partials(parts, count, outs[0])
    else:
        for part, out_ref in zip(parts, outs):
            store_partials([part], count, out_ref)
    if tokened:
        refs[-1][...] = jnp.zeros_like(refs[-1])


def partials(weights, after, chunk, rows, count, tokened=1):
    hidden, width = weights.shape[1:]
    kinds = kinds_of(chunk)
    total = sum(rows) * hidden * count
    return pl.pallas_call(
        functools.partial(partial_kernel, kinds, count, tokened),
        in_specs=[whole(), unread()] + [whole()] * len(kinds),
        out_specs=[whole()] * (len(rows) + tokened),
        out_shape=[jax.ShapeDtypeStruct((k * hidden, count), jnp.bfloat16) for k in rows]
        + [jax.ShapeDtypeStruct((8, 128), jnp.float32)] * tokened,
        compiler_params=params(),
        cost_estimate=cost(2 * total * width, 6 * total),
    )(weights, after, *values_of(chunk))


def side_kernel(kinds, count, gu_row, down_row, has_send, w_ref, *refs):
    n = len(kinds)
    xs, ys, gates = views(refs[:n], kinds, count)
    send_ref, token_ref = refs[n + has_send :]
    mats, hidden, width = w_ref.shape
    gu = contract_last(w_ref[0:2].reshape(2 * hidden, width), joined(xs))
    down = contract_last(w_ref[2], joined(ys))
    for row, part in ((gu_row, gu), (down_row, down)):
        rows = part.shape[1] // count * part.shape[0]
        store_partials([part], count, send_ref.at[row : row + rows, :])
    token_ref[...] = jnp.zeros_like(token_ref)


def side_partials(weights, chunk, send, blocks, first_gu, first_down, count):
    hidden, width = weights.shape[1:]
    kinds = kinds_of(chunk)
    operands = [weights, *values_of(chunk)] + ([] if send is None else [send])
    gu_row = first_gu * 2 * hidden
    down_row = (2 * blocks[0] + first_down) * hidden
    shape = ((2 * blocks[0] + blocks[1]) * hidden, count)
    return pl.pallas_call(
        functools.partial(side_kernel, kinds, count, gu_row, down_row, send is not None),
        in_specs=[whole()] * len(operands),
        out_specs=[whole()] * 2,
        out_shape=[
            jax.ShapeDtypeStruct(shape, jnp.bfloat16),
            jax.ShapeDtypeStruct((8, 128), jnp.float32),
        ],
        input_output_aliases={} if send is None else {len(operands) - 1: 0},
        compiler_params=params(),
        cost_estimate=cost(shape[0] * count * width, 3 * shape[0] * count),
    )(*operands)


def start_kernel(kinds, count, w_hbm, *refs):
    n = len(kinds)
    out_ref, token_ref, w_ref, sems = refs[n:]
    mats, hidden, width = w_ref.shape
    copies = [pltpu.make_async_copy(w_hbm.at[m], w_ref.at[m], sems.at[m]) for m in range(mats)]
    for copy in copies:
        copy.start()
    xs, ys, gates = views(refs[:n], kinds, count)
    token_ref[...] = jnp.zeros_like(token_ref)
    parts = []
    for k, right in enumerate((joined(xs), joined(xs), joined(ys))):
        copies[k].wait()
        parts.append(contract_last(w_ref[k], right))
    gate, up, down = parts
    for k in range(gate.shape[1] // count):
        side = slice(k * count, (k + 1) * count)
        for m, part in ((2 * k, gate), (2 * k + 1, up), (gate.shape[1] // count * 2 + k, down)):
            out_ref[m * hidden : (m + 1) * hidden, :] = part[:, side].astype(jnp.bfloat16)


def start_partials(weights, chunk, rows, count):
    mats, hidden, width = weights.shape
    kinds = kinds_of(chunk)
    total = rows * hidden * count
    return pl.pallas_call(
        functools.partial(start_kernel, kinds, count),
        in_specs=[in_hbm()] + [whole()] * len(kinds),
        out_specs=[whole()] * 3,
        out_shape=[
            jax.ShapeDtypeStruct((rows * hidden, count), jnp.bfloat16),
            jax.ShapeDtypeStruct((8, 128), jnp.float32),
            jax.ShapeDtypeStruct(weights.shape, weights.dtype),
        ],
        scratch_shapes=[pltpu.SemaphoreType.DMA((mats,))],
        compiler_params=params(),
        cost_estimate=cost(2 * total * width, 6 * total),
    )(keep_hbm(weights), *values_of(chunk))


def gate_row(gates):
    rows = []
    expert = expert_here()
    for held in gates:
        held = held.astype(jnp.float32)
        index = lax.broadcasted_iota(jnp.int32, held.shape, 0)
        rows.append(jnp.sum(jnp.where(index == expert, held, 0.0), 0, keepdims=True))
    return rows[0] if len(rows) == 1 else jnp.concatenate(rows, 1)


def summed(pairs):
    parts = []
    for own, *got in pairs:
        part = own[...].astype(jnp.float32)
        parts.append(part + got[0][...].astype(jnp.float32) if got else part)
    return parts[0] if len(parts) == 1 else jnp.concatenate(parts, 0)


def beside(total, hidden, firsts):
    parts = [total[first * hidden : (first + 1) * hidden] for first in firsts]
    return jnp.concatenate(parts, 1)


def activation(hg, hu, gate):
    sig = jax.nn.sigmoid(hg)
    silu = hg * sig
    return sig, silu, (gate * (silu * hu)).astype(jnp.bfloat16)


def hidden_slopes(hg, hu, sig, silu, dact):
    dhg = (dact * hu * sig * (1.0 + hg * (1.0 - sig))).astype(jnp.bfloat16)
    dhu = (dact * silu).astype(jnp.bfloat16)
    return dhg, dhu


def hidden_grads(gate, pairs):
    total = summed(pairs)
    blocks = gate.shape[1] // total.shape[1]
    hidden = total.shape[0] // (3 * blocks)
    hg = beside(total, hidden, range(0, 2 * blocks, 2))
    hu = beside(total, hidden, range(1, 2 * blocks, 2))
    dact = gate * beside(total, hidden, range(2 * blocks, 3 * blocks))
    sig, silu, act = activation(hg, hu, gate)
    return (*hidden_slopes(hg, hu, sig, silu, dact), act)


def plain(left, right):
    return lax.dot_general(
        left, right, (((1,), (0,)), ((), ())), preferred_element_type=jnp.float32
    )


def onward_kernel(kinds, after_ref, own, got, near_own, near_got, *refs):
    x0_ref, x1_ref, s0_ref, y0_ref, y1_ref = refs[:5]
    pair_ref, rest_ref, out_ref, first_ref, sum_ref, gate_ref = refs[5 + len(kinds) :]
    count, rows = x0_ref.shape[0], y0_ref.shape[0]
    gates = views(refs[5 : 5 + len(kinds)], kinds, count)[2]
    gate_ref[...] = jnp.broadcast_to(gate_row(gates), gate_ref.shape)
    pair_ref[0] = x0_ref[...]
    pair_ref[1] = s0_ref[...]
    rest_ref[0:count, :] = x1_ref[...]
    rest_ref[count : count + rows, :] = y0_ref[...]
    rest_ref[count + rows :, :] = y1_ref[...]
    out_ref[0:count, :] = x0_ref[...]
    out_ref[count:, :] = y0_ref[...]
    first_ref[...] = own[...].astype(jnp.float32) + got[...].astype(jnp.float32)
    sum_ref[...] = near_own[...].astype(jnp.float32) + near_got[...].astype(jnp.float32)


def pick_onward(after, pair, near_pair, near_x, other_x, near_y, chunk):
    count, width = other_x.shape
    rows = near_y[0].shape[0]
    operands = [*pair, *near_pair, *near_x, other_x, *near_y, *values_of(chunk)]
    return pl.pallas_call(
        functools.partial(onward_kernel, kinds_of(chunk)),
        in_specs=[unread()] + [whole()] * len(operands),
        out_specs=[whole()] * 6,
        out_shape=[
            jax.ShapeDtypeStruct((2, count, width), jnp.bfloat16),
            jax.ShapeDtypeStruct((count + 2 * rows, width), jnp.bfloat16),
            jax.ShapeDtypeStruct((count + rows, width), jnp.bfloat16),
            jax.ShapeDtypeStruct(pair[0].shape, jnp.float32),
            jax.ShapeDtypeStruct(near_pair[0].shape, jnp.float32),
            jax.ShapeDtypeStruct((8, 2 * count), jnp.float32),
        ],
        compiler_params=params(),
        cost_estimate=cost(1000, 8 * other_x.size),
    )(after, *operands)


def pass_kernel(after_ref, in_ref, *outs):
    row = 0
    for out_ref in outs:
        out_ref[...] = in_ref[row : row + out_ref.shape[0], :]
        row = row + out_ref.shape[0]


def passed_on(after, value, cuts):
    width = value.shape[1]
    return pl.pallas_call(
        pass_kernel,
        in_specs=[unread(), whole()],
        out_specs=[whole()] * len(cuts),
        out_shape=[jax.ShapeDtypeStruct((rows, width), value.dtype) for rows in cuts],
        compiler_params=params(),
        cost_estimate=cost(1000, 2 * value.size),
    )(after, value)


def first_kernel(kinds, count, gate_ref, after_ref, sum_ref, *refs):
    n = len(kinds)
    xs, ys, gates = views(refs[:n], kinds, count)
    out_ref, token_ref = refs[n:]
    lefts = hidden_grads(gate_ref[0:1, :], [(sum_ref,)])
    x = joined(xs)
    for m, right in enumerate((x, x, joined(ys))):
        out_ref[m] = plain(lefts[m], right)
    token_ref[...] = jnp.zeros_like(token_ref)


def first_grads(gate, after, total, chunk, hidden, count):
    kinds = kinds_of(chunk)
    width = chunk[0][1].shape[-1]
    return pl.pallas_call(
        functools.partial(first_kernel, kinds, count),
        in_specs=[whole(), unread()] + [whole()] * (1 + len(kinds)),
        out_specs=[whole()] * 2,
        out_shape=[
            jax.ShapeDtypeStruct((3, hidden, width), jnp.float32),
            jax.ShapeDtypeStruct((8, 128), jnp.float32),
        ],
        compiler_params=params(),
        cost_estimate=cost(2 * total.size * width, 12 * hidden * width),
    )(gate, after, total, *values_of(chunk))


def grad_kernel(kinds, count, sum_ref, own, got, *refs):
    n = len(kinds)
    xs, ys, gates = views(refs[:n], kinds, count)
    acc_ref, out_ref = refs[n:]
    lefts = hidden_grads(gate_row(gates), [(sum_ref,), (own, got)])
    x = joined(xs)
    for m, right in enumerate((x, x, joined(ys))):
        out_ref[m] = acc_ref[m] + plain(lefts[m], right)


def add_grads(near_sum, pair, chunk, acc, count):
    kinds = kinds_of(chunk)
    mats, hidden, width = acc.shape
    operands = [near_sum, *pair, *values_of(chunk), acc]
    return pl.pallas_call(
        functools.partial(grad_kernel, kinds, count),
        in_specs=[whole()] * len(operands),
        out_specs=whole(),
        out_shape=jax.ShapeDtypeStruct(acc.shape, jnp.float32),
        input_output_aliases={len(operands) - 1: 0},
        compiler_params=params(),
        cost_estimate=cost(
            2 * mats * hidden * width * 4 * count, 8 * mats * hidden * width
        ),
    )(*operands)


def adam(grad, first, second):
    moment_one = beta_one * first.astype(jnp.float32) + (1.0 - beta_one) * grad
    moment_two = beta_two * second.astype(jnp.float32) + (1.0 - beta_two) * (grad * grad)
    root = (1.0 / (1.0 - beta_two**step_count)) ** 0.5
    below = moment_two * lax.rsqrt(moment_two) + epsilon / root
    scaled = moment_one * (1.0 / (1.0 - beta_one**step_count) / root)
    step = scaled * pl.reciprocal(below, approx=True)
    return [value.astype(jnp.bfloat16) for value in (moment_one, moment_two, step)]


def gate_up(own, got):
    total = summed([(own, got)])
    hidden = total.shape[0] // 4
    return beside(total, hidden, (0, 2)), beside(total, hidden, (1, 3))


def down_kernel(kinds, count, own, got, *refs):
    n = len(kinds)
    acc_ref, first_ref, second_ref, *outs = refs[n:]
    xs, ys, gates = views(refs[:n], kinds, count)
    act = activation(*gate_up(own, got), gate_row(gates))[2]
    grad = acc_ref[2] + plain(act, joined(ys))
    for out_ref, value in zip(outs, adam(grad, first_ref[2], second_ref[2])):
        out_ref[...] = value


def down_update(pair, chunk, acc, moments, count):
    kinds = kinds_of(chunk)
    mats, hidden, width = acc.shape
    operands = [*pair, *values_of(chunk), acc, *moments]
    return pl.pallas_call(
        functools.partial(down_kernel, kinds, count),
        in_specs=[whole()] * len(operands),
        out_specs=[whole()] * 3,
        out_shape=[jax.ShapeDtypeStruct((hidden, width), jnp.bfloat16)] * 3,
        compiler_params=params(),
        cost_estimate=cost(4 * hidden * width * count, 14 * hidden * width),
    )(*operands)


def slopes_kernel(kinds, count, own, got, own_d, got_d, *refs):
    n = len(kinds)
    acc_ref, first_ref, second_ref = refs[n : n + 3]
    done, outs = refs[n + 3 : n + 6], refs[n + 6 : n + 9]
    held, sems = refs[n + 9 : n + 12], refs[n + 12]
    copies = [
        pltpu.make_async_copy(done[k], outs[k].at[2], sems.at[2, k]) for k in range(3)
    ]
    for copy in copies:
        copy.start()
    xs, ys, gates = views(refs[:n], kinds, count)
    hg, hu = gate_up(own, got)
    down = summed([(own_d, got_d)])
    dact = gate_row(gates) * beside(down, down.shape[0] // 2, (0, 1))
    sig, silu, act = activation(hg, hu, 1.0)
    right = joined(xs)
    for m, left in enumerate(hidden_slopes(hg, hu, sig, silu, dact)):
        grad = acc_ref[m] + plain(left, right)
        for k, value in enumerate(adam(grad, first_ref[m], second_ref[m])):
            held[k][m] = value
            copies.append(pltpu.make_async_copy(held[k].at[m], outs[k].at[m], sems.at[m, k]))
            copies[-1].start()
    for copy in copies:
        copy.wait()


def slopes_update(pair, down_pair, chunk, acc, moments, done, count):
    kinds = kinds_of(chunk)
    mats, hidden, width = acc.shape
    operands = [*pair, *down_pair, *values_of(chunk), acc, *moments, *done]
    return pl.pallas_call(
        functools.partial(slopes_kernel, kinds, count),
        in_specs=[whole()] * len(operands),
        out_specs=[in_hbm()] * 3,
        out_shape=[jax.ShapeDtypeStruct(acc.shape, jnp.bfloat16)] * 3,
        scratch_shapes=[pltpu.VMEM((2, hidden, width), jnp.bfloat16)] * 3
        + [pltpu.SemaphoreType.DMA((3, 3))],
        compiler_params=params(),
        cost_estimate=cost(8 * hidden * width * count, 28 * hidden * width),
    )(*operands)


def from_masked(value, axis, mask):
    pairs = [(source, source ^ mask) for source in range(lax.axis_size(axis))]
    return lax.ppermute(value, axis, pairs)


def dense_plan(tokens, cotangent, expert_ids, gate_probs, weights, first_moment, second_moment):
    n_data = lax.axis_size("dp")
    slices = min(4, lax.axis_size("expert") // 2)
    experts_total = lax.axis_size("expert") // (2 * slices) * n_data
    count = tokens.shape[0]
    hidden, width = weights.shape[1:]
    slots = -(-experts_total // 16) * 16
    other = lambda value: from_masked(value, "dp", 1)
    partner = lambda value: from_masked(value, "expert", 1)
    x_own, y_own, own, weights = pack_own(
        expert_ids, gate_probs, tokens, cotangent, weights, slots
    )
    first = [("xy", own), ("xy", other(own))]
    send, token = partials(weights, own, first, (6,), count)
    first_pair = (send, partner(send))
    along = [[(p, p ^ (2 if p % 2 == k else 4)) for p in range(n_data)] for k in (0, 1)]
    near_x = [lax.ppermute(x_own, "dp", pairs) for pairs in along]
    near_y = [lax.ppermute(y_own, "dp", pairs) for pairs in along]
    send, token = partials(weights, token, [("x", near_x[0]), ("", near_x[1])], (2,), count)
    near_pair = (send, partner(send))
    x_pair, rest, picked, first_sum, near_sum, gate = pick_onward(
        token, first_pair, near_pair, near_x, other(near_x[0]), near_y, first
    )
    far = lax.ppermute(picked, "dp", along[1])
    ends = [("x, y, y", rest), ("second x", x_pair), ("x, y, y", other(rest))]
    send, token = side_partials(weights, ends[:2], None, (3, 4), 0, 0, count)
    send, token = side_partials(weights, ends[2:], send, (3, 4), 2, 2, count)
    more_pair = (send, partner(send))
    acc, token = first_grads(gate, token, first_sum, first, hidden, count)
    pieces = passed_on(token, far, (count // 2, count // 2, count // 2, count // 2 + slots))
    pieces = [*pieces, *[other(value) for value in pieces]]
    final = list(zip(("x", "x", "y", "half y, gates") * 2, pieces))
    send, send_d = partials(weights, token, final, (4, 2), count, 0)
    pair, down_pair = (send, partner(send)), (send_d, partner(send_d))
    near = [("first x", x_pair), *ends]
    acc = add_grads(near_sum, more_pair, near, acc, count)
    moments = (first_moment, second_moment)
    final_y = [block for block in final if block[0] != "x"]
    final_x = [block for block in final if block[0] != "y"]
    done = down_update(pair, final_y, acc, moments, count)
    return tuple(slopes_update(pair, down_pair, final_x, acc, moments, done, count))


def per_device(tokens, cotangent, expert_ids, gate_probs, weights, first_moment, second_moment):
    n_expert = lax.axis_size("expert")
    n_data = lax.axis_size("dp")
    slices = min(4, n_expert // 2)
    experts_total = n_expert // (2 * slices) * n_data
    half = tokens.shape[0] // 2
    dense = 2 * half * expert_ids.shape[1] // experts_total >= half
    plan = dense_plan if dense and n_data == 8 else routed_plan
    return plan(
        tokens, cotangent, expert_ids, gate_probs, weights, first_moment, second_moment
    )


def solution(mesh):
    in_specs = (
        P("dp", None),
        P("dp", None),
        P("dp", None),
        P("dp", None),
        P(None, "dp", "expert"),
        P(None, "dp", "expert"),
        P(None, "dp", "expert"),
    )
    out_specs = (P(None, "dp", "expert"), P(None, "dp", "expert"), P(None, "dp", "expert"))
    return jax.shard_map(
        per_device, mesh=mesh, in_specs=in_specs, out_specs=out_specs, check_vma=False
    )
```

```python
import functools

import jax
import jax.numpy as jnp
from jax import lax
from jax.experimental import pallas as pl
from jax.experimental.pallas import tpu as pltpu
from jax.sharding import PartitionSpec as P

beta_one = 0.9
beta_two = 0.95
step_count = 10
epsilon = 1e-08


def from_partner(value, axis, distance):
    mask = 2**distance
    pairs = [(source, source ^ mask) for source in range(lax.axis_size(axis))]
    return lax.ppermute(value, axis, pairs)


def contract_last(left, right):
    return lax.dot_general(
        left, right, (((1,), (1,)), ((), ())), preferred_element_type=jnp.float32
    )


def contract_first(left, right):
    return lax.dot_general(
        left, right, (((0,), (0,)), ((), ())), preferred_element_type=jnp.float32
    )


def split_halves(grad, replica, width_half):
    keep = lax.dynamic_slice_in_dim(grad, replica * width_half, width_half, grad.ndim - 1)
    give = lax.dynamic_slice_in_dim(grad, (1 - replica) * width_half, width_half, grad.ndim - 1)
    return (keep, give)


def route_block(block_ids, block_gates, group, n_data, capacity):
    count = block_ids.shape[0]
    top = block_ids.shape[1]
    target = block_ids - group * n_data
    inside = block_ids // n_data == group
    onehot = (
        (target[:, :, None] == jnp.arange(n_data, dtype=jnp.int32)[None, None, :])
        & inside[:, :, None]
    ).astype(jnp.int32)
    per_token = jnp.sum(onehot, axis=1)
    earlier = jnp.cumsum(per_token, axis=0) - per_token
    rank = jnp.sum(onehot * earlier[:, None, :], axis=2)
    total_slots = n_data * capacity
    slot = jnp.where(inside, target * capacity + rank, total_slots).reshape(-1)
    token_of = jnp.broadcast_to(jnp.arange(count, dtype=jnp.int32)[:, None], (count, top)).reshape(
        -1
    )
    table = jnp.full((total_slots,), count, jnp.int32).at[slot].set(token_of, mode="drop")
    gate_slot = (
        jnp.zeros((total_slots,), jnp.bfloat16).at[slot].set(block_gates.reshape(-1), mode="drop")
    )
    return (table, gate_slot)


def routed_plan(tokens, cotangent, expert_ids, gate_probs, weights, first_moment, second_moment):
    n_expert = lax.axis_size("expert")
    n_data = lax.axis_size("dp")
    slices = min(4, n_expert // 2)
    place = lax.axis_index("expert")
    replica = place % 2
    group = place // (2 * slices)
    groups = n_expert // (2 * slices)
    experts_total = groups * n_data
    half = tokens.shape[0] // 2
    width_half = weights.shape[2]
    top = expert_ids.shape[1]
    capacity = max(2, 2 * half * top // experts_total)
    start = replica * half
    own_ids = lax.dynamic_slice_in_dim(expert_ids, start, half, 0)
    own_gates = lax.dynamic_slice_in_dim(gate_probs, start, half, 0)
    table, gate_slot = route_block(own_ids, own_gates, group, n_data, capacity)
    source_tokens = lax.dynamic_slice_in_dim(tokens, start, half, 0)
    source_cot = lax.dynamic_slice_in_dim(cotangent, start, half, 0)
    columns = source_tokens.shape[1]
    padded_tokens = jnp.concatenate([source_tokens, jnp.zeros((1, columns), jnp.bfloat16)], 0)
    padded_cot = jnp.concatenate([source_cot, jnp.zeros((1, columns), jnp.bfloat16)], 0)
    send_rows = padded_tokens[table].reshape(n_data, -1, columns)
    send_cot = padded_cot[table].reshape(n_data, -1, columns)
    send_gates = gate_slot.reshape(n_data, -1)
    rows_in, gates_in = (
        lax.all_to_all(send_rows, "dp", split_axis=0, concat_axis=0, tiled=True),
        lax.all_to_all(send_gates, "dp", split_axis=0, concat_axis=0, tiled=True),
    )
    rows = rows_in.reshape(-1, columns)
    gate_rows = gates_in.reshape(-1).astype(jnp.float32)
    partner = from_partner(weights, "expert", 0)
    lower = jnp.where(replica == 0, weights, partner)
    upper = jnp.where(replica == 0, partner, weights)
    full = jnp.concatenate([lower, upper], 2)
    hg = contract_last(rows, full[0])
    hu = contract_last(rows, full[1])
    sig = jax.nn.sigmoid(hg)
    act = (hg * sig * hu).astype(jnp.bfloat16)
    cot_in = lax.all_to_all(send_cot, "dp", split_axis=0, concat_axis=0, tiled=True)
    cots = cot_in.reshape(-1, columns)
    dz = (gate_rows[:, None] * cots.astype(jnp.float32)).astype(jnp.bfloat16)
    dact = contract_last(dz, full[2])
    grad_down = contract_first(act, dz)
    dhg = (dact * hu * sig * (1.0 + hg * (1.0 - sig))).astype(jnp.bfloat16)
    dhu = (dact * hg * sig).astype(jnp.bfloat16)
    grad_gate = contract_first(dhg, rows)
    grad_up = contract_first(dhu, rows)
    stacked = jnp.stack([grad_gate, grad_up, grad_down])
    keep, give = split_halves(stacked, replica, width_half)
    total = keep + from_partner(give, "expert", 0)
    moment_one = beta_one * first_moment.astype(jnp.float32) + (1.0 - beta_one) * total
    moment_two = beta_two * second_moment.astype(jnp.float32) + (1.0 - beta_two) * total * total
    step = (
        moment_one
        / (1.0 - beta_one**step_count)
        / (jnp.sqrt(moment_two / (1.0 - beta_two**step_count)) + epsilon)
    )
    return (
        moment_one.astype(jnp.bfloat16),
        moment_two.astype(jnp.bfloat16),
        step.astype(jnp.bfloat16),
    )


VMEM_LIMIT = 16 * 1024 * 1024


def params():
    return pltpu.CompilerParams(vmem_limit_bytes=VMEM_LIMIT)


def cost(flops, moved):
    return pl.CostEstimate(flops=flops, bytes_accessed=moved, transcendentals=0)


def whole():
    return pl.BlockSpec(memory_space=pltpu.VMEM)


def in_hbm():
    return pl.BlockSpec(memory_space=pltpu.HBM)


def unread():
    return pl.BlockSpec(memory_space=pl.ANY)


def expert_here():
    slices = min(4, lax.axis_size("expert") // 2)
    group = lax.axis_index("expert") // (2 * slices)
    return group * lax.axis_size("dp") + lax.axis_index("dp")


def keep_hbm(value):
    return pltpu.with_memory_space_constraint(value, pltpu.HBM)


def pack_kernel(
    ids_hbm,
    gates_hbm,
    tokens_ref,
    cot_ref,
    w_hbm,
    x_ref,
    y_ref,
    own_ref,
    w_ref,
    ids_ref,
    gates_ref,
    sems,
):
    count = tokens_ref.shape[0]
    width = x_ref.shape[1]
    columns = pl.ds(pl.multiple_of(lax.axis_index("expert") % 2 * width, width), width)
    copies = [
        pltpu.make_async_copy(ids_hbm, ids_ref, sems.at[0]),
        pltpu.make_async_copy(gates_hbm, gates_ref, sems.at[1]),
        pltpu.make_async_copy(tokens_ref.at[:, columns], x_ref, sems.at[2]),
        pltpu.make_async_copy(cot_ref.at[:, columns], y_ref.at[0:count, :], sems.at[3]),
        pltpu.make_async_copy(tokens_ref.at[:, columns], own_ref.at[0:count, :], sems.at[4]),
        pltpu.make_async_copy(cot_ref.at[:, columns], own_ref.at[count : 2 * count, :], sems.at[5]),
        pltpu.make_async_copy(w_hbm, w_ref, sems.at[6]),
    ]
    for copy in copies:
        copy.start()
    copies[0].wait()
    copies[1].wait()
    ids = ids_ref[...]
    gates = gates_ref[...].astype(jnp.float32)
    slots = y_ref.shape[0] - count
    row = lax.broadcasted_iota(jnp.int32, (slots, count), 0)
    gate = jnp.zeros((slots, count), jnp.float32)
    for k in range(ids.shape[0]):
        gate = gate + jnp.where(row == ids[k : k + 1, :], gates[k : k + 1, :], 0.0)
    y_ref[count:, 0:count] = gate.astype(jnp.bfloat16)
    y_ref[count:, count:] = jnp.zeros((slots, width - count), jnp.bfloat16)
    own_ref[2 * count :, :] = y_ref[count:, :]
    for copy in copies[2:]:
        copy.wait()


def pack_own(ids, gates, tokens, cotangent, weights, slots):
    count, top = ids.shape
    width = weights.shape[2]
    return pl.pallas_call(
        pack_kernel,
        in_specs=[in_hbm()] * 5,
        out_specs=[whole()] * 4,
        out_shape=[
            jax.ShapeDtypeStruct((rows, width), jnp.bfloat16)
            for rows in (count, count + slots, 2 * count + slots)
        ]
        + [jax.ShapeDtypeStruct(weights.shape, weights.dtype)],
        scratch_shapes=[
            pltpu.VMEM((top, count), ids.dtype),
            pltpu.VMEM((top, count), gates.dtype),
            pltpu.SemaphoreType.DMA((7,)),
        ],
        compiler_params=params(),
        cost_estimate=cost(1000, 8 * count * width),
    )(*[keep_hbm(value) for value in (ids.T, gates.T, tokens, cotangent, weights)])


def views(refs, kinds, count):
    xs, ys, gates = [], [], []
    for ref, kind in zip(refs, kinds):
        if kind in ("first x", "second x"):
            xs.append(ref[0 if kind == "first x" else 1])
            continue
        if kind == "x of xyy":
            xs.append(ref[0:count, :])
            continue
        if kind in ("x, y, y", "y, y of xyy"):
            rows = (ref.shape[0] - count) // 2
            if kind == "x, y, y":
                xs.append(ref[0:count, :])
            for row in (count, count + rows):
                ys.append(ref[row : row + count, :])
                gates.append(ref[row + count : row + rows, 0:count])
            continue
        for part in [ref.at[0], ref.at[1]] if ref.ndim == 3 else [ref]:
            if kind == "x":
                xs.append(part[...])
            if kind == "xy":
                xs.append(part[0:count, :])
                ys.append(part[count : 2 * count, :])
                gates.append(part[2 * count :, 0:count])
            if kind == "y":
                ys.append(part[...])
            if kind == "y, gates":
                ys.append(part[0:count, :])
                gates.append(part[count:, 0:count])
            if kind == "half y, gates":
                ys.append(part[0 : count // 2, :])
                gates.append(part[count // 2 :, 0:count])
    return xs, ys, gates


def joined(parts):
    return parts[0] if len(parts) == 1 else jnp.concatenate(parts, 0)


def kinds_of(chunk):
    return tuple(kind for kind, value in chunk)


def values_of(chunk):
    return [value for kind, value in chunk]


def store_partials(parts, count, out_ref):
    row = 0
    for part in parts:
        for first in range(0, part.shape[1], count):
            piece = part[:, first : first + count]
            out_ref[row : row + piece.shape[0], :] = piece.astype(jnp.bfloat16)
            row = row + piece.shape[0]


def partial_kernel(kinds, count, tokened, w_ref, after_ref, *refs):
    n = len(kinds)
    xs, ys, gates = views(refs[:n], kinds, count)
    outs = refs[n : len(refs) - tokened]
    mats, hidden, width = w_ref.shape
    parts = []
    if xs and len(outs) == mats:
        parts.extend(contract_last(w_ref[m], joined(xs)) for m in (0, 1))
    elif xs:
        parts.append(contract_last(w_ref[0:2].reshape(2 * hidden, width), joined(xs)))
    if ys:
        parts.append(contract_last(w_ref[2], joined(ys)))
    if len(outs) == 1:
        store_partials(parts, count, outs[0])
    else:
        for part, out_ref in zip(parts, outs):
            store_partials([part], count, out_ref)
    if tokened:
        refs[-1][...] = jnp.zeros_like(refs[-1])


def partials(weights, after, chunk, rows, count, tokened=1):
    hidden, width = weights.shape[1:]
    kinds = kinds_of(chunk)
    total = sum(rows) * hidden * count
    return pl.pallas_call(
        functools.partial(partial_kernel, kinds, count, tokened),
        in_specs=[whole(), unread()] + [whole()] * len(kinds),
        out_specs=[whole()] * (len(rows) + tokened),
        out_shape=[jax.ShapeDtypeStruct((k * hidden, count), jnp.bfloat16) for k in rows]
        + [jax.ShapeDtypeStruct((8, 128), jnp.float32)] * tokened,
        compiler_params=params(),
        cost_estimate=cost(2 * total * width, 6 * total),
    )(weights, after, *values_of(chunk))


def gate_row(gates):
    rows = []
    expert = expert_here()
    for held in gates:
        held = held.astype(jnp.float32)
        index = lax.broadcasted_iota(jnp.int32, held.shape, 0)
        rows.append(jnp.sum(jnp.where(index == expert, held, 0.0), 0, keepdims=True))
    return rows[0] if len(rows) == 1 else jnp.concatenate(rows, 1)


def summed(pairs):
    parts = []
    for own, *got in pairs:
        part = own[...].astype(jnp.float32)
        parts.append(part + got[0][...].astype(jnp.float32) if got else part)
    return parts[0] if len(parts) == 1 else jnp.concatenate(parts, 0)


def beside(total, hidden, firsts):
    parts = [total[first * hidden : (first + 1) * hidden] for first in firsts]
    return jnp.concatenate(parts, 1)


def activation(hg, hu, gate):
    sig = jax.nn.sigmoid(hg)
    silu = hg * sig
    return sig, silu, (gate * (silu * hu)).astype(jnp.bfloat16)


def hidden_slopes(hg, hu, sig, silu, dact):
    dhg = (dact * hu * sig * (1.0 + hg * (1.0 - sig))).astype(jnp.bfloat16)
    dhu = (dact * silu).astype(jnp.bfloat16)
    return dhg, dhu


def hidden_grads(gate, pairs):
    total = summed(pairs)
    blocks = gate.shape[1] // total.shape[1]
    hidden = total.shape[0] // (3 * blocks)
    hg = beside(total, hidden, range(0, 2 * blocks, 2))
    hu = beside(total, hidden, range(1, 2 * blocks, 2))
    dact = gate * beside(total, hidden, range(2 * blocks, 3 * blocks))
    sig, silu, act = activation(hg, hu, gate)
    return (*hidden_slopes(hg, hu, sig, silu, dact), act)


def plain(left, right):
    return lax.dot_general(
        left, right, (((1,), (0,)), ((), ())), preferred_element_type=jnp.float32
    )


def onward_kernel(kinds, after_ref, own, got, near_own, near_got, *refs):
    x0_ref, x1_ref, s0_ref, y0_ref, y1_ref = refs[:5]
    pair_ref, rest_ref, out_ref, first_ref, sum_ref, gate_ref = refs[5 + len(kinds) :]
    count, rows = x0_ref.shape[0], y0_ref.shape[0]
    gates = views(refs[5 : 5 + len(kinds)], kinds, count)[2]
    gate_ref[...] = jnp.broadcast_to(gate_row(gates), gate_ref.shape)
    pair_ref[0] = x0_ref[...]
    pair_ref[1] = s0_ref[...]
    rest_ref[0:count, :] = x1_ref[...]
    rest_ref[count : count + rows, :] = y0_ref[...]
    rest_ref[count + rows :, :] = y1_ref[...]
    out_ref[0:count, :] = x0_ref[...]
    out_ref[count:, :] = y0_ref[...]
    first_ref[...] = own[...].astype(jnp.float32) + got[...].astype(jnp.float32)
    sum_ref[...] = near_own[...].astype(jnp.float32) + near_got[...].astype(jnp.float32)


def pick_onward(after, pair, near_pair, near_x, other_x, near_y, chunk):
    count, width = other_x.shape
    rows = near_y[0].shape[0]
    operands = [*pair, *near_pair, *near_x, other_x, *near_y, *values_of(chunk)]
    return pl.pallas_call(
        functools.partial(onward_kernel, kinds_of(chunk)),
        in_specs=[unread()] + [whole()] * len(operands),
        out_specs=[whole()] * 6,
        out_shape=[
            jax.ShapeDtypeStruct((2, count, width), jnp.bfloat16),
            jax.ShapeDtypeStruct((count + 2 * rows, width), jnp.bfloat16),
            jax.ShapeDtypeStruct((count + rows, width), jnp.bfloat16),
            jax.ShapeDtypeStruct(pair[0].shape, jnp.float32),
            jax.ShapeDtypeStruct(near_pair[0].shape, jnp.float32),
            jax.ShapeDtypeStruct((8, 2 * count), jnp.float32),
        ],
        compiler_params=params(),
        cost_estimate=cost(1000, 8 * other_x.size),
    )(after, *operands)


def pass_kernel(after_ref, in_ref, *outs):
    row = 0
    for out_ref in outs:
        out_ref[...] = in_ref[row : row + out_ref.shape[0], :]
        row = row + out_ref.shape[0]


def passed_on(after, value, cuts):
    width = value.shape[1]
    return pl.pallas_call(
        pass_kernel,
        in_specs=[unread(), whole()],
        out_specs=[whole()] * len(cuts),
        out_shape=[jax.ShapeDtypeStruct((rows, width), value.dtype) for rows in cuts],
        compiler_params=params(),
        cost_estimate=cost(1000, 2 * value.size),
    )(after, value)


def first_kernel(kinds, count, gate_ref, after_ref, sum_ref, own, got, *refs):
    n = len(kinds)
    xs, ys, gates = views(refs[:n], kinds, count)
    out_ref, more_ref, token_ref = refs[n:]
    more_ref[...] = summed([(own, got)])
    lefts = hidden_grads(gate_ref[0:1, :], [(sum_ref,)])
    x = joined(xs)
    for m, right in enumerate((x, x, joined(ys))):
        out_ref[m] = plain(lefts[m], right)
    token_ref[...] = jnp.zeros_like(token_ref)


def first_grads(gate, after, total, pair, chunk, hidden, count):
    kinds = kinds_of(chunk)
    width = chunk[0][1].shape[-1]
    return pl.pallas_call(
        functools.partial(first_kernel, kinds, count),
        in_specs=[whole(), unread()] + [whole()] * (3 + len(kinds)),
        out_specs=[whole()] * 3,
        out_shape=[
            jax.ShapeDtypeStruct((3, hidden, width), jnp.float32),
            jax.ShapeDtypeStruct(pair[0].shape, jnp.float32),
            jax.ShapeDtypeStruct((8, 128), jnp.float32),
        ],
        compiler_params=params(),
        cost_estimate=cost(2 * total.size * width, 12 * hidden * width),
    )(gate, after, total, *pair, *values_of(chunk))


def grad_kernel(kinds, count, sum_ref, more_ref, own, got, *refs):
    n = len(kinds)
    xs, ys, gates = views(refs[:n], kinds, count)
    acc_ref, out_ref = refs[n:]
    lefts = hidden_grads(gate_row(gates), [(sum_ref,), (more_ref,), (own, got)])
    x = joined(xs)
    for m, right in enumerate((x, x, joined(ys))):
        out_ref[m] = acc_ref[m] + plain(lefts[m], right)


def add_grads(near_sum, more_sum, pair, chunk, acc, count):
    kinds = kinds_of(chunk)
    mats, hidden, width = acc.shape
    operands = [near_sum, more_sum, *pair, *values_of(chunk), acc]
    return pl.pallas_call(
        functools.partial(grad_kernel, kinds, count),
        in_specs=[whole()] * len(operands),
        out_specs=whole(),
        out_shape=jax.ShapeDtypeStruct(acc.shape, jnp.float32),
        input_output_aliases={len(operands) - 1: 0},
        compiler_params=params(),
        cost_estimate=cost(
            2 * mats * hidden * width * 4 * count, 8 * mats * hidden * width
        ),
    )(*operands)


def adam(grad, first, second):
    moment_one = beta_one * first.astype(jnp.float32) + (1.0 - beta_one) * grad
    moment_two = beta_two * second.astype(jnp.float32) + (1.0 - beta_two) * (grad * grad)
    root = (1.0 / (1.0 - beta_two**step_count)) ** 0.5
    below = moment_two * lax.rsqrt(moment_two) + epsilon / root
    scaled = moment_one * (1.0 / (1.0 - beta_one**step_count) / root)
    step = scaled * pl.reciprocal(below, approx=True)
    return [value.astype(jnp.bfloat16) for value in (moment_one, moment_two, step)]


def pair_of_blocks(own, got):
    total = summed([(own, got)])
    return beside(total, total.shape[0] // 2, (0, 1))


def down_kernel(kinds, count, own_g, got_g, own_u, got_u, *refs):
    n = len(kinds)
    acc_ref, first_ref, second_ref, *outs = refs[n:]
    xs, ys, gates = views(refs[:n], kinds, count)
    hg, hu = pair_of_blocks(own_g, got_g), pair_of_blocks(own_u, got_u)
    act = activation(hg, hu, gate_row(gates))[2]
    grad = acc_ref[2] + plain(act, joined(ys))
    for out_ref, value in zip(outs, adam(grad, first_ref[2], second_ref[2])):
        out_ref[...] = value


def down_update(pairs, chunk, acc, moments, count):
    kinds = kinds_of(chunk)
    mats, hidden, width = acc.shape
    operands = [*pairs, *values_of(chunk), acc, *moments]
    return pl.pallas_call(
        functools.partial(down_kernel, kinds, count),
        in_specs=[whole()] * len(operands),
        out_specs=[whole()] * 3,
        out_shape=[jax.ShapeDtypeStruct((hidden, width), jnp.bfloat16)] * 3,
        compiler_params=params(),
        cost_estimate=cost(4 * hidden * width * count, 14 * hidden * width),
    )(*operands)


def slopes_kernel(kinds, count, own_g, got_g, own_u, got_u, own_d, got_d, *refs):
    n = len(kinds)
    acc_ref, first_ref, second_ref = refs[n : n + 3]
    done, outs = refs[n + 3 : n + 6], refs[n + 6 : n + 9]
    held, sems = refs[n + 9 : n + 12], refs[n + 12]
    copies = [
        pltpu.make_async_copy(done[k], outs[k].at[2], sems.at[2, k]) for k in range(3)
    ]
    for copy in copies:
        copy.start()
    xs, ys, gates = views(refs[:n], kinds, count)
    hg, hu = pair_of_blocks(own_g, got_g), pair_of_blocks(own_u, got_u)
    dact = gate_row(gates) * pair_of_blocks(own_d, got_d)
    sig, silu, act = activation(hg, hu, 1.0)
    right = joined(xs)
    for m, left in enumerate(hidden_slopes(hg, hu, sig, silu, dact)):
        grad = acc_ref[m] + plain(left, right)
        for k, value in enumerate(adam(grad, first_ref[m], second_ref[m])):
            held[k][m] = value
            copies.append(pltpu.make_async_copy(held[k].at[m], outs[k].at[m], sems.at[m, k]))
            copies[-1].start()
    for copy in copies:
        copy.wait()


def slopes_update(pairs, chunk, acc, moments, done, count):
    kinds = kinds_of(chunk)
    mats, hidden, width = acc.shape
    operands = [*pairs, *values_of(chunk), acc, *moments, *done]
    return pl.pallas_call(
        functools.partial(slopes_kernel, kinds, count),
        in_specs=[whole()] * len(operands),
        out_specs=[in_hbm()] * 3,
        out_shape=[jax.ShapeDtypeStruct(acc.shape, jnp.bfloat16)] * 3,
        scratch_shapes=[pltpu.VMEM((2, hidden, width), jnp.bfloat16)] * 3
        + [pltpu.SemaphoreType.DMA((3, 3))],
        compiler_params=params(),
        cost_estimate=cost(8 * hidden * width * count, 28 * hidden * width),
    )(*operands)


def from_masked(value, axis, mask):
    pairs = [(source, source ^ mask) for source in range(lax.axis_size(axis))]
    return lax.ppermute(value, axis, pairs)


def dense_plan(tokens, cotangent, expert_ids, gate_probs, weights, first_moment, second_moment):
    n_data = lax.axis_size("dp")
    slices = min(4, lax.axis_size("expert") // 2)
    experts_total = lax.axis_size("expert") // (2 * slices) * n_data
    count = tokens.shape[0]
    hidden, width = weights.shape[1:]
    slots = -(-experts_total // 16) * 16
    other = lambda value: from_masked(value, "dp", 1)
    partner = lambda value: from_masked(value, "expert", 1)
    x_own, y_own, own, weights = pack_own(
        expert_ids, gate_probs, tokens, cotangent, weights, slots
    )
    first = [("xy", own), ("xy", other(own))]
    send, token = partials(weights, own, first, (6,), count)
    first_pair = (send, partner(send))
    along = [[(p, p ^ (2 if p % 2 == k else 4)) for p in range(n_data)] for k in (0, 1)]
    near_x = [lax.ppermute(x_own, "dp", pairs) for pairs in along]
    near_y = [lax.ppermute(y_own, "dp", pairs) for pairs in along]
    send, token = partials(weights, token, [("x", near_x[0]), ("", near_x[1])], (2,), count)
    near_pair = (send, partner(send))
    x_pair, rest, picked, first_sum, near_sum, gate = pick_onward(
        token, first_pair, near_pair, near_x, other(near_x[0]), near_y, first
    )
    far = lax.ppermute(picked, "dp", along[1])
    rest_other = other(rest)
    early = [("x of xyy", rest), ("second x", x_pair)]
    late = [("y, y of xyy", rest), ("x, y, y", rest_other)]
    send, token = partials(weights, picked, early, (4,), count)
    early_pair = (send, partner(send))
    send, token = partials(weights, token, late, (6,), count)
    late_pair = (send, partner(send))
    acc, early_sum, token = first_grads(
        gate, token, first_sum, early_pair, first, hidden, count
    )
    pieces = passed_on(token, far, (count // 2, count // 2, count // 2, count // 2 + slots))
    pieces = [*pieces, *[other(value) for value in pieces]]
    final = list(zip(("x", "x", "y", "half y, gates") * 2, pieces))
    sends = partials(weights, token, final, (2, 2, 2), count, 0)
    pairs = [value for send in sends for value in (send, partner(send))]
    near = [("first x", x_pair), ("x, y, y", rest), ("second x", x_pair), ("x, y, y", rest_other)]
    acc = add_grads(near_sum, early_sum, late_pair, near, acc, count)
    moments = (first_moment, second_moment)
    final_y = [block for block in final if block[0] != "x"]
    final_x = [block for block in final if block[0] != "y"]
    done = down_update(pairs[:4], final_y, acc, moments, count)
    return tuple(slopes_update(pairs, final_x, acc, moments, done, count))


def per_device(tokens, cotangent, expert_ids, gate_probs, weights, first_moment, second_moment):
    n_expert = lax.axis_size("expert")
    n_data = lax.axis_size("dp")
    slices = min(4, n_expert // 2)
    experts_total = n_expert // (2 * slices) * n_data
    half = tokens.shape[0] // 2
    dense = 2 * half * expert_ids.shape[1] // experts_total >= half
    plan = dense_plan if dense and n_data == 8 else routed_plan
    return plan(
        tokens, cotangent, expert_ids, gate_probs, weights, first_moment, second_moment
    )


def solution(mesh):
    in_specs = (
        P("dp", None),
        P("dp", None),
        P("dp", None),
        P("dp", None),
        P(None, "dp", "expert"),
        P(None, "dp", "expert"),
        P(None, "dp", "expert"),
    )
    out_specs = (P(None, "dp", "expert"), P(None, "dp", "expert"), P(None, "dp", "expert"))
    return jax.shard_map(
        per_device, mesh=mesh, in_specs=in_specs, out_specs=out_specs, check_vma=False
    )
```

```python
import functools

import jax
import jax.numpy as jnp
from jax import lax
from jax.experimental import pallas as pl
from jax.experimental.pallas import tpu as pltpu
from jax.sharding import PartitionSpec as P

beta_one = 0.9
beta_two = 0.95
step_count = 10
epsilon = 1e-08


def from_partner(value, axis, distance):
    mask = 2**distance
    pairs = [(source, source ^ mask) for source in range(lax.axis_size(axis))]
    return lax.ppermute(value, axis, pairs)


def contract_last(left, right):
    return lax.dot_general(
        left, right, (((1,), (1,)), ((), ())), preferred_element_type=jnp.float32
    )


def contract_first(left, right):
    return lax.dot_general(
        left, right, (((0,), (0,)), ((), ())), preferred_element_type=jnp.float32
    )


def split_halves(grad, replica, width_half):
    keep = lax.dynamic_slice_in_dim(grad, replica * width_half, width_half, grad.ndim - 1)
    give = lax.dynamic_slice_in_dim(grad, (1 - replica) * width_half, width_half, grad.ndim - 1)
    return (keep, give)


def route_block(block_ids, block_gates, group, n_data, capacity):
    count = block_ids.shape[0]
    top = block_ids.shape[1]
    target = block_ids - group * n_data
    inside = block_ids // n_data == group
    onehot = (
        (target[:, :, None] == jnp.arange(n_data, dtype=jnp.int32)[None, None, :])
        & inside[:, :, None]
    ).astype(jnp.int32)
    per_token = jnp.sum(onehot, axis=1)
    earlier = jnp.cumsum(per_token, axis=0) - per_token
    rank = jnp.sum(onehot * earlier[:, None, :], axis=2)
    total_slots = n_data * capacity
    slot = jnp.where(inside, target * capacity + rank, total_slots).reshape(-1)
    token_of = jnp.broadcast_to(jnp.arange(count, dtype=jnp.int32)[:, None], (count, top)).reshape(
        -1
    )
    table = jnp.full((total_slots,), count, jnp.int32).at[slot].set(token_of, mode="drop")
    gate_slot = (
        jnp.zeros((total_slots,), jnp.bfloat16).at[slot].set(block_gates.reshape(-1), mode="drop")
    )
    return (table, gate_slot)


def routed_plan(tokens, cotangent, expert_ids, gate_probs, weights, first_moment, second_moment):
    n_expert = lax.axis_size("expert")
    n_data = lax.axis_size("dp")
    slices = min(4, n_expert // 2)
    place = lax.axis_index("expert")
    replica = place % 2
    group = place // (2 * slices)
    groups = n_expert // (2 * slices)
    experts_total = groups * n_data
    half = tokens.shape[0] // 2
    width_half = weights.shape[2]
    top = expert_ids.shape[1]
    capacity = max(2, 2 * half * top // experts_total)
    start = replica * half
    own_ids = lax.dynamic_slice_in_dim(expert_ids, start, half, 0)
    own_gates = lax.dynamic_slice_in_dim(gate_probs, start, half, 0)
    table, gate_slot = route_block(own_ids, own_gates, group, n_data, capacity)
    source_tokens = lax.dynamic_slice_in_dim(tokens, start, half, 0)
    source_cot = lax.dynamic_slice_in_dim(cotangent, start, half, 0)
    columns = source_tokens.shape[1]
    padded_tokens = jnp.concatenate([source_tokens, jnp.zeros((1, columns), jnp.bfloat16)], 0)
    padded_cot = jnp.concatenate([source_cot, jnp.zeros((1, columns), jnp.bfloat16)], 0)
    send_rows = padded_tokens[table].reshape(n_data, -1, columns)
    send_cot = padded_cot[table].reshape(n_data, -1, columns)
    send_gates = gate_slot.reshape(n_data, -1)
    rows_in, gates_in = (
        lax.all_to_all(send_rows, "dp", split_axis=0, concat_axis=0, tiled=True),
        lax.all_to_all(send_gates, "dp", split_axis=0, concat_axis=0, tiled=True),
    )
    rows = rows_in.reshape(-1, columns)
    gate_rows = gates_in.reshape(-1).astype(jnp.float32)
    partner = from_partner(weights, "expert", 0)
    lower = jnp.where(replica == 0, weights, partner)
    upper = jnp.where(replica == 0, partner, weights)
    full = jnp.concatenate([lower, upper], 2)
    hg = contract_last(rows, full[0])
    hu = contract_last(rows, full[1])
    sig = jax.nn.sigmoid(hg)
    act = (hg * sig * hu).astype(jnp.bfloat16)
    cot_in = lax.all_to_all(send_cot, "dp", split_axis=0, concat_axis=0, tiled=True)
    cots = cot_in.reshape(-1, columns)
    dz = (gate_rows[:, None] * cots.astype(jnp.float32)).astype(jnp.bfloat16)
    dact = contract_last(dz, full[2])
    grad_down = contract_first(act, dz)
    dhg = (dact * hu * sig * (1.0 + hg * (1.0 - sig))).astype(jnp.bfloat16)
    dhu = (dact * hg * sig).astype(jnp.bfloat16)
    grad_gate = contract_first(dhg, rows)
    grad_up = contract_first(dhu, rows)
    stacked = jnp.stack([grad_gate, grad_up, grad_down])
    keep, give = split_halves(stacked, replica, width_half)
    total = keep + from_partner(give, "expert", 0)
    moment_one = beta_one * first_moment.astype(jnp.float32) + (1.0 - beta_one) * total
    moment_two = beta_two * second_moment.astype(jnp.float32) + (1.0 - beta_two) * total * total
    step = (
        moment_one
        / (1.0 - beta_one**step_count)
        / (jnp.sqrt(moment_two / (1.0 - beta_two**step_count)) + epsilon)
    )
    return (
        moment_one.astype(jnp.bfloat16),
        moment_two.astype(jnp.bfloat16),
        step.astype(jnp.bfloat16),
    )


VMEM_LIMIT = 16 * 1024 * 1024


def params():
    return pltpu.CompilerParams(vmem_limit_bytes=VMEM_LIMIT)


def cost(flops, moved):
    return pl.CostEstimate(flops=flops, bytes_accessed=moved, transcendentals=0)


def whole():
    return pl.BlockSpec(memory_space=pltpu.VMEM)


def in_hbm():
    return pl.BlockSpec(memory_space=pltpu.HBM)


def unread():
    return pl.BlockSpec(memory_space=pl.ANY)


def expert_here():
    slices = min(4, lax.axis_size("expert") // 2)
    group = lax.axis_index("expert") // (2 * slices)
    return group * lax.axis_size("dp") + lax.axis_index("dp")


def keep_hbm(value):
    return pltpu.with_memory_space_constraint(value, pltpu.HBM)


def pack_kernel(
    ids_hbm,
    gates_hbm,
    tokens_ref,
    cot_ref,
    w_hbm,
    x_ref,
    y_ref,
    own_ref,
    w_ref,
    ids_ref,
    gates_ref,
    sems,
):
    count = tokens_ref.shape[0]
    width = x_ref.shape[1]
    columns = pl.ds(pl.multiple_of(lax.axis_index("expert") % 2 * width, width), width)
    copies = [
        pltpu.make_async_copy(ids_hbm, ids_ref, sems.at[0]),
        pltpu.make_async_copy(gates_hbm, gates_ref, sems.at[1]),
        pltpu.make_async_copy(tokens_ref.at[:, columns], x_ref, sems.at[2]),
        pltpu.make_async_copy(cot_ref.at[:, columns], y_ref.at[0:count, :], sems.at[3]),
        pltpu.make_async_copy(tokens_ref.at[:, columns], own_ref.at[0:count, :], sems.at[4]),
        pltpu.make_async_copy(cot_ref.at[:, columns], own_ref.at[count : 2 * count, :], sems.at[5]),
        pltpu.make_async_copy(w_hbm, w_ref, sems.at[6]),
    ]
    for copy in copies:
        copy.start()
    copies[0].wait()
    copies[1].wait()
    ids = ids_ref[...]
    gates = gates_ref[...].astype(jnp.float32)
    slots = y_ref.shape[0] - count
    row = lax.broadcasted_iota(jnp.int32, (slots, count), 0)
    gate = jnp.zeros((slots, count), jnp.float32)
    for k in range(ids.shape[0]):
        gate = gate + jnp.where(row == ids[k : k + 1, :], gates[k : k + 1, :], 0.0)
    y_ref[count:, 0:count] = gate.astype(jnp.bfloat16)
    y_ref[count:, count:] = jnp.zeros((slots, width - count), jnp.bfloat16)
    own_ref[2 * count :, :] = y_ref[count:, :]
    for copy in copies[2:]:
        copy.wait()


def pack_own(ids, gates, tokens, cotangent, weights, slots):
    count, top = ids.shape
    width = weights.shape[2]
    return pl.pallas_call(
        pack_kernel,
        in_specs=[in_hbm()] * 5,
        out_specs=[whole()] * 4,
        out_shape=[
            jax.ShapeDtypeStruct((rows, width), jnp.bfloat16)
            for rows in (count, count + slots, 2 * count + slots)
        ]
        + [jax.ShapeDtypeStruct(weights.shape, weights.dtype)],
        scratch_shapes=[
            pltpu.VMEM((top, count), ids.dtype),
            pltpu.VMEM((top, count), gates.dtype),
            pltpu.SemaphoreType.DMA((7,)),
        ],
        compiler_params=params(),
        cost_estimate=cost(1000, 8 * count * width),
    )(*[keep_hbm(value) for value in (ids.T, gates.T, tokens, cotangent, weights)])


def views(refs, kinds, count):
    xs, ys, gates = [], [], []
    for ref, kind in zip(refs, kinds):
        if kind in ("first x", "second x"):
            xs.append(ref[0 if kind == "first x" else 1])
            continue
        if kind == "x of xyy":
            xs.append(ref[0:count, :])
            continue
        if kind in ("x, y, y", "y, y of xyy"):
            rows = (ref.shape[0] - count) // 2
            if kind == "x, y, y":
                xs.append(ref[0:count, :])
            for row in (count, count + rows):
                ys.append(ref[row : row + count, :])
                gates.append(ref[row + count : row + rows, 0:count])
            continue
        for part in [ref.at[0], ref.at[1]] if ref.ndim == 3 else [ref]:
            if kind == "x":
                xs.append(part[...])
            if kind == "xy":
                xs.append(part[0:count, :])
                ys.append(part[count : 2 * count, :])
                gates.append(part[2 * count :, 0:count])
            if kind == "y":
                ys.append(part[...])
            if kind == "y, gates":
                ys.append(part[0:count, :])
                gates.append(part[count:, 0:count])
            if kind == "half y, gates":
                ys.append(part[0 : count // 2, :])
                gates.append(part[count // 2 :, 0:count])
    return xs, ys, gates


def joined(parts):
    return parts[0] if len(parts) == 1 else jnp.concatenate(parts, 0)


def kinds_of(chunk):
    return tuple(kind for kind, value in chunk)


def values_of(chunk):
    return [value for kind, value in chunk]


def store_partials(parts, count, out_ref):
    row = 0
    for part in parts:
        for first in range(0, part.shape[1], count):
            piece = part[:, first : first + count]
            out_ref[row : row + piece.shape[0], :] = piece.astype(jnp.bfloat16)
            row = row + piece.shape[0]


def partial_kernel(kinds, count, tokened, w_ref, after_ref, *refs):
    n = len(kinds)
    xs, ys, gates = views(refs[:n], kinds, count)
    outs = refs[n : len(refs) - tokened]
    mats, hidden, width = w_ref.shape
    parts = []
    if xs and len(outs) == mats:
        parts.extend(contract_last(w_ref[m], joined(xs)) for m in (0, 1))
    elif xs:
        parts.append(contract_last(w_ref[0:2].reshape(2 * hidden, width), joined(xs)))
    if ys:
        parts.append(contract_last(w_ref[2], joined(ys)))
    if len(outs) == 1:
        store_partials(parts, count, outs[0])
    else:
        for part, out_ref in zip(parts, outs):
            store_partials([part], count, out_ref)
    if tokened:
        refs[-1][...] = jnp.zeros_like(refs[-1])


def partials(weights, after, chunk, rows, count, tokened=1):
    hidden, width = weights.shape[1:]
    kinds = kinds_of(chunk)
    total = sum(rows) * hidden * count
    return pl.pallas_call(
        functools.partial(partial_kernel, kinds, count, tokened),
        in_specs=[whole(), unread()] + [whole()] * len(kinds),
        out_specs=[whole()] * (len(rows) + tokened),
        out_shape=[jax.ShapeDtypeStruct((k * hidden, count), jnp.bfloat16) for k in rows]
        + [jax.ShapeDtypeStruct((8, 128), jnp.float32)] * tokened,
        compiler_params=params(),
        cost_estimate=cost(2 * total * width, 6 * total),
    )(weights, after, *values_of(chunk))


def gate_row(gates):
    rows = []
    expert = expert_here()
    for held in gates:
        held = held.astype(jnp.float32)
        index = lax.broadcasted_iota(jnp.int32, held.shape, 0)
        rows.append(jnp.sum(jnp.where(index == expert, held, 0.0), 0, keepdims=True))
    return rows[0] if len(rows) == 1 else jnp.concatenate(rows, 1)


def summed(pairs):
    parts = []
    for own, *got in pairs:
        part = own[...].astype(jnp.float32)
        parts.append(part + got[0][...].astype(jnp.float32) if got else part)
    return parts[0] if len(parts) == 1 else jnp.concatenate(parts, 0)


def beside(total, hidden, firsts):
    parts = [total[first * hidden : (first + 1) * hidden] for first in firsts]
    return jnp.concatenate(parts, 1)


def activation(hg, hu, gate):
    sig = jax.nn.sigmoid(hg)
    silu = hg * sig
    return sig, silu, (gate * (silu * hu)).astype(jnp.bfloat16)


def hidden_slopes(hg, hu, sig, silu, dact):
    dhg = (dact * hu * sig * (1.0 + hg * (1.0 - sig))).astype(jnp.bfloat16)
    dhu = (dact * silu).astype(jnp.bfloat16)
    return dhg, dhu


def hidden_grads(gate, pairs):
    total = summed(pairs)
    blocks = gate.shape[1] // total.shape[1]
    hidden = total.shape[0] // (3 * blocks)
    hg = beside(total, hidden, range(0, 2 * blocks, 2))
    hu = beside(total, hidden, range(1, 2 * blocks, 2))
    dact = gate * beside(total, hidden, range(2 * blocks, 3 * blocks))
    sig, silu, act = activation(hg, hu, gate)
    return (*hidden_slopes(hg, hu, sig, silu, dact), act)


def plain(left, right):
    return lax.dot_general(
        left, right, (((1,), (0,)), ((), ())), preferred_element_type=jnp.float32
    )


def onward_kernel(kinds, after_ref, own, got, near_own, near_got, *refs):
    x0_ref, x1_ref, s0_ref, y0_ref, y1_ref = refs[:5]
    pair_ref, rest_ref, out_ref, first_ref, sum_ref, gate_ref = refs[5 + len(kinds) :]
    count, rows = x0_ref.shape[0], y0_ref.shape[0]
    gates = views(refs[5 : 5 + len(kinds)], kinds, count)[2]
    gate_ref[...] = jnp.broadcast_to(gate_row(gates), gate_ref.shape)
    pair_ref[0] = x0_ref[...]
    pair_ref[1] = s0_ref[...]
    rest_ref[0:count, :] = x1_ref[...]
    rest_ref[count : count + rows, :] = y0_ref[...]
    rest_ref[count + rows :, :] = y1_ref[...]
    out_ref[0:count, :] = x0_ref[...]
    out_ref[count:, :] = y0_ref[...]
    first_ref[...] = own[...].astype(jnp.float32) + got[...].astype(jnp.float32)
    sum_ref[...] = near_own[...].astype(jnp.float32) + near_got[...].astype(jnp.float32)


def pick_onward(after, pair, near_pair, near_x, other_x, near_y, chunk):
    count, width = other_x.shape
    rows = near_y[0].shape[0]
    operands = [*pair, *near_pair, *near_x, other_x, *near_y, *values_of(chunk)]
    return pl.pallas_call(
        functools.partial(onward_kernel, kinds_of(chunk)),
        in_specs=[unread()] + [whole()] * len(operands),
        out_specs=[whole()] * 6,
        out_shape=[
            jax.ShapeDtypeStruct((2, count, width), jnp.bfloat16),
            jax.ShapeDtypeStruct((count + 2 * rows, width), jnp.bfloat16),
            jax.ShapeDtypeStruct((count + rows, width), jnp.bfloat16),
            jax.ShapeDtypeStruct(pair[0].shape, jnp.float32),
            jax.ShapeDtypeStruct(near_pair[0].shape, jnp.float32),
            jax.ShapeDtypeStruct((8, 2 * count), jnp.float32),
        ],
        compiler_params=params(),
        cost_estimate=cost(1000, 8 * other_x.size),
    )(after, *operands)


def pass_kernel(after_ref, in_ref, *outs):
    row = 0
    for out_ref in outs:
        out_ref[...] = in_ref[row : row + out_ref.shape[0], :]
        row = row + out_ref.shape[0]


def passed_on(after, value, cuts):
    width = value.shape[1]
    return pl.pallas_call(
        pass_kernel,
        in_specs=[unread(), whole()],
        out_specs=[whole()] * len(cuts),
        out_shape=[jax.ShapeDtypeStruct((rows, width), value.dtype) for rows in cuts],
        compiler_params=params(),
        cost_estimate=cost(1000, 2 * value.size),
    )(after, value)


def first_kernel(kinds, count, gate_ref, after_ref, sum_ref, own, got, *refs):
    n = len(kinds)
    xs, ys, gates = views(refs[:n], kinds, count)
    out_ref, more_ref, token_ref = refs[n:]
    more_ref[...] = summed([(own, got)])
    lefts = hidden_grads(gate_ref[0:1, :], [(sum_ref,)])
    x = joined(xs)
    for m, right in enumerate((x, x, joined(ys))):
        out_ref[m] = plain(lefts[m], right)
    token_ref[...] = jnp.zeros_like(token_ref)


def first_grads(gate, after, total, pair, chunk, hidden, count):
    kinds = kinds_of(chunk)
    width = chunk[0][1].shape[-1]
    return pl.pallas_call(
        functools.partial(first_kernel, kinds, count),
        in_specs=[whole(), unread()] + [whole()] * (3 + len(kinds)),
        out_specs=[whole()] * 3,
        out_shape=[
            jax.ShapeDtypeStruct((3, hidden, width), jnp.float32),
            jax.ShapeDtypeStruct(pair[0].shape, jnp.float32),
            jax.ShapeDtypeStruct((8, 128), jnp.float32),
        ],
        compiler_params=params(),
        cost_estimate=cost(2 * total.size * width, 12 * hidden * width),
    )(gate, after, total, *pair, *values_of(chunk))


def grad_kernel(kinds, count, sum_ref, more_ref, own, got, *refs):
    n = len(kinds)
    xs, ys, gates = views(refs[:n], kinds, count)
    acc_ref, out_ref = refs[n:]
    lefts = hidden_grads(gate_row(gates), [(sum_ref,), (more_ref,), (own, got)])
    x = joined(xs)
    for m, right in enumerate((x, x, joined(ys))):
        out_ref[m] = acc_ref[m] + plain(lefts[m], right)


def add_grads(near_sum, more_sum, pair, chunk, acc, count):
    kinds = kinds_of(chunk)
    mats, hidden, width = acc.shape
    operands = [near_sum, more_sum, *pair, *values_of(chunk), acc]
    return pl.pallas_call(
        functools.partial(grad_kernel, kinds, count),
        in_specs=[whole()] * len(operands),
        out_specs=whole(),
        out_shape=jax.ShapeDtypeStruct(acc.shape, jnp.float32),
        input_output_aliases={len(operands) - 1: 0},
        compiler_params=params(),
        cost_estimate=cost(
            2 * mats * hidden * width * 4 * count, 8 * mats * hidden * width
        ),
    )(*operands)


def adam(grad, first, second):
    moment_one = beta_one * first.astype(jnp.float32) + (1.0 - beta_one) * grad
    moment_two = beta_two * second.astype(jnp.float32) + (1.0 - beta_two) * (grad * grad)
    root = (1.0 / (1.0 - beta_two**step_count)) ** 0.5
    below = moment_two * lax.rsqrt(moment_two) + epsilon / root
    scaled = moment_one * (1.0 / (1.0 - beta_one**step_count) / root)
    step = scaled * pl.reciprocal(below, approx=True)
    return [value.astype(jnp.bfloat16) for value in (moment_one, moment_two, step)]


def pair_of_blocks(own, got):
    total = summed([(own, got)])
    return beside(total, total.shape[0] // 2, (0, 1))


def down_kernel(kinds, count, own_g, got_g, own_u, got_u, *refs):
    n = len(kinds)
    acc_ref, first_ref, second_ref, *outs = refs[n:]
    xs, ys, gates = views(refs[:n], kinds, count)
    hg, hu = pair_of_blocks(own_g, got_g), pair_of_blocks(own_u, got_u)
    act = activation(hg, hu, gate_row(gates))[2]
    grad = acc_ref[2] + plain(act, joined(ys))
    for out_ref, value in zip(outs, adam(grad, first_ref[2], second_ref[2])):
        out_ref[...] = value


def down_update(pairs, chunk, acc, moments, count):
    kinds = kinds_of(chunk)
    mats, hidden, width = acc.shape
    operands = [*pairs, *values_of(chunk), acc, *moments]
    return pl.pallas_call(
        functools.partial(down_kernel, kinds, count),
        in_specs=[whole()] * len(operands),
        out_specs=[whole()] * 3,
        out_shape=[jax.ShapeDtypeStruct((hidden, width), jnp.bfloat16)] * 3,
        compiler_params=params(),
        cost_estimate=cost(4 * hidden * width * count, 14 * hidden * width),
    )(*operands)


def slopes_kernel(kinds, count, own_g, got_g, own_u, got_u, own_d, got_d, *refs):
    n = len(kinds)
    acc_ref, first_ref, second_ref = refs[n : n + 3]
    done, outs = refs[n + 3 : n + 6], refs[n + 6 : n + 9]
    held, sems = refs[n + 9 : n + 12], refs[n + 12]
    copies = [
        pltpu.make_async_copy(done[k], outs[k].at[2], sems.at[2, k]) for k in range(3)
    ]
    for copy in copies:
        copy.start()
    xs, ys, gates = views(refs[:n], kinds, count)
    hg, hu = pair_of_blocks(own_g, got_g), pair_of_blocks(own_u, got_u)
    dact = gate_row(gates) * pair_of_blocks(own_d, got_d)
    sig, silu, act = activation(hg, hu, 1.0)
    right = joined(xs)
    for m, left in enumerate(hidden_slopes(hg, hu, sig, silu, dact)):
        grad = acc_ref[m] + plain(left, right)
        for k, value in enumerate(adam(grad, first_ref[m], second_ref[m])):
            held[k][m] = value
            copies.append(pltpu.make_async_copy(held[k].at[m], outs[k].at[m], sems.at[m, k]))
            copies[-1].start()
    for copy in copies:
        copy.wait()


def slopes_update(pairs, chunk, acc, moments, done, count):
    kinds = kinds_of(chunk)
    mats, hidden, width = acc.shape
    operands = [*pairs, *values_of(chunk), acc, *moments, *done]
    return pl.pallas_call(
        functools.partial(slopes_kernel, kinds, count),
        in_specs=[whole()] * len(operands),
        out_specs=[in_hbm()] * 3,
        out_shape=[jax.ShapeDtypeStruct(acc.shape, jnp.bfloat16)] * 3,
        scratch_shapes=[pltpu.VMEM((2, hidden, width), jnp.bfloat16)] * 3
        + [pltpu.SemaphoreType.DMA((3, 3))],
        compiler_params=params(),
        cost_estimate=cost(8 * hidden * width * count, 28 * hidden * width),
    )(*operands)


def from_masked(value, axis, mask):
    pairs = [(source, source ^ mask) for source in range(lax.axis_size(axis))]
    return lax.ppermute(value, axis, pairs)


def dense_plan(tokens, cotangent, expert_ids, gate_probs, weights, first_moment, second_moment):
    n_data = lax.axis_size("dp")
    slices = min(4, lax.axis_size("expert") // 2)
    experts_total = lax.axis_size("expert") // (2 * slices) * n_data
    count = tokens.shape[0]
    hidden, width = weights.shape[1:]
    slots = -(-experts_total // 16) * 16
    other = lambda value: from_masked(value, "dp", 1)
    partner = lambda value: from_masked(value, "expert", 1)
    x_own, y_own, own, weights = pack_own(
        expert_ids, gate_probs, tokens, cotangent, weights, slots
    )
    first = [("xy", own), ("xy", other(own))]
    send, token = partials(weights, own, first, (6,), count)
    first_pair = (send, partner(send))
    along = [[(p, p ^ (2 if p % 2 == k else 4)) for p in range(n_data)] for k in (0, 1)]
    near_x = [lax.ppermute(x_own, "dp", pairs) for pairs in along]
    near_y = [lax.ppermute(y_own, "dp", pairs) for pairs in along]
    send, token = partials(weights, token, [("x", near_x[0]), ("", near_x[1])], (2,), count)
    near_pair = (send, partner(send))
    x_pair, rest, picked, first_sum, near_sum, gate = pick_onward(
        token, first_pair, near_pair, near_x, other(near_x[0]), near_y, first
    )
    far = lax.ppermute(picked, "dp", along[1])
    rest_other = other(rest)
    early = [("x of xyy", rest), ("second x", x_pair)]
    late = [("y, y of xyy", rest), ("x, y, y", rest_other)]
    send, token = partials(weights, picked, early, (4,), count)
    early_pair = (send, partner(send))
    send, token = partials(weights, token, late, (6,), count)
    late_pair = (send, partner(send))
    pieces = passed_on(token, far, (count // 2, count // 2, count // 2, count // 2 + slots))
    acc, early_sum, token = first_grads(
        gate, pieces[0], first_sum, early_pair, first, hidden, count
    )
    pieces = [*pieces, *[other(value) for value in pieces]]
    final = list(zip(("x", "x", "y", "half y, gates") * 2, pieces))
    sends = partials(weights, token, final, (2, 2, 2), count, 0)
    pairs = [value for send in sends for value in (send, partner(send))]
    near = [("first x", x_pair), ("x, y, y", rest), ("second x", x_pair), ("x, y, y", rest_other)]
    acc = add_grads(near_sum, early_sum, late_pair, near, acc, count)
    moments = (first_moment, second_moment)
    final_y = [block for block in final if block[0] != "x"]
    final_x = [block for block in final if block[0] != "y"]
    done = down_update(pairs[:4], final_y, acc, moments, count)
    return tuple(slopes_update(pairs, final_x, acc, moments, done, count))


def per_device(tokens, cotangent, expert_ids, gate_probs, weights, first_moment, second_moment):
    n_expert = lax.axis_size("expert")
    n_data = lax.axis_size("dp")
    slices = min(4, n_expert // 2)
    experts_total = n_expert // (2 * slices) * n_data
    half = tokens.shape[0] // 2
    dense = 2 * half * expert_ids.shape[1] // experts_total >= half
    plan = dense_plan if dense and n_data == 8 else routed_plan
    return plan(
        tokens, cotangent, expert_ids, gate_probs, weights, first_moment, second_moment
    )


def solution(mesh):
    in_specs = (
        P("dp", None),
        P("dp", None),
        P("dp", None),
        P("dp", None),
        P(None, "dp", "expert"),
        P(None, "dp", "expert"),
        P(None, "dp", "expert"),
    )
    out_specs = (P(None, "dp", "expert"), P(None, "dp", "expert"), P(None, "dp", "expert"))
    return jax.shard_map(
        per_device, mesh=mesh, in_specs=in_specs, out_specs=out_specs, check_vma=False
    )
```

```python
import functools

import jax
import jax.numpy as jnp
from jax import lax
from jax.experimental import pallas as pl
from jax.experimental.pallas import tpu as pltpu
from jax.sharding import PartitionSpec as P

beta_one = 0.9
beta_two = 0.95
step_count = 10
epsilon = 1e-08


def from_partner(value, axis, distance):
    mask = 2**distance
    pairs = [(source, source ^ mask) for source in range(lax.axis_size(axis))]
    return lax.ppermute(value, axis, pairs)


def contract_last(left, right):
    return lax.dot_general(
        left, right, (((1,), (1,)), ((), ())), preferred_element_type=jnp.float32
    )


def contract_first(left, right):
    return lax.dot_general(
        left, right, (((0,), (0,)), ((), ())), preferred_element_type=jnp.float32
    )


def split_halves(grad, replica, width_half):
    keep = lax.dynamic_slice_in_dim(grad, replica * width_half, width_half, grad.ndim - 1)
    give = lax.dynamic_slice_in_dim(grad, (1 - replica) * width_half, width_half, grad.ndim - 1)
    return (keep, give)


def route_block(block_ids, block_gates, group, n_data, capacity):
    count = block_ids.shape[0]
    top = block_ids.shape[1]
    target = block_ids - group * n_data
    inside = block_ids // n_data == group
    onehot = (
        (target[:, :, None] == jnp.arange(n_data, dtype=jnp.int32)[None, None, :])
        & inside[:, :, None]
    ).astype(jnp.int32)
    per_token = jnp.sum(onehot, axis=1)
    earlier = jnp.cumsum(per_token, axis=0) - per_token
    rank = jnp.sum(onehot * earlier[:, None, :], axis=2)
    total_slots = n_data * capacity
    slot = jnp.where(inside, target * capacity + rank, total_slots).reshape(-1)
    token_of = jnp.broadcast_to(jnp.arange(count, dtype=jnp.int32)[:, None], (count, top)).reshape(
        -1
    )
    table = jnp.full((total_slots,), count, jnp.int32).at[slot].set(token_of, mode="drop")
    gate_slot = (
        jnp.zeros((total_slots,), jnp.bfloat16).at[slot].set(block_gates.reshape(-1), mode="drop")
    )
    return (table, gate_slot)


def routed_plan(tokens, cotangent, expert_ids, gate_probs, weights, first_moment, second_moment):
    n_expert = lax.axis_size("expert")
    n_data = lax.axis_size("dp")
    slices = min(4, n_expert // 2)
    place = lax.axis_index("expert")
    replica = place % 2
    group = place // (2 * slices)
    groups = n_expert // (2 * slices)
    experts_total = groups * n_data
    half = tokens.shape[0] // 2
    width_half = weights.shape[2]
    top = expert_ids.shape[1]
    capacity = max(2, 2 * half * top // experts_total)
    start = replica * half
    own_ids = lax.dynamic_slice_in_dim(expert_ids, start, half, 0)
    own_gates = lax.dynamic_slice_in_dim(gate_probs, start, half, 0)
    table, gate_slot = route_block(own_ids, own_gates, group, n_data, capacity)
    source_tokens = lax.dynamic_slice_in_dim(tokens, start, half, 0)
    source_cot = lax.dynamic_slice_in_dim(cotangent, start, half, 0)
    columns = source_tokens.shape[1]
    padded_tokens = jnp.concatenate([source_tokens, jnp.zeros((1, columns), jnp.bfloat16)], 0)
    padded_cot = jnp.concatenate([source_cot, jnp.zeros((1, columns), jnp.bfloat16)], 0)
    send_rows = padded_tokens[table].reshape(n_data, -1, columns)
    send_cot = padded_cot[table].reshape(n_data, -1, columns)
    send_gates = gate_slot.reshape(n_data, -1)
    rows_in, gates_in = (
        lax.all_to_all(send_rows, "dp", split_axis=0, concat_axis=0, tiled=True),
        lax.all_to_all(send_gates, "dp", split_axis=0, concat_axis=0, tiled=True),
    )
    rows = rows_in.reshape(-1, columns)
    gate_rows = gates_in.reshape(-1).astype(jnp.float32)
    partner = from_partner(weights, "expert", 0)
    lower = jnp.where(replica == 0, weights, partner)
    upper = jnp.where(replica == 0, partner, weights)
    full = jnp.concatenate([lower, upper], 2)
    hg = contract_last(rows, full[0])
    hu = contract_last(rows, full[1])
    sig = jax.nn.sigmoid(hg)
    act = (hg * sig * hu).astype(jnp.bfloat16)
    cot_in = lax.all_to_all(send_cot, "dp", split_axis=0, concat_axis=0, tiled=True)
    cots = cot_in.reshape(-1, columns)
    dz = (gate_rows[:, None] * cots.astype(jnp.float32)).astype(jnp.bfloat16)
    dact = contract_last(dz, full[2])
    grad_down = contract_first(act, dz)
    dhg = (dact * hu * sig * (1.0 + hg * (1.0 - sig))).astype(jnp.bfloat16)
    dhu = (dact * hg * sig).astype(jnp.bfloat16)
    grad_gate = contract_first(dhg, rows)
    grad_up = contract_first(dhu, rows)
    stacked = jnp.stack([grad_gate, grad_up, grad_down])
    keep, give = split_halves(stacked, replica, width_half)
    total = keep + from_partner(give, "expert", 0)
    moment_one = beta_one * first_moment.astype(jnp.float32) + (1.0 - beta_one) * total
    moment_two = beta_two * second_moment.astype(jnp.float32) + (1.0 - beta_two) * total * total
    step = (
        moment_one
        / (1.0 - beta_one**step_count)
        / (jnp.sqrt(moment_two / (1.0 - beta_two**step_count)) + epsilon)
    )
    return (
        moment_one.astype(jnp.bfloat16),
        moment_two.astype(jnp.bfloat16),
        step.astype(jnp.bfloat16),
    )


VMEM_LIMIT = 16 * 1024 * 1024


def params():
    return pltpu.CompilerParams(vmem_limit_bytes=VMEM_LIMIT)


def cost(flops, moved):
    return pl.CostEstimate(flops=flops, bytes_accessed=moved, transcendentals=0)


def whole():
    return pl.BlockSpec(memory_space=pltpu.VMEM)


def in_hbm():
    return pl.BlockSpec(memory_space=pltpu.HBM)


def unread():
    return pl.BlockSpec(memory_space=pl.ANY)


def expert_here():
    slices = min(4, lax.axis_size("expert") // 2)
    group = lax.axis_index("expert") // (2 * slices)
    return group * lax.axis_size("dp") + lax.axis_index("dp")


def keep_hbm(value):
    return pltpu.with_memory_space_constraint(value, pltpu.HBM)


def pack_kernel(
    ids_hbm,
    gates_hbm,
    tokens_ref,
    cot_ref,
    w_hbm,
    x_ref,
    y_ref,
    own_ref,
    w_ref,
    ids_ref,
    gates_ref,
    sems,
):
    count = tokens_ref.shape[0]
    width = x_ref.shape[1]
    columns = pl.ds(pl.multiple_of(lax.axis_index("expert") % 2 * width, width), width)
    copies = [
        pltpu.make_async_copy(ids_hbm, ids_ref, sems.at[0]),
        pltpu.make_async_copy(gates_hbm, gates_ref, sems.at[1]),
        pltpu.make_async_copy(tokens_ref.at[:, columns], x_ref, sems.at[2]),
        pltpu.make_async_copy(cot_ref.at[:, columns], y_ref.at[0:count, :], sems.at[3]),
        pltpu.make_async_copy(tokens_ref.at[:, columns], own_ref.at[0:count, :], sems.at[4]),
        pltpu.make_async_copy(cot_ref.at[:, columns], own_ref.at[count : 2 * count, :], sems.at[5]),
        pltpu.make_async_copy(w_hbm, w_ref, sems.at[6]),
    ]
    for copy in copies:
        copy.start()
    copies[0].wait()
    copies[1].wait()
    ids = ids_ref[...]
    gates = gates_ref[...].astype(jnp.float32)
    slots = y_ref.shape[0] - count
    row = lax.broadcasted_iota(jnp.int32, (slots, count), 0)
    gate = jnp.zeros((slots, count), jnp.float32)
    for k in range(ids.shape[0]):
        gate = gate + jnp.where(row == ids[k : k + 1, :], gates[k : k + 1, :], 0.0)
    y_ref[count:, 0:count] = gate.astype(jnp.bfloat16)
    y_ref[count:, count:] = jnp.zeros((slots, width - count), jnp.bfloat16)
    own_ref[2 * count :, :] = y_ref[count:, :]
    for copy in copies[2:]:
        copy.wait()


def pack_own(ids, gates, tokens, cotangent, weights, slots):
    count, top = ids.shape
    width = weights.shape[2]
    return pl.pallas_call(
        pack_kernel,
        in_specs=[in_hbm()] * 5,
        out_specs=[whole()] * 4,
        out_shape=[
            jax.ShapeDtypeStruct((rows, width), jnp.bfloat16)
            for rows in (count, count + slots, 2 * count + slots)
        ]
        + [jax.ShapeDtypeStruct(weights.shape, weights.dtype)],
        scratch_shapes=[
            pltpu.VMEM((top, count), ids.dtype),
            pltpu.VMEM((top, count), gates.dtype),
            pltpu.SemaphoreType.DMA((7,)),
        ],
        compiler_params=params(),
        cost_estimate=cost(1000, 8 * count * width),
    )(*[keep_hbm(value) for value in (ids.T, gates.T, tokens, cotangent, weights)])


def views(refs, kinds, count):
    xs, ys, gates = [], [], []
    for ref, kind in zip(refs, kinds):
        if kind in ("first x", "second x"):
            xs.append(ref[0 if kind == "first x" else 1])
            continue
        if kind == "x of xyy":
            xs.append(ref[0:count, :])
            continue
        if kind in ("x, y, y", "y, y of xyy"):
            rows = (ref.shape[0] - count) // 2
            if kind == "x, y, y":
                xs.append(ref[0:count, :])
            for row in (count, count + rows):
                ys.append(ref[row : row + count, :])
                gates.append(ref[row + count : row + rows, 0:count])
            continue
        for part in [ref.at[0], ref.at[1]] if ref.ndim == 3 else [ref]:
            if kind == "x":
                xs.append(part[...])
            if kind == "xy":
                xs.append(part[0:count, :])
                ys.append(part[count : 2 * count, :])
                gates.append(part[2 * count :, 0:count])
            if kind == "y":
                ys.append(part[...])
            if kind == "y, gates":
                ys.append(part[0:count, :])
                gates.append(part[count:, 0:count])
            if kind == "half y, gates":
                ys.append(part[0 : count // 2, :])
                gates.append(part[count // 2 :, 0:count])
    return xs, ys, gates


def joined(parts):
    return parts[0] if len(parts) == 1 else jnp.concatenate(parts, 0)


def kinds_of(chunk):
    return tuple(kind for kind, value in chunk)


def values_of(chunk):
    return [value for kind, value in chunk]


def store_partials(parts, count, out_ref):
    row = 0
    for part in parts:
        for first in range(0, part.shape[1], count):
            piece = part[:, first : first + count]
            out_ref[row : row + piece.shape[0], :] = piece.astype(jnp.bfloat16)
            row = row + piece.shape[0]


def partial_kernel(kinds, count, tokened, w_ref, after_ref, *refs):
    n = len(kinds)
    xs, ys, gates = views(refs[:n], kinds, count)
    outs = refs[n : len(refs) - tokened]
    mats, hidden, width = w_ref.shape
    parts = []
    if xs and len(outs) == mats:
        parts.extend(contract_last(w_ref[m], joined(xs)) for m in (0, 1))
    elif xs:
        parts.append(contract_last(w_ref[0:2].reshape(2 * hidden, width), joined(xs)))
    if ys:
        parts.append(contract_last(w_ref[2], joined(ys)))
    if len(outs) == 1:
        store_partials(parts, count, outs[0])
    else:
        for part, out_ref in zip(parts, outs):
            store_partials([part], count, out_ref)
    if tokened:
        refs[-1][...] = jnp.zeros_like(refs[-1])


def partials(weights, after, chunk, rows, count, tokened=1):
    hidden, width = weights.shape[1:]
    kinds = kinds_of(chunk)
    total = sum(rows) * hidden * count
    return pl.pallas_call(
        functools.partial(partial_kernel, kinds, count, tokened),
        in_specs=[whole(), unread()] + [whole()] * len(kinds),
        out_specs=[whole()] * (len(rows) + tokened),
        out_shape=[jax.ShapeDtypeStruct((k * hidden, count), jnp.bfloat16) for k in rows]
        + [jax.ShapeDtypeStruct((8, 128), jnp.float32)] * tokened,
        compiler_params=params(),
        cost_estimate=cost(2 * total * width, 6 * total),
    )(weights, after, *values_of(chunk))


def gate_row(gates):
    rows = []
    expert = expert_here()
    for held in gates:
        held = held.astype(jnp.float32)
        index = lax.broadcasted_iota(jnp.int32, held.shape, 0)
        rows.append(jnp.sum(jnp.where(index == expert, held, 0.0), 0, keepdims=True))
    return rows[0] if len(rows) == 1 else jnp.concatenate(rows, 1)


def summed(pairs):
    parts = []
    for own, *got in pairs:
        part = own[...].astype(jnp.float32)
        parts.append(part + got[0][...].astype(jnp.float32) if got else part)
    return parts[0] if len(parts) == 1 else jnp.concatenate(parts, 0)


def beside(total, hidden, firsts):
    parts = [total[first * hidden : (first + 1) * hidden] for first in firsts]
    return jnp.concatenate(parts, 1)


def activation(hg, hu, gate):
    sig = jax.nn.sigmoid(hg)
    silu = hg * sig
    return sig, silu, (gate * (silu * hu)).astype(jnp.bfloat16)


def hidden_slopes(hg, hu, sig, silu, dact):
    dhg = (dact * hu * sig * (1.0 + hg * (1.0 - sig))).astype(jnp.bfloat16)
    dhu = (dact * silu).astype(jnp.bfloat16)
    return dhg, dhu


def hidden_grads(gate, pairs):
    total = summed(pairs)
    blocks = gate.shape[1] // total.shape[1]
    hidden = total.shape[0] // (3 * blocks)
    hg = beside(total, hidden, range(0, 2 * blocks, 2))
    hu = beside(total, hidden, range(1, 2 * blocks, 2))
    dact = gate * beside(total, hidden, range(2 * blocks, 3 * blocks))
    sig, silu, act = activation(hg, hu, gate)
    return (*hidden_slopes(hg, hu, sig, silu, dact), act)


def plain(left, right):
    return lax.dot_general(
        left, right, (((1,), (0,)), ((), ())), preferred_element_type=jnp.float32
    )


def onward_kernel(kinds, after_ref, own, got, near_own, near_got, *refs):
    x0_ref, x1_ref, s0_ref, y0_ref, y1_ref = refs[:5]
    pair_ref, rest_ref, out_ref, first_ref, sum_ref, gate_ref = refs[5 + len(kinds) :]
    count, rows = x0_ref.shape[0], y0_ref.shape[0]
    gates = views(refs[5 : 5 + len(kinds)], kinds, count)[2]
    gate_ref[...] = jnp.broadcast_to(gate_row(gates), gate_ref.shape)
    pair_ref[0] = x0_ref[...]
    pair_ref[1] = s0_ref[...]
    rest_ref[0:count, :] = x1_ref[...]
    rest_ref[count : count + rows, :] = y0_ref[...]
    rest_ref[count + rows :, :] = y1_ref[...]
    out_ref[0:count, :] = x0_ref[...]
    out_ref[count:, :] = y0_ref[...]
    first_ref[...] = own[...].astype(jnp.float32) + got[...].astype(jnp.float32)
    sum_ref[...] = near_own[...].astype(jnp.float32) + near_got[...].astype(jnp.float32)


def pick_onward(after, pair, near_pair, near_x, other_x, near_y, chunk):
    count, width = other_x.shape
    rows = near_y[0].shape[0]
    operands = [*pair, *near_pair, *near_x, other_x, *near_y, *values_of(chunk)]
    return pl.pallas_call(
        functools.partial(onward_kernel, kinds_of(chunk)),
        in_specs=[unread()] + [whole()] * len(operands),
        out_specs=[whole()] * 6,
        out_shape=[
            jax.ShapeDtypeStruct((2, count, width), jnp.bfloat16),
            jax.ShapeDtypeStruct((count + 2 * rows, width), jnp.bfloat16),
            jax.ShapeDtypeStruct((count + rows, width), jnp.bfloat16),
            jax.ShapeDtypeStruct(pair[0].shape, jnp.float32),
            jax.ShapeDtypeStruct(near_pair[0].shape, jnp.float32),
            jax.ShapeDtypeStruct((8, 2 * count), jnp.float32),
        ],
        compiler_params=params(),
        cost_estimate=cost(1000, 8 * other_x.size),
    )(after, *operands)


def pass_kernel(after_ref, in_ref, *outs):
    row = 0
    for out_ref in outs:
        out_ref[...] = in_ref[row : row + out_ref.shape[0], :]
        row = row + out_ref.shape[0]


def passed_on(after, value, cuts):
    width = value.shape[1]
    return pl.pallas_call(
        pass_kernel,
        in_specs=[unread(), whole()],
        out_specs=[whole()] * len(cuts),
        out_shape=[jax.ShapeDtypeStruct((rows, width), value.dtype) for rows in cuts],
        compiler_params=params(),
        cost_estimate=cost(1000, 2 * value.size),
    )(after, value)


def first_kernel(kinds, count, gate_ref, after_ref, sum_ref, own, got, *refs):
    n = len(kinds)
    xs, ys, gates = views(refs[:n], kinds, count)
    out_ref, more_ref, token_ref = refs[n:]
    more_ref[...] = summed([(own, got)])
    lefts = hidden_grads(gate_ref[0:1, :], [(sum_ref,)])
    x = joined(xs)
    for m, right in enumerate((x, x, joined(ys))):
        out_ref[m] = plain(lefts[m], right)
    token_ref[...] = jnp.zeros_like(token_ref)


def first_grads(gate, after, total, pair, chunk, hidden, count):
    kinds = kinds_of(chunk)
    width = chunk[0][1].shape[-1]
    return pl.pallas_call(
        functools.partial(first_kernel, kinds, count),
        in_specs=[whole(), unread()] + [whole()] * (3 + len(kinds)),
        out_specs=[whole()] * 3,
        out_shape=[
            jax.ShapeDtypeStruct((3, hidden, width), jnp.float32),
            jax.ShapeDtypeStruct(pair[0].shape, jnp.float32),
            jax.ShapeDtypeStruct((8, 128), jnp.float32),
        ],
        compiler_params=params(),
        cost_estimate=cost(2 * total.size * width, 12 * hidden * width),
    )(gate, after, total, *pair, *values_of(chunk))


def grad_kernel(kinds, count, sum_ref, more_ref, own, got, *refs):
    n = len(kinds)
    xs, ys, gates = views(refs[:n], kinds, count)
    acc_ref, out_ref = refs[n:]
    lefts = hidden_grads(gate_row(gates), [(sum_ref,), (more_ref,), (own, got)])
    x = joined(xs)
    for m, right in enumerate((x, x, joined(ys))):
        out_ref[m] = acc_ref[m] + plain(lefts[m], right)


def add_grads(near_sum, more_sum, pair, chunk, acc, count):
    kinds = kinds_of(chunk)
    mats, hidden, width = acc.shape
    operands = [near_sum, more_sum, *pair, *values_of(chunk), acc]
    return pl.pallas_call(
        functools.partial(grad_kernel, kinds, count),
        in_specs=[whole()] * len(operands),
        out_specs=whole(),
        out_shape=jax.ShapeDtypeStruct(acc.shape, jnp.float32),
        input_output_aliases={len(operands) - 1: 0},
        compiler_params=params(),
        cost_estimate=cost(
            2 * mats * hidden * width * 4 * count, 8 * mats * hidden * width
        ),
    )(*operands)


def adam(grad, first, second):
    moment_one = beta_one * first.astype(jnp.float32) + (1.0 - beta_one) * grad
    moment_two = beta_two * second.astype(jnp.float32) + (1.0 - beta_two) * (grad * grad)
    root = (1.0 / (1.0 - beta_two**step_count)) ** 0.5
    below = moment_two * lax.rsqrt(moment_two) + epsilon / root
    scaled = moment_one * (1.0 / (1.0 - beta_one**step_count) / root)
    step = scaled * pl.reciprocal(below, approx=True)
    return [value.astype(jnp.bfloat16) for value in (moment_one, moment_two, step)]


def pair_of_blocks(own, got):
    total = summed([(own, got)])
    return beside(total, total.shape[0] // 2, (0, 1))


def down_kernel(kinds, count, own_g, got_g, own_u, got_u, *refs):
    n = len(kinds)
    acc_ref, first_ref, second_ref, *outs, gate_factor_ref, up_factor_ref = refs[n:]
    xs, ys, gates = views(refs[:n], kinds, count)
    hg, hu = pair_of_blocks(own_g, got_g), pair_of_blocks(own_u, got_u)
    gate = gate_row(gates)
    sig, silu, act = activation(hg, hu, gate)
    gate_factor_ref[...] = gate * (hu * sig * (1.0 + hg * (1.0 - sig)))
    up_factor_ref[...] = gate * silu
    grad = acc_ref[2] + plain(act, joined(ys))
    for out_ref, value in zip(outs, adam(grad, first_ref[2], second_ref[2])):
        out_ref[...] = value


def down_update(pairs, chunk, acc, moments, count):
    kinds = kinds_of(chunk)
    mats, hidden, width = acc.shape
    operands = [*pairs, *values_of(chunk), acc, *moments]
    return pl.pallas_call(
        functools.partial(down_kernel, kinds, count),
        in_specs=[whole()] * len(operands),
        out_specs=[whole()] * 5,
        out_shape=[jax.ShapeDtypeStruct((hidden, width), jnp.bfloat16)] * 3
        + [jax.ShapeDtypeStruct((hidden, 2 * count), jnp.float32)] * 2,
        compiler_params=params(),
        cost_estimate=cost(4 * hidden * width * count, 14 * hidden * width),
    )(*operands)


def slopes_kernel(kinds, count, own_d, got_d, gate_factor_ref, up_factor_ref, *refs):
    n = len(kinds)
    acc_ref, first_ref, second_ref = refs[n : n + 3]
    done, outs = refs[n + 3 : n + 6], refs[n + 6 : n + 9]
    held, sems = refs[n + 9 : n + 12], refs[n + 12]
    copies = [
        pltpu.make_async_copy(done[k], outs[k].at[2], sems.at[2, 0, k]) for k in range(3)
    ]
    for copy in copies:
        copy.start()
    xs, ys, gates = views(refs[:n], kinds, count)
    dact = pair_of_blocks(own_d, got_d)
    half = acc_ref.shape[2] // 2
    for m, factor_ref in enumerate((gate_factor_ref, up_factor_ref)):
        left = (dact * factor_ref[...]).astype(jnp.bfloat16)
        for side in (0, 1):
            columns = slice(side * half, (side + 1) * half)
            right = jnp.concatenate([x[:, columns] for x in xs], 0)
            grad = acc_ref[m, :, columns] + plain(left, right)
            values = adam(grad, first_ref[m, :, columns], second_ref[m, :, columns])
            for k, value in enumerate(values):
                held[k][m, side] = value
                copies.append(
                    pltpu.make_async_copy(
                        held[k].at[m, side], outs[k].at[m, :, columns], sems.at[m, side, k]
                    )
                )
                copies[-1].start()
    for copy in copies:
        copy.wait()


def slopes_update(pair, factors, chunk, acc, moments, done, count):
    kinds = kinds_of(chunk)
    mats, hidden, width = acc.shape
    operands = [*pair, *factors, *values_of(chunk), acc, *moments, *done]
    return pl.pallas_call(
        functools.partial(slopes_kernel, kinds, count),
        in_specs=[whole()] * len(operands),
        out_specs=[in_hbm()] * 3,
        out_shape=[jax.ShapeDtypeStruct(acc.shape, jnp.bfloat16)] * 3,
        scratch_shapes=[pltpu.VMEM((2, 2, hidden, width // 2), jnp.bfloat16)] * 3
        + [pltpu.SemaphoreType.DMA((3, 2, 3))],
        compiler_params=params(),
        cost_estimate=cost(8 * hidden * width * count, 28 * hidden * width),
    )(*operands)


def from_masked(value, axis, mask):
    pairs = [(source, source ^ mask) for source in range(lax.axis_size(axis))]
    return lax.ppermute(value, axis, pairs)


def dense_plan(tokens, cotangent, expert_ids, gate_probs, weights, first_moment, second_moment):
    n_data = lax.axis_size("dp")
    slices = min(4, lax.axis_size("expert") // 2)
    experts_total = lax.axis_size("expert") // (2 * slices) * n_data
    count = tokens.shape[0]
    hidden, width = weights.shape[1:]
    slots = -(-experts_total // 16) * 16
    other = lambda value: from_masked(value, "dp", 1)
    partner = lambda value: from_masked(value, "expert", 1)
    x_own, y_own, own, weights = pack_own(
        expert_ids, gate_probs, tokens, cotangent, weights, slots
    )
    first = [("xy", own), ("xy", other(own))]
    send, token = partials(weights, own, first, (6,), count)
    first_pair = (send, partner(send))
    along = [[(p, p ^ (2 if p % 2 == k else 4)) for p in range(n_data)] for k in (0, 1)]
    near_x = [lax.ppermute(x_own, "dp", pairs) for pairs in along]
    near_y = [lax.ppermute(y_own, "dp", pairs) for pairs in along]
    send, token = partials(weights, token, [("x", near_x[0]), ("", near_x[1])], (2,), count)
    near_pair = (send, partner(send))
    x_pair, rest, picked, first_sum, near_sum, gate = pick_onward(
        token, first_pair, near_pair, near_x, other(near_x[0]), near_y, first
    )
    far = lax.ppermute(picked, "dp", along[1])
    rest_other = other(rest)
    early = [("x of xyy", rest), ("second x", x_pair)]
    late = [("y, y of xyy", rest), ("x, y, y", rest_other)]
    send, token = partials(weights, picked, early, (4,), count)
    early_pair = (send, partner(send))
    send, token = partials(weights, token, late, (6,), count)
    late_pair = (send, partner(send))
    pieces = passed_on(token, far, (count // 2, count // 2, count // 2, count // 2 + slots))
    acc, early_sum, token = first_grads(
        gate, pieces[0], first_sum, early_pair, first, hidden, count
    )
    pieces = [*pieces, *[other(value) for value in pieces]]
    final = list(zip(("x", "x", "y", "half y, gates") * 2, pieces))
    sends = partials(weights, token, final, (2, 2, 2), count, 0)
    pairs = [value for send in sends for value in (send, partner(send))]
    near = [("first x", x_pair), ("x, y, y", rest), ("second x", x_pair), ("x, y, y", rest_other)]
    acc = add_grads(near_sum, early_sum, late_pair, near, acc, count)
    moments = (first_moment, second_moment)
    final_y = [block for block in final if block[0] != "x"]
    final_x = [block for block in final if block[0] == "x"]
    *done, gate_factor, up_factor = down_update(pairs[:4], final_y, acc, moments, count)
    factors = (gate_factor, up_factor)
    return tuple(slopes_update(pairs[4:], factors, final_x, acc, moments, done, count))


def per_device(tokens, cotangent, expert_ids, gate_probs, weights, first_moment, second_moment):
    n_expert = lax.axis_size("expert")
    n_data = lax.axis_size("dp")
    slices = min(4, n_expert // 2)
    experts_total = n_expert // (2 * slices) * n_data
    half = tokens.shape[0] // 2
    dense = 2 * half * expert_ids.shape[1] // experts_total >= half
    plan = dense_plan if dense and n_data == 8 else routed_plan
    return plan(
        tokens, cotangent, expert_ids, gate_probs, weights, first_moment, second_moment
    )


def solution(mesh):
    in_specs = (
        P("dp", None),
        P("dp", None),
        P("dp", None),
        P("dp", None),
        P(None, "dp", "expert"),
        P(None, "dp", "expert"),
        P(None, "dp", "expert"),
    )
    out_specs = (P(None, "dp", "expert"), P(None, "dp", "expert"), P(None, "dp", "expert"))
    return jax.shard_map(
        per_device, mesh=mesh, in_specs=in_specs, out_specs=out_specs, check_vma=False
    )
```

```python
import functools

import jax
import jax.numpy as jnp
from jax import lax
from jax.experimental import pallas as pl
from jax.experimental.pallas import tpu as pltpu
from jax.sharding import PartitionSpec as P

beta_one = 0.9
beta_two = 0.95
step_count = 10
epsilon = 1e-08


def from_partner(value, axis, distance):
    mask = 2**distance
    pairs = [(source, source ^ mask) for source in range(lax.axis_size(axis))]
    return lax.ppermute(value, axis, pairs)


def contract_last(left, right):
    return lax.dot_general(
        left, right, (((1,), (1,)), ((), ())), preferred_element_type=jnp.float32
    )


def contract_first(left, right):
    return lax.dot_general(
        left, right, (((0,), (0,)), ((), ())), preferred_element_type=jnp.float32
    )


def split_halves(grad, replica, width_half):
    keep = lax.dynamic_slice_in_dim(grad, replica * width_half, width_half, grad.ndim - 1)
    give = lax.dynamic_slice_in_dim(grad, (1 - replica) * width_half, width_half, grad.ndim - 1)
    return (keep, give)


def route_block(block_ids, block_gates, group, n_data, capacity):
    count = block_ids.shape[0]
    top = block_ids.shape[1]
    target = block_ids - group * n_data
    inside = block_ids // n_data == group
    onehot = (
        (target[:, :, None] == jnp.arange(n_data, dtype=jnp.int32)[None, None, :])
        & inside[:, :, None]
    ).astype(jnp.int32)
    per_token = jnp.sum(onehot, axis=1)
    earlier = jnp.cumsum(per_token, axis=0) - per_token
    rank = jnp.sum(onehot * earlier[:, None, :], axis=2)
    total_slots = n_data * capacity
    slot = jnp.where(inside, target * capacity + rank, total_slots).reshape(-1)
    token_of = jnp.broadcast_to(jnp.arange(count, dtype=jnp.int32)[:, None], (count, top)).reshape(
        -1
    )
    table = jnp.full((total_slots,), count, jnp.int32).at[slot].set(token_of, mode="drop")
    gate_slot = (
        jnp.zeros((total_slots,), jnp.bfloat16).at[slot].set(block_gates.reshape(-1), mode="drop")
    )
    return (table, gate_slot)


def routed_plan(tokens, cotangent, expert_ids, gate_probs, weights, first_moment, second_moment):
    n_expert = lax.axis_size("expert")
    n_data = lax.axis_size("dp")
    slices = min(4, n_expert // 2)
    place = lax.axis_index("expert")
    replica = place % 2
    group = place // (2 * slices)
    groups = n_expert // (2 * slices)
    experts_total = groups * n_data
    half = tokens.shape[0] // 2
    width_half = weights.shape[2]
    top = expert_ids.shape[1]
    capacity = max(2, 2 * half * top // experts_total)
    start = replica * half
    own_ids = lax.dynamic_slice_in_dim(expert_ids, start, half, 0)
    own_gates = lax.dynamic_slice_in_dim(gate_probs, start, half, 0)
    table, gate_slot = route_block(own_ids, own_gates, group, n_data, capacity)
    source_tokens = lax.dynamic_slice_in_dim(tokens, start, half, 0)
    source_cot = lax.dynamic_slice_in_dim(cotangent, start, half, 0)
    columns = source_tokens.shape[1]
    padded_tokens = jnp.concatenate([source_tokens, jnp.zeros((1, columns), jnp.bfloat16)], 0)
    padded_cot = jnp.concatenate([source_cot, jnp.zeros((1, columns), jnp.bfloat16)], 0)
    send_rows = padded_tokens[table].reshape(n_data, -1, columns)
    send_cot = padded_cot[table].reshape(n_data, -1, columns)
    send_gates = gate_slot.reshape(n_data, -1)
    rows_in, gates_in = (
        lax.all_to_all(send_rows, "dp", split_axis=0, concat_axis=0, tiled=True),
        lax.all_to_all(send_gates, "dp", split_axis=0, concat_axis=0, tiled=True),
    )
    rows = rows_in.reshape(-1, columns)
    gate_rows = gates_in.reshape(-1).astype(jnp.float32)
    partner = from_partner(weights, "expert", 0)
    lower = jnp.where(replica == 0, weights, partner)
    upper = jnp.where(replica == 0, partner, weights)
    full = jnp.concatenate([lower, upper], 2)
    hg = contract_last(rows, full[0])
    hu = contract_last(rows, full[1])
    sig = jax.nn.sigmoid(hg)
    act = (hg * sig * hu).astype(jnp.bfloat16)
    cot_in = lax.all_to_all(send_cot, "dp", split_axis=0, concat_axis=0, tiled=True)
    cots = cot_in.reshape(-1, columns)
    dz = (gate_rows[:, None] * cots.astype(jnp.float32)).astype(jnp.bfloat16)
    dact = contract_last(dz, full[2])
    grad_down = contract_first(act, dz)
    dhg = (dact * hu * sig * (1.0 + hg * (1.0 - sig))).astype(jnp.bfloat16)
    dhu = (dact * hg * sig).astype(jnp.bfloat16)
    grad_gate = contract_first(dhg, rows)
    grad_up = contract_first(dhu, rows)
    stacked = jnp.stack([grad_gate, grad_up, grad_down])
    keep, give = split_halves(stacked, replica, width_half)
    total = keep + from_partner(give, "expert", 0)
    moment_one = beta_one * first_moment.astype(jnp.float32) + (1.0 - beta_one) * total
    moment_two = beta_two * second_moment.astype(jnp.float32) + (1.0 - beta_two) * total * total
    step = (
        moment_one
        / (1.0 - beta_one**step_count)
        / (jnp.sqrt(moment_two / (1.0 - beta_two**step_count)) + epsilon)
    )
    return (
        moment_one.astype(jnp.bfloat16),
        moment_two.astype(jnp.bfloat16),
        step.astype(jnp.bfloat16),
    )


VMEM_LIMIT = 16 * 1024 * 1024


def params():
    return pltpu.CompilerParams(vmem_limit_bytes=VMEM_LIMIT)


def cost(flops, moved):
    return pl.CostEstimate(flops=flops, bytes_accessed=moved, transcendentals=0)


def whole():
    return pl.BlockSpec(memory_space=pltpu.VMEM)


def in_hbm():
    return pl.BlockSpec(memory_space=pltpu.HBM)


def unread():
    return pl.BlockSpec(memory_space=pl.ANY)


def expert_here():
    slices = min(4, lax.axis_size("expert") // 2)
    group = lax.axis_index("expert") // (2 * slices)
    return group * lax.axis_size("dp") + lax.axis_index("dp")


def keep_hbm(value):
    return pltpu.with_memory_space_constraint(value, pltpu.HBM)


def pack_kernel(
    ids_hbm,
    gates_hbm,
    tokens_ref,
    cot_ref,
    w_hbm,
    x_ref,
    y_ref,
    own_ref,
    w_ref,
    ids_ref,
    gates_ref,
    sems,
):
    count = tokens_ref.shape[0]
    width = x_ref.shape[1]
    columns = pl.ds(pl.multiple_of(lax.axis_index("expert") % 2 * width, width), width)
    copies = [
        pltpu.make_async_copy(ids_hbm, ids_ref, sems.at[0]),
        pltpu.make_async_copy(gates_hbm, gates_ref, sems.at[1]),
        pltpu.make_async_copy(tokens_ref.at[:, columns], x_ref, sems.at[2]),
        pltpu.make_async_copy(cot_ref.at[:, columns], y_ref.at[0:count, :], sems.at[3]),
        pltpu.make_async_copy(tokens_ref.at[:, columns], own_ref.at[0:count, :], sems.at[4]),
        pltpu.make_async_copy(cot_ref.at[:, columns], own_ref.at[count : 2 * count, :], sems.at[5]),
        pltpu.make_async_copy(w_hbm, w_ref, sems.at[6]),
    ]
    for copy in copies:
        copy.start()
    copies[0].wait()
    copies[1].wait()
    ids = ids_ref[...]
    gates = gates_ref[...].astype(jnp.float32)
    slots = y_ref.shape[0] - count
    row = lax.broadcasted_iota(jnp.int32, (slots, count), 0)
    gate = jnp.zeros((slots, count), jnp.float32)
    for k in range(ids.shape[0]):
        gate = gate + jnp.where(row == ids[k : k + 1, :], gates[k : k + 1, :], 0.0)
    y_ref[count:, 0:count] = gate.astype(jnp.bfloat16)
    y_ref[count:, count:] = jnp.zeros((slots, width - count), jnp.bfloat16)
    own_ref[2 * count :, :] = y_ref[count:, :]
    for copy in copies[2:]:
        copy.wait()


def pack_own(ids, gates, tokens, cotangent, weights, slots):
    count, top = ids.shape
    width = weights.shape[2]
    return pl.pallas_call(
        pack_kernel,
        in_specs=[in_hbm()] * 5,
        out_specs=[whole()] * 4,
        out_shape=[
            jax.ShapeDtypeStruct((rows, width), jnp.bfloat16)
            for rows in (count, count + slots, 2 * count + slots)
        ]
        + [jax.ShapeDtypeStruct(weights.shape, weights.dtype)],
        scratch_shapes=[
            pltpu.VMEM((top, count), ids.dtype),
            pltpu.VMEM((top, count), gates.dtype),
            pltpu.SemaphoreType.DMA((7,)),
        ],
        compiler_params=params(),
        cost_estimate=cost(1000, 8 * count * width),
    )(*[keep_hbm(value) for value in (ids.T, gates.T, tokens, cotangent, weights)])


def views(refs, kinds, count):
    xs, ys, gates = [], [], []
    for ref, kind in zip(refs, kinds):
        if kind in ("first x", "second x"):
            xs.append(ref[0 if kind == "first x" else 1])
            continue
        if kind == "x of xyy":
            xs.append(ref[0:count, :])
            continue
        if kind in ("x, y, y", "y, y of xyy"):
            rows = (ref.shape[0] - count) // 2
            if kind == "x, y, y":
                xs.append(ref[0:count, :])
            for row in (count, count + rows):
                ys.append(ref[row : row + count, :])
                gates.append(ref[row + count : row + rows, 0:count])
            continue
        for part in [ref.at[0], ref.at[1]] if ref.ndim == 3 else [ref]:
            if kind == "x":
                xs.append(part[...])
            if kind == "xy":
                xs.append(part[0:count, :])
                ys.append(part[count : 2 * count, :])
                gates.append(part[2 * count :, 0:count])
            if kind == "y":
                ys.append(part[...])
            if kind == "y, gates":
                ys.append(part[0:count, :])
                gates.append(part[count:, 0:count])
            if kind == "half y, gates":
                ys.append(part[0 : count // 2, :])
                gates.append(part[count // 2 :, 0:count])
    return xs, ys, gates


def joined(parts):
    return parts[0] if len(parts) == 1 else jnp.concatenate(parts, 0)


def kinds_of(chunk):
    return tuple(kind for kind, value in chunk)


def values_of(chunk):
    return [value for kind, value in chunk]


def store_partials(parts, count, out_ref):
    row = 0
    for part in parts:
        for first in range(0, part.shape[1], count):
            piece = part[:, first : first + count]
            out_ref[row : row + piece.shape[0], :] = piece.astype(jnp.bfloat16)
            row = row + piece.shape[0]


def partial_kernel(kinds, count, tokened, w_ref, after_ref, *refs):
    n = len(kinds)
    xs, ys, gates = views(refs[:n], kinds, count)
    outs = refs[n : len(refs) - tokened]
    mats, hidden, width = w_ref.shape
    parts = []
    if xs and len(outs) == mats:
        parts.extend(contract_last(w_ref[m], joined(xs)) for m in (0, 1))
    elif xs:
        parts.append(contract_last(w_ref[0:2].reshape(2 * hidden, width), joined(xs)))
    if ys:
        parts.append(contract_last(w_ref[2], joined(ys)))
    if len(outs) == 1:
        store_partials(parts, count, outs[0])
    else:
        for part, out_ref in zip(parts, outs):
            store_partials([part], count, out_ref)
    if tokened:
        refs[-1][...] = jnp.zeros_like(refs[-1])


def partials(weights, after, chunk, rows, count, tokened=1):
    hidden, width = weights.shape[1:]
    kinds = kinds_of(chunk)
    total = sum(rows) * hidden * count
    return pl.pallas_call(
        functools.partial(partial_kernel, kinds, count, tokened),
        in_specs=[whole(), unread()] + [whole()] * len(kinds),
        out_specs=[whole()] * (len(rows) + tokened),
        out_shape=[jax.ShapeDtypeStruct((k * hidden, count), jnp.bfloat16) for k in rows]
        + [jax.ShapeDtypeStruct((8, 128), jnp.float32)] * tokened,
        compiler_params=params(),
        cost_estimate=cost(2 * total * width, 6 * total),
    )(weights, after, *values_of(chunk))


def gate_row(gates):
    rows = []
    expert = expert_here()
    for held in gates:
        held = held.astype(jnp.float32)
        index = lax.broadcasted_iota(jnp.int32, held.shape, 0)
        rows.append(jnp.sum(jnp.where(index == expert, held, 0.0), 0, keepdims=True))
    return rows[0] if len(rows) == 1 else jnp.concatenate(rows, 1)


def summed(pairs):
    parts = []
    for own, *got in pairs:
        part = own[...].astype(jnp.float32)
        parts.append(part + got[0][...].astype(jnp.float32) if got else part)
    return parts[0] if len(parts) == 1 else jnp.concatenate(parts, 0)


def beside(total, hidden, firsts):
    parts = [total[first * hidden : (first + 1) * hidden] for first in firsts]
    return jnp.concatenate(parts, 1)


def activation(hg, hu, gate):
    sig = jax.nn.sigmoid(hg)
    silu = hg * sig
    return sig, silu, (gate * (silu * hu)).astype(jnp.bfloat16)


def hidden_slopes(hg, hu, sig, silu, dact):
    dhg = (dact * hu * sig * (1.0 + hg * (1.0 - sig))).astype(jnp.bfloat16)
    dhu = (dact * silu).astype(jnp.bfloat16)
    return dhg, dhu


def hidden_grads(gate, pairs):
    total = summed(pairs)
    blocks = gate.shape[1] // total.shape[1]
    hidden = total.shape[0] // (3 * blocks)
    hg = beside(total, hidden, range(0, 2 * blocks, 2))
    hu = beside(total, hidden, range(1, 2 * blocks, 2))
    dact = gate * beside(total, hidden, range(2 * blocks, 3 * blocks))
    sig, silu, act = activation(hg, hu, gate)
    return (*hidden_slopes(hg, hu, sig, silu, dact), act)


def plain(left, right):
    return lax.dot_general(
        left, right, (((1,), (0,)), ((), ())), preferred_element_type=jnp.float32
    )


def onward_kernel(kinds, after_ref, own, got, near_own, near_got, *refs):
    x0_ref, x1_ref, s0_ref, y0_ref, y1_ref = refs[:5]
    pair_ref, rest_ref, out_ref, first_ref, sum_ref, gate_ref = refs[5 + len(kinds) :]
    count, rows = x0_ref.shape[0], y0_ref.shape[0]
    gates = views(refs[5 : 5 + len(kinds)], kinds, count)[2]
    gate_ref[...] = jnp.broadcast_to(gate_row(gates), gate_ref.shape)
    pair_ref[0] = x0_ref[...]
    pair_ref[1] = s0_ref[...]
    rest_ref[0:count, :] = x1_ref[...]
    rest_ref[count : count + rows, :] = y0_ref[...]
    rest_ref[count + rows :, :] = y1_ref[...]
    out_ref[0:count, :] = x0_ref[...]
    out_ref[count:, :] = y0_ref[...]
    first_ref[...] = own[...].astype(jnp.float32) + got[...].astype(jnp.float32)
    sum_ref[...] = near_own[...].astype(jnp.float32) + near_got[...].astype(jnp.float32)


def pick_onward(after, pair, near_pair, near_x, other_x, near_y, chunk):
    count, width = other_x.shape
    rows = near_y[0].shape[0]
    operands = [*pair, *near_pair, *near_x, other_x, *near_y, *values_of(chunk)]
    return pl.pallas_call(
        functools.partial(onward_kernel, kinds_of(chunk)),
        in_specs=[unread()] + [whole()] * len(operands),
        out_specs=[whole()] * 6,
        out_shape=[
            jax.ShapeDtypeStruct((2, count, width), jnp.bfloat16),
            jax.ShapeDtypeStruct((count + 2 * rows, width), jnp.bfloat16),
            jax.ShapeDtypeStruct((count + rows, width), jnp.bfloat16),
            jax.ShapeDtypeStruct(pair[0].shape, jnp.float32),
            jax.ShapeDtypeStruct(near_pair[0].shape, jnp.float32),
            jax.ShapeDtypeStruct((8, 2 * count), jnp.float32),
        ],
        compiler_params=params(),
        cost_estimate=cost(1000, 8 * other_x.size),
    )(after, *operands)


def pass_kernel(after_ref, in_ref, *outs):
    row = 0
    for out_ref in outs:
        out_ref[...] = in_ref[row : row + out_ref.shape[0], :]
        row = row + out_ref.shape[0]


def passed_on(after, value, cuts):
    width = value.shape[1]
    return pl.pallas_call(
        pass_kernel,
        in_specs=[unread(), whole()],
        out_specs=[whole()] * len(cuts),
        out_shape=[jax.ShapeDtypeStruct((rows, width), value.dtype) for rows in cuts],
        compiler_params=params(),
        cost_estimate=cost(1000, 2 * value.size),
    )(after, value)


def first_kernel(kinds, count, gate_ref, after_ref, sum_ref, own, got, *refs):
    n = len(kinds)
    xs, ys, gates = views(refs[:n], kinds, count)
    out_ref, more_ref, token_ref = refs[n:]
    more_ref[...] = summed([(own, got)])
    lefts = hidden_grads(gate_ref[0:1, :], [(sum_ref,)])
    x = joined(xs)
    for m, right in enumerate((x, x, joined(ys))):
        out_ref[m] = plain(lefts[m], right)
    token_ref[...] = jnp.zeros_like(token_ref)


def first_grads(gate, after, total, pair, chunk, hidden, count):
    kinds = kinds_of(chunk)
    width = chunk[0][1].shape[-1]
    return pl.pallas_call(
        functools.partial(first_kernel, kinds, count),
        in_specs=[whole(), unread()] + [whole()] * (3 + len(kinds)),
        out_specs=[whole()] * 3,
        out_shape=[
            jax.ShapeDtypeStruct((3, hidden, width), jnp.float32),
            jax.ShapeDtypeStruct(pair[0].shape, jnp.float32),
            jax.ShapeDtypeStruct((8, 128), jnp.float32),
        ],
        compiler_params=params(),
        cost_estimate=cost(2 * total.size * width, 12 * hidden * width),
    )(gate, after, total, *pair, *values_of(chunk))


def grad_kernel(kinds, count, sum_ref, more_ref, own, got, *refs):
    n = len(kinds)
    xs, ys, gates = views(refs[:n], kinds, count)
    acc_ref, out_ref = refs[n:]
    lefts = hidden_grads(gate_row(gates), [(sum_ref,), (more_ref,), (own, got)])
    x = joined(xs)
    for m, right in enumerate((x, x, joined(ys))):
        out_ref[m] = acc_ref[m] + plain(lefts[m], right)


def add_grads(near_sum, more_sum, pair, chunk, acc, count):
    kinds = kinds_of(chunk)
    mats, hidden, width = acc.shape
    operands = [near_sum, more_sum, *pair, *values_of(chunk), acc]
    return pl.pallas_call(
        functools.partial(grad_kernel, kinds, count),
        in_specs=[whole()] * len(operands),
        out_specs=whole(),
        out_shape=jax.ShapeDtypeStruct(acc.shape, jnp.float32),
        input_output_aliases={len(operands) - 1: 0},
        compiler_params=params(),
        cost_estimate=cost(
            2 * mats * hidden * width * 4 * count, 8 * mats * hidden * width
        ),
    )(*operands)


def adam(grad, first, second):
    moment_one = beta_one * first.astype(jnp.float32) + (1.0 - beta_one) * grad
    moment_two = beta_two * second.astype(jnp.float32) + (1.0 - beta_two) * (grad * grad)
    root = (1.0 / (1.0 - beta_two**step_count)) ** 0.5
    below = moment_two * lax.rsqrt(moment_two) + epsilon / root
    scaled = moment_one * (1.0 / (1.0 - beta_one**step_count) / root)
    step = scaled * pl.reciprocal(below, approx=True)
    return [value.astype(jnp.bfloat16) for value in (moment_one, moment_two, step)]


def far_kernel(kinds, count, w_ref, after_ref, *refs):
    n = len(kinds)
    xs, ys, gates = views(refs[:n], kinds, count)
    outs = refs[n:]
    x, y = joined(xs), joined(ys)
    third = w_ref.shape[1] // len(outs)
    for m, right in enumerate((x, x, y)):
        part = contract_last(w_ref[m], right).astype(jnp.bfloat16)
        for k, out_ref in enumerate(outs):
            for side in (0, 1):
                row = (2 * m + side) * third
                out_ref[row : row + third, :] = part[
                    k * third : (k + 1) * third, side * count : (side + 1) * count
                ]


def far_partials(weights, after, chunk, pieces, count):
    mats, hidden, width = weights.shape
    kinds = kinds_of(chunk)
    rows = 2 * mats * hidden // pieces
    return pl.pallas_call(
        functools.partial(far_kernel, kinds, count),
        in_specs=[whole(), unread()] + [whole()] * len(kinds),
        out_specs=[whole()] * pieces,
        out_shape=[jax.ShapeDtypeStruct((rows, count), jnp.bfloat16)] * pieces,
        compiler_params=params(),
        cost_estimate=cost(4 * mats * hidden * count * width, 12 * mats * hidden * count),
    )(weights, after, *values_of(chunk))


def update_kernel(kinds, count, piece, last, own, got, *refs):
    n = len(kinds)
    acc_ref, first_ref, second_ref = refs[n : n + 3]
    rest = refs[n + 3 :]
    third = own.shape[0] // 6
    copies = []
    if piece > 0:
        done = rest[:3]
        rest = rest[3 + 3 * last :]
        outs, rest = rest[:3], rest[3:]
        sems = rest[-1]
        before = slice((piece - 1) * third, piece * third)
        for k in range(3):
            copies.append(
                pltpu.make_async_copy(done[k], outs[k].at[:, before, :], sems.at[3, k])
            )
            copies[-1].start()
    held = rest[:3]
    xs, ys, gates = views(refs[:n], kinds, count)
    total = summed([(own, got)])
    hg, hu, down = [beside(total, third, (2 * m, 2 * m + 1)) for m in range(3)]
    gate = gate_row(gates)
    sig, silu, act = activation(hg, hu, gate)
    lefts = (*hidden_slopes(hg, hu, sig, silu, gate * down), act)
    x = joined(xs)
    rows = slice(piece * third, (piece + 1) * third)
    for m, right in enumerate((x, x, joined(ys))):
        grad = acc_ref[m, rows, :] + plain(lefts[m], right)
        for k, value in enumerate(adam(grad, first_ref[m, rows, :], second_ref[m, rows, :])):
            held[k][m] = value
            if last:
                copies.append(
                    pltpu.make_async_copy(held[k].at[m], outs[k].at[m, rows, :], sems.at[m, k])
                )
                copies[-1].start()
    for copy in copies:
        copy.wait()


def update_piece(piece, last, pair, chunk, acc, moments, done, whole_outs, count):
    kinds = kinds_of(chunk)
    mats, hidden, width = acc.shape
    third = pair[0].shape[0] // 6
    operands = [*pair, *values_of(chunk), acc, *moments, *done]
    in_specs = [whole()] * len(operands) + [unread()] * len(whole_outs)
    large = [jax.ShapeDtypeStruct(acc.shape, jnp.bfloat16)] * 3
    small = [jax.ShapeDtypeStruct((mats, third, width), jnp.bfloat16)] * 3
    scratch = [pltpu.VMEM((mats, third, width), jnp.bfloat16)] * 3
    return pl.pallas_call(
        functools.partial(update_kernel, kinds, count, piece, last),
        in_specs=in_specs,
        out_specs=([in_hbm()] * 3 if piece else []) + ([] if last else [whole()] * 3),
        out_shape=(large if piece else []) + ([] if last else small),
        input_output_aliases={len(operands) + k: k for k in range(3)} if last else {},
        scratch_shapes=(scratch if last else [])
        + ([pltpu.SemaphoreType.DMA((mats + 1, 3))] if piece else []),
        compiler_params=params(),
        cost_estimate=cost(4 * mats * third * width * count, 14 * mats * third * width),
    )(*operands, *whole_outs)


def from_masked(value, axis, mask):
    pairs = [(source, source ^ mask) for source in range(lax.axis_size(axis))]
    return lax.ppermute(value, axis, pairs)


def dense_plan(tokens, cotangent, expert_ids, gate_probs, weights, first_moment, second_moment):
    n_data = lax.axis_size("dp")
    slices = min(4, lax.axis_size("expert") // 2)
    experts_total = lax.axis_size("expert") // (2 * slices) * n_data
    count = tokens.shape[0]
    hidden, width = weights.shape[1:]
    slots = -(-experts_total // 16) * 16
    other = lambda value: from_masked(value, "dp", 1)
    partner = lambda value: from_masked(value, "expert", 1)
    x_own, y_own, own, weights = pack_own(
        expert_ids, gate_probs, tokens, cotangent, weights, slots
    )
    first = [("xy", own), ("xy", other(own))]
    send, token = partials(weights, own, first, (6,), count)
    first_pair = (send, partner(send))
    along = [[(p, p ^ (2 if p % 2 == k else 4)) for p in range(n_data)] for k in (0, 1)]
    near_x = [lax.ppermute(x_own, "dp", pairs) for pairs in along]
    near_y = [lax.ppermute(y_own, "dp", pairs) for pairs in along]
    send, token = partials(weights, token, [("x", near_x[0]), ("", near_x[1])], (2,), count)
    near_pair = (send, partner(send))
    x_pair, rest, picked, first_sum, near_sum, gate = pick_onward(
        token, first_pair, near_pair, near_x, other(near_x[0]), near_y, first
    )
    far = lax.ppermute(picked, "dp", along[1])
    rest_other = other(rest)
    early = [("x of xyy", rest), ("second x", x_pair)]
    late = [("y, y of xyy", rest), ("x, y, y", rest_other)]
    send, token = partials(weights, picked, early, (4,), count)
    early_pair = (send, partner(send))
    send, token = partials(weights, token, late, (6,), count)
    late_pair = (send, partner(send))
    pieces = passed_on(token, far, (count // 2, count // 2, count // 2, count // 2 + slots))
    acc, early_sum, token = first_grads(
        gate, pieces[0], first_sum, early_pair, first, hidden, count
    )
    pieces = [*pieces, *[other(value) for value in pieces]]
    final = list(zip(("x", "x", "y", "half y, gates") * 2, pieces))
    sends = far_partials(weights, token, final, 3, count)
    pairs = [(send, partner(send)) for send in sends]
    near = [("first x", x_pair), ("x, y, y", rest), ("second x", x_pair), ("x, y, y", rest_other)]
    acc = add_grads(near_sum, early_sum, late_pair, near, acc, count)
    moments = (first_moment, second_moment)
    done = update_piece(0, False, pairs[0], final, acc, moments, (), (), count)
    outs = update_piece(1, False, pairs[1], final, acc, moments, done, (), count)
    outs = update_piece(2, True, pairs[2], final, acc, moments, outs[3:], outs[:3], count)
    return tuple(outs)


def per_device(tokens, cotangent, expert_ids, gate_probs, weights, first_moment, second_moment):
    n_expert = lax.axis_size("expert")
    n_data = lax.axis_size("dp")
    slices = min(4, n_expert // 2)
    experts_total = n_expert // (2 * slices) * n_data
    half = tokens.shape[0] // 2
    dense = 2 * half * expert_ids.shape[1] // experts_total >= half
    plan = dense_plan if dense and n_data == 8 else routed_plan
    return plan(
        tokens, cotangent, expert_ids, gate_probs, weights, first_moment, second_moment
    )


def solution(mesh):
    in_specs = (
        P("dp", None),
        P("dp", None),
        P("dp", None),
        P("dp", None),
        P(None, "dp", "expert"),
        P(None, "dp", "expert"),
        P(None, "dp", "expert"),
    )
    out_specs = (P(None, "dp", "expert"), P(None, "dp", "expert"), P(None, "dp", "expert"))
    return jax.shard_map(
        per_device, mesh=mesh, in_specs=in_specs, out_specs=out_specs, check_vma=False
    )
```

```python
import functools

import jax
import jax.numpy as jnp
from jax import lax
from jax.experimental import pallas as pl
from jax.experimental.pallas import tpu as pltpu
from jax.sharding import PartitionSpec as P

beta_one = 0.9
beta_two = 0.95
step_count = 10
epsilon = 1e-08


def from_partner(value, axis, distance):
    mask = 2**distance
    pairs = [(source, source ^ mask) for source in range(lax.axis_size(axis))]
    return lax.ppermute(value, axis, pairs)


def contract_last(left, right):
    return lax.dot_general(
        left, right, (((1,), (1,)), ((), ())), preferred_element_type=jnp.float32
    )


def contract_first(left, right):
    return lax.dot_general(
        left, right, (((0,), (0,)), ((), ())), preferred_element_type=jnp.float32
    )


def split_halves(grad, replica, width_half):
    keep = lax.dynamic_slice_in_dim(grad, replica * width_half, width_half, grad.ndim - 1)
    give = lax.dynamic_slice_in_dim(grad, (1 - replica) * width_half, width_half, grad.ndim - 1)
    return (keep, give)


def route_block(block_ids, block_gates, group, n_data, capacity):
    count = block_ids.shape[0]
    top = block_ids.shape[1]
    target = block_ids - group * n_data
    inside = block_ids // n_data == group
    onehot = (
        (target[:, :, None] == jnp.arange(n_data, dtype=jnp.int32)[None, None, :])
        & inside[:, :, None]
    ).astype(jnp.int32)
    per_token = jnp.sum(onehot, axis=1)
    earlier = jnp.cumsum(per_token, axis=0) - per_token
    rank = jnp.sum(onehot * earlier[:, None, :], axis=2)
    total_slots = n_data * capacity
    slot = jnp.where(inside, target * capacity + rank, total_slots).reshape(-1)
    token_of = jnp.broadcast_to(jnp.arange(count, dtype=jnp.int32)[:, None], (count, top)).reshape(
        -1
    )
    table = jnp.full((total_slots,), count, jnp.int32).at[slot].set(token_of, mode="drop")
    gate_slot = (
        jnp.zeros((total_slots,), jnp.bfloat16).at[slot].set(block_gates.reshape(-1), mode="drop")
    )
    return (table, gate_slot)


def routed_plan(tokens, cotangent, expert_ids, gate_probs, weights, first_moment, second_moment):
    n_expert = lax.axis_size("expert")
    n_data = lax.axis_size("dp")
    slices = min(4, n_expert // 2)
    place = lax.axis_index("expert")
    replica = place % 2
    group = place // (2 * slices)
    groups = n_expert // (2 * slices)
    experts_total = groups * n_data
    half = tokens.shape[0] // 2
    width_half = weights.shape[2]
    top = expert_ids.shape[1]
    capacity = max(2, 2 * half * top // experts_total)
    start = replica * half
    own_ids = lax.dynamic_slice_in_dim(expert_ids, start, half, 0)
    own_gates = lax.dynamic_slice_in_dim(gate_probs, start, half, 0)
    table, gate_slot = route_block(own_ids, own_gates, group, n_data, capacity)
    source_tokens = lax.dynamic_slice_in_dim(tokens, start, half, 0)
    source_cot = lax.dynamic_slice_in_dim(cotangent, start, half, 0)
    columns = source_tokens.shape[1]
    padded_tokens = jnp.concatenate([source_tokens, jnp.zeros((1, columns), jnp.bfloat16)], 0)
    padded_cot = jnp.concatenate([source_cot, jnp.zeros((1, columns), jnp.bfloat16)], 0)
    send_rows = padded_tokens[table].reshape(n_data, -1, columns)
    send_cot = padded_cot[table].reshape(n_data, -1, columns)
    send_gates = gate_slot.reshape(n_data, -1)
    rows_in, gates_in = (
        lax.all_to_all(send_rows, "dp", split_axis=0, concat_axis=0, tiled=True),
        lax.all_to_all(send_gates, "dp", split_axis=0, concat_axis=0, tiled=True),
    )
    rows = rows_in.reshape(-1, columns)
    gate_rows = gates_in.reshape(-1).astype(jnp.float32)
    partner = from_partner(weights, "expert", 0)
    lower = jnp.where(replica == 0, weights, partner)
    upper = jnp.where(replica == 0, partner, weights)
    full = jnp.concatenate([lower, upper], 2)
    hg = contract_last(rows, full[0])
    hu = contract_last(rows, full[1])
    sig = jax.nn.sigmoid(hg)
    act = (hg * sig * hu).astype(jnp.bfloat16)
    cot_in = lax.all_to_all(send_cot, "dp", split_axis=0, concat_axis=0, tiled=True)
    cots = cot_in.reshape(-1, columns)
    dz = (gate_rows[:, None] * cots.astype(jnp.float32)).astype(jnp.bfloat16)
    dact = contract_last(dz, full[2])
    grad_down = contract_first(act, dz)
    dhg = (dact * hu * sig * (1.0 + hg * (1.0 - sig))).astype(jnp.bfloat16)
    dhu = (dact * hg * sig).astype(jnp.bfloat16)
    grad_gate = contract_first(dhg, rows)
    grad_up = contract_first(dhu, rows)
    stacked = jnp.stack([grad_gate, grad_up, grad_down])
    keep, give = split_halves(stacked, replica, width_half)
    total = keep + from_partner(give, "expert", 0)
    moment_one = beta_one * first_moment.astype(jnp.float32) + (1.0 - beta_one) * total
    moment_two = beta_two * second_moment.astype(jnp.float32) + (1.0 - beta_two) * total * total
    step = (
        moment_one
        / (1.0 - beta_one**step_count)
        / (jnp.sqrt(moment_two / (1.0 - beta_two**step_count)) + epsilon)
    )
    return (
        moment_one.astype(jnp.bfloat16),
        moment_two.astype(jnp.bfloat16),
        step.astype(jnp.bfloat16),
    )


VMEM_LIMIT = 16 * 1024 * 1024


def params():
    return pltpu.CompilerParams(vmem_limit_bytes=VMEM_LIMIT)


def cost(flops, moved):
    return pl.CostEstimate(flops=flops, bytes_accessed=moved, transcendentals=0)


def whole():
    return pl.BlockSpec(memory_space=pltpu.VMEM)


def in_hbm():
    return pl.BlockSpec(memory_space=pltpu.HBM)


def unread():
    return pl.BlockSpec(memory_space=pl.ANY)


def expert_here():
    slices = min(4, lax.axis_size("expert") // 2)
    group = lax.axis_index("expert") // (2 * slices)
    return group * lax.axis_size("dp") + lax.axis_index("dp")


def keep_hbm(value):
    return pltpu.with_memory_space_constraint(value, pltpu.HBM)


def pack_kernel(
    ids_hbm,
    gates_hbm,
    tokens_ref,
    cot_ref,
    w_hbm,
    x_ref,
    y_ref,
    own_ref,
    w_ref,
    ids_ref,
    gates_ref,
    sems,
):
    count = tokens_ref.shape[0]
    width = x_ref.shape[1]
    columns = pl.ds(pl.multiple_of(lax.axis_index("expert") % 2 * width, width), width)
    copies = [
        pltpu.make_async_copy(ids_hbm, ids_ref, sems.at[0]),
        pltpu.make_async_copy(gates_hbm, gates_ref, sems.at[1]),
        pltpu.make_async_copy(tokens_ref.at[:, columns], x_ref, sems.at[2]),
        pltpu.make_async_copy(cot_ref.at[:, columns], y_ref.at[0:count, :], sems.at[3]),
        pltpu.make_async_copy(tokens_ref.at[:, columns], own_ref.at[0:count, :], sems.at[4]),
        pltpu.make_async_copy(cot_ref.at[:, columns], own_ref.at[count : 2 * count, :], sems.at[5]),
        pltpu.make_async_copy(w_hbm, w_ref, sems.at[6]),
    ]
    for copy in copies:
        copy.start()
    copies[0].wait()
    copies[1].wait()
    ids = ids_ref[...]
    gates = gates_ref[...].astype(jnp.float32)
    slots = y_ref.shape[0] - count
    row = lax.broadcasted_iota(jnp.int32, (slots, count), 0)
    gate = jnp.zeros((slots, count), jnp.float32)
    for k in range(ids.shape[0]):
        gate = gate + jnp.where(row == ids[k : k + 1, :], gates[k : k + 1, :], 0.0)
    y_ref[count:, 0:count] = gate.astype(jnp.bfloat16)
    y_ref[count:, count:] = jnp.zeros((slots, width - count), jnp.bfloat16)
    own_ref[2 * count :, :] = y_ref[count:, :]
    for copy in copies[2:]:
        copy.wait()


def pack_own(ids, gates, tokens, cotangent, weights, slots):
    count, top = ids.shape
    width = weights.shape[2]
    return pl.pallas_call(
        pack_kernel,
        in_specs=[in_hbm()] * 5,
        out_specs=[whole()] * 4,
        out_shape=[
            jax.ShapeDtypeStruct((rows, width), jnp.bfloat16)
            for rows in (count, count + slots, 2 * count + slots)
        ]
        + [jax.ShapeDtypeStruct(weights.shape, weights.dtype)],
        scratch_shapes=[
            pltpu.VMEM((top, count), ids.dtype),
            pltpu.VMEM((top, count), gates.dtype),
            pltpu.SemaphoreType.DMA((7,)),
        ],
        compiler_params=params(),
        cost_estimate=cost(1000, 8 * count * width),
    )(*[keep_hbm(value) for value in (ids.T, gates.T, tokens, cotangent, weights)])


def views(refs, kinds, count):
    xs, ys, gates = [], [], []
    for ref, kind in zip(refs, kinds):
        if kind in ("first x", "second x"):
            xs.append(ref[0 if kind == "first x" else 1])
            continue
        if kind == "x of xyy":
            xs.append(ref[0:count, :])
            continue
        if kind in ("x, y, y", "y, y of xyy"):
            rows = (ref.shape[0] - count) // 2
            if kind == "x, y, y":
                xs.append(ref[0:count, :])
            for row in (count, count + rows):
                ys.append(ref[row : row + count, :])
                gates.append(ref[row + count : row + rows, 0:count])
            continue
        for part in [ref.at[0], ref.at[1]] if ref.ndim == 3 else [ref]:
            if kind == "x":
                xs.append(part[...])
            if kind == "xy":
                xs.append(part[0:count, :])
                ys.append(part[count : 2 * count, :])
                gates.append(part[2 * count :, 0:count])
            if kind == "y":
                ys.append(part[...])
            if kind == "y, gates":
                ys.append(part[0:count, :])
                gates.append(part[count:, 0:count])
            if kind == "half y, gates":
                ys.append(part[0 : count // 2, :])
                gates.append(part[count // 2 :, 0:count])
    return xs, ys, gates


def joined(parts):
    return parts[0] if len(parts) == 1 else jnp.concatenate(parts, 0)


def kinds_of(chunk):
    return tuple(kind for kind, value in chunk)


def values_of(chunk):
    return [value for kind, value in chunk]


def store_partials(parts, count, out_ref):
    row = 0
    used = sum(part.size for part in parts) // count
    if used < out_ref.shape[0]:
        out_ref[used:, :] = jnp.zeros((out_ref.shape[0] - used, count), jnp.bfloat16)
    for part in parts:
        for first in range(0, part.shape[1], count):
            piece = part[:, first : first + count]
            out_ref[row : row + piece.shape[0], :] = piece.astype(jnp.bfloat16)
            row = row + piece.shape[0]


def partial_kernel(kinds, count, tokened, w_ref, after_ref, *refs):
    n = len(kinds)
    xs, ys, gates = views(refs[:n], kinds, count)
    outs = refs[n : len(refs) - tokened]
    mats, hidden, width = w_ref.shape
    parts = []
    if xs and len(outs) == mats:
        parts.extend(contract_last(w_ref[m], joined(xs)) for m in (0, 1))
    elif xs:
        parts.append(contract_last(w_ref[0:2].reshape(2 * hidden, width), joined(xs)))
    if ys:
        parts.append(contract_last(w_ref[2], joined(ys)))
    if len(outs) == 1:
        store_partials(parts, count, outs[0])
    else:
        for part, out_ref in zip(parts, outs):
            store_partials([part], count, out_ref)
    if tokened:
        refs[-1][...] = jnp.zeros_like(refs[-1])


def partials(weights, after, chunk, rows, count, tokened=1, spare=0):
    hidden, width = weights.shape[1:]
    kinds = kinds_of(chunk)
    total = sum(rows) * hidden * count
    return pl.pallas_call(
        functools.partial(partial_kernel, kinds, count, tokened),
        in_specs=[whole(), unread()] + [whole()] * len(kinds),
        out_specs=[whole()] * (len(rows) + tokened),
        out_shape=[jax.ShapeDtypeStruct((k * hidden + spare, count), jnp.bfloat16) for k in rows]
        + [jax.ShapeDtypeStruct((8, 128), jnp.float32)] * tokened,
        compiler_params=params(),
        cost_estimate=cost(2 * total * width, 6 * total),
    )(weights, after, *values_of(chunk))


def gate_row(gates):
    rows = []
    expert = expert_here()
    for held in gates:
        held = held.astype(jnp.float32)
        index = lax.broadcasted_iota(jnp.int32, held.shape, 0)
        rows.append(jnp.sum(jnp.where(index == expert, held, 0.0), 0, keepdims=True))
    return rows[0] if len(rows) == 1 else jnp.concatenate(rows, 1)


def summed(pairs):
    parts = []
    for own, *got in pairs:
        part = own[...].astype(jnp.float32)
        parts.append(part + got[0][...].astype(jnp.float32) if got else part)
    return parts[0] if len(parts) == 1 else jnp.concatenate(parts, 0)


def beside(total, hidden, firsts):
    parts = [total[first * hidden : (first + 1) * hidden] for first in firsts]
    return jnp.concatenate(parts, 1)


def activation(hg, hu, gate):
    sig = jax.nn.sigmoid(hg)
    silu = hg * sig
    return sig, silu, (gate * (silu * hu)).astype(jnp.bfloat16)


def hidden_slopes(hg, hu, sig, silu, dact):
    dhg = (dact * hu * sig * (1.0 + hg * (1.0 - sig))).astype(jnp.bfloat16)
    dhu = (dact * silu).astype(jnp.bfloat16)
    return dhg, dhu


def hidden_grads(gate, pairs):
    total = summed(pairs)
    blocks = gate.shape[1] // total.shape[1]
    hidden = total.shape[0] // (3 * blocks)
    hg = beside(total, hidden, range(0, 2 * blocks, 2))
    hu = beside(total, hidden, range(1, 2 * blocks, 2))
    dact = gate * beside(total, hidden, range(2 * blocks, 3 * blocks))
    sig, silu, act = activation(hg, hu, gate)
    return (*hidden_slopes(hg, hu, sig, silu, dact), act)


def plain(left, right):
    return lax.dot_general(
        left, right, (((1,), (0,)), ((), ())), preferred_element_type=jnp.float32
    )


def onward_kernel(kinds, after_ref, own, got, near_own, near_got, *refs):
    x0_ref, x1_ref, s0_ref, y0_ref, y1_ref = refs[:5]
    pair_ref, rest_ref, out_ref, first_ref, sum_ref, gate_ref = refs[5 + len(kinds) :]
    count, rows = x0_ref.shape[0], y0_ref.shape[0]
    gates = views(refs[5 : 5 + len(kinds)], kinds, count)[2]
    gate_ref[...] = jnp.broadcast_to(gate_row(gates), gate_ref.shape)
    pair_ref[0] = x0_ref[...]
    pair_ref[1] = s0_ref[...]
    rest_ref[0:count, :] = x1_ref[...]
    rest_ref[count : count + rows, :] = y0_ref[...]
    rest_ref[count + rows :, :] = y1_ref[...]
    out_ref[0:count, :] = x0_ref[...]
    out_ref[count:, :] = y0_ref[...]
    used = first_ref.shape[0]
    first_ref[...] = own[0:used, :].astype(jnp.float32) + got[0:used, :].astype(jnp.float32)
    sum_ref[...] = near_own[...].astype(jnp.float32) + near_got[...].astype(jnp.float32)


def pick_onward(after, pair, near_pair, near_x, other_x, near_y, chunk):
    count, width = other_x.shape
    rows = near_y[0].shape[0]
    operands = [*pair, *near_pair, *near_x, other_x, *near_y, *values_of(chunk)]
    return pl.pallas_call(
        functools.partial(onward_kernel, kinds_of(chunk)),
        in_specs=[unread()] + [whole()] * len(operands),
        out_specs=[whole()] * 6,
        out_shape=[
            jax.ShapeDtypeStruct((2, count, width), jnp.bfloat16),
            jax.ShapeDtypeStruct((count + 2 * rows, width), jnp.bfloat16),
            jax.ShapeDtypeStruct((count + rows, width), jnp.bfloat16),
            jax.ShapeDtypeStruct((3 * near_pair[0].shape[0], count), jnp.float32),
            jax.ShapeDtypeStruct(near_pair[0].shape, jnp.float32),
            jax.ShapeDtypeStruct((8, 2 * count), jnp.float32),
        ],
        compiler_params=params(),
        cost_estimate=cost(1000, 8 * other_x.size),
    )(after, *operands)


def pass_kernel(after_ref, in_ref, *outs):
    row = 0
    for out_ref in outs:
        out_ref[...] = in_ref[row : row + out_ref.shape[0], :]
        row = row + out_ref.shape[0]


def passed_on(after, value, cuts):
    width = value.shape[1]
    return pl.pallas_call(
        pass_kernel,
        in_specs=[unread(), whole()],
        out_specs=[whole()] * len(cuts),
        out_shape=[jax.ShapeDtypeStruct((rows, width), value.dtype) for rows in cuts],
        compiler_params=params(),
        cost_estimate=cost(1000, 2 * value.size),
    )(after, value)


def first_kernel(kinds, count, gate_ref, after_ref, sum_ref, own, got, *refs):
    n = len(kinds)
    xs, ys, gates = views(refs[:n], kinds, count)
    out_ref, more_ref, token_ref = refs[n:]
    more_ref[...] = summed([(own, got)])
    lefts = hidden_grads(gate_ref[0:1, :], [(sum_ref,)])
    x = joined(xs)
    for m, right in enumerate((x, x, joined(ys))):
        out_ref[m] = plain(lefts[m], right)
    token_ref[...] = jnp.zeros_like(token_ref)


def first_grads(gate, after, total, pair, chunk, hidden, count):
    kinds = kinds_of(chunk)
    width = chunk[0][1].shape[-1]
    return pl.pallas_call(
        functools.partial(first_kernel, kinds, count),
        in_specs=[whole(), unread()] + [whole()] * (3 + len(kinds)),
        out_specs=[whole()] * 3,
        out_shape=[
            jax.ShapeDtypeStruct((3, hidden, width), jnp.float32),
            jax.ShapeDtypeStruct(pair[0].shape, jnp.float32),
            jax.ShapeDtypeStruct((8, 128), jnp.float32),
        ],
        compiler_params=params(),
        cost_estimate=cost(2 * total.size * width, 12 * hidden * width),
    )(gate, after, total, *pair, *values_of(chunk))


def grad_kernel(kinds, count, sum_ref, more_ref, own, got, *refs):
    n = len(kinds)
    xs, ys, gates = views(refs[:n], kinds, count)
    acc_ref, out_ref = refs[n:]
    lefts = hidden_grads(gate_row(gates), [(sum_ref,), (more_ref,), (own, got)])
    x = joined(xs)
    for m, right in enumerate((x, x, joined(ys))):
        out_ref[m] = acc_ref[m] + plain(lefts[m], right)


def add_grads(near_sum, more_sum, pair, chunk, acc, count):
    kinds = kinds_of(chunk)
    mats, hidden, width = acc.shape
    operands = [near_sum, more_sum, *pair, *values_of(chunk), acc]
    return pl.pallas_call(
        functools.partial(grad_kernel, kinds, count),
        in_specs=[whole()] * len(operands),
        out_specs=whole(),
        out_shape=jax.ShapeDtypeStruct(acc.shape, jnp.float32),
        input_output_aliases={len(operands) - 1: 0},
        compiler_params=params(),
        cost_estimate=cost(
            2 * mats * hidden * width * 4 * count, 8 * mats * hidden * width
        ),
    )(*operands)


def adam(grad, first, second):
    moment_one = beta_one * first.astype(jnp.float32) + (1.0 - beta_one) * grad
    moment_two = beta_two * second.astype(jnp.float32) + (1.0 - beta_two) * (grad * grad)
    root = (1.0 / (1.0 - beta_two**step_count)) ** 0.5
    below = moment_two * lax.rsqrt(moment_two) + epsilon / root
    scaled = moment_one * (1.0 / (1.0 - beta_one**step_count) / root)
    step = scaled * pl.reciprocal(below, approx=True)
    return [value.astype(jnp.bfloat16) for value in (moment_one, moment_two, step)]


def far_kernel(kinds, count, w_ref, after_ref, *refs):
    n = len(kinds)
    xs, ys, gates = views(refs[:n], kinds, count)
    outs = refs[n:]
    x, y = joined(xs), joined(ys)
    third = w_ref.shape[1] // len(outs)
    for m, right in enumerate((x, x, y)):
        part = contract_last(w_ref[m], right).astype(jnp.bfloat16)
        for k, out_ref in enumerate(outs):
            for side in (0, 1):
                row = (2 * m + side) * third
                out_ref[row : row + third, :] = part[
                    k * third : (k + 1) * third, side * count : (side + 1) * count
                ]


def far_partials(weights, after, chunk, pieces, count):
    mats, hidden, width = weights.shape
    kinds = kinds_of(chunk)
    rows = 2 * mats * hidden // pieces
    return pl.pallas_call(
        functools.partial(far_kernel, kinds, count),
        in_specs=[whole(), unread()] + [whole()] * len(kinds),
        out_specs=[whole()] * pieces,
        out_shape=[jax.ShapeDtypeStruct((rows, count), jnp.bfloat16)] * pieces,
        compiler_params=params(),
        cost_estimate=cost(4 * mats * hidden * count * width, 12 * mats * hidden * count),
    )(weights, after, *values_of(chunk))


def update_kernel(kinds, count, piece, last, own, got, *refs):
    n = len(kinds)
    acc_ref, first_ref, second_ref = refs[n : n + 3]
    rest = refs[n + 3 :]
    third = own.shape[0] // 6
    copies = []
    if piece > 0:
        done = rest[:3]
        rest = rest[3 + 3 * last :]
        outs, rest = rest[:3], rest[3:]
        sems = rest[-1]
        before = slice((piece - 1) * third, piece * third)
        for k in range(3):
            copies.append(
                pltpu.make_async_copy(done[k], outs[k].at[:, before, :], sems.at[3, k])
            )
            copies[-1].start()
    held = rest[:3]
    xs, ys, gates = views(refs[:n], kinds, count)
    total = summed([(own, got)])
    hg, hu, down = [beside(total, third, (2 * m, 2 * m + 1)) for m in range(3)]
    gate = gate_row(gates)
    sig, silu, act = activation(hg, hu, gate)
    lefts = (*hidden_slopes(hg, hu, sig, silu, gate * down), act)
    x = joined(xs)
    rows = slice(piece * third, (piece + 1) * third)
    for m, right in enumerate((x, x, joined(ys))):
        grad = acc_ref[m, rows, :] + plain(lefts[m], right)
        for k, value in enumerate(adam(grad, first_ref[m, rows, :], second_ref[m, rows, :])):
            held[k][m] = value
            if last:
                copies.append(
                    pltpu.make_async_copy(held[k].at[m], outs[k].at[m, rows, :], sems.at[m, k])
                )
                copies[-1].start()
    for copy in copies:
        copy.wait()


def update_piece(piece, last, pair, chunk, acc, moments, done, whole_outs, count):
    kinds = kinds_of(chunk)
    mats, hidden, width = acc.shape
    third = pair[0].shape[0] // 6
    operands = [*pair, *values_of(chunk), acc, *moments, *done]
    in_specs = [whole()] * len(operands) + [unread()] * len(whole_outs)
    large = [jax.ShapeDtypeStruct(acc.shape, jnp.bfloat16)] * 3
    small = [jax.ShapeDtypeStruct((mats, third, width), jnp.bfloat16)] * 3
    scratch = [pltpu.VMEM((mats, third, width), jnp.bfloat16)] * 3
    return pl.pallas_call(
        functools.partial(update_kernel, kinds, count, piece, last),
        in_specs=in_specs,
        out_specs=([in_hbm()] * 3 if piece else []) + ([] if last else [whole()] * 3),
        out_shape=(large if piece else []) + ([] if last else small),
        input_output_aliases={len(operands) + k: k for k in range(3)} if last else {},
        scratch_shapes=(scratch if last else [])
        + ([pltpu.SemaphoreType.DMA((mats + 1, 3))] if piece else []),
        compiler_params=params(),
        cost_estimate=cost(4 * mats * third * width * count, 14 * mats * third * width),
    )(*operands, *whole_outs)


def from_masked(value, axis, mask):
    pairs = [(source, source ^ mask) for source in range(lax.axis_size(axis))]
    return lax.ppermute(value, axis, pairs)


def dense_plan(tokens, cotangent, expert_ids, gate_probs, weights, first_moment, second_moment):
    n_data = lax.axis_size("dp")
    slices = min(4, lax.axis_size("expert") // 2)
    experts_total = lax.axis_size("expert") // (2 * slices) * n_data
    count = tokens.shape[0]
    hidden, width = weights.shape[1:]
    slots = -(-experts_total // 16) * 16
    other = lambda value: from_masked(value, "dp", 1)
    partner = lambda value: from_masked(value, "expert", 1)
    x_own, y_own, own, weights = pack_own(
        expert_ids, gate_probs, tokens, cotangent, weights, slots
    )
    first = [("xy", own), ("xy", other(own))]
    send, token = partials(weights, own, first, (6,), count, 1, 16)
    first_pair = (send, partner(send))
    along = [[(p, p ^ (2 if p % 2 == k else 4)) for p in range(n_data)] for k in (0, 1)]
    near_x = [lax.ppermute(x_own, "dp", pairs) for pairs in along]
    near_y = [lax.ppermute(y_own, "dp", pairs) for pairs in along]
    send, token = partials(weights, token, [("x", near_x[0]), ("", near_x[1])], (2,), count)
    near_pair = (send, partner(send))
    x_pair, rest, picked, first_sum, near_sum, gate = pick_onward(
        token, first_pair, near_pair, near_x, other(near_x[0]), near_y, first
    )
    far = lax.ppermute(picked, "dp", along[1])
    rest_other = other(rest)
    early = [("x of xyy", rest), ("second x", x_pair)]
    late = [("y, y of xyy", rest), ("x, y, y", rest_other)]
    send, token = partials(weights, picked, early, (4,), count)
    early_pair = (send, partner(send))
    send, token = partials(weights, token, late, (6,), count)
    late_pair = (send, partner(send))
    pieces = passed_on(token, far, (count // 2, count // 2, count // 2, count // 2 + slots))
    acc, early_sum, token = first_grads(
        gate, pieces[0], first_sum, early_pair, first, hidden, count
    )
    pieces = [*pieces, *[other(value) for value in pieces]]
    final = list(zip(("x", "x", "y", "half y, gates") * 2, pieces))
    sends = far_partials(weights, token, final, 3, count)
    pairs = [(send, partner(send)) for send in sends]
    near = [("first x", x_pair), ("x, y, y", rest), ("second x", x_pair), ("x, y, y", rest_other)]
    acc = add_grads(near_sum, early_sum, late_pair, near, acc, count)
    moments = (first_moment, second_moment)
    done = update_piece(0, False, pairs[0], final, acc, moments, (), (), count)
    outs = update_piece(1, False, pairs[1], final, acc, moments, done, (), count)
    outs = update_piece(2, True, pairs[2], final, acc, moments, outs[3:], outs[:3], count)
    return tuple(outs)


def per_device(tokens, cotangent, expert_ids, gate_probs, weights, first_moment, second_moment):
    n_expert = lax.axis_size("expert")
    n_data = lax.axis_size("dp")
    slices = min(4, n_expert // 2)
    experts_total = n_expert // (2 * slices) * n_data
    half = tokens.shape[0] // 2
    dense = 2 * half * expert_ids.shape[1] // experts_total >= half
    plan = dense_plan if dense and n_data == 8 else routed_plan
    return plan(
        tokens, cotangent, expert_ids, gate_probs, weights, first_moment, second_moment
    )


def solution(mesh):
    in_specs = (
        P("dp", None),
        P("dp", None),
        P("dp", None),
        P("dp", None),
        P(None, "dp", "expert"),
        P(None, "dp", "expert"),
        P(None, "dp", "expert"),
    )
    out_specs = (P(None, "dp", "expert"), P(None, "dp", "expert"), P(None, "dp", "expert"))
    return jax.shard_map(
        per_device, mesh=mesh, in_specs=in_specs, out_specs=out_specs, check_vma=False
    )
```

```python
import functools

import jax
import jax.numpy as jnp
from jax import lax
from jax.experimental import pallas as pl
from jax.experimental.pallas import tpu as pltpu
from jax.sharding import PartitionSpec as P

beta_one = 0.9
beta_two = 0.95
step_count = 10
epsilon = 1e-08


def from_partner(value, axis, distance):
    mask = 2**distance
    pairs = [(source, source ^ mask) for source in range(lax.axis_size(axis))]
    return lax.ppermute(value, axis, pairs)


def contract_last(left, right):
    return lax.dot_general(
        left, right, (((1,), (1,)), ((), ())), preferred_element_type=jnp.float32
    )


def contract_first(left, right):
    return lax.dot_general(
        left, right, (((0,), (0,)), ((), ())), preferred_element_type=jnp.float32
    )


def split_halves(grad, replica, width_half):
    keep = lax.dynamic_slice_in_dim(grad, replica * width_half, width_half, grad.ndim - 1)
    give = lax.dynamic_slice_in_dim(grad, (1 - replica) * width_half, width_half, grad.ndim - 1)
    return (keep, give)


def route_block(block_ids, block_gates, group, n_data, capacity):
    count = block_ids.shape[0]
    top = block_ids.shape[1]
    target = block_ids - group * n_data
    inside = block_ids // n_data == group
    onehot = (
        (target[:, :, None] == jnp.arange(n_data, dtype=jnp.int32)[None, None, :])
        & inside[:, :, None]
    ).astype(jnp.int32)
    per_token = jnp.sum(onehot, axis=1)
    earlier = jnp.cumsum(per_token, axis=0) - per_token
    rank = jnp.sum(onehot * earlier[:, None, :], axis=2)
    total_slots = n_data * capacity
    slot = jnp.where(inside, target * capacity + rank, total_slots).reshape(-1)
    token_of = jnp.broadcast_to(jnp.arange(count, dtype=jnp.int32)[:, None], (count, top)).reshape(
        -1
    )
    table = jnp.full((total_slots,), count, jnp.int32).at[slot].set(token_of, mode="drop")
    gate_slot = (
        jnp.zeros((total_slots,), jnp.bfloat16).at[slot].set(block_gates.reshape(-1), mode="drop")
    )
    return (table, gate_slot)


def routed_plan(tokens, cotangent, expert_ids, gate_probs, weights, first_moment, second_moment):
    n_expert = lax.axis_size("expert")
    n_data = lax.axis_size("dp")
    slices = min(4, n_expert // 2)
    place = lax.axis_index("expert")
    replica = place % 2
    group = place // (2 * slices)
    groups = n_expert // (2 * slices)
    experts_total = groups * n_data
    half = tokens.shape[0] // 2
    width_half = weights.shape[2]
    top = expert_ids.shape[1]
    capacity = max(2, 2 * half * top // experts_total)
    start = replica * half
    own_ids = lax.dynamic_slice_in_dim(expert_ids, start, half, 0)
    own_gates = lax.dynamic_slice_in_dim(gate_probs, start, half, 0)
    table, gate_slot = route_block(own_ids, own_gates, group, n_data, capacity)
    source_tokens = lax.dynamic_slice_in_dim(tokens, start, half, 0)
    source_cot = lax.dynamic_slice_in_dim(cotangent, start, half, 0)
    columns = source_tokens.shape[1]
    padded_tokens = jnp.concatenate([source_tokens, jnp.zeros((1, columns), jnp.bfloat16)], 0)
    padded_cot = jnp.concatenate([source_cot, jnp.zeros((1, columns), jnp.bfloat16)], 0)
    send_rows = padded_tokens[table].reshape(n_data, -1, columns)
    send_cot = padded_cot[table].reshape(n_data, -1, columns)
    send_gates = gate_slot.reshape(n_data, -1)
    rows_in, gates_in = (
        lax.all_to_all(send_rows, "dp", split_axis=0, concat_axis=0, tiled=True),
        lax.all_to_all(send_gates, "dp", split_axis=0, concat_axis=0, tiled=True),
    )
    rows = rows_in.reshape(-1, columns)
    gate_rows = gates_in.reshape(-1).astype(jnp.float32)
    partner = from_partner(weights, "expert", 0)
    lower = jnp.where(replica == 0, weights, partner)
    upper = jnp.where(replica == 0, partner, weights)
    full = jnp.concatenate([lower, upper], 2)
    hg = contract_last(rows, full[0])
    hu = contract_last(rows, full[1])
    sig = jax.nn.sigmoid(hg)
    act = (hg * sig * hu).astype(jnp.bfloat16)
    cot_in = lax.all_to_all(send_cot, "dp", split_axis=0, concat_axis=0, tiled=True)
    cots = cot_in.reshape(-1, columns)
    dz = (gate_rows[:, None] * cots.astype(jnp.float32)).astype(jnp.bfloat16)
    dact = contract_last(dz, full[2])
    grad_down = contract_first(act, dz)
    dhg = (dact * hu * sig * (1.0 + hg * (1.0 - sig))).astype(jnp.bfloat16)
    dhu = (dact * hg * sig).astype(jnp.bfloat16)
    grad_gate = contract_first(dhg, rows)
    grad_up = contract_first(dhu, rows)
    stacked = jnp.stack([grad_gate, grad_up, grad_down])
    keep, give = split_halves(stacked, replica, width_half)
    total = keep + from_partner(give, "expert", 0)
    moment_one = beta_one * first_moment.astype(jnp.float32) + (1.0 - beta_one) * total
    moment_two = beta_two * second_moment.astype(jnp.float32) + (1.0 - beta_two) * total * total
    step = (
        moment_one
        / (1.0 - beta_one**step_count)
        / (jnp.sqrt(moment_two / (1.0 - beta_two**step_count)) + epsilon)
    )
    return (
        moment_one.astype(jnp.bfloat16),
        moment_two.astype(jnp.bfloat16),
        step.astype(jnp.bfloat16),
    )


VMEM_LIMIT = 16 * 1024 * 1024


def params():
    return pltpu.CompilerParams(vmem_limit_bytes=VMEM_LIMIT)


def cost(flops, moved):
    return pl.CostEstimate(flops=flops, bytes_accessed=moved, transcendentals=0)


def whole():
    return pl.BlockSpec(memory_space=pltpu.VMEM)


def in_hbm():
    return pl.BlockSpec(memory_space=pltpu.HBM)


def unread():
    return pl.BlockSpec(memory_space=pl.ANY)


def expert_here():
    slices = min(4, lax.axis_size("expert") // 2)
    group = lax.axis_index("expert") // (2 * slices)
    return group * lax.axis_size("dp") + lax.axis_index("dp")


def keep_hbm(value):
    return pltpu.with_memory_space_constraint(value, pltpu.HBM)


def pack_kernel(
    ids_hbm,
    gates_hbm,
    tokens_ref,
    cot_ref,
    w_hbm,
    x_ref,
    y_ref,
    own_ref,
    w_ref,
    ids_ref,
    gates_ref,
    sems,
):
    count = tokens_ref.shape[0]
    width = x_ref.shape[1]
    columns = pl.ds(pl.multiple_of(lax.axis_index("expert") % 2 * width, width), width)
    copies = [
        pltpu.make_async_copy(ids_hbm, ids_ref, sems.at[0]),
        pltpu.make_async_copy(gates_hbm, gates_ref, sems.at[1]),
        pltpu.make_async_copy(tokens_ref.at[:, columns], x_ref, sems.at[2]),
        pltpu.make_async_copy(cot_ref.at[:, columns], y_ref.at[0:count, :], sems.at[3]),
        pltpu.make_async_copy(tokens_ref.at[:, columns], own_ref.at[0:count, :], sems.at[4]),
        pltpu.make_async_copy(cot_ref.at[:, columns], own_ref.at[count : 2 * count, :], sems.at[5]),
        pltpu.make_async_copy(w_hbm, w_ref, sems.at[6]),
    ]
    for copy in copies:
        copy.start()
    copies[0].wait()
    copies[1].wait()
    ids = ids_ref[...]
    gates = gates_ref[...].astype(jnp.float32)
    slots = y_ref.shape[0] - count
    row = lax.broadcasted_iota(jnp.int32, (slots, count), 0)
    gate = jnp.zeros((slots, count), jnp.float32)
    for k in range(ids.shape[0]):
        gate = gate + jnp.where(row == ids[k : k + 1, :], gates[k : k + 1, :], 0.0)
    y_ref[count:, 0:count] = gate.astype(jnp.bfloat16)
    y_ref[count:, count:] = jnp.zeros((slots, width - count), jnp.bfloat16)
    own_ref[2 * count :, :] = y_ref[count:, :]
    for copy in copies[2:]:
        copy.wait()


def pack_own(ids, gates, tokens, cotangent, weights, slots):
    count, top = ids.shape
    width = weights.shape[2]
    return pl.pallas_call(
        pack_kernel,
        in_specs=[in_hbm()] * 5,
        out_specs=[whole()] * 4,
        out_shape=[
            jax.ShapeDtypeStruct((rows, width), jnp.bfloat16)
            for rows in (count, count + slots, 2 * count + slots)
        ]
        + [jax.ShapeDtypeStruct(weights.shape, weights.dtype)],
        scratch_shapes=[
            pltpu.VMEM((top, count), ids.dtype),
            pltpu.VMEM((top, count), gates.dtype),
            pltpu.SemaphoreType.DMA((7,)),
        ],
        compiler_params=params(),
        cost_estimate=cost(1000, 8 * count * width),
    )(*[keep_hbm(value) for value in (ids.T, gates.T, tokens, cotangent, weights)])


def views(refs, kinds, count):
    xs, ys, gates = [], [], []
    for ref, kind in zip(refs, kinds):
        if kind in ("first x", "second x"):
            xs.append(ref[0 if kind == "first x" else 1])
            continue
        if kind == "x of xyy":
            xs.append(ref[0:count, :])
            continue
        if kind in ("x, y, y", "y, y of xyy"):
            rows = (ref.shape[0] - count) // 2
            if kind == "x, y, y":
                xs.append(ref[0:count, :])
            for row in (count, count + rows):
                ys.append(ref[row : row + count, :])
                gates.append(ref[row + count : row + rows, 0:count])
            continue
        for part in [ref.at[0], ref.at[1]] if ref.ndim == 3 else [ref]:
            if kind == "x":
                xs.append(part[...])
            if kind == "xy":
                xs.append(part[0:count, :])
                ys.append(part[count : 2 * count, :])
                gates.append(part[2 * count :, 0:count])
            if kind == "y":
                ys.append(part[...])
            if kind == "y, gates":
                ys.append(part[0:count, :])
                gates.append(part[count:, 0:count])
            if kind == "half y, gates":
                ys.append(part[0 : count // 2, :])
                gates.append(part[count // 2 :, 0:count])
    return xs, ys, gates


def joined(parts):
    return parts[0] if len(parts) == 1 else jnp.concatenate(parts, 0)


def kinds_of(chunk):
    return tuple(kind for kind, value in chunk)


def values_of(chunk):
    return [value for kind, value in chunk]


def store_partials(parts, count, out_ref):
    row = 0
    used = sum(part.size for part in parts) // count
    if used < out_ref.shape[0]:
        out_ref[used:, :] = jnp.zeros((out_ref.shape[0] - used, count), jnp.bfloat16)
    for part in parts:
        for first in range(0, part.shape[1], count):
            piece = part[:, first : first + count]
            out_ref[row : row + piece.shape[0], :] = piece.astype(jnp.bfloat16)
            row = row + piece.shape[0]


def partial_kernel(kinds, count, tokened, w_ref, after_ref, *refs):
    n = len(kinds)
    xs, ys, gates = views(refs[:n], kinds, count)
    outs = refs[n : len(refs) - tokened]
    mats, hidden, width = w_ref.shape
    parts = []
    if xs and len(outs) == mats:
        parts.extend(contract_last(w_ref[m], joined(xs)) for m in (0, 1))
    elif xs:
        parts.append(contract_last(w_ref[0:2].reshape(2 * hidden, width), joined(xs)))
    if ys:
        parts.append(contract_last(w_ref[2], joined(ys)))
    if len(outs) == 1:
        store_partials(parts, count, outs[0])
    else:
        for part, out_ref in zip(parts, outs):
            store_partials([part], count, out_ref)
    if tokened:
        refs[-1][...] = jnp.zeros_like(refs[-1])


def partials(weights, after, chunk, rows, count, tokened=1, spare=0):
    hidden, width = weights.shape[1:]
    kinds = kinds_of(chunk)
    total = sum(rows) * hidden * count
    return pl.pallas_call(
        functools.partial(partial_kernel, kinds, count, tokened),
        in_specs=[whole(), unread()] + [whole()] * len(kinds),
        out_specs=[whole()] * (len(rows) + tokened),
        out_shape=[jax.ShapeDtypeStruct((k * hidden + spare, count), jnp.bfloat16) for k in rows]
        + [jax.ShapeDtypeStruct((8, 128), jnp.float32)] * tokened,
        compiler_params=params(),
        cost_estimate=cost(2 * total * width, 6 * total),
    )(weights, after, *values_of(chunk))


def gate_row(gates):
    rows = []
    expert = expert_here()
    for held in gates:
        held = held.astype(jnp.float32)
        index = lax.broadcasted_iota(jnp.int32, held.shape, 0)
        rows.append(jnp.sum(jnp.where(index == expert, held, 0.0), 0, keepdims=True))
    return rows[0] if len(rows) == 1 else jnp.concatenate(rows, 1)


def summed(pairs):
    parts = []
    for own, *got in pairs:
        part = own[...].astype(jnp.float32)
        parts.append(part + got[0][...].astype(jnp.float32) if got else part)
    return parts[0] if len(parts) == 1 else jnp.concatenate(parts, 0)


def beside(total, hidden, firsts):
    parts = [total[first * hidden : (first + 1) * hidden] for first in firsts]
    return jnp.concatenate(parts, 1)


def activation(hg, hu, gate):
    sig = jax.nn.sigmoid(hg)
    silu = hg * sig
    return sig, silu, (gate * (silu * hu)).astype(jnp.bfloat16)


def hidden_slopes(hg, hu, sig, silu, dact):
    dhg = (dact * hu * sig * (1.0 + hg * (1.0 - sig))).astype(jnp.bfloat16)
    dhu = (dact * silu).astype(jnp.bfloat16)
    return dhg, dhu


def hidden_grads(gate, pairs):
    total = summed(pairs)
    blocks = gate.shape[1] // total.shape[1]
    hidden = total.shape[0] // (3 * blocks)
    hg = beside(total, hidden, range(0, 2 * blocks, 2))
    hu = beside(total, hidden, range(1, 2 * blocks, 2))
    dact = gate * beside(total, hidden, range(2 * blocks, 3 * blocks))
    sig, silu, act = activation(hg, hu, gate)
    return (*hidden_slopes(hg, hu, sig, silu, dact), act)


def plain(left, right):
    return lax.dot_general(
        left, right, (((1,), (0,)), ((), ())), preferred_element_type=jnp.float32
    )


def onward_kernel(kinds, after_ref, own, got, near_own, near_got, *refs):
    x0_ref, x1_ref, s0_ref, s1_ref, y0_ref, y1_ref = refs[:6]
    pair_ref, rest_ref, out_ref, first_ref, sum_ref, gate_ref = refs[7 + len(kinds) :]
    count, rows = x0_ref.shape[0], y0_ref.shape[0]
    gates = views(refs[6 : 6 + len(kinds)], kinds, count)[2]
    gate_ref[...] = jnp.broadcast_to(gate_row(gates), gate_ref.shape)
    pair_ref[0] = x0_ref[...]
    pair_ref[1, 0 : count // 2, :] = s0_ref[...]
    pair_ref[1, count // 2 :, :] = s1_ref[...]
    rest_ref[0:count, :] = x1_ref[...]
    rest_ref[count : count + rows, :] = y0_ref[...]
    rest_ref[count + rows :, :] = y1_ref[...]
    out_ref[0:count, :] = x0_ref[...]
    out_ref[count:, :] = y0_ref[...]
    used = first_ref.shape[0]
    first_ref[...] = own[0:used, :].astype(jnp.float32) + got[0:used, :].astype(jnp.float32)
    sum_ref[...] = near_own[...].astype(jnp.float32) + near_got[...].astype(jnp.float32)


def pick_onward(after, pair, near_pair, near_x, other_x, near_y, chunk, held):
    count, width = near_x[0].shape
    rows = near_y[0].shape[0]
    operands = [*pair, *near_pair, *near_x, *other_x, *near_y, *values_of(chunk), held]
    return pl.pallas_call(
        functools.partial(onward_kernel, kinds_of(chunk)),
        in_specs=[unread()] + [whole()] * len(operands),
        out_specs=[whole()] * 6,
        out_shape=[
            jax.ShapeDtypeStruct((2, count, width), jnp.bfloat16),
            jax.ShapeDtypeStruct((count + 2 * rows, width), jnp.bfloat16),
            jax.ShapeDtypeStruct((count + rows, width), jnp.bfloat16),
            jax.ShapeDtypeStruct((3 * near_pair[0].shape[0], count), jnp.float32),
            jax.ShapeDtypeStruct(near_pair[0].shape, jnp.float32),
            jax.ShapeDtypeStruct((8, 2 * count), jnp.float32),
        ],
        compiler_params=params(),
        cost_estimate=cost(1000, 8 * near_x[0].size),
    )(after, *operands)


def pass_kernel(after_ref, in_ref, *outs):
    row = 0
    for out_ref in outs:
        out_ref[...] = in_ref[row : row + out_ref.shape[0], :]
        row = row + out_ref.shape[0]


def passed_on(after, value, cuts):
    width = value.shape[1]
    return pl.pallas_call(
        pass_kernel,
        in_specs=[unread(), whole()],
        out_specs=[whole()] * len(cuts),
        out_shape=[jax.ShapeDtypeStruct((rows, width), value.dtype) for rows in cuts],
        compiler_params=params(),
        cost_estimate=cost(1000, 2 * value.size),
    )(after, value)


def first_kernel(kinds, count, gate_ref, after_ref, sum_ref, own, got, *refs):
    n = len(kinds)
    xs, ys, gates = views(refs[:n], kinds, count)
    out_ref, more_ref, token_ref = refs[n:]
    more_ref[...] = summed([(own, got)])
    lefts = hidden_grads(gate_ref[0:1, :], [(sum_ref,)])
    x = joined(xs)
    for m, right in enumerate((x, x, joined(ys))):
        out_ref[m] = plain(lefts[m], right)
    token_ref[...] = jnp.zeros_like(token_ref)


def first_grads(gate, after, total, pair, chunk, hidden, count):
    kinds = kinds_of(chunk)
    width = chunk[0][1].shape[-1]
    return pl.pallas_call(
        functools.partial(first_kernel, kinds, count),
        in_specs=[whole(), unread()] + [whole()] * (3 + len(kinds)),
        out_specs=[whole()] * 3,
        out_shape=[
            jax.ShapeDtypeStruct((3, hidden, width), jnp.float32),
            jax.ShapeDtypeStruct(pair[0].shape, jnp.float32),
            jax.ShapeDtypeStruct((8, 128), jnp.float32),
        ],
        compiler_params=params(),
        cost_estimate=cost(2 * total.size * width, 12 * hidden * width),
    )(gate, after, total, *pair, *values_of(chunk))


def grad_kernel(kinds, count, sum_ref, more_ref, own, got, *refs):
    n = len(kinds)
    xs, ys, gates = views(refs[:n], kinds, count)
    acc_ref, out_ref = refs[n:]
    lefts = hidden_grads(gate_row(gates), [(sum_ref,), (more_ref,), (own, got)])
    x = joined(xs)
    for m, right in enumerate((x, x, joined(ys))):
        out_ref[m] = acc_ref[m] + plain(lefts[m], right)


def add_grads(near_sum, more_sum, pair, chunk, acc, count):
    kinds = kinds_of(chunk)
    mats, hidden, width = acc.shape
    operands = [near_sum, more_sum, *pair, *values_of(chunk), acc]
    return pl.pallas_call(
        functools.partial(grad_kernel, kinds, count),
        in_specs=[whole()] * len(operands),
        out_specs=whole(),
        out_shape=jax.ShapeDtypeStruct(acc.shape, jnp.float32),
        input_output_aliases={len(operands) - 1: 0},
        compiler_params=params(),
        cost_estimate=cost(
            2 * mats * hidden * width * 4 * count, 8 * mats * hidden * width
        ),
    )(*operands)


def adam(grad, first, second):
    moment_one = beta_one * first.astype(jnp.float32) + (1.0 - beta_one) * grad
    moment_two = beta_two * second.astype(jnp.float32) + (1.0 - beta_two) * (grad * grad)
    root = (1.0 / (1.0 - beta_two**step_count)) ** 0.5
    below = moment_two * lax.rsqrt(moment_two) + epsilon / root
    scaled = moment_one * (1.0 / (1.0 - beta_one**step_count) / root)
    step = scaled * pl.reciprocal(below, approx=True)
    return [value.astype(jnp.bfloat16) for value in (moment_one, moment_two, step)]


def far_kernel(kinds, count, w_ref, after_ref, *refs):
    n = len(kinds)
    xs, ys, gates = views(refs[:n], kinds, count)
    outs = refs[n:]
    x, y = joined(xs), joined(ys)
    third = w_ref.shape[1] // len(outs)
    for m, right in enumerate((x, x, y)):
        part = contract_last(w_ref[m], right).astype(jnp.bfloat16)
        for k, out_ref in enumerate(outs):
            for side in (0, 1):
                row = (2 * m + side) * third
                out_ref[row : row + third, :] = part[
                    k * third : (k + 1) * third, side * count : (side + 1) * count
                ]


def far_partials(weights, after, chunk, pieces, count):
    mats, hidden, width = weights.shape
    kinds = kinds_of(chunk)
    rows = 2 * mats * hidden // pieces
    return pl.pallas_call(
        functools.partial(far_kernel, kinds, count),
        in_specs=[whole(), unread()] + [whole()] * len(kinds),
        out_specs=[whole()] * pieces,
        out_shape=[jax.ShapeDtypeStruct((rows, count), jnp.bfloat16)] * pieces,
        compiler_params=params(),
        cost_estimate=cost(4 * mats * hidden * count * width, 12 * mats * hidden * count),
    )(weights, after, *values_of(chunk))


def update_kernel(kinds, count, piece, last, own, got, *refs):
    n = len(kinds)
    acc_ref, first_ref, second_ref = refs[n : n + 3]
    rest = refs[n + 3 :]
    third = own.shape[0] // 6
    copies = []
    if piece > 0:
        done = rest[:3]
        rest = rest[3 + 3 * last :]
        outs, rest = rest[:3], rest[3:]
        sems = rest[-1]
        before = slice((piece - 1) * third, piece * third)
        for k in range(3):
            copies.append(
                pltpu.make_async_copy(done[k], outs[k].at[:, before, :], sems.at[3, k])
            )
            copies[-1].start()
    held = rest[:3]
    xs, ys, gates = views(refs[:n], kinds, count)
    total = summed([(own, got)])
    hg, hu, down = [beside(total, third, (2 * m, 2 * m + 1)) for m in range(3)]
    gate = gate_row(gates)
    sig, silu, act = activation(hg, hu, gate)
    lefts = (*hidden_slopes(hg, hu, sig, silu, gate * down), act)
    x = joined(xs)
    rows = slice(piece * third, (piece + 1) * third)
    for m, right in enumerate((x, x, joined(ys))):
        grad = acc_ref[m, rows, :] + plain(lefts[m], right)
        for k, value in enumerate(adam(grad, first_ref[m, rows, :], second_ref[m, rows, :])):
            held[k][m] = value
            if last:
                copies.append(
                    pltpu.make_async_copy(held[k].at[m], outs[k].at[m, rows, :], sems.at[m, k])
                )
                copies[-1].start()
    for copy in copies:
        copy.wait()


def update_piece(piece, last, pair, chunk, acc, moments, done, whole_outs, count):
    kinds = kinds_of(chunk)
    mats, hidden, width = acc.shape
    third = pair[0].shape[0] // 6
    operands = [*pair, *values_of(chunk), acc, *moments, *done]
    in_specs = [whole()] * len(operands) + [unread()] * len(whole_outs)
    large = [jax.ShapeDtypeStruct(acc.shape, jnp.bfloat16)] * 3
    small = [jax.ShapeDtypeStruct((mats, third, width), jnp.bfloat16)] * 3
    scratch = [pltpu.VMEM((mats, third, width), jnp.bfloat16)] * 3
    return pl.pallas_call(
        functools.partial(update_kernel, kinds, count, piece, last),
        in_specs=in_specs,
        out_specs=([in_hbm()] * 3 if piece else []) + ([] if last else [whole()] * 3),
        out_shape=(large if piece else []) + ([] if last else small),
        input_output_aliases={len(operands) + k: k for k in range(3)} if last else {},
        scratch_shapes=(scratch if last else [])
        + ([pltpu.SemaphoreType.DMA((mats + 1, 3))] if piece else []),
        compiler_params=params(),
        cost_estimate=cost(4 * mats * third * width * count, 14 * mats * third * width),
    )(*operands, *whole_outs)


def from_masked(value, axis, mask):
    pairs = [(source, source ^ mask) for source in range(lax.axis_size(axis))]
    return lax.ppermute(value, axis, pairs)


def dense_plan(tokens, cotangent, expert_ids, gate_probs, weights, first_moment, second_moment):
    n_data = lax.axis_size("dp")
    slices = min(4, lax.axis_size("expert") // 2)
    experts_total = lax.axis_size("expert") // (2 * slices) * n_data
    count = tokens.shape[0]
    hidden, width = weights.shape[1:]
    slots = -(-experts_total // 16) * 16
    other = lambda value: from_masked(value, "dp", 1)
    partner = lambda value: from_masked(value, "expert", 1)
    x_own, y_own, own, weights = pack_own(
        expert_ids, gate_probs, tokens, cotangent, weights, slots
    )
    first = [("xy", own), ("xy", other(own))]
    send, token = partials(weights, own, first, (6,), count, 1, 16)
    first_pair = (send, partner(send))
    along = [[(p, p ^ (2 if p % 2 == k else 4)) for p in range(n_data)] for k in (0, 1)]
    near_x = [lax.ppermute(x_own, "dp", pairs) for pairs in along]
    near_y = [lax.ppermute(y_own, "dp", pairs) for pairs in along]
    other_x = [other(value) for value in passed_on(token, near_x[0], (count // 2, count // 2))]
    early = [("x", value) for value in (near_x[1], *other_x)]
    early_send, token = partials(weights, token, early, (4,), count)
    send, token = partials(weights, token, [("x", near_x[0])], (2,), count)
    near_pair = (send, partner(send))
    x_pair, rest, picked, first_sum, near_sum, gate = pick_onward(
        token, first_pair, near_pair, near_x, other_x, near_y, first, early_send
    )
    far = lax.ppermute(picked, "dp", along[1])
    rest_other = other(rest)
    late = [("y, y of xyy", rest), ("x, y, y", rest_other)]
    early_pair = (early_send, partner(early_send))
    send, token = partials(weights, picked, late, (6,), count)
    late_pair = (send, partner(send))
    pieces = passed_on(token, far, (count // 2, count // 2, count // 2, count // 2 + slots))
    acc, early_sum, token = first_grads(
        gate, pieces[0], first_sum, early_pair, first, hidden, count
    )
    pieces = [*pieces, *[other(value) for value in pieces]]
    final = list(zip(("x", "x", "y", "half y, gates") * 2, pieces))
    sends = far_partials(weights, token, final, 3, count)
    pairs = [(send, partner(send)) for send in sends]
    near = [("first x", x_pair), ("x, y, y", rest), ("second x", x_pair), ("x, y, y", rest_other)]
    acc = add_grads(near_sum, early_sum, late_pair, near, acc, count)
    moments = (first_moment, second_moment)
    done = update_piece(0, False, pairs[0], final, acc, moments, (), (), count)
    outs = update_piece(1, False, pairs[1], final, acc, moments, done, (), count)
    outs = update_piece(2, True, pairs[2], final, acc, moments, outs[3:], outs[:3], count)
    return tuple(outs)


def per_device(tokens, cotangent, expert_ids, gate_probs, weights, first_moment, second_moment):
    n_expert = lax.axis_size("expert")
    n_data = lax.axis_size("dp")
    slices = min(4, n_expert // 2)
    experts_total = n_expert // (2 * slices) * n_data
    half = tokens.shape[0] // 2
    dense = 2 * half * expert_ids.shape[1] // experts_total >= half
    plan = dense_plan if dense and n_data == 8 else routed_plan
    return plan(
        tokens, cotangent, expert_ids, gate_probs, weights, first_moment, second_moment
    )


def solution(mesh):
    in_specs = (
        P("dp", None),
        P("dp", None),
        P("dp", None),
        P("dp", None),
        P(None, "dp", "expert"),
        P(None, "dp", "expert"),
        P(None, "dp", "expert"),
    )
    out_specs = (P(None, "dp", "expert"), P(None, "dp", "expert"), P(None, "dp", "expert"))
    return jax.shard_map(
        per_device, mesh=mesh, in_specs=in_specs, out_specs=out_specs, check_vma=False
    )
```

```python
import functools

import jax
import jax.numpy as jnp
from jax import lax
from jax.experimental import pallas as pl
from jax.experimental.pallas import tpu as pltpu
from jax.sharding import PartitionSpec as P

beta_one = 0.9
beta_two = 0.95
step_count = 10
epsilon = 1e-08


def from_partner(value, axis, distance):
    mask = 2**distance
    pairs = [(source, source ^ mask) for source in range(lax.axis_size(axis))]
    return lax.ppermute(value, axis, pairs)


def contract_last(left, right):
    return lax.dot_general(
        left, right, (((1,), (1,)), ((), ())), preferred_element_type=jnp.float32
    )


def contract_first(left, right):
    return lax.dot_general(
        left, right, (((0,), (0,)), ((), ())), preferred_element_type=jnp.float32
    )


def split_halves(grad, replica, width_half):
    keep = lax.dynamic_slice_in_dim(grad, replica * width_half, width_half, grad.ndim - 1)
    give = lax.dynamic_slice_in_dim(grad, (1 - replica) * width_half, width_half, grad.ndim - 1)
    return (keep, give)


def route_block(block_ids, block_gates, group, n_data, capacity):
    count = block_ids.shape[0]
    top = block_ids.shape[1]
    target = block_ids - group * n_data
    inside = block_ids // n_data == group
    onehot = (
        (target[:, :, None] == jnp.arange(n_data, dtype=jnp.int32)[None, None, :])
        & inside[:, :, None]
    ).astype(jnp.int32)
    per_token = jnp.sum(onehot, axis=1)
    earlier = jnp.cumsum(per_token, axis=0) - per_token
    rank = jnp.sum(onehot * earlier[:, None, :], axis=2)
    total_slots = n_data * capacity
    slot = jnp.where(inside, target * capacity + rank, total_slots).reshape(-1)
    token_of = jnp.broadcast_to(jnp.arange(count, dtype=jnp.int32)[:, None], (count, top)).reshape(
        -1
    )
    table = jnp.full((total_slots,), count, jnp.int32).at[slot].set(token_of, mode="drop")
    gate_slot = (
        jnp.zeros((total_slots,), jnp.bfloat16).at[slot].set(block_gates.reshape(-1), mode="drop")
    )
    return (table, gate_slot)


def routed_plan(tokens, cotangent, expert_ids, gate_probs, weights, first_moment, second_moment):
    n_expert = lax.axis_size("expert")
    n_data = lax.axis_size("dp")
    slices = min(4, n_expert // 2)
    place = lax.axis_index("expert")
    replica = place % 2
    group = place // (2 * slices)
    groups = n_expert // (2 * slices)
    experts_total = groups * n_data
    half = tokens.shape[0] // 2
    width_half = weights.shape[2]
    top = expert_ids.shape[1]
    capacity = max(2, 2 * half * top // experts_total)
    start = replica * half
    own_ids = lax.dynamic_slice_in_dim(expert_ids, start, half, 0)
    own_gates = lax.dynamic_slice_in_dim(gate_probs, start, half, 0)
    table, gate_slot = route_block(own_ids, own_gates, group, n_data, capacity)
    source_tokens = lax.dynamic_slice_in_dim(tokens, start, half, 0)
    source_cot = lax.dynamic_slice_in_dim(cotangent, start, half, 0)
    columns = source_tokens.shape[1]
    padded_tokens = jnp.concatenate([source_tokens, jnp.zeros((1, columns), jnp.bfloat16)], 0)
    padded_cot = jnp.concatenate([source_cot, jnp.zeros((1, columns), jnp.bfloat16)], 0)
    send_rows = padded_tokens[table].reshape(n_data, -1, columns)
    send_cot = padded_cot[table].reshape(n_data, -1, columns)
    send_gates = gate_slot.reshape(n_data, -1)
    rows_in, gates_in = (
        lax.all_to_all(send_rows, "dp", split_axis=0, concat_axis=0, tiled=True),
        lax.all_to_all(send_gates, "dp", split_axis=0, concat_axis=0, tiled=True),
    )
    rows = rows_in.reshape(-1, columns)
    gate_rows = gates_in.reshape(-1).astype(jnp.float32)
    partner = from_partner(weights, "expert", 0)
    lower = jnp.where(replica == 0, weights, partner)
    upper = jnp.where(replica == 0, partner, weights)
    full = jnp.concatenate([lower, upper], 2)
    hg = contract_last(rows, full[0])
    hu = contract_last(rows, full[1])
    sig = jax.nn.sigmoid(hg)
    act = (hg * sig * hu).astype(jnp.bfloat16)
    cot_in = lax.all_to_all(send_cot, "dp", split_axis=0, concat_axis=0, tiled=True)
    cots = cot_in.reshape(-1, columns)
    dz = (gate_rows[:, None] * cots.astype(jnp.float32)).astype(jnp.bfloat16)
    dact = contract_last(dz, full[2])
    grad_down = contract_first(act, dz)
    dhg = (dact * hu * sig * (1.0 + hg * (1.0 - sig))).astype(jnp.bfloat16)
    dhu = (dact * hg * sig).astype(jnp.bfloat16)
    grad_gate = contract_first(dhg, rows)
    grad_up = contract_first(dhu, rows)
    stacked = jnp.stack([grad_gate, grad_up, grad_down])
    keep, give = split_halves(stacked, replica, width_half)
    total = keep + from_partner(give, "expert", 0)
    moment_one = beta_one * first_moment.astype(jnp.float32) + (1.0 - beta_one) * total
    moment_two = beta_two * second_moment.astype(jnp.float32) + (1.0 - beta_two) * total * total
    step = (
        moment_one
        / (1.0 - beta_one**step_count)
        / (jnp.sqrt(moment_two / (1.0 - beta_two**step_count)) + epsilon)
    )
    return (
        moment_one.astype(jnp.bfloat16),
        moment_two.astype(jnp.bfloat16),
        step.astype(jnp.bfloat16),
    )


VMEM_LIMIT = 16 * 1024 * 1024


def params():
    return pltpu.CompilerParams(vmem_limit_bytes=VMEM_LIMIT)


def cost(flops, moved):
    return pl.CostEstimate(flops=flops, bytes_accessed=moved, transcendentals=0)


def whole():
    return pl.BlockSpec(memory_space=pltpu.VMEM)


def in_hbm():
    return pl.BlockSpec(memory_space=pltpu.HBM)


def unread():
    return pl.BlockSpec(memory_space=pl.ANY)


def expert_here():
    slices = min(4, lax.axis_size("expert") // 2)
    group = lax.axis_index("expert") // (2 * slices)
    return group * lax.axis_size("dp") + lax.axis_index("dp")


def keep_hbm(value):
    return pltpu.with_memory_space_constraint(value, pltpu.HBM)


def pack_kernel(
    ids_hbm,
    gates_hbm,
    tokens_ref,
    cot_ref,
    w_hbm,
    x_ref,
    y_ref,
    own_ref,
    w_ref,
    ids_ref,
    gates_ref,
    sems,
):
    count = tokens_ref.shape[0]
    width = x_ref.shape[1]
    columns = pl.ds(pl.multiple_of(lax.axis_index("expert") % 2 * width, width), width)
    copies = [
        pltpu.make_async_copy(ids_hbm, ids_ref, sems.at[0]),
        pltpu.make_async_copy(gates_hbm, gates_ref, sems.at[1]),
        pltpu.make_async_copy(tokens_ref.at[:, columns], x_ref, sems.at[2]),
        pltpu.make_async_copy(cot_ref.at[:, columns], y_ref.at[0:count, :], sems.at[3]),
        pltpu.make_async_copy(tokens_ref.at[:, columns], own_ref.at[0:count, :], sems.at[4]),
        pltpu.make_async_copy(cot_ref.at[:, columns], own_ref.at[count : 2 * count, :], sems.at[5]),
        pltpu.make_async_copy(w_hbm, w_ref, sems.at[6]),
    ]
    for copy in copies:
        copy.start()
    copies[0].wait()
    copies[1].wait()
    ids = ids_ref[...]
    gates = gates_ref[...].astype(jnp.float32)
    slots = y_ref.shape[0] - count
    row = lax.broadcasted_iota(jnp.int32, (slots, count), 0)
    gate = jnp.zeros((slots, count), jnp.float32)
    for k in range(ids.shape[0]):
        gate = gate + jnp.where(row == ids[k : k + 1, :], gates[k : k + 1, :], 0.0)
    y_ref[count:, 0:count] = gate.astype(jnp.bfloat16)
    y_ref[count:, count:] = jnp.zeros((slots, width - count), jnp.bfloat16)
    own_ref[2 * count :, :] = y_ref[count:, :]
    for copy in copies[2:]:
        copy.wait()


def pack_own(ids, gates, tokens, cotangent, weights, slots):
    count, top = ids.shape
    width = weights.shape[2]
    return pl.pallas_call(
        pack_kernel,
        in_specs=[in_hbm()] * 5,
        out_specs=[whole()] * 4,
        out_shape=[
            jax.ShapeDtypeStruct((rows, width), jnp.bfloat16)
            for rows in (count, count + slots, 2 * count + slots)
        ]
        + [jax.ShapeDtypeStruct(weights.shape, weights.dtype)],
        scratch_shapes=[
            pltpu.VMEM((top, count), ids.dtype),
            pltpu.VMEM((top, count), gates.dtype),
            pltpu.SemaphoreType.DMA((7,)),
        ],
        compiler_params=params(),
        cost_estimate=cost(1000, 8 * count * width),
    )(*[keep_hbm(value) for value in (ids.T, gates.T, tokens, cotangent, weights)])


def views(refs, kinds, count):
    xs, ys, gates = [], [], []
    for ref, kind in zip(refs, kinds):
        if kind in ("first x", "second x"):
            xs.append(ref[0 if kind == "first x" else 1])
            continue
        if kind == "x of xyy":
            xs.append(ref[0:count, :])
            continue
        if kind in ("x, y, y", "y, y of xyy"):
            rows = (ref.shape[0] - count) // 2
            if kind == "x, y, y":
                xs.append(ref[0:count, :])
            for row in (count, count + rows):
                ys.append(ref[row : row + count, :])
                gates.append(ref[row + count : row + rows, 0:count])
            continue
        for part in [ref.at[0], ref.at[1]] if ref.ndim == 3 else [ref]:
            if kind == "x":
                xs.append(part[...])
            if kind == "xy":
                xs.append(part[0:count, :])
                ys.append(part[count : 2 * count, :])
                gates.append(part[2 * count :, 0:count])
            if kind == "y":
                ys.append(part[...])
            if kind == "y, gates":
                ys.append(part[0:count, :])
                gates.append(part[count:, 0:count])
            if kind == "half y, gates":
                ys.append(part[0 : count // 2, :])
                gates.append(part[count // 2 :, 0:count])
    return xs, ys, gates


def joined(parts):
    return parts[0] if len(parts) == 1 else jnp.concatenate(parts, 0)


def kinds_of(chunk):
    return tuple(kind for kind, value in chunk)


def values_of(chunk):
    return [value for kind, value in chunk]


def store_partials(parts, count, out_ref):
    row = 0
    used = sum(part.size for part in parts) // count
    if used < out_ref.shape[0]:
        out_ref[used:, :] = jnp.zeros((out_ref.shape[0] - used, count), jnp.bfloat16)
    for part in parts:
        for first in range(0, part.shape[1], count):
            piece = part[:, first : first + count]
            out_ref[row : row + piece.shape[0], :] = piece.astype(jnp.bfloat16)
            row = row + piece.shape[0]


def partial_kernel(kinds, count, tokened, w_ref, after_ref, *refs):
    n = len(kinds)
    xs, ys, gates = views(refs[:n], kinds, count)
    outs = refs[n : len(refs) - tokened]
    mats, hidden, width = w_ref.shape
    parts = []
    if xs and len(outs) == mats:
        parts.extend(contract_last(w_ref[m], joined(xs)) for m in (0, 1))
    elif xs:
        parts.append(contract_last(w_ref[0:2].reshape(2 * hidden, width), joined(xs)))
    if ys:
        parts.append(contract_last(w_ref[2], joined(ys)))
    if len(outs) == 1:
        store_partials(parts, count, outs[0])
    else:
        for part, out_ref in zip(parts, outs):
            store_partials([part], count, out_ref)
    if tokened:
        refs[-1][...] = jnp.zeros_like(refs[-1])


def partials(weights, after, chunk, rows, count, tokened=1, spare=0):
    hidden, width = weights.shape[1:]
    kinds = kinds_of(chunk)
    total = sum(rows) * hidden * count
    return pl.pallas_call(
        functools.partial(partial_kernel, kinds, count, tokened),
        in_specs=[whole(), unread()] + [whole()] * len(kinds),
        out_specs=[whole()] * (len(rows) + tokened),
        out_shape=[jax.ShapeDtypeStruct((k * hidden + spare, count), jnp.bfloat16) for k in rows]
        + [jax.ShapeDtypeStruct((8, 128), jnp.float32)] * tokened,
        compiler_params=params(),
        cost_estimate=cost(2 * total * width, 6 * total),
    )(weights, after, *values_of(chunk))


def gate_row(gates):
    rows = []
    expert = expert_here()
    for held in gates:
        held = held.astype(jnp.float32)
        index = lax.broadcasted_iota(jnp.int32, held.shape, 0)
        rows.append(jnp.sum(jnp.where(index == expert, held, 0.0), 0, keepdims=True))
    return rows[0] if len(rows) == 1 else jnp.concatenate(rows, 1)


def summed(pairs):
    parts = []
    for own, *got in pairs:
        part = own[...].astype(jnp.float32)
        parts.append(part + got[0][...].astype(jnp.float32) if got else part)
    return parts[0] if len(parts) == 1 else jnp.concatenate(parts, 0)


def beside(total, hidden, firsts):
    parts = [total[first * hidden : (first + 1) * hidden] for first in firsts]
    return jnp.concatenate(parts, 1)


def activation(hg, hu, gate):
    sig = jax.nn.sigmoid(hg)
    silu = hg * sig
    return sig, silu, (gate * (silu * hu)).astype(jnp.bfloat16)


def hidden_slopes(hg, hu, sig, silu, dact):
    dhg = (dact * hu * sig * (1.0 + hg * (1.0 - sig))).astype(jnp.bfloat16)
    dhu = (dact * silu).astype(jnp.bfloat16)
    return dhg, dhu


def hidden_grads(gate, pairs):
    total = summed(pairs)
    blocks = gate.shape[1] // total.shape[1]
    hidden = total.shape[0] // (3 * blocks)
    hg = beside(total, hidden, range(0, 2 * blocks, 2))
    hu = beside(total, hidden, range(1, 2 * blocks, 2))
    dact = gate * beside(total, hidden, range(2 * blocks, 3 * blocks))
    sig, silu, act = activation(hg, hu, gate)
    return (*hidden_slopes(hg, hu, sig, silu, dact), act)


def plain(left, right):
    return lax.dot_general(
        left, right, (((1,), (0,)), ((), ())), preferred_element_type=jnp.float32
    )


def onward_kernel(kinds, after_ref, own, got, near_own, near_got, *refs):
    x0_ref, x1_ref, s0_ref, y0_ref, y1_ref = refs[:5]
    pair_ref, rest_ref, out_ref, first_ref, sum_ref, gate_ref = refs[6 + len(kinds) :]
    count, rows = x0_ref.shape[0], y0_ref.shape[0]
    gates = views(refs[5 : 5 + len(kinds)], kinds, count)[2]
    gate_ref[...] = jnp.broadcast_to(gate_row(gates), gate_ref.shape)
    pair_ref[0] = x0_ref[...]
    pair_ref[1] = s0_ref[...]
    rest_ref[0:count, :] = x1_ref[...]
    rest_ref[count : count + rows, :] = y0_ref[...]
    rest_ref[count + rows :, :] = y1_ref[...]
    out_ref[0:count, :] = x0_ref[...]
    out_ref[count:, :] = y0_ref[...]
    used = first_ref.shape[0]
    first_ref[...] = own[0:used, :].astype(jnp.float32) + got[0:used, :].astype(jnp.float32)
    sum_ref[...] = near_own[...].astype(jnp.float32) + near_got[...].astype(jnp.float32)


def pick_onward(after, pair, near_pair, near_x, other_x, near_y, chunk, held):
    count, width = other_x.shape
    rows = near_y[0].shape[0]
    operands = [*pair, *near_pair, *near_x, other_x, *near_y, *values_of(chunk), held]
    return pl.pallas_call(
        functools.partial(onward_kernel, kinds_of(chunk)),
        in_specs=[unread()] + [whole()] * len(operands),
        out_specs=[whole()] * 6,
        out_shape=[
            jax.ShapeDtypeStruct((2, count, width), jnp.bfloat16),
            jax.ShapeDtypeStruct((count + 2 * rows, width), jnp.bfloat16),
            jax.ShapeDtypeStruct((count + rows, width), jnp.bfloat16),
            jax.ShapeDtypeStruct((3 * near_pair[0].shape[0], count), jnp.float32),
            jax.ShapeDtypeStruct(near_pair[0].shape, jnp.float32),
            jax.ShapeDtypeStruct((8, 2 * count), jnp.float32),
        ],
        compiler_params=params(),
        cost_estimate=cost(1000, 8 * other_x.size),
    )(after, *operands)


def pass_kernel(after_ref, in_ref, *outs):
    row = 0
    for out_ref in outs:
        out_ref[...] = in_ref[row : row + out_ref.shape[0], :]
        row = row + out_ref.shape[0]


def passed_on(after, value, cuts):
    width = value.shape[1]
    return pl.pallas_call(
        pass_kernel,
        in_specs=[unread(), whole()],
        out_specs=[whole()] * len(cuts),
        out_shape=[jax.ShapeDtypeStruct((rows, width), value.dtype) for rows in cuts],
        compiler_params=params(),
        cost_estimate=cost(1000, 2 * value.size),
    )(after, value)


def first_kernel(kinds, count, gate_ref, after_ref, sum_ref, own, got, *refs):
    n = len(kinds)
    xs, ys, gates = views(refs[:n], kinds, count)
    out_ref, more_ref, token_ref = refs[n:]
    more_ref[...] = summed([(own, got)])
    lefts = hidden_grads(gate_ref[0:1, :], [(sum_ref,)])
    x = joined(xs)
    for m, right in enumerate((x, x, joined(ys))):
        out_ref[m] = plain(lefts[m], right)
    token_ref[...] = jnp.zeros_like(token_ref)


def first_grads(gate, after, total, pair, chunk, hidden, count):
    kinds = kinds_of(chunk)
    width = chunk[0][1].shape[-1]
    return pl.pallas_call(
        functools.partial(first_kernel, kinds, count),
        in_specs=[whole(), unread()] + [whole()] * (3 + len(kinds)),
        out_specs=[whole()] * 3,
        out_shape=[
            jax.ShapeDtypeStruct((3, hidden, width), jnp.float32),
            jax.ShapeDtypeStruct(pair[0].shape, jnp.float32),
            jax.ShapeDtypeStruct((8, 128), jnp.float32),
        ],
        compiler_params=params(),
        cost_estimate=cost(2 * total.size * width, 12 * hidden * width),
    )(gate, after, total, *pair, *values_of(chunk))


def grad_kernel(kinds, count, sum_ref, more_ref, own, got, *refs):
    n = len(kinds)
    xs, ys, gates = views(refs[:n], kinds, count)
    acc_ref, out_ref = refs[n:]
    lefts = hidden_grads(gate_row(gates), [(sum_ref,), (more_ref,), (own, got)])
    x = joined(xs)
    for m, right in enumerate((x, x, joined(ys))):
        out_ref[m] = acc_ref[m] + plain(lefts[m], right)


def add_grads(near_sum, more_sum, pair, chunk, acc, count):
    kinds = kinds_of(chunk)
    mats, hidden, width = acc.shape
    operands = [near_sum, more_sum, *pair, *values_of(chunk), acc]
    return pl.pallas_call(
        functools.partial(grad_kernel, kinds, count),
        in_specs=[whole()] * len(operands),
        out_specs=whole(),
        out_shape=jax.ShapeDtypeStruct(acc.shape, jnp.float32),
        input_output_aliases={len(operands) - 1: 0},
        compiler_params=params(),
        cost_estimate=cost(
            2 * mats * hidden * width * 4 * count, 8 * mats * hidden * width
        ),
    )(*operands)


def adam(grad, first, second):
    moment_one = beta_one * first.astype(jnp.float32) + (1.0 - beta_one) * grad
    moment_two = beta_two * second.astype(jnp.float32) + (1.0 - beta_two) * (grad * grad)
    root = (1.0 / (1.0 - beta_two**step_count)) ** 0.5
    below = moment_two * lax.rsqrt(moment_two) + epsilon / root
    scaled = moment_one * (1.0 / (1.0 - beta_one**step_count) / root)
    step = scaled * pl.reciprocal(below, approx=True)
    return [value.astype(jnp.bfloat16) for value in (moment_one, moment_two, step)]


def far_kernel(kinds, count, w_ref, after_ref, *refs):
    n = len(kinds)
    xs, ys, gates = views(refs[:n], kinds, count)
    outs = refs[n:]
    x, y = joined(xs), joined(ys)
    third = w_ref.shape[1] // len(outs)
    for m, right in enumerate((x, x, y)):
        part = contract_last(w_ref[m], right).astype(jnp.bfloat16)
        for k, out_ref in enumerate(outs):
            for side in (0, 1):
                row = (2 * m + side) * third
                out_ref[row : row + third, :] = part[
                    k * third : (k + 1) * third, side * count : (side + 1) * count
                ]


def far_partials(weights, after, chunk, pieces, count):
    mats, hidden, width = weights.shape
    kinds = kinds_of(chunk)
    rows = 2 * mats * hidden // pieces
    return pl.pallas_call(
        functools.partial(far_kernel, kinds, count),
        in_specs=[whole(), unread()] + [whole()] * len(kinds),
        out_specs=[whole()] * pieces,
        out_shape=[jax.ShapeDtypeStruct((rows, count), jnp.bfloat16)] * pieces,
        compiler_params=params(),
        cost_estimate=cost(4 * mats * hidden * count * width, 12 * mats * hidden * count),
    )(weights, after, *values_of(chunk))


def update_kernel(kinds, count, piece, last, own, got, *refs):
    n = len(kinds)
    acc_ref, first_ref, second_ref = refs[n : n + 3]
    rest = refs[n + 3 :]
    third = own.shape[0] // 6
    copies = []
    if piece > 0:
        done = rest[:3]
        rest = rest[3 + 3 * last :]
        outs, rest = rest[:3], rest[3:]
        sems = rest[-1]
        before = slice((piece - 1) * third, piece * third)
        for k in range(3):
            copies.append(
                pltpu.make_async_copy(done[k], outs[k].at[:, before, :], sems.at[3, k])
            )
            copies[-1].start()
    held = rest[:3]
    xs, ys, gates = views(refs[:n], kinds, count)
    total = summed([(own, got)])
    hg, hu, down = [beside(total, third, (2 * m, 2 * m + 1)) for m in range(3)]
    gate = gate_row(gates)
    sig, silu, act = activation(hg, hu, gate)
    lefts = (*hidden_slopes(hg, hu, sig, silu, gate * down), act)
    x = joined(xs)
    rows = slice(piece * third, (piece + 1) * third)
    for m, right in enumerate((x, x, joined(ys))):
        grad = acc_ref[m, rows, :] + plain(lefts[m], right)
        for k, value in enumerate(adam(grad, first_ref[m, rows, :], second_ref[m, rows, :])):
            held[k][m] = value
            if last:
                copies.append(
                    pltpu.make_async_copy(held[k].at[m], outs[k].at[m, rows, :], sems.at[m, k])
                )
                copies[-1].start()
    for copy in copies:
        copy.wait()


def update_piece(piece, last, pair, chunk, acc, moments, done, whole_outs, count):
    kinds = kinds_of(chunk)
    mats, hidden, width = acc.shape
    third = pair[0].shape[0] // 6
    operands = [*pair, *values_of(chunk), acc, *moments, *done]
    in_specs = [whole()] * len(operands) + [unread()] * len(whole_outs)
    large = [jax.ShapeDtypeStruct(acc.shape, jnp.bfloat16)] * 3
    small = [jax.ShapeDtypeStruct((mats, third, width), jnp.bfloat16)] * 3
    scratch = [pltpu.VMEM((mats, third, width), jnp.bfloat16)] * 3
    return pl.pallas_call(
        functools.partial(update_kernel, kinds, count, piece, last),
        in_specs=in_specs,
        out_specs=([in_hbm()] * 3 if piece else []) + ([] if last else [whole()] * 3),
        out_shape=(large if piece else []) + ([] if last else small),
        input_output_aliases={len(operands) + k: k for k in range(3)} if last else {},
        scratch_shapes=(scratch if last else [])
        + ([pltpu.SemaphoreType.DMA((mats + 1, 3))] if piece else []),
        compiler_params=params(),
        cost_estimate=cost(4 * mats * third * width * count, 14 * mats * third * width),
    )(*operands, *whole_outs)


def from_masked(value, axis, mask):
    pairs = [(source, source ^ mask) for source in range(lax.axis_size(axis))]
    return lax.ppermute(value, axis, pairs)


def dense_plan(tokens, cotangent, expert_ids, gate_probs, weights, first_moment, second_moment):
    n_data = lax.axis_size("dp")
    slices = min(4, lax.axis_size("expert") // 2)
    experts_total = lax.axis_size("expert") // (2 * slices) * n_data
    count = tokens.shape[0]
    hidden, width = weights.shape[1:]
    slots = -(-experts_total // 16) * 16
    other = lambda value: from_masked(value, "dp", 1)
    partner = lambda value: from_masked(value, "expert", 1)
    x_own, y_own, own, weights = pack_own(
        expert_ids, gate_probs, tokens, cotangent, weights, slots
    )
    first = [("xy", own), ("xy", other(own))]
    send, token = partials(weights, own, first, (6,), count, 1, 16)
    first_pair = (send, partner(send))
    along = [[(p, p ^ (2 if p % 2 == k else 4)) for p in range(n_data)] for k in (0, 1)]
    near_x = [lax.ppermute(x_own, "dp", pairs) for pairs in along]
    near_y = [lax.ppermute(y_own, "dp", pairs) for pairs in along]
    other_x = other(near_x[0])
    send, token = partials(weights, token, [("x", near_x[0]), ("", near_x[1])], (2,), count)
    near_pair = (send, partner(send))
    early = [("x", near_x[1]), ("x", other_x)]
    early_send, token = partials(weights, token, early, (4,), count)
    x_pair, rest, picked, first_sum, near_sum, gate = pick_onward(
        token, first_pair, near_pair, near_x, other_x, near_y, first, early_send
    )
    far = lax.ppermute(picked, "dp", along[1])
    rest_other = other(rest)
    late = [("y, y of xyy", rest), ("x, y, y", rest_other)]
    early_pair = (early_send, partner(early_send))
    send, token = partials(weights, picked, late, (6,), count)
    late_pair = (send, partner(send))
    pieces = passed_on(token, far, (count // 2, count // 2, count // 2, count // 2 + slots))
    acc, early_sum, token = first_grads(
        gate, pieces[0], first_sum, early_pair, first, hidden, count
    )
    pieces = [*pieces, *[other(value) for value in pieces]]
    final = list(zip(("x", "x", "y", "half y, gates") * 2, pieces))
    sends = far_partials(weights, token, final, 3, count)
    pairs = [(send, partner(send)) for send in sends]
    near = [("first x", x_pair), ("x, y, y", rest), ("second x", x_pair), ("x, y, y", rest_other)]
    acc = add_grads(near_sum, early_sum, late_pair, near, acc, count)
    moments = (first_moment, second_moment)
    done = update_piece(0, False, pairs[0], final, acc, moments, (), (), count)
    outs = update_piece(1, False, pairs[1], final, acc, moments, done, (), count)
    outs = update_piece(2, True, pairs[2], final, acc, moments, outs[3:], outs[:3], count)
    return tuple(outs)


def per_device(tokens, cotangent, expert_ids, gate_probs, weights, first_moment, second_moment):
    n_expert = lax.axis_size("expert")
    n_data = lax.axis_size("dp")
    slices = min(4, n_expert // 2)
    experts_total = n_expert // (2 * slices) * n_data
    half = tokens.shape[0] // 2
    dense = 2 * half * expert_ids.shape[1] // experts_total >= half
    plan = dense_plan if dense and n_data == 8 else routed_plan
    return plan(
        tokens, cotangent, expert_ids, gate_probs, weights, first_moment, second_moment
    )


def solution(mesh):
    in_specs = (
        P("dp", None),
        P("dp", None),
        P("dp", None),
        P("dp", None),
        P(None, "dp", "expert"),
        P(None, "dp", "expert"),
        P(None, "dp", "expert"),
    )
    out_specs = (P(None, "dp", "expert"), P(None, "dp", "expert"), P(None, "dp", "expert"))
    return jax.shard_map(
        per_device, mesh=mesh, in_specs=in_specs, out_specs=out_specs, check_vma=False
    )
```

```python
import functools

import jax
import jax.numpy as jnp
from jax import lax
from jax.experimental import pallas as pl
from jax.experimental.pallas import tpu as pltpu
from jax.sharding import PartitionSpec as P

beta_one = 0.9
beta_two = 0.95
step_count = 10
epsilon = 1e-08


def from_partner(value, axis, distance):
    mask = 2**distance
    pairs = [(source, source ^ mask) for source in range(lax.axis_size(axis))]
    return lax.ppermute(value, axis, pairs)


def contract_last(left, right):
    return lax.dot_general(
        left, right, (((1,), (1,)), ((), ())), preferred_element_type=jnp.float32
    )


def contract_first(left, right):
    return lax.dot_general(
        left, right, (((0,), (0,)), ((), ())), preferred_element_type=jnp.float32
    )


def split_halves(grad, replica, width_half):
    keep = lax.dynamic_slice_in_dim(grad, replica * width_half, width_half, grad.ndim - 1)
    give = lax.dynamic_slice_in_dim(grad, (1 - replica) * width_half, width_half, grad.ndim - 1)
    return (keep, give)


def route_block(block_ids, block_gates, group, n_data, capacity):
    count = block_ids.shape[0]
    top = block_ids.shape[1]
    target = block_ids - group * n_data
    inside = block_ids // n_data == group
    onehot = (
        (target[:, :, None] == jnp.arange(n_data, dtype=jnp.int32)[None, None, :])
        & inside[:, :, None]
    ).astype(jnp.int32)
    per_token = jnp.sum(onehot, axis=1)
    earlier = jnp.cumsum(per_token, axis=0) - per_token
    rank = jnp.sum(onehot * earlier[:, None, :], axis=2)
    total_slots = n_data * capacity
    slot = jnp.where(inside, target * capacity + rank, total_slots).reshape(-1)
    token_of = jnp.broadcast_to(jnp.arange(count, dtype=jnp.int32)[:, None], (count, top)).reshape(
        -1
    )
    table = jnp.full((total_slots,), count, jnp.int32).at[slot].set(token_of, mode="drop")
    gate_slot = (
        jnp.zeros((total_slots,), jnp.bfloat16).at[slot].set(block_gates.reshape(-1), mode="drop")
    )
    return (table, gate_slot)


def routed_plan(tokens, cotangent, expert_ids, gate_probs, weights, first_moment, second_moment):
    n_expert = lax.axis_size("expert")
    n_data = lax.axis_size("dp")
    slices = min(4, n_expert // 2)
    place = lax.axis_index("expert")
    replica = place % 2
    group = place // (2 * slices)
    groups = n_expert // (2 * slices)
    experts_total = groups * n_data
    half = tokens.shape[0] // 2
    width_half = weights.shape[2]
    top = expert_ids.shape[1]
    capacity = max(2, 2 * half * top // experts_total)
    start = replica * half
    own_ids = lax.dynamic_slice_in_dim(expert_ids, start, half, 0)
    own_gates = lax.dynamic_slice_in_dim(gate_probs, start, half, 0)
    table, gate_slot = route_block(own_ids, own_gates, group, n_data, capacity)
    source_tokens = lax.dynamic_slice_in_dim(tokens, start, half, 0)
    source_cot = lax.dynamic_slice_in_dim(cotangent, start, half, 0)
    columns = source_tokens.shape[1]
    padded_tokens = jnp.concatenate([source_tokens, jnp.zeros((1, columns), jnp.bfloat16)], 0)
    padded_cot = jnp.concatenate([source_cot, jnp.zeros((1, columns), jnp.bfloat16)], 0)
    send_rows = padded_tokens[table].reshape(n_data, -1, columns)
    send_cot = padded_cot[table].reshape(n_data, -1, columns)
    send_gates = gate_slot.reshape(n_data, -1)
    rows_in, gates_in = (
        lax.all_to_all(send_rows, "dp", split_axis=0, concat_axis=0, tiled=True),
        lax.all_to_all(send_gates, "dp", split_axis=0, concat_axis=0, tiled=True),
    )
    rows = rows_in.reshape(-1, columns)
    gate_rows = gates_in.reshape(-1).astype(jnp.float32)
    partner = from_partner(weights, "expert", 0)
    lower = jnp.where(replica == 0, weights, partner)
    upper = jnp.where(replica == 0, partner, weights)
    full = jnp.concatenate([lower, upper], 2)
    hg = contract_last(rows, full[0])
    hu = contract_last(rows, full[1])
    sig = jax.nn.sigmoid(hg)
    act = (hg * sig * hu).astype(jnp.bfloat16)
    cot_in = lax.all_to_all(send_cot, "dp", split_axis=0, concat_axis=0, tiled=True)
    cots = cot_in.reshape(-1, columns)
    dz = (gate_rows[:, None] * cots.astype(jnp.float32)).astype(jnp.bfloat16)
    dact = contract_last(dz, full[2])
    grad_down = contract_first(act, dz)
    dhg = (dact * hu * sig * (1.0 + hg * (1.0 - sig))).astype(jnp.bfloat16)
    dhu = (dact * hg * sig).astype(jnp.bfloat16)
    grad_gate = contract_first(dhg, rows)
    grad_up = contract_first(dhu, rows)
    stacked = jnp.stack([grad_gate, grad_up, grad_down])
    keep, give = split_halves(stacked, replica, width_half)
    total = keep + from_partner(give, "expert", 0)
    moment_one = beta_one * first_moment.astype(jnp.float32) + (1.0 - beta_one) * total
    moment_two = beta_two * second_moment.astype(jnp.float32) + (1.0 - beta_two) * total * total
    step = (
        moment_one
        / (1.0 - beta_one**step_count)
        / (jnp.sqrt(moment_two / (1.0 - beta_two**step_count)) + epsilon)
    )
    return (
        moment_one.astype(jnp.bfloat16),
        moment_two.astype(jnp.bfloat16),
        step.astype(jnp.bfloat16),
    )


VMEM_LIMIT = 16 * 1024 * 1024


def params():
    return pltpu.CompilerParams(vmem_limit_bytes=VMEM_LIMIT)


def cost(flops, moved):
    return pl.CostEstimate(flops=flops, bytes_accessed=moved, transcendentals=0)


def whole():
    return pl.BlockSpec(memory_space=pltpu.VMEM)


def in_hbm():
    return pl.BlockSpec(memory_space=pltpu.HBM)


def unread():
    return pl.BlockSpec(memory_space=pl.ANY)


def expert_here():
    slices = min(4, lax.axis_size("expert") // 2)
    group = lax.axis_index("expert") // (2 * slices)
    return group * lax.axis_size("dp") + lax.axis_index("dp")


def keep_hbm(value):
    return pltpu.with_memory_space_constraint(value, pltpu.HBM)


def pack_kernel(
    ids_hbm,
    gates_hbm,
    tokens_ref,
    cot_ref,
    w_hbm,
    x_ref,
    y_ref,
    own_ref,
    w_ref,
    ids_ref,
    gates_ref,
    sems,
):
    count = tokens_ref.shape[0]
    width = x_ref.shape[1]
    columns = pl.ds(pl.multiple_of(lax.axis_index("expert") % 2 * width, width), width)
    copies = [
        pltpu.make_async_copy(ids_hbm, ids_ref, sems.at[0]),
        pltpu.make_async_copy(gates_hbm, gates_ref, sems.at[1]),
        pltpu.make_async_copy(tokens_ref.at[:, columns], x_ref, sems.at[2]),
        pltpu.make_async_copy(cot_ref.at[:, columns], y_ref.at[0:count, :], sems.at[3]),
        pltpu.make_async_copy(tokens_ref.at[:, columns], own_ref.at[0:count, :], sems.at[4]),
        pltpu.make_async_copy(cot_ref.at[:, columns], own_ref.at[count : 2 * count, :], sems.at[5]),
        pltpu.make_async_copy(w_hbm, w_ref, sems.at[6]),
    ]
    for copy in copies:
        copy.start()
    copies[0].wait()
    copies[1].wait()
    ids = ids_ref[...]
    gates = gates_ref[...].astype(jnp.float32)
    slots = y_ref.shape[0] - count
    row = lax.broadcasted_iota(jnp.int32, (slots, count), 0)
    gate = jnp.zeros((slots, count), jnp.float32)
    for k in range(ids.shape[0]):
        gate = gate + jnp.where(row == ids[k : k + 1, :], gates[k : k + 1, :], 0.0)
    y_ref[count:, 0:count] = gate.astype(jnp.bfloat16)
    y_ref[count:, count:] = jnp.zeros((slots, width - count), jnp.bfloat16)
    own_ref[2 * count :, :] = y_ref[count:, :]
    for copy in copies[2:]:
        copy.wait()


def pack_own(ids, gates, tokens, cotangent, weights, slots):
    count, top = ids.shape
    width = weights.shape[2]
    return pl.pallas_call(
        pack_kernel,
        in_specs=[in_hbm()] * 5,
        out_specs=[whole()] * 4,
        out_shape=[
            jax.ShapeDtypeStruct((rows, width), jnp.bfloat16)
            for rows in (count, count + slots, 2 * count + slots)
        ]
        + [jax.ShapeDtypeStruct(weights.shape, weights.dtype)],
        scratch_shapes=[
            pltpu.VMEM((top, count), ids.dtype),
            pltpu.VMEM((top, count), gates.dtype),
            pltpu.SemaphoreType.DMA((7,)),
        ],
        compiler_params=params(),
        cost_estimate=cost(1000, 8 * count * width),
    )(*[keep_hbm(value) for value in (ids.T, gates.T, tokens, cotangent, weights)])


def views(refs, kinds, count):
    xs, ys, gates = [], [], []
    for ref, kind in zip(refs, kinds):
        if kind in ("first x", "second x"):
            xs.append(ref[0 if kind == "first x" else 1])
            continue
        if kind == "x of xyy":
            xs.append(ref[0:count, :])
            continue
        if kind in ("x, y, y", "y, y of xyy"):
            rows = (ref.shape[0] - count) // 2
            if kind == "x, y, y":
                xs.append(ref[0:count, :])
            for row in (count, count + rows):
                ys.append(ref[row : row + count, :])
                gates.append(ref[row + count : row + rows, 0:count])
            continue
        for part in [ref.at[0], ref.at[1]] if ref.ndim == 3 else [ref]:
            if kind == "x":
                xs.append(part[...])
            if kind == "xy":
                xs.append(part[0:count, :])
                ys.append(part[count : 2 * count, :])
                gates.append(part[2 * count :, 0:count])
            if kind == "y":
                ys.append(part[...])
            if kind == "y, gates":
                ys.append(part[0:count, :])
                gates.append(part[count:, 0:count])
            if kind == "half y, gates":
                ys.append(part[0 : count // 2, :])
                gates.append(part[count // 2 :, 0:count])
    return xs, ys, gates


def joined(parts):
    return parts[0] if len(parts) == 1 else jnp.concatenate(parts, 0)


def kinds_of(chunk):
    return tuple(kind for kind, value in chunk)


def values_of(chunk):
    return [value for kind, value in chunk]


def store_partials(parts, count, out_ref):
    row = 0
    used = sum(part.size for part in parts) // count
    if used < out_ref.shape[0]:
        out_ref[used:, :] = jnp.zeros((out_ref.shape[0] - used, count), jnp.bfloat16)
    for part in parts:
        for first in range(0, part.shape[1], count):
            piece = part[:, first : first + count]
            out_ref[row : row + piece.shape[0], :] = piece.astype(jnp.bfloat16)
            row = row + piece.shape[0]


def partial_kernel(kinds, count, tokened, w_ref, after_ref, *refs):
    n = len(kinds)
    xs, ys, gates = views(refs[:n], kinds, count)
    outs = refs[n : len(refs) - tokened]
    mats, hidden, width = w_ref.shape
    parts = []
    if xs and len(outs) == mats:
        parts.extend(contract_last(w_ref[m], joined(xs)) for m in (0, 1))
    elif xs:
        parts.append(contract_last(w_ref[0:2].reshape(2 * hidden, width), joined(xs)))
    if ys:
        parts.append(contract_last(w_ref[2], joined(ys)))
    if len(outs) == 1:
        store_partials(parts, count, outs[0])
    else:
        for part, out_ref in zip(parts, outs):
            store_partials([part], count, out_ref)
    if tokened:
        refs[-1][...] = jnp.zeros_like(refs[-1])


def partials(weights, after, chunk, rows, count, tokened=1, spare=0):
    hidden, width = weights.shape[1:]
    kinds = kinds_of(chunk)
    total = sum(rows) * hidden * count
    return pl.pallas_call(
        functools.partial(partial_kernel, kinds, count, tokened),
        in_specs=[whole(), unread()] + [whole()] * len(kinds),
        out_specs=[whole()] * (len(rows) + tokened),
        out_shape=[jax.ShapeDtypeStruct((k * hidden + spare, count), jnp.bfloat16) for k in rows]
        + [jax.ShapeDtypeStruct((8, 128), jnp.float32)] * tokened,
        compiler_params=params(),
        cost_estimate=cost(2 * total * width, 6 * total),
    )(weights, after, *values_of(chunk))


def gate_row(gates):
    rows = []
    expert = expert_here()
    for held in gates:
        held = held.astype(jnp.float32)
        index = lax.broadcasted_iota(jnp.int32, held.shape, 0)
        rows.append(jnp.sum(jnp.where(index == expert, held, 0.0), 0, keepdims=True))
    return rows[0] if len(rows) == 1 else jnp.concatenate(rows, 1)


def summed(pairs):
    parts = []
    for own, *got in pairs:
        part = own[...].astype(jnp.float32)
        parts.append(part + got[0][...].astype(jnp.float32) if got else part)
    return parts[0] if len(parts) == 1 else jnp.concatenate(parts, 0)


def beside(total, hidden, firsts):
    parts = [total[first * hidden : (first + 1) * hidden] for first in firsts]
    return jnp.concatenate(parts, 1)


def activation(hg, hu, gate):
    sig = jax.nn.sigmoid(hg)
    silu = hg * sig
    return sig, silu, (gate * (silu * hu)).astype(jnp.bfloat16)


def hidden_slopes(hg, hu, sig, silu, dact):
    dhg = (dact * hu * sig * (1.0 + hg * (1.0 - sig))).astype(jnp.bfloat16)
    dhu = (dact * silu).astype(jnp.bfloat16)
    return dhg, dhu


def hidden_grads(gate, pairs):
    total = summed(pairs)
    blocks = gate.shape[1] // total.shape[1]
    hidden = total.shape[0] // (3 * blocks)
    hg = beside(total, hidden, range(0, 2 * blocks, 2))
    hu = beside(total, hidden, range(1, 2 * blocks, 2))
    dact = gate * beside(total, hidden, range(2 * blocks, 3 * blocks))
    sig, silu, act = activation(hg, hu, gate)
    return (*hidden_slopes(hg, hu, sig, silu, dact), act)


def plain(left, right):
    return lax.dot_general(
        left, right, (((1,), (0,)), ((), ())), preferred_element_type=jnp.float32
    )


def onward_kernel(kinds, after_ref, own, got, near_own, near_got, *refs):
    x0_ref, x1_ref, s0_ref, y0_ref, y1_ref = refs[:5]
    pair_ref, rest_ref, out_ref, first_ref, sum_ref, gate_ref = refs[6 + len(kinds) :]
    count, rows = x0_ref.shape[0], y0_ref.shape[0]
    gates = views(refs[5 : 5 + len(kinds)], kinds, count)[2]
    gate_ref[...] = jnp.broadcast_to(gate_row(gates), gate_ref.shape)
    pair_ref[0] = x0_ref[...]
    pair_ref[1] = s0_ref[...]
    rest_ref[0:count, :] = x1_ref[...]
    rest_ref[count : count + rows, :] = y0_ref[...]
    rest_ref[count + rows :, :] = y1_ref[...]
    out_ref[0:count, :] = x0_ref[...]
    out_ref[count:, :] = y0_ref[...]
    used = first_ref.shape[0]
    first_ref[...] = own[0:used, :].astype(jnp.float32) + got[0:used, :].astype(jnp.float32)
    sum_ref[...] = near_own[...].astype(jnp.float32) + near_got[...].astype(jnp.float32)


def pick_onward(after, pair, near_pair, near_x, other_x, near_y, chunk, held):
    count, width = other_x.shape
    rows = near_y[0].shape[0]
    operands = [*pair, *near_pair, *near_x, other_x, *near_y, *values_of(chunk), held]
    return pl.pallas_call(
        functools.partial(onward_kernel, kinds_of(chunk)),
        in_specs=[unread()] + [whole()] * len(operands),
        out_specs=[whole()] * 6,
        out_shape=[
            jax.ShapeDtypeStruct((2, count, width), jnp.bfloat16),
            jax.ShapeDtypeStruct((count + 2 * rows, width), jnp.bfloat16),
            jax.ShapeDtypeStruct((count + rows, width), jnp.bfloat16),
            jax.ShapeDtypeStruct((3 * near_pair[0].shape[0], count), jnp.float32),
            jax.ShapeDtypeStruct(near_pair[0].shape, jnp.float32),
            jax.ShapeDtypeStruct((8, 2 * count), jnp.float32),
        ],
        compiler_params=params(),
        cost_estimate=cost(1000, 8 * other_x.size),
    )(after, *operands)


def pass_kernel(after_ref, in_ref, *outs):
    row = 0
    for out_ref in outs:
        out_ref[...] = in_ref[row : row + out_ref.shape[0], :]
        row = row + out_ref.shape[0]


def passed_on(after, value, cuts):
    width = value.shape[1]
    return pl.pallas_call(
        pass_kernel,
        in_specs=[unread(), whole()],
        out_specs=[whole()] * len(cuts),
        out_shape=[jax.ShapeDtypeStruct((rows, width), value.dtype) for rows in cuts],
        compiler_params=params(),
        cost_estimate=cost(1000, 2 * value.size),
    )(after, value)


def first_kernel(kinds, count, gate_ref, after_ref, sum_ref, own, got, *refs):
    n = len(kinds)
    xs, ys, gates = views(refs[:n], kinds, count)
    out_ref, more_ref, token_ref = refs[n:]
    more_ref[...] = summed([(own, got)])
    lefts = hidden_grads(gate_ref[0:1, :], [(sum_ref,)])
    x = joined(xs)
    for m, right in enumerate((x, x, joined(ys))):
        out_ref[m] = plain(lefts[m], right)
    token_ref[...] = jnp.zeros_like(token_ref)


def first_grads(gate, after, total, pair, chunk, hidden, count):
    kinds = kinds_of(chunk)
    width = chunk[0][1].shape[-1]
    return pl.pallas_call(
        functools.partial(first_kernel, kinds, count),
        in_specs=[whole(), unread()] + [whole()] * (3 + len(kinds)),
        out_specs=[whole()] * 3,
        out_shape=[
            jax.ShapeDtypeStruct((3, hidden, width), jnp.float32),
            jax.ShapeDtypeStruct(pair[0].shape, jnp.float32),
            jax.ShapeDtypeStruct((8, 128), jnp.float32),
        ],
        compiler_params=params(),
        cost_estimate=cost(2 * total.size * width, 12 * hidden * width),
    )(gate, after, total, *pair, *values_of(chunk))


def grad_kernel(kinds, count, sum_ref, more_ref, own, got, *refs):
    n = len(kinds)
    xs, ys, gates = views(refs[:n], kinds, count)
    acc_ref, out_ref = refs[n:]
    lefts = hidden_grads(gate_row(gates), [(sum_ref,), (more_ref,), (own, got)])
    x = joined(xs)
    for m, right in enumerate((x, x, joined(ys))):
        out_ref[m] = acc_ref[m] + plain(lefts[m], right)


def add_grads(near_sum, more_sum, pair, chunk, acc, count):
    kinds = kinds_of(chunk)
    mats, hidden, width = acc.shape
    operands = [near_sum, more_sum, *pair, *values_of(chunk), acc]
    return pl.pallas_call(
        functools.partial(grad_kernel, kinds, count),
        in_specs=[whole()] * len(operands),
        out_specs=whole(),
        out_shape=jax.ShapeDtypeStruct(acc.shape, jnp.float32),
        input_output_aliases={len(operands) - 1: 0},
        compiler_params=params(),
        cost_estimate=cost(
            2 * mats * hidden * width * 4 * count, 8 * mats * hidden * width
        ),
    )(*operands)


def adam(grad, first, second):
    moment_one = beta_one * first.astype(jnp.float32) + (1.0 - beta_one) * grad
    moment_two = beta_two * second.astype(jnp.float32) + (1.0 - beta_two) * (grad * grad)
    root = (1.0 / (1.0 - beta_two**step_count)) ** 0.5
    below = moment_two * lax.rsqrt(moment_two) + epsilon / root
    scaled = moment_one * (1.0 / (1.0 - beta_one**step_count) / root)
    step = scaled * pl.reciprocal(below, approx=True)
    return [value.astype(jnp.bfloat16) for value in (moment_one, moment_two, step)]


def far_kernel(kinds, count, w_ref, after_ref, *refs):
    n = len(kinds)
    xs, ys, gates = views(refs[:n], kinds, count)
    outs = refs[n:]
    x, y = joined(xs), joined(ys)
    third = w_ref.shape[1] // len(outs)
    for m, right in enumerate((x, x, y)):
        part = contract_last(w_ref[m], right).astype(jnp.bfloat16)
        for k, out_ref in enumerate(outs):
            for side in (0, 1):
                row = (2 * m + side) * third
                out_ref[row : row + third, :] = part[
                    k * third : (k + 1) * third, side * count : (side + 1) * count
                ]


def far_partials(weights, after, chunk, pieces, count):
    mats, hidden, width = weights.shape
    kinds = kinds_of(chunk)
    rows = 2 * mats * hidden // pieces
    return pl.pallas_call(
        functools.partial(far_kernel, kinds, count),
        in_specs=[whole(), unread()] + [whole()] * len(kinds),
        out_specs=[whole()] * pieces,
        out_shape=[jax.ShapeDtypeStruct((rows, count), jnp.bfloat16)] * pieces,
        compiler_params=params(),
        cost_estimate=cost(4 * mats * hidden * count * width, 12 * mats * hidden * count),
    )(weights, after, *values_of(chunk))


def update_kernel(kinds, count, piece, last, own, got, *refs):
    n = len(kinds)
    acc_ref, first_ref, second_ref = refs[n : n + 3]
    rest = refs[n + 3 :]
    third = own.shape[0] // 6
    copies = []
    if piece > 0:
        done = rest[:3]
        rest = rest[3 + 3 * last :]
        outs, rest = rest[:3], rest[3:]
        sems = rest[-1]
        before = slice((piece - 1) * third, piece * third)
        for k in range(3):
            copies.append(
                pltpu.make_async_copy(done[k], outs[k].at[:, before, :], sems.at[3, k])
            )
            copies[-1].start()
    held = rest[:3]
    xs, ys, gates = views(refs[:n], kinds, count)
    total = summed([(own, got)])
    hg, hu, down = [beside(total, third, (2 * m, 2 * m + 1)) for m in range(3)]
    gate = gate_row(gates)
    sig, silu, act = activation(hg, hu, gate)
    lefts = (*hidden_slopes(hg, hu, sig, silu, gate * down), act)
    x = joined(xs)
    rows = slice(piece * third, (piece + 1) * third)
    for m, right in enumerate((x, x, joined(ys))):
        grad = acc_ref[m, rows, :] + plain(lefts[m], right)
        for k, value in enumerate(adam(grad, first_ref[m, rows, :], second_ref[m, rows, :])):
            held[k][m] = value
            if last:
                copies.append(
                    pltpu.make_async_copy(held[k].at[m], outs[k].at[m, rows, :], sems.at[m, k])
                )
                copies[-1].start()
    for copy in copies:
        copy.wait()


def update_piece(piece, last, pair, chunk, acc, moments, done, whole_outs, count):
    kinds = kinds_of(chunk)
    mats, hidden, width = acc.shape
    third = pair[0].shape[0] // 6
    operands = [*pair, *values_of(chunk), acc, *moments, *done]
    in_specs = [whole()] * len(operands) + [unread()] * len(whole_outs)
    large = [jax.ShapeDtypeStruct(acc.shape, jnp.bfloat16)] * 3
    small = [jax.ShapeDtypeStruct((mats, third, width), jnp.bfloat16)] * 3
    scratch = [pltpu.VMEM((mats, third, width), jnp.bfloat16)] * 3
    return pl.pallas_call(
        functools.partial(update_kernel, kinds, count, piece, last),
        in_specs=in_specs,
        out_specs=([in_hbm()] * 3 if piece else []) + ([] if last else [whole()] * 3),
        out_shape=(large if piece else []) + ([] if last else small),
        input_output_aliases={len(operands) + k: k for k in range(3)} if last else {},
        scratch_shapes=(scratch if last else [])
        + ([pltpu.SemaphoreType.DMA((mats + 1, 3))] if piece else []),
        compiler_params=params(),
        cost_estimate=cost(4 * mats * third * width * count, 14 * mats * third * width),
    )(*operands, *whole_outs)


def from_masked(value, axis, mask):
    pairs = [(source, source ^ mask) for source in range(lax.axis_size(axis))]
    return lax.ppermute(value, axis, pairs)


def dense_plan(tokens, cotangent, expert_ids, gate_probs, weights, first_moment, second_moment):
    n_data = lax.axis_size("dp")
    slices = min(4, lax.axis_size("expert") // 2)
    experts_total = lax.axis_size("expert") // (2 * slices) * n_data
    count = tokens.shape[0]
    hidden, width = weights.shape[1:]
    slots = -(-experts_total // 16) * 16
    other = lambda value: from_masked(value, "dp", 1)
    partner = lambda value: from_masked(value, "expert", 1)
    x_own, y_own, own, weights = pack_own(
        expert_ids, gate_probs, tokens, cotangent, weights, slots
    )
    first = [("xy", own), ("xy", other(own))]
    send, token = partials(weights, own, first, (6,), count, 1, 16)
    first_pair = (send, partner(send))
    along = [[(p, p ^ (2 if p % 2 == k else 4)) for p in range(n_data)] for k in (0, 1)]
    near_x = [lax.ppermute(x_own, "dp", pairs) for pairs in along]
    near_y = [lax.ppermute(y_own, "dp", pairs) for pairs in along]
    other_x = other(near_x[0])
    send, token = partials(weights, token, [("x", near_x[0])], (2,), count)
    near_pair = (send, partner(send))
    early = [("x", near_x[1]), ("x", other_x)]
    early_send, token = partials(weights, token, early, (4,), count)
    x_pair, rest, picked, first_sum, near_sum, gate = pick_onward(
        token, first_pair, near_pair, near_x, other_x, near_y, first, early_send
    )
    far = lax.ppermute(picked, "dp", along[1])
    rest_other = other(rest)
    late = [("y, y of xyy", rest), ("x, y, y", rest_other)]
    early_pair = (early_send, partner(early_send))
    send, token = partials(weights, picked, late, (6,), count)
    late_pair = (send, partner(send))
    pieces = passed_on(token, far, (count // 2, count // 2, count // 2, count // 2 + slots))
    acc, early_sum, token = first_grads(
        gate, pieces[0], first_sum, early_pair, first, hidden, count
    )
    pieces = [*pieces, *[other(value) for value in pieces]]
    final = list(zip(("x", "x", "y", "half y, gates") * 2, pieces))
    sends = far_partials(weights, token, final, 3, count)
    pairs = [(send, partner(send)) for send in sends]
    near = [("first x", x_pair), ("x, y, y", rest), ("second x", x_pair), ("x, y, y", rest_other)]
    acc = add_grads(near_sum, early_sum, late_pair, near, acc, count)
    moments = (first_moment, second_moment)
    done = update_piece(0, False, pairs[0], final, acc, moments, (), (), count)
    outs = update_piece(1, False, pairs[1], final, acc, moments, done, (), count)
    outs = update_piece(2, True, pairs[2], final, acc, moments, outs[3:], outs[:3], count)
    return tuple(outs)


def per_device(tokens, cotangent, expert_ids, gate_probs, weights, first_moment, second_moment):
    n_expert = lax.axis_size("expert")
    n_data = lax.axis_size("dp")
    slices = min(4, n_expert // 2)
    experts_total = n_expert // (2 * slices) * n_data
    half = tokens.shape[0] // 2
    dense = 2 * half * expert_ids.shape[1] // experts_total >= half
    plan = dense_plan if dense and n_data == 8 else routed_plan
    return plan(
        tokens, cotangent, expert_ids, gate_probs, weights, first_moment, second_moment
    )


def solution(mesh):
    in_specs = (
        P("dp", None),
        P("dp", None),
        P("dp", None),
        P("dp", None),
        P(None, "dp", "expert"),
        P(None, "dp", "expert"),
        P(None, "dp", "expert"),
    )
    out_specs = (P(None, "dp", "expert"), P(None, "dp", "expert"), P(None, "dp", "expert"))
    return jax.shard_map(
        per_device, mesh=mesh, in_specs=in_specs, out_specs=out_specs, check_vma=False
    )
```

```python
import functools

import jax
import jax.numpy as jnp
from jax import lax
from jax.experimental import pallas as pl
from jax.experimental.pallas import tpu as pltpu
from jax.sharding import PartitionSpec as P

beta_one = 0.9
beta_two = 0.95
step_count = 10
epsilon = 1e-08


def from_partner(value, axis, distance):
    mask = 2**distance
    pairs = [(source, source ^ mask) for source in range(lax.axis_size(axis))]
    return lax.ppermute(value, axis, pairs)


def contract_last(left, right):
    return lax.dot_general(
        left, right, (((1,), (1,)), ((), ())), preferred_element_type=jnp.float32
    )


def contract_first(left, right):
    return lax.dot_general(
        left, right, (((0,), (0,)), ((), ())), preferred_element_type=jnp.float32
    )


def split_halves(grad, replica, width_half):
    keep = lax.dynamic_slice_in_dim(grad, replica * width_half, width_half, grad.ndim - 1)
    give = lax.dynamic_slice_in_dim(grad, (1 - replica) * width_half, width_half, grad.ndim - 1)
    return (keep, give)


def route_block(block_ids, block_gates, group, n_data, capacity):
    count = block_ids.shape[0]
    top = block_ids.shape[1]
    target = block_ids - group * n_data
    inside = block_ids // n_data == group
    onehot = (
        (target[:, :, None] == jnp.arange(n_data, dtype=jnp.int32)[None, None, :])
        & inside[:, :, None]
    ).astype(jnp.int32)
    per_token = jnp.sum(onehot, axis=1)
    earlier = jnp.cumsum(per_token, axis=0) - per_token
    rank = jnp.sum(onehot * earlier[:, None, :], axis=2)
    total_slots = n_data * capacity
    slot = jnp.where(inside, target * capacity + rank, total_slots).reshape(-1)
    token_of = jnp.broadcast_to(jnp.arange(count, dtype=jnp.int32)[:, None], (count, top)).reshape(
        -1
    )
    table = jnp.full((total_slots,), count, jnp.int32).at[slot].set(token_of, mode="drop")
    gate_slot = (
        jnp.zeros((total_slots,), jnp.bfloat16).at[slot].set(block_gates.reshape(-1), mode="drop")
    )
    return (table, gate_slot)


def routed_plan(tokens, cotangent, expert_ids, gate_probs, weights, first_moment, second_moment):
    n_expert = lax.axis_size("expert")
    n_data = lax.axis_size("dp")
    slices = min(4, n_expert // 2)
    place = lax.axis_index("expert")
    replica = place % 2
    group = place // (2 * slices)
    groups = n_expert // (2 * slices)
    experts_total = groups * n_data
    half = tokens.shape[0] // 2
    width_half = weights.shape[2]
    top = expert_ids.shape[1]
    capacity = max(2, 2 * half * top // experts_total)
    start = replica * half
    own_ids = lax.dynamic_slice_in_dim(expert_ids, start, half, 0)
    own_gates = lax.dynamic_slice_in_dim(gate_probs, start, half, 0)
    table, gate_slot = route_block(own_ids, own_gates, group, n_data, capacity)
    source_tokens = lax.dynamic_slice_in_dim(tokens, start, half, 0)
    source_cot = lax.dynamic_slice_in_dim(cotangent, start, half, 0)
    columns = source_tokens.shape[1]
    padded_tokens = jnp.concatenate([source_tokens, jnp.zeros((1, columns), jnp.bfloat16)], 0)
    padded_cot = jnp.concatenate([source_cot, jnp.zeros((1, columns), jnp.bfloat16)], 0)
    send_rows = padded_tokens[table].reshape(n_data, -1, columns)
    send_cot = padded_cot[table].reshape(n_data, -1, columns)
    send_gates = gate_slot.reshape(n_data, -1)
    rows_in, gates_in = (
        lax.all_to_all(send_rows, "dp", split_axis=0, concat_axis=0, tiled=True),
        lax.all_to_all(send_gates, "dp", split_axis=0, concat_axis=0, tiled=True),
    )
    rows = rows_in.reshape(-1, columns)
    gate_rows = gates_in.reshape(-1).astype(jnp.float32)
    partner = from_partner(weights, "expert", 0)
    lower = jnp.where(replica == 0, weights, partner)
    upper = jnp.where(replica == 0, partner, weights)
    full = jnp.concatenate([lower, upper], 2)
    hg = contract_last(rows, full[0])
    hu = contract_last(rows, full[1])
    sig = jax.nn.sigmoid(hg)
    act = (hg * sig * hu).astype(jnp.bfloat16)
    cot_in = lax.all_to_all(send_cot, "dp", split_axis=0, concat_axis=0, tiled=True)
    cots = cot_in.reshape(-1, columns)
    dz = (gate_rows[:, None] * cots.astype(jnp.float32)).astype(jnp.bfloat16)
    dact = contract_last(dz, full[2])
    grad_down = contract_first(act, dz)
    dhg = (dact * hu * sig * (1.0 + hg * (1.0 - sig))).astype(jnp.bfloat16)
    dhu = (dact * hg * sig).astype(jnp.bfloat16)
    grad_gate = contract_first(dhg, rows)
    grad_up = contract_first(dhu, rows)
    stacked = jnp.stack([grad_gate, grad_up, grad_down])
    keep, give = split_halves(stacked, replica, width_half)
    total = keep + from_partner(give, "expert", 0)
    moment_one = beta_one * first_moment.astype(jnp.float32) + (1.0 - beta_one) * total
    moment_two = beta_two * second_moment.astype(jnp.float32) + (1.0 - beta_two) * total * total
    step = (
        moment_one
        / (1.0 - beta_one**step_count)
        / (jnp.sqrt(moment_two / (1.0 - beta_two**step_count)) + epsilon)
    )
    return (
        moment_one.astype(jnp.bfloat16),
        moment_two.astype(jnp.bfloat16),
        step.astype(jnp.bfloat16),
    )


VMEM_LIMIT = 16 * 1024 * 1024


def params():
    return pltpu.CompilerParams(vmem_limit_bytes=VMEM_LIMIT)


def cost(flops, moved):
    return pl.CostEstimate(flops=flops, bytes_accessed=moved, transcendentals=0)


def whole():
    return pl.BlockSpec(memory_space=pltpu.VMEM)


def in_hbm():
    return pl.BlockSpec(memory_space=pltpu.HBM)


def unread():
    return pl.BlockSpec(memory_space=pl.ANY)


def expert_here():
    slices = min(4, lax.axis_size("expert") // 2)
    group = lax.axis_index("expert") // (2 * slices)
    return group * lax.axis_size("dp") + lax.axis_index("dp")


def keep_hbm(value):
    return pltpu.with_memory_space_constraint(value, pltpu.HBM)


def pack_kernel(
    ids_hbm,
    gates_hbm,
    tokens_ref,
    cot_ref,
    w_hbm,
    x_ref,
    y_ref,
    own_ref,
    w_ref,
    ids_ref,
    gates_ref,
    sems,
):
    count = tokens_ref.shape[0]
    width = x_ref.shape[1]
    columns = pl.ds(pl.multiple_of(lax.axis_index("expert") % 2 * width, width), width)
    copies = [
        pltpu.make_async_copy(ids_hbm, ids_ref, sems.at[0]),
        pltpu.make_async_copy(gates_hbm, gates_ref, sems.at[1]),
        pltpu.make_async_copy(tokens_ref.at[:, columns], x_ref, sems.at[2]),
        pltpu.make_async_copy(cot_ref.at[:, columns], y_ref.at[0:count, :], sems.at[3]),
        pltpu.make_async_copy(tokens_ref.at[:, columns], own_ref.at[0:count, :], sems.at[4]),
        pltpu.make_async_copy(cot_ref.at[:, columns], own_ref.at[count : 2 * count, :], sems.at[5]),
        *[pltpu.make_async_copy(w_hbm.at[m], w_ref.at[m], sems.at[6 + m]) for m in range(3)],
    ]
    for copy in copies:
        copy.start()
    copies[0].wait()
    copies[1].wait()
    ids = ids_ref[...]
    gates = gates_ref[...].astype(jnp.float32)
    slots = y_ref.shape[0] - count
    row = lax.broadcasted_iota(jnp.int32, (slots, count), 0)
    gate = jnp.zeros((slots, count), jnp.float32)
    for k in range(ids.shape[0]):
        gate = gate + jnp.where(row == ids[k : k + 1, :], gates[k : k + 1, :], 0.0)
    y_ref[count:, 0:count] = gate.astype(jnp.bfloat16)
    y_ref[count:, count:] = jnp.zeros((slots, width - count), jnp.bfloat16)
    own_ref[2 * count :, :] = y_ref[count:, :]
    for copy in copies[2:]:
        copy.wait()


def pack_own(ids, gates, tokens, cotangent, weights, slots):
    count, top = ids.shape
    width = weights.shape[2]
    return pl.pallas_call(
        pack_kernel,
        in_specs=[in_hbm()] * 5,
        out_specs=[whole()] * 4,
        out_shape=[
            jax.ShapeDtypeStruct((rows, width), jnp.bfloat16)
            for rows in (count, count + slots, 2 * count + slots)
        ]
        + [jax.ShapeDtypeStruct(weights.shape, weights.dtype)],
        scratch_shapes=[
            pltpu.VMEM((top, count), ids.dtype),
            pltpu.VMEM((top, count), gates.dtype),
            pltpu.SemaphoreType.DMA((9,)),
        ],
        compiler_params=params(),
        cost_estimate=cost(1000, 8 * count * width),
    )(*[keep_hbm(value) for value in (ids.T, gates.T, tokens, cotangent, weights)])


def views(refs, kinds, count):
    xs, ys, gates = [], [], []
    for ref, kind in zip(refs, kinds):
        if kind in ("first x", "second x"):
            xs.append(ref[0 if kind == "first x" else 1])
            continue
        if kind == "x of xyy":
            xs.append(ref[0:count, :])
            continue
        if kind in ("x, y, y", "y, y of xyy"):
            rows = (ref.shape[0] - count) // 2
            if kind == "x, y, y":
                xs.append(ref[0:count, :])
            for row in (count, count + rows):
                ys.append(ref[row : row + count, :])
                gates.append(ref[row + count : row + rows, 0:count])
            continue
        for part in [ref.at[0], ref.at[1]] if ref.ndim == 3 else [ref]:
            if kind == "x":
                xs.append(part[...])
            if kind == "xy":
                xs.append(part[0:count, :])
                ys.append(part[count : 2 * count, :])
                gates.append(part[2 * count :, 0:count])
            if kind == "y":
                ys.append(part[...])
            if kind == "y, gates":
                ys.append(part[0:count, :])
                gates.append(part[count:, 0:count])
            if kind == "half y, gates":
                ys.append(part[0 : count // 2, :])
                gates.append(part[count // 2 :, 0:count])
    return xs, ys, gates


def joined(parts):
    return parts[0] if len(parts) == 1 else jnp.concatenate(parts, 0)


def kinds_of(chunk):
    return tuple(kind for kind, value in chunk)


def values_of(chunk):
    return [value for kind, value in chunk]


def store_partials(parts, count, out_ref):
    row = 0
    used = sum(part.size for part in parts) // count
    if used < out_ref.shape[0]:
        out_ref[used:, :] = jnp.zeros((out_ref.shape[0] - used, count), jnp.bfloat16)
    for part in parts:
        for first in range(0, part.shape[1], count):
            piece = part[:, first : first + count]
            out_ref[row : row + piece.shape[0], :] = piece.astype(jnp.bfloat16)
            row = row + piece.shape[0]


def partial_kernel(kinds, count, tokened, w_ref, after_ref, *refs):
    n = len(kinds)
    xs, ys, gates = views(refs[:n], kinds, count)
    outs = refs[n : len(refs) - tokened]
    mats, hidden, width = w_ref.shape
    parts = []
    if xs and len(outs) == mats:
        parts.extend(contract_last(w_ref[m], joined(xs)) for m in (0, 1))
    elif xs:
        parts.append(contract_last(w_ref[0:2].reshape(2 * hidden, width), joined(xs)))
    if ys:
        parts.append(contract_last(w_ref[2], joined(ys)))
    if len(outs) == 1:
        store_partials(parts, count, outs[0])
    else:
        for part, out_ref in zip(parts, outs):
            store_partials([part], count, out_ref)
    if tokened:
        refs[-1][...] = jnp.zeros_like(refs[-1])


def partials(weights, after, chunk, rows, count, tokened=1, spare=0):
    hidden, width = weights.shape[1:]
    kinds = kinds_of(chunk)
    total = sum(rows) * hidden * count
    return pl.pallas_call(
        functools.partial(partial_kernel, kinds, count, tokened),
        in_specs=[whole(), unread()] + [whole()] * len(kinds),
        out_specs=[whole()] * (len(rows) + tokened),
        out_shape=[jax.ShapeDtypeStruct((k * hidden + spare, count), jnp.bfloat16) for k in rows]
        + [jax.ShapeDtypeStruct((8, 128), jnp.float32)] * tokened,
        compiler_params=params(),
        cost_estimate=cost(2 * total * width, 6 * total),
    )(weights, after, *values_of(chunk))


def gate_row(gates):
    rows = []
    expert = expert_here()
    for held in gates:
        held = held.astype(jnp.float32)
        index = lax.broadcasted_iota(jnp.int32, held.shape, 0)
        rows.append(jnp.sum(jnp.where(index == expert, held, 0.0), 0, keepdims=True))
    return rows[0] if len(rows) == 1 else jnp.concatenate(rows, 1)


def summed(pairs):
    parts = []
    for own, *got in pairs:
        part = own[...].astype(jnp.float32)
        parts.append(part + got[0][...].astype(jnp.float32) if got else part)
    return parts[0] if len(parts) == 1 else jnp.concatenate(parts, 0)


def beside(total, hidden, firsts):
    parts = [total[first * hidden : (first + 1) * hidden] for first in firsts]
    return jnp.concatenate(parts, 1)


def activation(hg, hu, gate):
    sig = jax.nn.sigmoid(hg)
    silu = hg * sig
    return sig, silu, (gate * (silu * hu)).astype(jnp.bfloat16)


def hidden_slopes(hg, hu, sig, silu, dact):
    dhg = (dact * hu * sig * (1.0 + hg * (1.0 - sig))).astype(jnp.bfloat16)
    dhu = (dact * silu).astype(jnp.bfloat16)
    return dhg, dhu


def hidden_grads(gate, pairs):
    total = summed(pairs)
    blocks = gate.shape[1] // total.shape[1]
    hidden = total.shape[0] // (3 * blocks)
    hg = beside(total, hidden, range(0, 2 * blocks, 2))
    hu = beside(total, hidden, range(1, 2 * blocks, 2))
    dact = gate * beside(total, hidden, range(2 * blocks, 3 * blocks))
    sig, silu, act = activation(hg, hu, gate)
    return (*hidden_slopes(hg, hu, sig, silu, dact), act)


def plain(left, right):
    return lax.dot_general(
        left, right, (((1,), (0,)), ((), ())), preferred_element_type=jnp.float32
    )


def onward_kernel(kinds, after_ref, own, got, near_own, near_got, *refs):
    x0_ref, x1_ref, s0_ref, y0_ref, y1_ref = refs[:5]
    pair_ref, rest_ref, out_ref, first_ref, sum_ref, gate_ref = refs[6 + len(kinds) :]
    count, rows = x0_ref.shape[0], y0_ref.shape[0]
    gates = views(refs[5 : 5 + len(kinds)], kinds, count)[2]
    gate_ref[...] = jnp.broadcast_to(gate_row(gates), gate_ref.shape)
    pair_ref[0] = x0_ref[...]
    pair_ref[1] = s0_ref[...]
    rest_ref[0:count, :] = x1_ref[...]
    rest_ref[count : count + rows, :] = y0_ref[...]
    rest_ref[count + rows :, :] = y1_ref[...]
    out_ref[0:count, :] = x0_ref[...]
    out_ref[count:, :] = y0_ref[...]
    used = first_ref.shape[0]
    first_ref[...] = own[0:used, :].astype(jnp.float32) + got[0:used, :].astype(jnp.float32)
    sum_ref[...] = near_own[...].astype(jnp.float32) + near_got[...].astype(jnp.float32)


def pick_onward(after, pair, near_pair, near_x, other_x, near_y, chunk, held):
    count, width = other_x.shape
    rows = near_y[0].shape[0]
    operands = [*pair, *near_pair, *near_x, other_x, *near_y, *values_of(chunk), held]
    return pl.pallas_call(
        functools.partial(onward_kernel, kinds_of(chunk)),
        in_specs=[unread()] + [whole()] * len(operands),
        out_specs=[whole()] * 6,
        out_shape=[
            jax.ShapeDtypeStruct((2, count, width), jnp.bfloat16),
            jax.ShapeDtypeStruct((count + 2 * rows, width), jnp.bfloat16),
            jax.ShapeDtypeStruct((count + rows, width), jnp.bfloat16),
            jax.ShapeDtypeStruct((3 * near_pair[0].shape[0], count), jnp.float32),
            jax.ShapeDtypeStruct(near_pair[0].shape, jnp.float32),
            jax.ShapeDtypeStruct((8, 2 * count), jnp.float32),
        ],
        compiler_params=params(),
        cost_estimate=cost(1000, 8 * other_x.size),
    )(after, *operands)


def pass_kernel(after_ref, in_ref, *outs):
    row = 0
    for out_ref in outs:
        out_ref[...] = in_ref[row : row + out_ref.shape[0], :]
        row = row + out_ref.shape[0]


def passed_on(after, value, cuts):
    width = value.shape[1]
    return pl.pallas_call(
        pass_kernel,
        in_specs=[unread(), whole()],
        out_specs=[whole()] * len(cuts),
        out_shape=[jax.ShapeDtypeStruct((rows, width), value.dtype) for rows in cuts],
        compiler_params=params(),
        cost_estimate=cost(1000, 2 * value.size),
    )(after, value)


def first_kernel(kinds, count, gate_ref, after_ref, sum_ref, own, got, *refs):
    n = len(kinds)
    xs, ys, gates = views(refs[:n], kinds, count)
    out_ref, more_ref, token_ref = refs[n:]
    more_ref[...] = summed([(own, got)])
    lefts = hidden_grads(gate_ref[0:1, :], [(sum_ref,)])
    x = joined(xs)
    for m, right in enumerate((x, x, joined(ys))):
        out_ref[m] = plain(lefts[m], right)
    token_ref[...] = jnp.zeros_like(token_ref)


def first_grads(gate, after, total, pair, chunk, hidden, count):
    kinds = kinds_of(chunk)
    width = chunk[0][1].shape[-1]
    return pl.pallas_call(
        functools.partial(first_kernel, kinds, count),
        in_specs=[whole(), unread()] + [whole()] * (3 + len(kinds)),
        out_specs=[whole()] * 3,
        out_shape=[
            jax.ShapeDtypeStruct((3, hidden, width), jnp.float32),
            jax.ShapeDtypeStruct(pair[0].shape, jnp.float32),
            jax.ShapeDtypeStruct((8, 128), jnp.float32),
        ],
        compiler_params=params(),
        cost_estimate=cost(2 * total.size * width, 12 * hidden * width),
    )(gate, after, total, *pair, *values_of(chunk))


def grad_kernel(kinds, count, sum_ref, more_ref, own, got, *refs):
    n = len(kinds)
    xs, ys, gates = views(refs[:n], kinds, count)
    acc_ref, out_ref = refs[n:]
    lefts = hidden_grads(gate_row(gates), [(sum_ref,), (more_ref,), (own, got)])
    x = joined(xs)
    for m, right in enumerate((x, x, joined(ys))):
        out_ref[m] = acc_ref[m] + plain(lefts[m], right)


def add_grads(near_sum, more_sum, pair, chunk, acc, count):
    kinds = kinds_of(chunk)
    mats, hidden, width = acc.shape
    operands = [near_sum, more_sum, *pair, *values_of(chunk), acc]
    return pl.pallas_call(
        functools.partial(grad_kernel, kinds, count),
        in_specs=[whole()] * len(operands),
        out_specs=whole(),
        out_shape=jax.ShapeDtypeStruct(acc.shape, jnp.float32),
        input_output_aliases={len(operands) - 1: 0},
        compiler_params=params(),
        cost_estimate=cost(
            2 * mats * hidden * width * 4 * count, 8 * mats * hidden * width
        ),
    )(*operands)


def adam(grad, first, second):
    moment_one = beta_one * first.astype(jnp.float32) + (1.0 - beta_one) * grad
    moment_two = beta_two * second.astype(jnp.float32) + (1.0 - beta_two) * (grad * grad)
    root = (1.0 / (1.0 - beta_two**step_count)) ** 0.5
    below = moment_two * lax.rsqrt(moment_two) + epsilon / root
    scaled = moment_one * (1.0 / (1.0 - beta_one**step_count) / root)
    step = scaled * pl.reciprocal(below, approx=True)
    return [value.astype(jnp.bfloat16) for value in (moment_one, moment_two, step)]


def far_kernel(kinds, count, w_ref, after_ref, *refs):
    n = len(kinds)
    xs, ys, gates = views(refs[:n], kinds, count)
    outs = refs[n:]
    x, y = joined(xs), joined(ys)
    third = w_ref.shape[1] // len(outs)
    for m, right in enumerate((x, x, y)):
        part = contract_last(w_ref[m], right).astype(jnp.bfloat16)
        for k, out_ref in enumerate(outs):
            for side in (0, 1):
                row = (2 * m + side) * third
                out_ref[row : row + third, :] = part[
                    k * third : (k + 1) * third, side * count : (side + 1) * count
                ]


def far_partials(weights, after, chunk, pieces, count):
    mats, hidden, width = weights.shape
    kinds = kinds_of(chunk)
    rows = 2 * mats * hidden // pieces
    return pl.pallas_call(
        functools.partial(far_kernel, kinds, count),
        in_specs=[whole(), unread()] + [whole()] * len(kinds),
        out_specs=[whole()] * pieces,
        out_shape=[jax.ShapeDtypeStruct((rows, count), jnp.bfloat16)] * pieces,
        compiler_params=params(),
        cost_estimate=cost(4 * mats * hidden * count * width, 12 * mats * hidden * count),
    )(weights, after, *values_of(chunk))


def update_kernel(kinds, count, piece, last, own, got, *refs):
    n = len(kinds)
    acc_ref, first_ref, second_ref = refs[n : n + 3]
    rest = refs[n + 3 :]
    third = own.shape[0] // 6
    copies = []
    if piece > 0:
        done = rest[:3]
        rest = rest[3 + 3 * last :]
        outs, rest = rest[:3], rest[3:]
        sems = rest[-1]
        before = slice((piece - 1) * third, piece * third)
        for k in range(3):
            copies.append(
                pltpu.make_async_copy(done[k], outs[k].at[:, before, :], sems.at[3, k])
            )
            copies[-1].start()
    held = rest[:3]
    xs, ys, gates = views(refs[:n], kinds, count)
    total = summed([(own, got)])
    hg, hu, down = [beside(total, third, (2 * m, 2 * m + 1)) for m in range(3)]
    gate = gate_row(gates)
    sig, silu, act = activation(hg, hu, gate)
    lefts = (*hidden_slopes(hg, hu, sig, silu, gate * down), act)
    x = joined(xs)
    rows = slice(piece * third, (piece + 1) * third)
    for m, right in enumerate((x, x, joined(ys))):
        grad = acc_ref[m, rows, :] + plain(lefts[m], right)
        for k, value in enumerate(adam(grad, first_ref[m, rows, :], second_ref[m, rows, :])):
            held[k][m] = value
            if last:
                copies.append(
                    pltpu.make_async_copy(held[k].at[m], outs[k].at[m, rows, :], sems.at[m, k])
                )
                copies[-1].start()
    for copy in copies:
        copy.wait()


def update_piece(piece, last, pair, chunk, acc, moments, done, whole_outs, count):
    kinds = kinds_of(chunk)
    mats, hidden, width = acc.shape
    third = pair[0].shape[0] // 6
    operands = [*pair, *values_of(chunk), acc, *moments, *done]
    in_specs = [whole()] * len(operands) + [unread()] * len(whole_outs)
    large = [jax.ShapeDtypeStruct(acc.shape, jnp.bfloat16)] * 3
    small = [jax.ShapeDtypeStruct((mats, third, width), jnp.bfloat16)] * 3
    scratch = [pltpu.VMEM((mats, third, width), jnp.bfloat16)] * 3
    return pl.pallas_call(
        functools.partial(update_kernel, kinds, count, piece, last),
        in_specs=in_specs,
        out_specs=([in_hbm()] * 3 if piece else []) + ([] if last else [whole()] * 3),
        out_shape=(large if piece else []) + ([] if last else small),
        input_output_aliases={len(operands) + k: k for k in range(3)} if last else {},
        scratch_shapes=(scratch if last else [])
        + ([pltpu.SemaphoreType.DMA((mats + 1, 3))] if piece else []),
        compiler_params=params(),
        cost_estimate=cost(4 * mats * third * width * count, 14 * mats * third * width),
    )(*operands, *whole_outs)


def from_masked(value, axis, mask):
    pairs = [(source, source ^ mask) for source in range(lax.axis_size(axis))]
    return lax.ppermute(value, axis, pairs)


def dense_plan(tokens, cotangent, expert_ids, gate_probs, weights, first_moment, second_moment):
    n_data = lax.axis_size("dp")
    slices = min(4, lax.axis_size("expert") // 2)
    experts_total = lax.axis_size("expert") // (2 * slices) * n_data
    count = tokens.shape[0]
    hidden, width = weights.shape[1:]
    slots = -(-experts_total // 16) * 16
    other = lambda value: from_masked(value, "dp", 1)
    partner = lambda value: from_masked(value, "expert", 1)
    x_own, y_own, own, weights = pack_own(
        expert_ids, gate_probs, tokens, cotangent, weights, slots
    )
    first = [("xy", own), ("xy", other(own))]
    send, token = partials(weights, own, first, (6,), count, 1, 16)
    first_pair = (send, partner(send))
    along = [[(p, p ^ (2 if p % 2 == k else 4)) for p in range(n_data)] for k in (0, 1)]
    near_x = [lax.ppermute(x_own, "dp", pairs) for pairs in along]
    near_y = [lax.ppermute(y_own, "dp", pairs) for pairs in along]
    other_x = other(near_x[0])
    send, token = partials(weights, token, [("x", near_x[0])], (2,), count)
    near_pair = (send, partner(send))
    early = [("x", near_x[1]), ("x", other_x)]
    early_send, token = partials(weights, token, early, (4,), count)
    x_pair, rest, picked, first_sum, near_sum, gate = pick_onward(
        token, first_pair, near_pair, near_x, other_x, near_y, first, early_send
    )
    far = lax.ppermute(picked, "dp", along[1])
    rest_other = other(rest)
    late = [("y, y of xyy", rest), ("x, y, y", rest_other)]
    early_pair = (early_send, partner(early_send))
    send, token = partials(weights, picked, late, (6,), count)
    late_pair = (send, partner(send))
    pieces = passed_on(token, far, (count // 2, count // 2, count // 2, count // 2 + slots))
    acc, early_sum, token = first_grads(
        gate, pieces[0], first_sum, early_pair, first, hidden, count
    )
    pieces = [*pieces, *[other(value) for value in pieces]]
    final = list(zip(("x", "x", "y", "half y, gates") * 2, pieces))
    sends = far_partials(weights, token, final, 3, count)
    pairs = [(send, partner(send)) for send in sends]
    near = [("first x", x_pair), ("x, y, y", rest), ("second x", x_pair), ("x, y, y", rest_other)]
    acc = add_grads(near_sum, early_sum, late_pair, near, acc, count)
    moments = (first_moment, second_moment)
    done = update_piece(0, False, pairs[0], final, acc, moments, (), (), count)
    outs = update_piece(1, False, pairs[1], final, acc, moments, done, (), count)
    outs = update_piece(2, True, pairs[2], final, acc, moments, outs[3:], outs[:3], count)
    return tuple(outs)


def per_device(tokens, cotangent, expert_ids, gate_probs, weights, first_moment, second_moment):
    n_expert = lax.axis_size("expert")
    n_data = lax.axis_size("dp")
    slices = min(4, n_expert // 2)
    experts_total = n_expert // (2 * slices) * n_data
    half = tokens.shape[0] // 2
    dense = 2 * half * expert_ids.shape[1] // experts_total >= half
    plan = dense_plan if dense and n_data == 8 else routed_plan
    return plan(
        tokens, cotangent, expert_ids, gate_probs, weights, first_moment, second_moment
    )


def solution(mesh):
    in_specs = (
        P("dp", None),
        P("dp", None),
        P("dp", None),
        P("dp", None),
        P(None, "dp", "expert"),
        P(None, "dp", "expert"),
        P(None, "dp", "expert"),
    )
    out_specs = (P(None, "dp", "expert"), P(None, "dp", "expert"), P(None, "dp", "expert"))
    return jax.shard_map(
        per_device, mesh=mesh, in_specs=in_specs, out_specs=out_specs, check_vma=False
    )
```
